32 devices in a mesh: ens: 4 (over y, x), lat: 2 (over core), lon: 4 (over z).
Axes of the slice: x: 2, y: 2, z: 4, core: 2. Of those that a mesh axis runs over, the one named last changes fastest.
Arguments:
- state: bfloat16 [2, 72, 8, 1024], P(None, None, 'lat', 'lon'), may hold values from -6 to 6
- noise_field: bfloat16 [4, 8, 8, 1024], P('ens', None, 'lat', 'lon'), may hold values from -6 to 6
- cotangent: bfloat16 [4, 72, 8, 1024], P('ens', None, 'lat', 'lon'), may hold values from -6 to 6
- slot_date: int32 [4], P('ens'), may hold values from -1 to 1, as said below
- lon_reach: int32 [4], replicated, may hold values from 1 to 2
- enc_taps: float32 [3, 4, 25], replicated, may hold values from -1.2 to 1.2
- proc_taps: float32 [3, 4, 25], replicated, may hold values from -1.2 to 1.2
- dec_taps: float32 [3, 8, 9], replicated, may hold values from -1.2 to 1.2
- enc_weight: bfloat16 [3, 641, 80], replicated, may hold values from -0.375 to 0.375
- enc_bias: float32 [641], replicated, may hold values from -1.5 to 1.5
- gain_one: float32 [641], replicated, may hold values from 0.25 to 1.75
- shift_one: float32 [641], replicated, may hold values from -1.5 to 1.5
- proc_weight: bfloat16 [3, 641, 641], replicated, may hold values from -0.125 to 0.125
- proc_bias: float32 [641], replicated, may hold values from -1.5 to 1.5
- gain_two: float32 [641], replicated, may hold values from 0.25 to 1.75
- shift_two: float32 [641], replicated, may hold values from -1.5 to 1.5
- up_weight: bfloat16 [1282, 641], replicated, may hold values from -0.25 to 0.25
- up_bias: float32 [1282], replicated, may hold values from -1.5 to 1.5
- down_weight: bfloat16 [641, 1282], replicated, may hold values from -0.15625 to 0.15625
- down_bias: float32 [641], replicated, may hold values from -1.5 to 1.5
- dec_weight: bfloat16 [3, 72, 641], replicated, may hold values from -0.25 to 0.25
- dec_bias: float32 [72], replicated, may hold values from -1.5 to 1.5
Outputs:
- output: bfloat16 [4, 72, 8, 1024], P('ens', None, 'lat', 'lon')
- state_grad: bfloat16 [2, 72, 8, 1024], P(None, None, 'lat', 'lon')
- enc_weight_grad: float32 [3, 641, 80], replicated
- enc_bias_grad: float32 [641], replicated
- gain_one_grad: float32 [641], replicated
- shift_one_grad: float32 [641], replicated
- proc_weight_grad: float32 [3, 641, 641], replicated
- proc_bias_grad: float32 [641], replicated
- gain_two_grad: float32 [641], replicated
- shift_two_grad: float32 [641], replicated
- up_weight_grad: float32 [1282, 641], replicated
- up_bias_grad: float32 [1282], replicated
- down_weight_grad: float32 [641, 1282], replicated
- down_bias_grad: float32 [641], replicated
- dec_weight_grad: float32 [3, 72, 641], replicated
- dec_bias_grad: float32 [72], replicated
- mean_one: float32 [4, 641], P('ens')
- var_one: float32 [4, 641], P('ens')
- mean_two: float32 [4, 641], P('ens')
- var_two: float32 [4, 641], P('ens')
The draws below stay inside these ranges and needn't reach their ends.
Inputs may be any that keep to these rules, and one draw needn't show every extreme that they name: `slot_date`: exactly 1 slots hold date 0 and exactly 2 hold date 1; the other slots hold -1. Which slots is drawn.
All inputs are finite; a program needn't handle non-finite values.
Results may differ from the reference program's by a relative error of at most 0.014.
Values may be sent and summed in bfloat16 or wider, within the bound.
A program may use at most 128 MiB of HBM per device.

```python
import jax
import jax.numpy as jnp
import numpy as np
from jax import lax

C = 641
FF = 1282
CIN = 72
NOISE = 8
NB = 3
DATES = 2
MEM0 = 1
MEM1 = 2
SLOTS_ALL = 4
NLATH = 4
NLONH = 512
NLAT = 8
NLON = 1024


def draw_state(key, part):
    key = jax.random.fold_in(key, 11)
    latitude = jnp.arange(NLAT).astype(jnp.float32) / NLAT
    shape = (DATES, CIN, NLAT, NLON)
    base = jnp.clip(jax.random.normal(key, shape, jnp.float32), -4.0, 4.0)
    factor = 0.5 + latitude
    values = base * factor[None, None, :, None]
    return values.astype(jnp.bfloat16)


def draw_slot_date(key, part):
    key = jax.random.fold_in(key, 12)
    order = jax.random.permutation(key, SLOTS_ALL)
    dates = jnp.where(order < MEM0, 0, jnp.where(order < MEM0 + MEM1, 1, -1))
    return dates.astype(jnp.int32)


def draw_lon_reach(key, part):
    key = jax.random.fold_in(key, 13)
    reach_rows = jax.random.randint(key, (NLATH,), 1, 3)
    reach_rows = reach_rows.at[0].set(2).at[NLATH - 1].set(1)
    return reach_rows.astype(jnp.int32)


def block_scale(rng, shape, cuts, least, high):
    loudness, own = 1.0, jax.random.fold_in(rng, 6)
    for axis_at, parts in cuts:
        heights = jnp.exp(jax.random.uniform(jax.random.fold_in(own, axis_at), (parts,), jnp.float32, least / len(cuts), high / len(cuts)))
        loudness = loudness * jnp.repeat(heights, shape[axis_at] // parts).reshape([-1 if axis == axis_at else 1 for axis in range(len(shape))])
    return loudness


def bell_draw(rng, shape, scale, reach, cuts=(), kind=jnp.bfloat16):
    level = block_scale(rng, shape, cuts, -0.22, 0.18) if cuts else 1.0
    drawn = jax.random.normal(rng, shape, jnp.float32) * scale * level
    return jnp.minimum(jnp.maximum(drawn, -reach), reach).astype(kind)


def setup_inputs(seed: int = 0) -> dict:
    arg_keys = jax.random.split(jax.random.key(seed), 23)
    return {
        "state": draw_state(jax.random.fold_in(arg_keys[22], 71), 0),
        "noise_field": bell_draw(arg_keys[1], (SLOTS_ALL, NOISE, NLAT, NLON), 1.0, 6.0, ((0, 4), (2, 2), (3, 4))),
        "cotangent": bell_draw(arg_keys[2], (SLOTS_ALL, CIN, NLAT, NLON), 1.0, 6.0, ((0, 4), (2, 2), (3, 4))),
        "slot_date": draw_slot_date(jax.random.fold_in(arg_keys[22], 71), 0),
        "lon_reach": draw_lon_reach(jax.random.fold_in(arg_keys[22], 71), 0),
        "enc_taps": bell_draw(arg_keys[5], (NB, NLATH, 25), 0.2, 1.2, (), jnp.float32),
        "proc_taps": bell_draw(arg_keys[6], (NB, NLATH, 25), 0.2, 1.2, (), jnp.float32),
        "dec_taps": bell_draw(arg_keys[7], (NB, NLAT, 9), 0.2, 1.2, (), jnp.float32),
        "enc_weight": bell_draw(arg_keys[8], (NB, C, CIN + NOISE), (NB * (CIN + NOISE)) ** -0.5, 0.375),
        "enc_bias": bell_draw(arg_keys[9], (C,), 0.3, 1.5, (), jnp.float32),
        "gain_one": jnp.clip(1.0 + 0.15 * jax.random.normal(arg_keys[10], (C,), jnp.float32), 0.25, 1.75),
        "shift_one": bell_draw(arg_keys[11], (C,), 0.3, 1.5, (), jnp.float32),
        "proc_weight": bell_draw(arg_keys[12], (NB, C, C), (NB * C) ** -0.5, 0.125),
        "proc_bias": bell_draw(arg_keys[13], (C,), 0.3, 1.5, (), jnp.float32),
        "gain_two": jnp.clip(1.0 + 0.15 * jax.random.normal(arg_keys[14], (C,), jnp.float32), 0.25, 1.75),
        "shift_two": bell_draw(arg_keys[15], (C,), 0.3, 1.5, (), jnp.float32),
        "up_weight": bell_draw(arg_keys[16], (FF, C), C ** -0.5, 0.25),
        "up_bias": bell_draw(arg_keys[17], (FF,), 0.3, 1.5, (), jnp.float32),
        "down_weight": bell_draw(arg_keys[18], (C, FF), FF ** -0.5, 0.15625),
        "down_bias": bell_draw(arg_keys[19], (C,), 0.3, 1.5, (), jnp.float32),
        "dec_weight": bell_draw(arg_keys[20], (NB, CIN, C), C ** -0.5, 0.25),
        "dec_bias": bell_draw(arg_keys[21], (CIN,), 0.3, 1.5, (), jnp.float32),
    }


epsilon = 1e-05
highest = lax.Precision.HIGHEST

@jax.custom_vjp
def low(v):
    return lax.optimization_barrier(v.astype(jnp.bfloat16)).astype(jnp.float32)

@jax.custom_vjp
def low_back(v):
    return v

def low_keep(v):
    return (low(v), None)

def low_pass(kept, grad):
    return (grad,)

def back_keep(v):
    return (v, None)

def back_low(kept, grad):
    return (low(grad),)
low.defvjp(low_keep, low_pass)
low_back.defvjp(back_keep, back_low)

def tap_list(half_span):
    return [(row_step, col_step) for row_step in range(-half_span, half_span + 1) for col_step in range(-half_span, half_span + 1)]

def masked_taps(tap_table, reach_rows, half_span, reduce_by):
    offsets = np.array([abs(col_step) for row_step, col_step in tap_list(half_span)], dtype=np.int32)
    inside = (jnp.asarray(offsets)[None, :] <= reach_rows[:, None] - reduce_by).astype(jnp.float32)
    return tap_table * inside[None]

def disco_filter(padded, weights, stride, half_span, row_count, col_count):
    running = None
    for position, (row_step, col_step) in enumerate(tap_list(half_span)):
        top = half_span + row_step
        left = half_span + col_step
        sliced = padded[..., top:top + stride * (row_count - 1) + 1:stride, left:left + stride * (col_count - 1) + 1:stride]
        weighted = weights[:, None, :, position, None] * sliced[..., None, :, :, :]
        running = weighted if running is None else running + weighted
    return running

def upfilter(padded, weights, row_count, col_count):
    running = None
    for position, (row_step, col_step) in enumerate(tap_list(1)):
        sliced = padded[..., 1 + row_step:1 + row_step + row_count, 1 + col_step:1 + col_step + col_count]
        doubled = jnp.repeat(jnp.repeat(sliced, 2, axis=-2), 2, axis=-1)
        weighted = lax.optimization_barrier(jnp.sum(weights[:, None, :, position, None] * doubled, axis=-4))
        running = weighted if running is None else running + weighted
    return running

def pad_grid(values, margin):
    wrapped = jnp.concatenate([values[..., -margin:], values, values[..., :margin]], axis=-1)
    widths = [(0, 0)] * (values.ndim - 2) + [(margin, margin), (0, 0)]
    return jnp.pad(wrapped, widths)

def spatial_norm(values, gain_vector, shift_vector):
    average = lax.optimization_barrier(jnp.mean(values, axis=(1, 2)))
    centred = values - average[:, None, None]
    variance = lax.optimization_barrier(jnp.mean(centred * centred, axis=(1, 2)))
    result = centred * lax.rsqrt(variance + epsilon)[:, None, None] * gain_vector[:, None, None] + shift_vector[:, None, None]
    return (result, average, variance)

def slot_forward(inputs, noise_slot, params, enc_eff, proc_eff, dec_eff):
    enc_weight, enc_bias, gain_one, shift_one, proc_weight, proc_bias, gain_two, shift_two, up_weight, up_bias, down_weight, down_bias, dec_weight, dec_bias = params
    joined = jnp.concatenate([inputs, noise_slot], 0)
    filtered = low_back(low(disco_filter(pad_grid(joined, 2), enc_eff, 2, 2, NLATH, NLONH)))
    h_zero = low_back(jnp.einsum('kdc,kchw->dhw', enc_weight, filtered, precision=highest) + enc_bias[:, None, None])
    norm_one, mean_one, var_one = spatial_norm(h_zero, gain_one, shift_one)
    norm_one = low(norm_one)
    proc_filt = low_back(low(disco_filter(pad_grid(norm_one, 2), proc_eff, 1, 2, NLATH, NLONH)))
    branch = low_back(jnp.einsum('kdc,kchw->dhw', proc_weight, proc_filt, precision=highest) + proc_bias[:, None, None])
    h_one = h_zero + branch
    norm_two, mean_two, var_two = spatial_norm(h_one, gain_two, shift_two)
    norm_two = low(norm_two)
    hidden_pre = low_back(jnp.einsum('fc,chw->fhw', up_weight, norm_two, precision=highest) + up_bias[:, None, None])
    activated = low(jax.nn.gelu(hidden_pre))
    mixed = low_back(jnp.einsum('cf,fhw->chw', down_weight, activated, precision=highest) + down_bias[:, None, None])
    h_two = h_one + mixed
    projected = low_back(low(jnp.einsum('kic,chw->kihw', dec_weight, low(h_two), precision=highest)))
    result = upfilter(pad_grid(projected, 1), dec_eff, NLATH, NLONH) + dec_bias[:, None, None]
    return (result, (mean_one, var_one, mean_two, var_two))

def reference(state, noise_field, cotangent, slot_date, lon_reach, enc_taps, proc_taps, dec_taps, enc_weight, enc_bias, gain_one, shift_one, proc_weight, proc_bias, gain_two, shift_two, up_weight, up_bias, down_weight, down_bias, dec_weight, dec_bias):
    enc_eff = masked_taps(enc_taps, lon_reach, 2, 0)
    proc_eff = masked_taps(proc_taps, lon_reach, 2, 0)
    dec_eff = masked_taps(dec_taps, jnp.repeat(lon_reach, 2), 1, 1)
    params = tuple((entry.astype(jnp.float32) for entry in (enc_weight, enc_bias, gain_one, shift_one, proc_weight, proc_bias, gain_two, shift_two, up_weight, up_bias, down_weight, down_bias, dec_weight, dec_bias)))
    inputs_all = state.astype(jnp.float32)
    date_ids = jnp.arange(DATES)

    def one_slot(carry, items):
        grad_total, input_total = carry
        date_value, noise_slot, cot_slot = items
        date_pick = (date_ids == date_value).astype(jnp.float32)
        slot_live = (date_value >= 0).astype(jnp.float32)
        inputs = lax.optimization_barrier(jnp.sum(date_pick[:, None, None, None] * inputs_all, axis=0))

        def forward(inputs_now, params_now):
            return slot_forward(inputs_now, noise_slot.astype(jnp.float32), params_now, enc_eff, proc_eff, dec_eff)
        result, pull_back, stats = jax.vjp(forward, inputs, params, has_aux=True)
        input_grad, param_grad = pull_back(cot_slot.astype(jnp.float32) * slot_live)
        grad_total = jax.tree.map(jnp.add, grad_total, param_grad)
        input_total = input_total + date_pick[:, None, None, None] * input_grad[None]
        kept = tuple((entry * slot_live for entry in stats))
        return ((grad_total, input_total), ((result * slot_live).astype(jnp.bfloat16),) + kept)
    start = (jax.tree.map(jnp.zeros_like, params), jnp.zeros_like(inputs_all))
    (grad_total, input_total), stacked = lax.scan(one_slot, start, (slot_date, noise_field, cotangent))
    output, mean_one, var_one, mean_two, var_two = stacked
    enc_weight_grad, enc_bias_grad, gain_one_grad, shift_one_grad, proc_weight_grad, proc_bias_grad, gain_two_grad, shift_two_grad, up_weight_grad, up_bias_grad, down_weight_grad, down_bias_grad, dec_weight_grad, dec_bias_grad = grad_total
    return (output, input_total.astype(jnp.bfloat16), enc_weight_grad, enc_bias_grad, gain_one_grad, shift_one_grad, proc_weight_grad, proc_bias_grad, gain_two_grad, shift_two_grad, up_weight_grad, up_bias_grad, down_weight_grad, down_bias_grad, dec_weight_grad, dec_bias_grad, mean_one, var_one, mean_two, var_two)
```

```python
import functools

import jax
import jax.numpy as jnp
from jax import lax
from jax.experimental import pallas as pl
from jax.experimental.pallas import tpu as pltpu
from jax.sharding import PartitionSpec as P

MESH = pl.DeviceIdType.MESH
f32 = jnp.float32
bf16 = jnp.bfloat16
i32 = jnp.int32
EPS = 1e-05
LANES = 128
AXES = ("ens", "lat", "lon")


def nn(a, b):
    return lax.dot_general(a, b, (((1,), (0,)), ((), ())), preferred_element_type=f32)


def nt(a, b):
    return lax.dot_general(a, b, (((1,), (1,)), ((), ())), preferred_element_type=f32)


def tn(a, b):
    return lax.dot_general(a, b, (((0,), (0,)), ((), ())), preferred_element_type=f32)


def up_to(n, m):
    return -(-n // m) * m


class Sizes:
    def __init__(self, mesh, state, noise, enc_taps, enc_weight, up_weight):
        self.ne, self.nl, self.nz = (mesh.shape[a] for a in AXES)
        self.dates, self.cin, self.full_rows, self.full_cols = state
        self.noise = noise[1]
        self.full_rows = state[2] // self.nl
        self.full_cols = state[3] // self.nz
        self.hr, self.hc = self.full_rows // 2, self.full_cols // 2
        assert self.hr == 2 and self.hc == LANES and self.ne == 4
        self.lat_total = enc_taps[1]
        self.nb = enc_taps[0]
        self.c = enc_weight[1]
        self.cj = enc_weight[2]
        self.ff = up_weight[0]
        self.px = self.hr * self.hc
        self.pixels = float(self.px * self.nl * self.nz)
        self.c5 = self.c // LANES
        self.f10 = self.ff // LANES
        self.r641 = up_to(self.c, 16)
        self.r1282 = up_to(self.ff, 16)
        self.r80 = up_to(self.cj, 16)
        self.off_down = self.c5 * self.r1282
        self.off_dec = self.off_down + self.f10 * self.r641
        used1 = self.off_dec + self.nb * self.c5 * self.r80
        used2 = self.nb * self.c5 * self.r641
        used3 = self.nb * self.c5 * self.r80
        many = 2 if self.nl == 2 else 1
        unit = 16 * self.nl * self.ne * self.nz
        self.colors = (many, many, 1, 1)
        self.rows = (
            up_to(used1, unit * many),
            up_to(used2, unit * many),
            up_to(used3, unit),
            up_to(24 * 6, unit // 2),
        )


def add_into(dst, at, sources, count):
    step = next(s for s in (256, 128, 64, 32, 16, 8) if count % s == 0)

    def body(n, carry):
        lo = pl.multiple_of(n * step, 8 if step == 8 else 16)
        there = pl.ds(pl.multiple_of(at + lo, 8 if step == 8 else 16), step)
        value = dst[there, :].astype(f32)
        for source in sources:
            value = value + source[pl.ds(lo, step), :].astype(f32)
        dst[there, :] = value.astype(dst.dtype)
        return carry

    lax.fori_loop(0, count // step, body, 0)


class Links:
    def __init__(self, z, sems=None):
        self.s = z
        self.sems = sems
        self.used = 0
        if sems is not None:
            self.e, self.l, self.z = (lax.axis_index(a) for a in AXES)

    def take(self):
        self.used += 1
        return self.used - 1

    def at(self, de, dl, dz):
        s = self.s
        return (
            lax.rem(self.e + (de + s.ne), s.ne),
            lax.rem(self.l + (dl + s.nl), s.nl),
            lax.rem(self.z + (dz + s.nz), s.nz),
        )

    def bit(self, which):
        return lax.rem(self.e // (1 << which), 2)

    def flip(self, which):
        return (self.e + (1 << which) * (1 - 2 * self.bit(which)), self.l, self.z)

    def has_up(self):
        return self.l > 0

    def has_down(self):
        return self.l < self.s.nl - 1


class Send:
    def __init__(self, links, src, dst, device, dl=0):
        self.links = links
        self.ids = (links.take(), links.take())
        self.what = (src, dst, device)
        self.dl = dl

    def copy(self):
        src, dst, device = self.what
        return pltpu.make_async_remote_copy(
            src_ref=src,
            dst_ref=dst,
            send_sem=self.links.sems.at[self.ids[0]],
            recv_sem=self.links.sems.at[self.ids[1]],
            device_id=device,
            device_id_type=MESH,
        )

    def under(self, sending, act):
        if self.dl == 0:
            act()
        else:
            up = (self.dl < 0) == sending
            pl.when(self.links.has_up() if up else self.links.has_down())(act)

    def start(self):
        self.under(True, lambda: self.copy().start())

    def wait_recv(self):
        self.under(False, lambda: self.copy().wait_recv())

    def wait_send(self):
        self.under(True, lambda: self.copy().wait_send())


class AllReduce:
    def __init__(self, links, partial, total, rows, colors, bufs, own_sems):
        s = links.s
        self.k, self.g, self.h, self.nc = links, partial, total, colors
        self.rc, self.r1, self.r2, self.rz = bufs
        self.own_sems = own_sems
        self.b0 = rows // s.nl
        self.b1 = self.b0 // colors
        self.half, self.quarter = self.b1 // 2, self.b1 // 4
        self.zs = self.quarter // s.nz
        self.sent = []
        self.waiting = []
        self.locals = []
        self.stage = 0
        al = lambda v: pl.multiple_of(v, 8)
        self.base, self.keep1, self.keep2, self.mine = [], [], [], []
        for c in range(colors):
            first, second = self.bits(c)
            base = links.l * self.b0 + c * self.b1
            keep1 = base + links.bit(first) * self.half
            keep2 = keep1 + links.bit(second) * self.quarter
            self.base.append(al(base))
            self.keep1.append(al(keep1))
            self.keep2.append(al(keep2))
            self.mine.append(al(keep2 + links.z * self.zs))

    @staticmethod
    def shapes(s, rows, colors, dtype):
        b0 = rows // s.nl
        b1 = b0 // colors
        return [
            pltpu.VMEM((s.nl - 1, b0, LANES), dtype),
            pltpu.VMEM((colors, b1 // 2, LANES), dtype),
            pltpu.VMEM((colors, b1 // 4, LANES), dtype),
            pltpu.VMEM((colors, s.nz - 1, b1 // 4 // s.nz, LANES), dtype),
        ]

    def bits(self, c):
        return (0, 1) if c == 0 else (1, 0)

    def send(self, src, dst, device):
        m = Send(self.k, src, dst, device)
        m.start()
        self.sent.append(m)
        self.waiting.append(m)

    def arrive(self):
        for m in self.waiting:
            m.wait_recv()
        self.waiting = []

    def step(self):
        k, s, g, h = self.k, self.k.s, self.g, self.h
        al = lambda v: pl.multiple_of(v, 8)
        stage, self.stage = self.stage, self.stage + 1
        colors = range(self.nc)
        self.arrive()
        if stage == 0:
            for d in range(1, s.nl):
                to = k.at(0, d, 0)
                self.send(g.at[pl.ds(al(to[1] * self.b0), self.b0)], self.rc.at[d - 1], to)
        elif stage == 1:
            add_into(g, self.base[0], [self.rc.at[d] for d in range(s.nl - 1)], self.b0)
            for c in colors:
                first = self.bits(c)[0]
                away = al(self.base[c] + (1 - k.bit(first)) * self.half)
                self.send(g.at[pl.ds(away, self.half)], self.r1.at[c], k.flip(first))
        elif stage == 2:
            for c in colors:
                add_into(g, self.keep1[c], [self.r1.at[c]], self.half)
                second = self.bits(c)[1]
                away = al(self.keep1[c] + (1 - k.bit(second)) * self.quarter)
                self.send(g.at[pl.ds(away, self.quarter)], self.r2.at[c], k.flip(second))
        elif stage == 3:
            for c in colors:
                add_into(g, self.keep2[c], [self.r2.at[c]], self.quarter)
                for d in range(1, s.nz):
                    to = k.at(0, 0, d)
                    away = al(self.keep2[c] + to[2] * self.zs)
                    self.send(g.at[pl.ds(away, self.zs)], self.rz.at[c, d - 1], to)
        elif stage == 4:
            for c in colors:
                add_into(g, self.mine[c], [self.rz.at[c, d] for d in range(s.nz - 1)], self.zs)
                here = pl.ds(self.mine[c], self.zs)
                for d in range(1, s.nz):
                    self.send(g.at[here], h.at[here], k.at(0, 0, d))
                own = pltpu.make_async_copy(g.at[here], h.at[here], self.own_sems.at[c])
                own.start()
                self.locals.append(own)
        elif stage == 5:
            for own in self.locals:
                own.wait()
            for c in colors:
                here = pl.ds(self.keep2[c], self.quarter)
                self.send(h.at[here], h.at[here], k.flip(self.bits(c)[1]))
        elif stage == 6:
            for c in colors:
                here = pl.ds(self.keep1[c], self.half)
                self.send(h.at[here], h.at[here], k.flip(self.bits(c)[0]))
        elif stage == 7:
            here = pl.ds(self.base[0], self.b0)
            for d in range(1, s.nl):
                self.send(h.at[here], h.at[here], k.at(0, d, 0))
        else:
            for m in self.sent:
                m.wait_send()

    stages = 9


def misc_slots():
    names = [
        ("down_bias", 1),
        ("up_bias", 2),
        ("gain_two", 1),
        ("shift_two", 1),
        ("proc_bias", 1),
        ("gain_one", 1),
        ("shift_one", 1),
        ("enc_bias", 1),
        ("up_last", 2),
        ("down_last", 2),
        ("proc_last", 3),
        ("enc_last", 3),
        ("dec_last", 3),
        ("dec_bias", 1),
    ]
    table, at = {}, 0
    for name, count in names:
        table[name] = at
        at += count
    return table


MISC = misc_slots()


def put_misc(misc, slot, row):
    width = row.shape[1]
    for t in range(-(-width // LANES)):
        lo, hi = t * LANES, min(width, (t + 1) * LANES)
        misc[slot * 6 + t : slot * 6 + t + 1, 0 : hi - lo] = row[:, lo:hi]


def get_misc(misc, slot, width):
    parts = []
    for t in range(-(-width // LANES)):
        lo, hi = t * LANES, min(width, (t + 1) * LANES)
        parts.append(misc[slot * 6 + t : slot * 6 + t + 1, 0 : hi - lo])
    return parts


def scratch_list(s):
    c, ff, px = s.c, s.ff, s.px
    big = s.full_cols
    wide = 8 * big + LANES
    V = pltpu.VMEM
    shapes = {
        "xin": V((160, s.full_rows, big), f32),
        "xj": V((160, wide), bf16),
        "eb": V((2, 160, LANES), bf16),
        "eslot": V((6, 160, LANES), bf16),
        "em": V((2, s.nb * LANES, 5 * big + LANES), bf16),
        "dm": V((2, s.nb * LANES, 6 * big + LANES), bf16),
        "tm": V((s.nb * px, 6 * LANES + 48), bf16),
        "ew": V((s.nb, c, s.cj), bf16),
        "pw": V((s.nb, c, c), bf16),
        "uw": V((ff, c), bf16),
        "dw": V((c, ff), bf16),
        "cw": V((s.nb, s.cin, c), bf16),
        "filte": V((s.nb, px, s.cj), bf16),
        "hx": V((6 * LANES + 48, c), f32),
        "nx": V((6 * LANES + 48, c), bf16),
        "pe": V((2, 8, c), f32),
        "filt": V((s.nb * px, c), bf16),
        "h1": V((px, c), f32),
        "n2": V((px, c), bf16),
        "hp": V((px, ff), f32),
        "ag": V((px, ff), f32),
        "act": V((px, ff), bf16),
        "hg": V((px, ff), bf16),
        "hgt": V((ff, px), bf16),
        "h2": V((px, c), bf16),
        "pgr": V((s.nb, px, s.cin), bf16),
        "projt": V((2, 80, s.nb * LANES), bf16),
        "partt": V((2, 80, s.nb * LANES), bf16),
        "two": V((px, c), f32),
        "mg": V((px, c), bf16),
        "mgt": V((c, px), bf16),
        "ntg": V((px, c), f32),
        "one": V((px, c), f32),
        "br": V((px, c), bf16),
        "brt": V((c, px), bf16),
        "fg": V((s.nb * px, c), bf16),
        "con": V((6 * LANES + 48, c), f32),
        "rup": V((px, c), f32),
        "rdn": V((px, c), f32),
        "reg": V((6, 8, c), f32),
        "ng": V((px, c), f32),
        "zg": V((px, c), bf16),
        "sgx": V((160, wide), f32),
        "sgb": V((160, 4 * big + LANES), bf16),
        "sgu": V((160, 2 * big), bf16),
        "sgd": V((160, 2 * big), bf16),
        "sge": V((6, 160, LANES), bf16),
        "orow": V((s.cin, s.full_rows, big), f32),
        "st7": V((s.ne, 80, 4 * big), bf16),
        "dates": V((s.ne, 8, LANES), f32),
        "cbt": V((8, LANES), f32),
        "slat": V((4, s.nl, 2, c), f32),
        "slon": V((4, s.nz, 2, c), f32),
        "g1": V((s.rows[0], LANES), bf16),
        "g2": V((s.rows[1], LANES), bf16),
        "g3": V((s.rows[2], LANES), bf16),
        "gm": V((s.rows[3], LANES), f32),
    }
    for i in range(4):
        kinds = AllReduce.shapes(s, s.rows[i], s.colors[i], f32 if i == 3 else bf16)
        for j, kind in enumerate(kinds):
            shapes[f"ar{i}_{j}"] = kind
    shapes["wsem"] = pltpu.SemaphoreType.DMA((5,))
    shapes["osem"] = pltpu.SemaphoreType.DMA((4, 2))
    return shapes


def sem_count(s):
    per = lambda nc: 2 * (2 * (s.nl - 1) + 4 * nc + 2 * nc * (s.nz - 1))
    total = sum(per(nc) for nc in s.colors)
    total += 2 * (8 + 8 + 8 + 8) + 2 * 2 * (s.ne - 1)
    total += 4 * 2 * (s.nl - 1 + s.nz - 1)
    return total + 8


def main_kernel(s, names, *refs):
    n_in, n_out = 22, 10
    (
        state, noise, cot, date_ref, reach, enc_taps, proc_taps, dec_taps,
        ew_h, eb, gain1, shift1, pw_h, pb, gain2, shift2, uw_h, ub, dw_h, db, cw_h, cb,
    ) = refs[:n_in]
    h1o, h2o, h3o, hmo, out, sgrad, m1o, v1o, m2o, v2o = refs[n_in : n_in + n_out]
    S = dict(zip(names, refs[n_in + n_out :]))
    sems = S["sems"]
    k = Links(s, sems)
    c, ff, px, nb, cin, cj = s.c, s.ff, s.px, s.nb, s.cin, s.cj
    big = s.full_cols
    l = k.l
    row0 = l * s.hr
    edge0 = 8 * big

    loads = {}
    for n, (name, src) in enumerate(
        (("ew", ew_h), ("pw", pw_h), ("uw", uw_h), ("dw", dw_h), ("cw", cw_h))
    ):
        loads[name] = pltpu.make_async_copy(src, S[name], S["wsem"].at[n])
        loads[name].start()

    date = date_ref[0]
    live = jnp.where(date >= 0, 1.0, 0.0).astype(f32)
    xin, xj = S["xin"], S["xj"]
    picked = jnp.zeros((cin, s.full_rows, big), f32)
    for d in range(s.dates):
        picked = picked + state[d].astype(f32) * jnp.where(date == d, 1.0, 0.0).astype(f32)
    xin[0:cin] = picked
    xin[cin:cj] = noise[0].astype(f32)
    xin[80 : 80 + cin] = cot[0].astype(f32) * live
    xin[80 + cin : 160] = jnp.zeros((160 - 80 - cin, s.full_rows, big), f32)
    lane = lax.broadcasted_iota(i32, (160, LANES), 1)
    left = jnp.zeros((160, LANES), f32)
    right = jnp.zeros((160, LANES), f32)
    for q in range(4):
        row = xin[:, q, :]
        xj[:, (2 + q) * big : (3 + q) * big] = row.astype(bf16)
        rows_there = [q + 2] + ([q + 6] if q < 2 else [q - 2])
        for r in rows_there:
            moved = pltpu.roll(row[:, 0:LANES], (r * 4 + 2) % LANES, 1)
            left = jnp.where((lane >> 1) == (r * 2 + 1), moved, left)
            moved = pltpu.roll(row[:, big - LANES : big], (r * 4 + 2) % LANES, 1)
            right = jnp.where((lane >> 1) == (r * 2), moved, right)
    S["eb"][0] = left.astype(bf16)
    S["eb"][1] = right.astype(bf16)
    S["dates"][k.e] = jnp.full((8, LANES), date.astype(f32), f32)

    @pl.when(jnp.logical_not(k.has_up()))
    def _():
        xj[:, 0 : 2 * big] = jnp.zeros((160, 2 * big), bf16)
        S["hx"][0:px] = jnp.zeros((px, c), f32)
        for side in range(2):
            S["hx"][768 + side * 8 : 776 + side * 8] = jnp.zeros((8, c), f32)

    @pl.when(jnp.logical_not(k.has_down()))
    def _():
        xj[:, 6 * big : 8 * big] = jnp.zeros((160, 2 * big), bf16)
        S["hx"][2 * px : 3 * px] = jnp.zeros((px, c), f32)
        for side in range(2):
            S["hx"][768 + 32 + side * 8 : 776 + 32 + side * 8] = jnp.zeros((8, c), f32)

    offsets = {(d, 0, 0) for d in range(1, s.ne)}
    offsets |= {(0, d, 0) for d in range(1, s.nl)} | {(0, 0, d) for d in range(1, s.nz)}
    offsets |= {(0, a % s.nl, b % s.nz) for a in (1, -1) for b in (1, -1)}
    offsets = sorted(offsets)
    barrier = pltpu.get_barrier_semaphore()
    for o in offsets:
        pl.semaphore_signal(barrier, 1, device_id=k.at(*o), device_id_type=MESH)
    pl.semaphore_wait(barrier, len(offsets))

    pending = []

    def start(sends):
        for m in sends:
            m.start()
        pending.extend(sends)
        return sends

    def arrive(sends):
        for m in sends:
            m.wait_recv()

    dirs = [(dl, ds) for dl in (-1, 0, 1) for ds in (-1, 1)]

    def slot_of(dl, ds):
        return (1 - dl) * 2 + (1 - ds) // 2

    sends = [
        Send(k, xj.at[:, pl.ds(2 * big, 2 * big)], xj.at[:, pl.ds(6 * big, 2 * big)], k.at(0, -1, 0), -1),
        Send(k, xj.at[:, pl.ds(4 * big, 2 * big)], xj.at[:, pl.ds(0, 2 * big)], k.at(0, 1, 0), 1),
    ]
    for dl, ds in dirs:
        sends.append(
            Send(k, S["eb"].at[(ds + 1) // 2], S["eslot"].at[slot_of(dl, ds)], k.at(0, dl, ds), dl)
        )
    first_halo = start(sends)
    date_sends = start(
        [
            Send(k, S["dates"].at[k.e], S["dates"].at[k.e], k.at(d, 0, 0))
            for d in range(1, s.ne)
        ]
    )

    gm = S["gm"]
    gm[0:144] = jnp.zeros((144, LANES), f32)

    def band(shape, column_of):
        rows = lax.broadcasted_iota(i32, shape, 0)
        cols = lax.broadcasted_iota(i32, shape, 1)
        return column_of(rows, cols)

    def pick(d, table, like):
        value = jnp.zeros(like, f32)
        for key, scalar in table:
            value = jnp.where(d == key, scalar, value)
        return value

    def inside(grow, total):
        return jnp.logical_and(grow >= 0, grow < total)

    def edge_lane(shape):
        at = lax.broadcasted_iota(i32, shape, 1)
        r, side, m = at >> 2, (at >> 1) & 1, at & 1
        return r, jnp.where(side == 0, m - 2, big + m), at

    def build_encoder():
        em = S["em"]
        d_main = band((LANES, big), lambda j, J: J - 2 * j)
        r, J, at = edge_lane((16, LANES))
        j = lax.broadcasted_iota(i32, (16, LANES), 0)
        codes = []
        for start_row in (0, LANES - 16):
            d = J - 2 * (j + start_row)
            codes.append(jnp.where(at < 32, r * 1024 + d, -5000))
        for i in range(2):
            reached = reach[row0 + i]
            edges = [[jnp.zeros((16, LANES), f32) for _ in range(2)] for _ in range(nb)]
            for a in range(-2, 3):
                r_in = 2 * i + a + 2
                ok = inside(4 * l + r_in - 2, 2 * s.lat_total)
                masks = [d_main == b for b in range(-2, 3)]
                for kk in range(nb):
                    value = jnp.zeros((LANES, big), f32)
                    for b in range(-2, 3):
                        tap = enc_taps[kk, row0 + i, 5 * (a + 2) + b + 2]
                        tap = jnp.where(jnp.logical_and(ok, abs(b) <= reached), tap, 0.0)
                        value = jnp.where(masks[b + 2], tap, value)
                        for part in range(2):
                            edges[kk][part] = jnp.where(
                                codes[part] == r_in * 1024 + b, tap, edges[kk][part]
                            )
                    em[i, kk * LANES : (kk + 1) * LANES, (a + 2) * big : (a + 3) * big] = value.astype(bf16)
            for kk in range(nb):
                lo = kk * LANES
                em[i, lo : lo + 16, 5 * big :] = edges[kk][0].astype(bf16)
                em[i, lo + 16 : lo + LANES - 16, 5 * big :] = jnp.zeros((LANES - 32, LANES), bf16)
                em[i, lo + LANES - 16 : lo + LANES, 5 * big :] = edges[kk][1].astype(bf16)

    def build_decoder():
        dm = S["dm"]
        d_main = band((LANES, big), lambda j, J: j - (J >> 1))
        r, J, at = edge_lane((16, LANES))
        j = lax.broadcasted_iota(i32, (16, LANES), 0)
        codes = []
        for start_row in (0, LANES - 16):
            d = (j + start_row) - (J >> 1)
            codes.append(jnp.where(at < 32, r * 1024 + d, -5000))
        for i in range(2):
            edges = [[jnp.zeros((16, LANES), f32) for _ in range(2)] for _ in range(nb)]
            for n in range(6):
                r_in = 2 * i + n
                a = i + 1 - r_in // 2
                full = 4 * l + r_in - 2
                ok = inside(full, 2 * s.lat_total)
                full = jnp.clip(full, 0, 2 * s.lat_total - 1)
                reached = reach[full // 2] - 1
                masks = [d_main == b for b in range(-1, 2)]
                for kk in range(nb):
                    value = jnp.zeros((LANES, big), f32)
                    for b in range(-1, 2):
                        tap = dec_taps[kk, full, 3 * (a + 1) + b + 1]
                        tap = jnp.where(jnp.logical_and(ok, abs(b) <= reached), tap, 0.0)
                        value = jnp.where(masks[b + 1], tap, value)
                        for part in range(2):
                            edges[kk][part] = jnp.where(
                                codes[part] == r_in * 1024 + b, tap, edges[kk][part]
                            )
                    dm[i, kk * LANES : (kk + 1) * LANES, n * big : (n + 1) * big] = value.astype(bf16)
            for kk in range(nb):
                lo = kk * LANES
                dm[i, lo : lo + 16, 6 * big :] = edges[kk][0].astype(bf16)
                dm[i, lo + 16 : lo + LANES - 16, 6 * big :] = jnp.zeros((LANES - 32, LANES), bf16)
                dm[i, lo + LANES - 16 : lo + LANES, 6 * big :] = edges[kk][1].astype(bf16)

    def build_processor():
        tm = S["tm"]
        d_main = band((LANES, LANES), lambda j, J: J - j)
        at = lax.broadcasted_iota(i32, (16, 48), 1)
        slot, idx = at >> 3, at & 7
        r = 2 * (slot >> 1) + (idx >> 1)
        m = idx & 1
        J = jnp.where((slot & 1) == 0, m - 2, LANES + m)
        j = lax.broadcasted_iota(i32, (16, 48), 0)
        codes = []
        for start_row in (0, LANES - 16):
            d = J - (j + start_row)
            codes.append(jnp.where(idx < 4, r * 1024 + d, -5000))
        for i in range(2):
            reached = reach[row0 + i]
            edges = [[jnp.zeros((16, 48), f32) for _ in range(2)] for _ in range(nb)]
            for r_in in range(6):
                a = r_in - 2 - i
                if abs(a) > 2:
                    for kk in range(nb):
                        lo = kk * px + i * LANES
                        tm[lo : lo + LANES, r_in * LANES : (r_in + 1) * LANES] = jnp.zeros((LANES, LANES), bf16)
                    continue
                ok = inside(row0 + r_in - 2, s.lat_total)
                masks = [d_main == b for b in range(-2, 3)]
                for kk in range(nb):
                    value = jnp.zeros((LANES, LANES), f32)
                    for b in range(-2, 3):
                        tap = proc_taps[kk, row0 + i, 5 * (a + 2) + b + 2]
                        tap = jnp.where(jnp.logical_and(ok, abs(b) <= reached), tap, 0.0)
                        value = jnp.where(masks[b + 2], tap, value)
                        for part in range(2):
                            edges[kk][part] = jnp.where(
                                codes[part] == r_in * 1024 + b, tap, edges[kk][part]
                            )
                    lo = kk * px + i * LANES
                    tm[lo : lo + LANES, r_in * LANES : (r_in + 1) * LANES] = value.astype(bf16)
            for kk in range(nb):
                lo = kk * px + i * LANES
                tm[lo : lo + 16, 768:816] = edges[kk][0].astype(bf16)
                tm[lo + 16 : lo + LANES - 16, 768:816] = jnp.zeros((LANES - 32, 48), bf16)
                tm[lo + LANES - 16 : lo + LANES, 768:816] = edges[kk][1].astype(bf16)

    slat, slon = S["slat"], S["slon"]

    def fold(values, kind, count):
        total_a, total_b = values[0]
        for a, b in values[1:]:
            total_a = total_a + a
            total_b = total_b + b
        if kind == "moments":
            total_a = total_a * (1.0 / len(values))
            for a, b in values:
                total_b = total_b + (a - total_a) * (a - total_a) * count
        return total_a, total_b

    def stat_start(rd, a, b):
        slat[rd, k.l, 0:1, :] = a
        slat[rd, k.l, 1:2, :] = b
        return start(
            [
                Send(k, slat.at[rd, k.l], slat.at[rd, k.l], k.at(0, d, 0))
                for d in range(1, s.nl)
            ]
        )

    def stat_middle(rd, sends, kind):
        arrive(sends)
        values = [(slat[rd, n, 0:1, :], slat[rd, n, 1:2, :]) for n in range(s.nl)]
        a, b = fold(values, kind, float(px))
        slon[rd, k.z, 0:1, :] = a
        slon[rd, k.z, 1:2, :] = b
        return start(
            [
                Send(k, slon.at[rd, k.z], slon.at[rd, k.z], k.at(0, 0, d))
                for d in range(1, s.nz)
            ]
        )

    def stat_end(rd, sends, kind):
        arrive(sends)
        values = [(slon[rd, n, 0:1, :], slon[rd, n, 1:2, :]) for n in range(s.nz)]
        return fold(values, kind, float(px * s.nl))

    def moments(values):
        mean = jnp.sum(values, axis=0, keepdims=True) * (1.0 / px)
        centred = values - mean
        return mean, jnp.sum(centred * centred, axis=0, keepdims=True)

    def vec(ref):
        n = ref.shape[0]
        return ref[...].reshape(1, n)

    build_encoder()

    arrive(first_halo)
    edge = jnp.zeros((160, LANES), f32)
    for sl in (-1, 0, 1):
        for ss in (-1, 1):
            there = S["eslot"][(sl + 1) * 2 + (ss + 1) // 2].astype(f32)
            r_lo, r_hi = {-1: (0, 2), 0: (2, 6), 1: (6, 8)}[sl]
            side = (ss + 1) // 2
            lo = r_lo * 4
            if sl == -1:
                lo = jnp.where(k.has_up(), lo, 1000)
            if sl == 1:
                lo = jnp.where(k.has_down(), lo, 1000)
            good = jnp.logical_and(lane >= lo, lane < r_hi * 4)
            good = jnp.logical_and(good, ((lane >> 1) & 1) == side)
            edge = jnp.where(good, there, edge)
    xj[:, edge0:] = edge.astype(bf16)

    filte, hx = S["filte"], S["hx"]
    for i in range(2):
        em = S["em"]
        got = nt(em[i, :, 0 : 5 * big], xj[0:80, 2 * i * big : (2 * i + 5) * big])
        got = got + nt(em[i, :, 5 * big :], xj[0:80, edge0:])
        for kk in range(nb):
            filte[kk, i * LANES : (i + 1) * LANES, :] = got[kk * LANES : (kk + 1) * LANES, 0:cj].astype(bf16)
    loads["ew"].wait()
    h0 = vec(eb) + jnp.zeros((px, c), f32)
    for kk in range(nb):
        h0 = h0 + nt(filte[kk], S["ew"][kk])
    hx[px : 2 * px, :] = h0
    own = slice(px, 2 * px)
    h0 = hx[own, :]
    stat_a = stat_start(0, *moments(h0))
    pe = S["pe"]
    for side, col in ((0, 0), (1, LANES - 2)):
        for q in range(2):
            lo = px + q * LANES + col
            pe[side, 2 * q : 2 * q + 2, :] = hx[lo : lo + 2, :]
            pe[side, 4 + 2 * q : 6 + 2 * q, :] = jnp.zeros((2, c), f32)
    sends = [
        Send(k, hx.at[pl.ds(px, px)], hx.at[pl.ds(2 * px, px)], k.at(0, -1, 0), -1),
        Send(k, hx.at[pl.ds(px, px)], hx.at[pl.ds(0, px)], k.at(0, 1, 0), 1),
    ]
    for dl, ds in dirs:
        sends.append(
            Send(
                k,
                pe.at[(ds + 1) // 2],
                hx.at[pl.ds(768 + slot_of(dl, ds) * 8, 8)],
                k.at(0, dl, ds),
                dl,
            )
        )
    zero_halo = start(sends)
    build_processor()
    stat_a = stat_middle(0, stat_a, "moments")

    build_decoder()
    dm, pgr = S["dm"], S["pgr"]
    for i in range(2):
        got = nt(dm[i, :, 0 : 6 * big], xj[80 : 80 + 80, 2 * i * big : (2 * i + 6) * big])
        got = got + nt(dm[i, :, 6 * big :], xj[80 : 80 + 80, edge0:])
        for kk in range(nb):
            pgr[kk, i * LANES : (i + 1) * LANES, :] = got[kk * LANES : (kk + 1) * LANES, 0:cin].astype(bf16)
    ones = jnp.ones((16, 4 * big), bf16)
    put_misc(gm, MISC["dec_bias"], nt(ones, xj[80:160, 2 * big : 6 * big])[0:1, 0:cin])

    mean1, m2 = stat_end(0, stat_a, "moments")
    var1 = m2 * (1.0 / s.pixels)
    rstd1 = lax.rsqrt(var1 + EPS)
    m1o[...] = mean1 * live
    v1o[...] = var1 * live
    arrive(zero_halo)
    nx = S["nx"]
    scale1 = rstd1 * vec(gain1)
    bias1 = vec(shift1)

    def norm_rows(n, carry):
        here = pl.ds(pl.multiple_of(n * 48, 16), 48)
        nx[here, :] = ((hx[here, :] - mean1) * scale1 + bias1).astype(bf16)
        return carry

    lax.fori_loop(0, 17, norm_rows, 0)

    filt, tm = S["filt"], S["tm"]
    loads["pw"].wait()
    h1 = S["h1"]
    acc = hx[own, :] + vec(pb)
    for kk in range(nb):
        here = slice(kk * px, (kk + 1) * px)
        filt[here, :] = nn(tm[here, :], nx[...]).astype(bf16)
        acc = acc + nt(filt[here, :], S["pw"][kk])
    h1[...] = acc
    stat_b = stat_start(1, *moments(h1[...]))
    loads["cw"].wait()
    two, mg = S["two"], S["mg"]
    acc = nn(pgr[0], S["cw"][0])
    for kk in range(1, nb):
        acc = acc + nn(pgr[kk], S["cw"][kk])
    two[...] = acc
    mg[...] = acc.astype(bf16)
    stat_b = stat_middle(1, stat_b, "moments")
    loads["dw"].wait()
    ag, hp = S["ag"], S["hp"]
    ag[...] = nn(mg[...], S["dw"][...])
    S["mgt"][...] = mg[...].T
    put_misc(gm, MISC["down_bias"], jnp.sum(mg[...].astype(f32), axis=0, keepdims=True))
    mean2, m2 = stat_end(1, stat_b, "moments")
    var2 = m2 * (1.0 / s.pixels)
    rstd2 = lax.rsqrt(var2 + EPS)
    m2o[...] = mean2 * live
    v2o[...] = var2 * live
    scale2 = rstd2 * vec(gain2)
    bias2 = vec(shift2)
    n2 = S["n2"]

    def norm_two_rows(n, carry):
        here = pl.ds(pl.multiple_of(n * 32, 16), 32)
        n2[here, :] = ((h1[here, :] - mean2) * scale2 + bias2).astype(bf16)
        return carry

    lax.fori_loop(0, px // 32, norm_two_rows, 0)

    loads["uw"].wait()
    hp[...] = nt(n2[...], S["uw"][...])
    act, hg = S["act"], S["hg"]
    ubias = vec(ub)
    root = 0.7978845608028654

    def gelu_rows(n, carry):
        here = pl.ds(pl.multiple_of(n * 16, 16), 16)
        v = hp[here, :] + ubias
        sq = v * v
        t = jnp.tanh(root * (v + 0.044715 * (sq * v)))
        act[here, :] = (0.5 * v * (1.0 + t)).astype(bf16)
        slope = 0.5 * (1.0 + t) + (0.5 * root) * v * (1.0 - t * t) * (1.0 + (3 * 0.044715) * sq)
        hg[here, :] = (slope * ag[here, :]).astype(bf16)
        return carry

    lax.fori_loop(0, px // 16, gelu_rows, 0)
    ntg = S["ntg"]
    ntg[...] = nn(hg[...], S["uw"][...])
    grad = ntg[...]
    standard = (h1[...] - mean2) * rstd2
    sum_a = jnp.sum(grad, axis=0, keepdims=True)
    sum_b = jnp.sum(grad * standard, axis=0, keepdims=True)
    put_misc(gm, MISC["shift_two"], sum_a)
    put_misc(gm, MISC["gain_two"], sum_b)
    stat_c = stat_start(2, sum_a, sum_b)

    g1 = S["g1"]
    cols = [(lo, min(256, s.c5 * LANES - lo)) for lo in range(0, s.c5 * LANES, 256)]

    def spread(g, off, height, pitch, value, lo, width):
        for n in range(width // LANES):
            at = off + (lo // LANES + n) * pitch
            g[at : at + height, :] = value[:, n * LANES : (n + 1) * LANES].astype(bf16)

    S["hgt"][...] = hg[...].T
    for lo, width in cols:
        spread(g1, 0, ff, s.r1282, nn(S["hgt"][...], n2[:, lo : lo + width]), lo, width)
    stat_c = stat_middle(2, stat_c, "sums")
    for lo in range(0, s.f10 * LANES, 256):
        spread(g1, s.off_down, c, s.r641, nn(S["mgt"][...], act[:, lo : lo + 256]), lo, 256)
    h2 = S["h2"]
    h2[...] = (h1[...] + nt(act[...], S["dw"][...]) + vec(db)).astype(bf16)
    for kk in range(nb):
        got = tn(pgr[kk], h2[:, 0 : s.c5 * LANES])
        spread(g1, s.off_dec + kk * s.c5 * s.r80, cin, s.r80, got, 0, s.c5 * LANES)
    ar1 = AllReduce(k, g1, h1o, s.rows[0], s.colors[0], [S[f"ar0_{j}"] for j in range(4)], S["osem"].at[0])
    ar1.step()

    def weighted(ref, column):
        return jnp.sum(ref.astype(f32) * column.astype(f32), axis=0, keepdims=True)

    def put_long(name, row):
        put_misc(gm, MISC[name], row[:, 0:768])
        put_misc(gm, MISC[name] + 1, row[:, 768:])

    put_long("up_bias", jnp.sum(hg[...].astype(f32), axis=0, keepdims=True))
    put_long("up_last", weighted(hg[...], n2[:, c - 1 : c]))
    for n in range(2):
        at = s.f10 * LANES + n
        put_misc(gm, MISC["down_last"] + n, weighted(mg[...], act[:, at : at + 1]))
    for kk in range(nb):
        put_misc(gm, MISC["dec_last"] + kk, weighted(pgr[kk], h2[:, c - 1 : c]))
    ar1.step()

    sum_a, sum_b = stat_end(2, stat_c, "sums")
    g_two = vec(gain2)
    part_a = g_two * sum_a * (1.0 / s.pixels)
    part_b = g_two * sum_b * (1.0 / s.pixels)
    one, br = S["one"], S["br"]

    def one_rows(n, carry):
        here = pl.ds(pl.multiple_of(n * 32, 16), 32)
        standard = (h1[here, :] - mean2) * rstd2
        value = rstd2 * (g_two * ntg[here, :] - part_a - standard * part_b) + two[here, :]
        one[here, :] = value
        br[here, :] = value.astype(bf16)
        return carry

    lax.fori_loop(0, px // 32, one_rows, 0)
    fg = S["fg"]
    for kk in range(nb):
        fg[kk * px : (kk + 1) * px, :] = nn(br[...], S["pw"][kk]).astype(bf16)
    con = S["con"]
    con[...] = tn(tm[...], fg[...])

    def sum_rows(n, carry):
        here = pl.ds(pl.multiple_of(n * 48, 16), 48)
        value = con[here, :]
        standard = (hx[here, :] - mean1) * rstd1
        return (
            carry[0] + jnp.sum(value, axis=0, keepdims=True),
            carry[1] + jnp.sum(value * standard, axis=0, keepdims=True),
        )

    zero_row = jnp.zeros((1, c), f32)
    sum_a, sum_b = lax.fori_loop(0, 17, sum_rows, (zero_row, zero_row))
    put_misc(gm, MISC["shift_one"], sum_a)
    put_misc(gm, MISC["gain_one"], sum_b)
    stat_d = stat_start(3, sum_a, sum_b)
    sends = [
        Send(k, con.at[pl.ds(0, px)], S["rdn"], k.at(0, -1, 0), -1),
        Send(k, con.at[pl.ds(2 * px, px)], S["rup"], k.at(0, 1, 0), 1),
    ]
    for dl, ds in dirs:
        mine = (dl + 1) * 2 + (ds + 1) // 2
        sends.append(
            Send(
                k,
                con.at[pl.ds(768 + mine * 8, 8)],
                S["reg"].at[slot_of(dl, ds)],
                k.at(0, dl, ds),
                dl,
            )
        )
    back_halo = start(sends)
    g2 = S["g2"]
    S["brt"][...] = br[...].T
    for kk in range(nb):
        if kk == 1:
            stat_d = stat_middle(3, stat_d, "sums")
        for lo, width in cols:
            got = nn(S["brt"][...], filt[kk * px : (kk + 1) * px, lo : lo + width])
            spread(g2, kk * s.c5 * s.r641, c, s.r641, got, lo, width)
    ar2 = AllReduce(k, g2, h2o, s.rows[1], s.colors[1], [S[f"ar1_{j}"] for j in range(4)], S["osem"].at[1])
    ar2.step()
    put_misc(gm, MISC["proc_bias"], jnp.sum(br[...].astype(f32), axis=0, keepdims=True))
    for kk in range(nb):
        put_misc(gm, MISC["proc_last"] + kk, weighted(br[...], filt[kk * px : (kk + 1) * px, c - 1 : c]))

    arrive(back_halo)
    ng = S["ng"]
    ng[...] = con[own, :]

    @pl.when(k.has_up())
    def _():
        ng[...] = ng[...] + S["rup"][...]

    @pl.when(k.has_down())
    def _():
        ng[...] = ng[...] + S["rdn"][...]

    def add_edges(sl):
        for ss in (-1, 1):
            got = S["reg"].at[(sl + 1) * 2 + (ss + 1) // 2]
            col = 0 if ss == -1 else LANES - 2
            for q in range(2):
                lo = q * LANES + col
                ng[lo : lo + 2, :] = ng[lo : lo + 2, :] + got[2 * q : 2 * q + 2, :]

    add_edges(0)
    pl.when(k.has_up())(lambda: add_edges(-1))
    pl.when(k.has_down())(lambda: add_edges(1))
    sum_a, sum_b = stat_end(3, stat_d, "sums")
    g_one = vec(gain1)
    part_a1 = g_one * sum_a * (1.0 / s.pixels)
    part_b1 = g_one * sum_b * (1.0 / s.pixels)
    zg = S["zg"]

    def zero_rows(n, carry):
        here = pl.ds(pl.multiple_of(n * 32, 16), 32)
        there = pl.ds(pl.multiple_of(px + n * 32, 16), 32)
        standard = (hx[there, :] - mean1) * rstd1
        value = rstd1 * (g_one * ng[here, :] - part_a1 - standard * part_b1) + one[here, :]
        zg[here, :] = value.astype(bf16)
        return carry

    lax.fori_loop(0, px // 32, zero_rows, 0)

    g3 = S["g3"]
    for kk in range(nb):
        got = tn(filte[kk], zg[:, 0 : s.c5 * LANES])
        spread(g3, kk * s.c5 * s.r80, cj, s.r80, got, 0, s.c5 * LANES)
        put_misc(gm, MISC["enc_last"] + kk, weighted(filte[kk], zg[:, c - 1 : c]))
    put_misc(gm, MISC["enc_bias"], jnp.sum(zg[...].astype(f32), axis=0, keepdims=True))
    ar3 = AllReduce(k, g3, h3o, s.rows[2], s.colors[2], [S[f"ar2_{j}"] for j in range(4)], S["osem"].at[2])
    ar4 = AllReduce(k, gm, hmo, s.rows[3], s.colors[3], [S[f"ar3_{j}"] for j in range(4)], S["osem"].at[3])
    ar3.step()
    ar4.step()
    ar1.step()
    ar2.step()

    projt, partt = S["projt"], S["partt"]
    for kk in range(nb):
        here = slice(kk * LANES, (kk + 1) * LANES)
        proj = nt(h2[...], S["cw"][kk])
        part = nn(zg[...], S["ew"][kk])[:, 0:cin]
        for i in range(2):
            for ref, value in ((projt, proj), (partt, part)):
                ref[i, 0:cin, here] = value[i * LANES : (i + 1) * LANES, :].T.astype(bf16)
                ref[i, cin:80, here] = jnp.zeros((80 - cin, LANES), bf16)
    sgx = S["sgx"]
    em = S["em"]
    sgx[...] = jnp.zeros(sgx.shape, f32)
    for i in range(2):
        lo = 2 * i * big
        got = nn(projt[i], dm[i])
        sgx[0:80, lo : lo + 6 * big] = sgx[0:80, lo : lo + 6 * big] + got[:, 0 : 6 * big]
        sgx[0:80, edge0:] = sgx[0:80, edge0:] + got[:, 6 * big :]
        got = nn(partt[i], em[i])
        sgx[80:160, lo : lo + 5 * big] = sgx[80:160, lo : lo + 5 * big] + got[:, 0 : 5 * big]
        sgx[80:160, edge0:] = sgx[80:160, edge0:] + got[:, 5 * big :]
    sgb, sgu, sgd, sge = S["sgb"], S["sgu"], S["sgd"], S["sge"]
    sgb[:, 0 : 2 * big] = sgx[:, 0 : 2 * big].astype(bf16)
    sgb[:, 2 * big : 4 * big] = sgx[:, 6 * big : 8 * big].astype(bf16)
    sgb[:, 4 * big :] = sgx[:, edge0:].astype(bf16)
    sends = [
        Send(k, sgb.at[:, pl.ds(0, 2 * big)], sgd, k.at(0, -1, 0), -1),
        Send(k, sgb.at[:, pl.ds(2 * big, 2 * big)], sgu, k.at(0, 1, 0), 1),
    ]
    for dl, ds in dirs:
        sends.append(
            Send(k, sgb.at[:, pl.ds(4 * big, LANES)], sge.at[slot_of(dl, ds)], k.at(0, dl, ds), dl)
        )
    out_halo = start(sends)
    ar3.step()
    ar4.step()
    ar1.step()
    ar2.step()
    arrive(out_halo)
    up_one = jnp.where(k.has_up(), 1, 0)
    down_one = jnp.where(k.has_down(), 1, 0)
    cbt = S["cbt"]
    cbt[...] = jnp.zeros((8, LANES), f32)
    cbt[0:1, 0:cin] = vec(cb)
    bias_col = cbt[...].T[0:cin, 0:1]
    orow, st7 = S["orow"], S["st7"]

    for q in range(4):
        lo = (2 + q) * big
        value = sgx[:, lo : lo + big]
        if q < 2:
            other = sgu[:, q * big : (q + 1) * big].astype(f32)
            value = value + jnp.where(up_one == 1, other, 0.0)
        else:
            other = sgd[:, (q - 2) * big : (q - 1) * big].astype(f32)
            value = value + jnp.where(down_one == 1, other, 0.0)
        head, tail = value[:, 0:LANES], value[:, big - LANES :]
        sources = [(0, q + 2, None)]
        sources += [(-1, q + 6, up_one)] if q < 2 else [(1, q - 2, down_one)]
        for sl, r, there in sources:
            for ss in (-1, 1):
                got = sge[(sl + 1) * 2 + (ss + 1) // 2].astype(f32)
                if ss == -1:
                    moved = pltpu.roll(got, (LANES - (r * 4 + 2)) % LANES, 1)
                    bound = 2 if there is None else there * 2
                    head = head + jnp.where(lane < bound, moved, 0.0)
                else:
                    moved = pltpu.roll(got, (2 * LANES - 2 - r * 4) % LANES, 1)
                    bound = LANES - 2 if there is None else LANES - there * 2
                    tail = tail + jnp.where(lane >= bound, moved, 0.0)
        orow[:, q, 0:LANES] = (head[0:cin] + bias_col) * live
        orow[:, q, LANES:big] = (tail[0:cin] + bias_col) * live
        st7[k.e, :, q * big : q * big + LANES] = head[80:160].astype(bf16)
        st7[k.e, :, q * big + LANES : (q + 1) * big] = tail[80:160].astype(bf16)
    out[0] = orow[...].astype(bf16)
    state_sends = start(
        [Send(k, st7.at[k.e], st7.at[k.e], k.at(d, 0, 0)) for d in range(1, s.ne)]
    )
    for _ in range(2):
        ar3.step()
        ar4.step()
        ar1.step()
        ar2.step()
    arrive(date_sends)
    arrive(state_sends)
    for d in range(s.dates):
        for q in range(4):
            value = jnp.zeros((80, big), f32)
            for n in range(s.ne):
                is_d = jnp.where(S["dates"][n, 0:1, :] == float(d), 1.0, 0.0)
                is_d = jnp.concatenate([is_d] * (big // LANES), axis=1)
                value = value + is_d * st7[n, :, q * big : (q + 1) * big].astype(f32)
            orow[:, q, :] = value[0:cin]
        sgrad[d] = orow[...].astype(bf16)

    rest = [ar1, ar2, ar3, ar4]
    while any(a.stage < AllReduce.stages for a in rest):
        for a in rest:
            if a.stage < AllReduce.stages:
                a.step()
    for m in pending:
        m.wait_send()


def finish_kernel(s, names, *refs):
    h1, h2, h3, hm = refs[:4]
    (
        enc_w, enc_b, g1o, s1o, proc_w, proc_b, g2o, s2o,
        up_w, up_b, down_w, down_b, dec_w, dec_b,
    ) = refs[4:18]
    c, ff, nb, cin, cj = s.c, s.ff, s.nb, s.cin, s.cj
    turned = hm[0:144, :].T

    def tall(slot, height):
        out = []
        for t in range(-(-height // LANES)):
            n = min(LANES, height - t * LANES)
            out.append((t * LANES, n, turned[0:n, slot * 6 + t : slot * 6 + t + 1]))
        return out

    last = s.c5 * LANES
    for n in range(s.c5):
        at = n * s.r1282
        up_w[:, n * LANES : (n + 1) * LANES] = h1[at : at + ff, :].astype(f32)
    for part in range(2):
        base = part * 768
        for lo, n, col in tall(MISC["up_last"] + part, min(768, ff - base)):
            up_w[base + lo : base + lo + n, last : last + 1] = col
    for n in range(s.f10):
        at = s.off_down + n * s.r641
        down_w[:, n * LANES : (n + 1) * LANES] = h1[at : at + c, :].astype(f32)
    for part in range(2):
        at = s.f10 * LANES + part
        for lo, n, col in tall(MISC["down_last"] + part, c):
            down_w[lo : lo + n, at : at + 1] = col
    for kk in range(nb):
        for n in range(s.c5):
            at = s.off_dec + (kk * s.c5 + n) * s.r80
            dec_w[kk, :, n * LANES : (n + 1) * LANES] = h1[at : at + cin, :].astype(f32)
            at = (kk * s.c5 + n) * s.r641
            proc_w[kk, :, n * LANES : (n + 1) * LANES] = h2[at : at + c, :].astype(f32)
            at = (kk * s.c5 + n) * s.r80
            enc_w[kk, n * LANES : (n + 1) * LANES, :] = h3[at : at + cj, :].astype(f32).T
        for lo, n, col in tall(MISC["dec_last"] + kk, cin):
            dec_w[kk, lo : lo + n, last : last + 1] = col
        for lo, n, col in tall(MISC["proc_last"] + kk, c):
            proc_w[kk, lo : lo + n, last : last + 1] = col
        enc_w[kk, last : last + 1, :] = get_misc(hm, MISC["enc_last"] + kk, cj)[0]

    def flat(ref, slots):
        at = 0
        for slot, width in slots:
            for piece in get_misc(hm, slot, width):
                n = piece.shape[1]
                ref[0:1, at : at + n] = piece
                at += n

    for ref, name in (
        (enc_b, "enc_bias"), (g1o, "gain_one"), (s1o, "shift_one"), (proc_b, "proc_bias"),
        (g2o, "gain_two"), (s2o, "shift_two"), (down_b, "down_bias"),
    ):
        flat(ref, [(MISC[name], c)])
    flat(up_b, [(MISC["up_bias"], 768), (MISC["up_bias"] + 1, ff - 768)])
    flat(dec_b, [(MISC["dec_bias"], cin)])


def per_device(s, *args):
    (
        state, noise, cot, slot_date, lon_reach, enc_taps, proc_taps, dec_taps,
        enc_weight, enc_bias, gain_one, shift_one, proc_weight, proc_bias, gain_two, shift_two,
        up_weight, up_bias, down_weight, down_bias, dec_weight, dec_bias,
    ) = args
    vm = pl.BlockSpec(memory_space=pltpu.VMEM)
    sm = pl.BlockSpec(memory_space=pltpu.SMEM)
    hbm = pl.BlockSpec(memory_space=pl.ANY)
    shapes = scratch_list(s)
    shapes["sems"] = pltpu.SemaphoreType.DMA((sem_count(s),))
    names = tuple(shapes)
    in_specs = [vm] * 3 + [sm] * 5 + [
        hbm, vm, vm, vm, hbm, vm, vm, vm, hbm, vm, hbm, vm, hbm, vm,
    ]
    sd = jax.ShapeDtypeStruct
    out_shape = [
        sd((s.rows[0], LANES), bf16),
        sd((s.rows[1], LANES), bf16),
        sd((s.rows[2], LANES), bf16),
        sd((s.rows[3], LANES), f32),
        sd((1, s.cin, s.full_rows, s.full_cols), bf16),
        sd((s.dates, s.cin, s.full_rows, s.full_cols), bf16),
    ] + [sd((1, s.c), f32)] * 4
    got = pl.pallas_call(
        functools.partial(main_kernel, s, names),
        out_shape=out_shape,
        in_specs=in_specs,
        out_specs=[hbm] * 4 + [vm] * 6,
        scratch_shapes=list(shapes.values()),
        compiler_params=pltpu.CompilerParams(
            collective_id=0, has_side_effects=True, vmem_limit_bytes=60 * 2**20
        ),
        name="forecast",
    )(*args)
    h1, h2, h3, hm, output, state_grad, mean1, var1, mean2, var2 = got
    c, ff, nb = s.c, s.ff, s.nb
    outs = [
        sd((nb, c, s.cj), f32), sd((1, c), f32), sd((1, c), f32), sd((1, c), f32),
        sd((nb, c, c), f32), sd((1, c), f32), sd((1, c), f32), sd((1, c), f32),
        sd((ff, c), f32), sd((1, ff), f32), sd((c, ff), f32), sd((1, c), f32),
        sd((nb, s.cin, c), f32), sd((1, s.cin), f32),
    ]
    grads = pl.pallas_call(
        functools.partial(finish_kernel, s, names),
        out_shape=outs,
        in_specs=[vm] * 4,
        out_specs=[vm] * len(outs),
        compiler_params=pltpu.CompilerParams(vmem_limit_bytes=60 * 2**20),
        name="finish",
    )(h1, h2, h3, hm)
    grads = [g.reshape(g.shape[1]) if g.shape[0] == 1 else g for g in grads]
    return (output, state_grad, *grads, mean1, var1, mean2, var2)


def solution(mesh):
    in_specs = (
        P(None, None, "lat", "lon"),
        P("ens", None, "lat", "lon"),
        P("ens", None, "lat", "lon"),
        P("ens"),
    ) + (P(),) * 18
    out_specs = (
        (P("ens", None, "lat", "lon"), P(None, None, "lat", "lon"))
        + (P(),) * 14
        + (P("ens", None),) * 4
    )

    def run(*args):
        s = Sizes(mesh, args[0].shape, args[1].shape, args[5].shape, args[8].shape, args[16].shape)
        return jax.shard_map(
            functools.partial(per_device, s),
            mesh=mesh,
            in_specs=in_specs,
            out_specs=out_specs,
            check_vma=False,
        )(*args)

    return run
```

```python
import functools

import jax
import jax.numpy as jnp
from jax import lax
from jax.experimental import pallas as pl
from jax.experimental.pallas import tpu as pltpu
from jax.sharding import PartitionSpec as P

MESH = pl.DeviceIdType.MESH
f32 = jnp.float32
bf16 = jnp.bfloat16
i32 = jnp.int32
EPS = 1e-05
LANES = 128
AXES = ("ens", "lat", "lon")


def nn(a, b):
    return lax.dot_general(a, b, (((1,), (0,)), ((), ())), preferred_element_type=f32)


def nt(a, b):
    return lax.dot_general(a, b, (((1,), (1,)), ((), ())), preferred_element_type=f32)


def tn(a, b):
    return lax.dot_general(a, b, (((0,), (0,)), ((), ())), preferred_element_type=f32)


def up_to(n, m):
    return -(-n // m) * m


class Sizes:
    def __init__(self, mesh, state, noise, enc_taps, enc_weight, up_weight):
        self.ne, self.nl, self.nz = (mesh.shape[a] for a in AXES)
        self.dates, self.cin, self.full_rows, self.full_cols = state
        self.noise = noise[1]
        self.full_rows = state[2] // self.nl
        self.full_cols = state[3] // self.nz
        self.hr, self.hc = self.full_rows // 2, self.full_cols // 2
        assert self.hr == 2 and self.hc == LANES and self.ne == 4
        self.lat_total = enc_taps[1]
        self.nb = enc_taps[0]
        self.c = enc_weight[1]
        self.cj = enc_weight[2]
        self.ff = up_weight[0]
        self.px = self.hr * self.hc
        self.pixels = float(self.px * self.nl * self.nz)
        self.c5 = self.c // LANES
        self.f10 = self.ff // LANES
        self.r641 = up_to(self.c, 16)
        self.r80 = up_to(self.cj, 16)
        self.off_down = self.f10 * self.r641
        self.off_dec = self.off_down + self.f10 * self.r641
        used1 = self.off_dec + self.nb * self.c5 * self.r80
        used2 = self.nb * self.c5 * self.r641
        used3 = self.nb * self.c5 * self.r80
        many = 2 if self.nl == 2 else 1
        unit = 16 * self.nl * self.ne * self.nz
        self.colors = (many, many, 1, 1)
        self.rows = (
            up_to(used1, unit * many),
            up_to(used2, unit * many),
            up_to(used3, unit),
            up_to(24 * 6, unit // 2),
        )


def add_into(dst, at, sources, count):
    step = next(s for s in (256, 128, 64, 32, 16, 8) if count % s == 0)

    def body(n, carry):
        lo = pl.multiple_of(n * step, 8 if step == 8 else 16)
        there = pl.ds(pl.multiple_of(at + lo, 8 if step == 8 else 16), step)
        value = dst[there, :].astype(f32)
        for source in sources:
            value = value + source[pl.ds(lo, step), :].astype(f32)
        dst[there, :] = value.astype(dst.dtype)
        return carry

    lax.fori_loop(0, count // step, body, 0)


class Links:
    def __init__(self, z, sems=None):
        self.s = z
        self.sems = sems
        self.used = 0
        if sems is not None:
            self.e, self.l, self.z = (lax.axis_index(a) for a in AXES)

    def take(self):
        self.used += 1
        return self.used - 1

    def at(self, de, dl, dz):
        s = self.s
        return (
            lax.rem(self.e + (de + s.ne), s.ne),
            lax.rem(self.l + (dl + s.nl), s.nl),
            lax.rem(self.z + (dz + s.nz), s.nz),
        )

    def bit(self, which):
        return lax.rem(self.e // (1 << which), 2)

    def flip(self, which):
        return (self.e + (1 << which) * (1 - 2 * self.bit(which)), self.l, self.z)

    def has_up(self):
        return self.l > 0

    def has_down(self):
        return self.l < self.s.nl - 1


class Send:
    def __init__(self, links, src, dst, device, dl=0):
        self.links = links
        self.ids = (links.take(), links.take())
        self.what = (src, dst, device)
        self.dl = dl

    def copy(self):
        src, dst, device = self.what
        return pltpu.make_async_remote_copy(
            src_ref=src,
            dst_ref=dst,
            send_sem=self.links.sems.at[self.ids[0]],
            recv_sem=self.links.sems.at[self.ids[1]],
            device_id=device,
            device_id_type=MESH,
        )

    def under(self, sending, act):
        if self.dl == 0:
            act()
        else:
            up = (self.dl < 0) == sending
            pl.when(self.links.has_up() if up else self.links.has_down())(act)

    def start(self):
        self.under(True, lambda: self.copy().start())

    def wait_recv(self):
        self.under(False, lambda: self.copy().wait_recv())

    def wait_send(self):
        self.under(True, lambda: self.copy().wait_send())


class AllReduce:
    def __init__(self, links, partial, total, rows, colors, bufs, own_sems):
        s = links.s
        self.k, self.g, self.h, self.nc = links, partial, total, colors
        self.rc, self.r1, self.r2, self.rz = bufs
        self.own_sems = own_sems
        self.b0 = rows // s.nl
        self.b1 = self.b0 // colors
        self.half, self.quarter = self.b1 // 2, self.b1 // 4
        self.zs = self.quarter // s.nz
        self.sent = []
        self.waiting = []
        self.locals = []
        self.stage = 0
        al = lambda v: pl.multiple_of(v, 8)
        self.base, self.keep1, self.keep2, self.mine = [], [], [], []
        for c in range(colors):
            first, second = self.bits(c)
            base = links.l * self.b0 + c * self.b1
            keep1 = base + links.bit(first) * self.half
            keep2 = keep1 + links.bit(second) * self.quarter
            self.base.append(al(base))
            self.keep1.append(al(keep1))
            self.keep2.append(al(keep2))
            self.mine.append(al(keep2 + links.z * self.zs))

    @staticmethod
    def shapes(s, rows, colors, dtype):
        b0 = rows // s.nl
        b1 = b0 // colors
        return [
            pltpu.VMEM((s.nl - 1, b0, LANES), dtype),
            pltpu.VMEM((colors, b1 // 2, LANES), dtype),
            pltpu.VMEM((colors, b1 // 4, LANES), dtype),
            pltpu.VMEM((colors, s.nz - 1, b1 // 4 // s.nz, LANES), dtype),
        ]

    def bits(self, c):
        return (0, 1) if c == 0 else (1, 0)

    def send(self, src, dst, device):
        m = Send(self.k, src, dst, device)
        m.start()
        self.sent.append(m)
        self.waiting.append(m)

    def arrive(self):
        for m in self.waiting:
            m.wait_recv()
        self.waiting = []

    def step(self):
        k, s, g, h = self.k, self.k.s, self.g, self.h
        al = lambda v: pl.multiple_of(v, 8)
        stage, self.stage = self.stage, self.stage + 1
        colors = range(self.nc)
        self.arrive()
        if stage == 0:
            for d in range(1, s.nl):
                to = k.at(0, d, 0)
                self.send(g.at[pl.ds(al(to[1] * self.b0), self.b0)], self.rc.at[d - 1], to)
        elif stage == 1:
            add_into(g, self.base[0], [self.rc.at[d] for d in range(s.nl - 1)], self.b0)
            for c in colors:
                first = self.bits(c)[0]
                away = al(self.base[c] + (1 - k.bit(first)) * self.half)
                self.send(g.at[pl.ds(away, self.half)], self.r1.at[c], k.flip(first))
        elif stage == 2:
            for c in colors:
                add_into(g, self.keep1[c], [self.r1.at[c]], self.half)
                second = self.bits(c)[1]
                away = al(self.keep1[c] + (1 - k.bit(second)) * self.quarter)
                self.send(g.at[pl.ds(away, self.quarter)], self.r2.at[c], k.flip(second))
        elif stage == 3:
            for c in colors:
                add_into(g, self.keep2[c], [self.r2.at[c]], self.quarter)
                for d in range(1, s.nz):
                    to = k.at(0, 0, d)
                    away = al(self.keep2[c] + to[2] * self.zs)
                    self.send(g.at[pl.ds(away, self.zs)], self.rz.at[c, d - 1], to)
        elif stage == 4:
            for c in colors:
                add_into(g, self.mine[c], [self.rz.at[c, d] for d in range(s.nz - 1)], self.zs)
                here = pl.ds(self.mine[c], self.zs)
                for d in range(1, s.nz):
                    self.send(g.at[here], h.at[here], k.at(0, 0, d))
                own = pltpu.make_async_copy(g.at[here], h.at[here], self.own_sems.at[c])
                own.start()
                self.locals.append(own)
        elif stage == 5:
            for own in self.locals:
                own.wait()
            for c in colors:
                here = pl.ds(self.keep2[c], self.quarter)
                self.send(h.at[here], h.at[here], k.flip(self.bits(c)[1]))
        elif stage == 6:
            for c in colors:
                here = pl.ds(self.keep1[c], self.half)
                self.send(h.at[here], h.at[here], k.flip(self.bits(c)[0]))
        elif stage == 7:
            here = pl.ds(self.base[0], self.b0)
            for d in range(1, s.nl):
                self.send(h.at[here], h.at[here], k.at(0, d, 0))
        else:
            for m in self.sent:
                m.wait_send()

    stages = 9


def misc_slots():
    names = [
        ("down_bias", 1),
        ("up_bias", 2),
        ("gain_two", 1),
        ("shift_two", 1),
        ("proc_bias", 1),
        ("gain_one", 1),
        ("shift_one", 1),
        ("enc_bias", 1),
        ("up_last", 2),
        ("down_last", 2),
        ("proc_last", 3),
        ("enc_last", 3),
        ("dec_last", 3),
        ("dec_bias", 1),
    ]
    table, at = {}, 0
    for name, count in names:
        table[name] = at
        at += count
    return table


MISC = misc_slots()


def put_misc(misc, slot, row):
    width = row.shape[1]
    for t in range(-(-width // LANES)):
        lo, hi = t * LANES, min(width, (t + 1) * LANES)
        misc[slot * 6 + t : slot * 6 + t + 1, 0 : hi - lo] = row[:, lo:hi]


def get_misc(misc, slot, width):
    parts = []
    for t in range(-(-width // LANES)):
        lo, hi = t * LANES, min(width, (t + 1) * LANES)
        parts.append(misc[slot * 6 + t : slot * 6 + t + 1, 0 : hi - lo])
    return parts


def scratch_list(s):
    c, ff, px = s.c, s.ff, s.px
    big = s.full_cols
    wide = 8 * big + LANES
    V = pltpu.VMEM
    shapes = {
        "xin": V((160, s.full_rows, big), f32),
        "xj": V((160, wide), bf16),
        "eb": V((2, 160, LANES), bf16),
        "eslot": V((6, 160, LANES), bf16),
        "em": V((2, s.nb * LANES, 5 * big + LANES), bf16),
        "dm": V((2, s.nb * LANES, 6 * big + LANES), bf16),
        "tm": V((s.nb * px, 6 * LANES + 48), bf16),
        "ew": V((s.nb, s.cj, c), bf16),
        "pw": V((s.nb, c, c), bf16),
        "uw": V((c, ff), bf16),
        "dw": V((c, ff), bf16),
        "cw": V((s.nb, s.cin, c), bf16),
        "filte": V((s.nb, px, s.cj), bf16),
        "hx": V((6 * LANES + 48, c), f32),
        "nx": V((6 * LANES + 48, c), bf16),
        "pe": V((2, 8, c), f32),
        "filt": V((s.nb * px, c), bf16),
        "h1": V((px, c), f32),
        "n2": V((px, c), bf16),
        "hp": V((px, ff), f32),
        "ag": V((px, ff), f32),
        "act": V((px, ff), bf16),
        "hg": V((px, ff), bf16),
        "n2t": V((c, px), bf16),
        "h2": V((px, c), bf16),
        "pgr": V((s.nb, px, s.cin), bf16),
        "projt": V((2, 80, s.nb * LANES), bf16),
        "partt": V((2, 80, s.nb * LANES), bf16),
        "two": V((px, c), f32),
        "mg": V((px, c), bf16),
        "mgt": V((c, px), bf16),
        "ntg": V((px, c), f32),
        "one": V((px, c), f32),
        "br": V((px, c), bf16),
        "brt": V((c, px), bf16),
        "fg": V((s.nb * px, c), bf16),
        "con": V((6 * LANES + 48, c), f32),
        "rup": V((px, c), f32),
        "rdn": V((px, c), f32),
        "reg": V((6, 8, c), f32),
        "ng": V((px, c), f32),
        "zg": V((px, c), bf16),
        "sgx": V((160, wide), f32),
        "sgb": V((160, 4 * big + LANES), bf16),
        "sgu": V((160, 2 * big), bf16),
        "sgd": V((160, 2 * big), bf16),
        "sge": V((6, 160, LANES), bf16),
        "orow": V((s.cin, s.full_rows, big), f32),
        "st7": V((s.ne, 80, 4 * big), bf16),
        "dates": V((s.ne, 8, LANES), f32),
        "cbt": V((8, LANES), f32),
        "slat": V((4, s.nl, 2, c), f32),
        "slon": V((4, s.nz, 2, c), f32),
        "g1": V((s.rows[0], LANES), bf16),
        "g2": V((s.rows[1], LANES), bf16),
        "g3": V((s.rows[2], LANES), bf16),
        "gm": V((s.rows[3], LANES), f32),
    }
    for i in range(4):
        kinds = AllReduce.shapes(s, s.rows[i], s.colors[i], f32 if i == 3 else bf16)
        for j, kind in enumerate(kinds):
            shapes[f"ar{i}_{j}"] = kind
    shapes["wsem"] = pltpu.SemaphoreType.DMA((5,))
    shapes["osem"] = pltpu.SemaphoreType.DMA((4, 2))
    return shapes


def sem_count(s):
    per = lambda nc: 2 * (2 * (s.nl - 1) + 4 * nc + 2 * nc * (s.nz - 1))
    total = sum(per(nc) for nc in s.colors)
    total += 2 * (8 + 8 + 8 + 8) + 2 * 2 * (s.ne - 1)
    total += 4 * 2 * (s.nl - 1 + s.nz - 1)
    return total + 8


def main_kernel(s, names, *refs):
    n_in, n_out = 22, 10
    (
        state, noise, cot, date_ref, reach, enc_taps, proc_taps, dec_taps,
        ew_h, eb, gain1, shift1, pw_h, pb, gain2, shift2, uw_h, ub, dw_h, db, cw_h, cb,
    ) = refs[:n_in]
    h1o, h2o, h3o, hmo, out, sgrad, m1o, v1o, m2o, v2o = refs[n_in : n_in + n_out]
    S = dict(zip(names, refs[n_in + n_out :]))
    sems = S["sems"]
    k = Links(s, sems)
    c, ff, px, nb, cin, cj = s.c, s.ff, s.px, s.nb, s.cin, s.cj
    big = s.full_cols
    l = k.l
    row0 = l * s.hr
    edge0 = 8 * big

    loads = {}
    for n, (name, src) in enumerate(
        (("ew", ew_h), ("pw", pw_h), ("uw", uw_h), ("dw", dw_h), ("cw", cw_h))
    ):
        loads[name] = pltpu.make_async_copy(src, S[name], S["wsem"].at[n])
        loads[name].start()

    date = date_ref[0]
    live = jnp.where(date >= 0, 1.0, 0.0).astype(f32)
    xin, xj = S["xin"], S["xj"]
    picked = jnp.zeros((cin, s.full_rows, big), f32)
    for d in range(s.dates):
        picked = picked + state[d].astype(f32) * jnp.where(date == d, 1.0, 0.0).astype(f32)
    xin[0:cin] = picked
    xin[cin:cj] = noise[0].astype(f32)
    xin[80 : 80 + cin] = cot[0].astype(f32) * live
    xin[80 + cin : 160] = jnp.zeros((160 - 80 - cin, s.full_rows, big), f32)
    lane = lax.broadcasted_iota(i32, (160, LANES), 1)
    left = jnp.zeros((160, LANES), f32)
    right = jnp.zeros((160, LANES), f32)
    for q in range(4):
        row = xin[:, q, :]
        xj[:, (2 + q) * big : (3 + q) * big] = row.astype(bf16)
        rows_there = [q + 2] + ([q + 6] if q < 2 else [q - 2])
        for r in rows_there:
            moved = pltpu.roll(row[:, 0:LANES], (r * 4 + 2) % LANES, 1)
            left = jnp.where((lane >> 1) == (r * 2 + 1), moved, left)
            moved = pltpu.roll(row[:, big - LANES : big], (r * 4 + 2) % LANES, 1)
            right = jnp.where((lane >> 1) == (r * 2), moved, right)
    S["eb"][0] = left.astype(bf16)
    S["eb"][1] = right.astype(bf16)
    S["dates"][k.e] = jnp.full((8, LANES), date.astype(f32), f32)

    @pl.when(jnp.logical_not(k.has_up()))
    def _():
        xj[:, 0 : 2 * big] = jnp.zeros((160, 2 * big), bf16)
        S["hx"][0:px] = jnp.zeros((px, c), f32)
        for side in range(2):
            S["hx"][768 + side * 8 : 776 + side * 8] = jnp.zeros((8, c), f32)

    @pl.when(jnp.logical_not(k.has_down()))
    def _():
        xj[:, 6 * big : 8 * big] = jnp.zeros((160, 2 * big), bf16)
        S["hx"][2 * px : 3 * px] = jnp.zeros((px, c), f32)
        for side in range(2):
            S["hx"][768 + 32 + side * 8 : 776 + 32 + side * 8] = jnp.zeros((8, c), f32)

    offsets = {(d, 0, 0) for d in range(1, s.ne)}
    offsets |= {(0, d, 0) for d in range(1, s.nl)} | {(0, 0, d) for d in range(1, s.nz)}
    offsets |= {(0, a % s.nl, b % s.nz) for a in (1, -1) for b in (1, -1)}
    offsets = sorted(offsets)
    barrier = pltpu.get_barrier_semaphore()
    for o in offsets:
        pl.semaphore_signal(barrier, 1, device_id=k.at(*o), device_id_type=MESH)
    pl.semaphore_wait(barrier, len(offsets))

    pending = []

    def start(sends):
        for m in sends:
            m.start()
        pending.extend(sends)
        return sends

    def arrive(sends):
        for m in sends:
            m.wait_recv()

    dirs = [(dl, ds) for dl in (-1, 0, 1) for ds in (-1, 1)]

    def slot_of(dl, ds):
        return (1 - dl) * 2 + (1 - ds) // 2

    sends = [
        Send(k, xj.at[:, pl.ds(2 * big, 2 * big)], xj.at[:, pl.ds(6 * big, 2 * big)], k.at(0, -1, 0), -1),
        Send(k, xj.at[:, pl.ds(4 * big, 2 * big)], xj.at[:, pl.ds(0, 2 * big)], k.at(0, 1, 0), 1),
    ]
    for dl, ds in dirs:
        sends.append(
            Send(k, S["eb"].at[(ds + 1) // 2], S["eslot"].at[slot_of(dl, ds)], k.at(0, dl, ds), dl)
        )
    first_halo = start(sends)
    date_sends = start(
        [
            Send(k, S["dates"].at[k.e], S["dates"].at[k.e], k.at(d, 0, 0))
            for d in range(1, s.ne)
        ]
    )

    gm = S["gm"]
    gm[0:144] = jnp.zeros((144, LANES), f32)

    def band(shape, column_of):
        rows = lax.broadcasted_iota(i32, shape, 0)
        cols = lax.broadcasted_iota(i32, shape, 1)
        return column_of(rows, cols)

    def pick(d, table, like):
        value = jnp.zeros(like, f32)
        for key, scalar in table:
            value = jnp.where(d == key, scalar, value)
        return value

    def inside(grow, total):
        return jnp.logical_and(grow >= 0, grow < total)

    def edge_lane(shape):
        at = lax.broadcasted_iota(i32, shape, 1)
        r, side, m = at >> 2, (at >> 1) & 1, at & 1
        return r, jnp.where(side == 0, m - 2, big + m), at

    def build_encoder():
        em = S["em"]
        d_main = band((LANES, big), lambda j, J: J - 2 * j)
        r, J, at = edge_lane((16, LANES))
        j = lax.broadcasted_iota(i32, (16, LANES), 0)
        codes = []
        for start_row in (0, LANES - 16):
            d = J - 2 * (j + start_row)
            codes.append(jnp.where(at < 32, r * 1024 + d, -5000))
        for i in range(2):
            reached = reach[row0 + i]
            edges = [[jnp.zeros((16, LANES), f32) for _ in range(2)] for _ in range(nb)]
            for a in range(-2, 3):
                r_in = 2 * i + a + 2
                ok = inside(4 * l + r_in - 2, 2 * s.lat_total)
                masks = [d_main == b for b in range(-2, 3)]
                for kk in range(nb):
                    value = jnp.zeros((LANES, big), f32)
                    for b in range(-2, 3):
                        tap = enc_taps[kk, row0 + i, 5 * (a + 2) + b + 2]
                        tap = jnp.where(jnp.logical_and(ok, abs(b) <= reached), tap, 0.0)
                        value = jnp.where(masks[b + 2], tap, value)
                        for part in range(2):
                            edges[kk][part] = jnp.where(
                                codes[part] == r_in * 1024 + b, tap, edges[kk][part]
                            )
                    em[i, kk * LANES : (kk + 1) * LANES, (a + 2) * big : (a + 3) * big] = value.astype(bf16)
            for kk in range(nb):
                lo = kk * LANES
                em[i, lo : lo + 16, 5 * big :] = edges[kk][0].astype(bf16)
                em[i, lo + 16 : lo + LANES - 16, 5 * big :] = jnp.zeros((LANES - 32, LANES), bf16)
                em[i, lo + LANES - 16 : lo + LANES, 5 * big :] = edges[kk][1].astype(bf16)

    def build_decoder():
        dm = S["dm"]
        d_main = band((LANES, big), lambda j, J: j - (J >> 1))
        r, J, at = edge_lane((16, LANES))
        j = lax.broadcasted_iota(i32, (16, LANES), 0)
        codes = []
        for start_row in (0, LANES - 16):
            d = (j + start_row) - (J >> 1)
            codes.append(jnp.where(at < 32, r * 1024 + d, -5000))
        for i in range(2):
            edges = [[jnp.zeros((16, LANES), f32) for _ in range(2)] for _ in range(nb)]
            for n in range(6):
                r_in = 2 * i + n
                a = i + 1 - r_in // 2
                full = 4 * l + r_in - 2
                ok = inside(full, 2 * s.lat_total)
                full = jnp.clip(full, 0, 2 * s.lat_total - 1)
                reached = reach[full // 2] - 1
                masks = [d_main == b for b in range(-1, 2)]
                for kk in range(nb):
                    value = jnp.zeros((LANES, big), f32)
                    for b in range(-1, 2):
                        tap = dec_taps[kk, full, 3 * (a + 1) + b + 1]
                        tap = jnp.where(jnp.logical_and(ok, abs(b) <= reached), tap, 0.0)
                        value = jnp.where(masks[b + 1], tap, value)
                        for part in range(2):
                            edges[kk][part] = jnp.where(
                                codes[part] == r_in * 1024 + b, tap, edges[kk][part]
                            )
                    dm[i, kk * LANES : (kk + 1) * LANES, n * big : (n + 1) * big] = value.astype(bf16)
            for kk in range(nb):
                lo = kk * LANES
                dm[i, lo : lo + 16, 6 * big :] = edges[kk][0].astype(bf16)
                dm[i, lo + 16 : lo + LANES - 16, 6 * big :] = jnp.zeros((LANES - 32, LANES), bf16)
                dm[i, lo + LANES - 16 : lo + LANES, 6 * big :] = edges[kk][1].astype(bf16)

    def build_processor():
        tm = S["tm"]
        d_main = band((LANES, LANES), lambda j, J: J - j)
        at = lax.broadcasted_iota(i32, (16, 48), 1)
        slot, idx = at >> 3, at & 7
        r = 2 * (slot >> 1) + (idx >> 1)
        m = idx & 1
        J = jnp.where((slot & 1) == 0, m - 2, LANES + m)
        j = lax.broadcasted_iota(i32, (16, 48), 0)
        codes = []
        for start_row in (0, LANES - 16):
            d = J - (j + start_row)
            codes.append(jnp.where(idx < 4, r * 1024 + d, -5000))
        for i in range(2):
            reached = reach[row0 + i]
            edges = [[jnp.zeros((16, 48), f32) for _ in range(2)] for _ in range(nb)]
            for r_in in range(6):
                a = r_in - 2 - i
                if abs(a) > 2:
                    for kk in range(nb):
                        lo = kk * px + i * LANES
                        tm[lo : lo + LANES, r_in * LANES : (r_in + 1) * LANES] = jnp.zeros((LANES, LANES), bf16)
                    continue
                ok = inside(row0 + r_in - 2, s.lat_total)
                masks = [d_main == b for b in range(-2, 3)]
                for kk in range(nb):
                    value = jnp.zeros((LANES, LANES), f32)
                    for b in range(-2, 3):
                        tap = proc_taps[kk, row0 + i, 5 * (a + 2) + b + 2]
                        tap = jnp.where(jnp.logical_and(ok, abs(b) <= reached), tap, 0.0)
                        value = jnp.where(masks[b + 2], tap, value)
                        for part in range(2):
                            edges[kk][part] = jnp.where(
                                codes[part] == r_in * 1024 + b, tap, edges[kk][part]
                            )
                    lo = kk * px + i * LANES
                    tm[lo : lo + LANES, r_in * LANES : (r_in + 1) * LANES] = value.astype(bf16)
            for kk in range(nb):
                lo = kk * px + i * LANES
                tm[lo : lo + 16, 768:816] = edges[kk][0].astype(bf16)
                tm[lo + 16 : lo + LANES - 16, 768:816] = jnp.zeros((LANES - 32, 48), bf16)
                tm[lo + LANES - 16 : lo + LANES, 768:816] = edges[kk][1].astype(bf16)

    slat, slon = S["slat"], S["slon"]

    def fold(values, kind, count):
        total_a, total_b = values[0]
        for a, b in values[1:]:
            total_a = total_a + a
            total_b = total_b + b
        if kind == "moments":
            total_a = total_a * (1.0 / len(values))
            for a, b in values:
                total_b = total_b + (a - total_a) * (a - total_a) * count
        return total_a, total_b

    def stat_start(rd, a, b):
        slat[rd, k.l, 0:1, :] = a
        slat[rd, k.l, 1:2, :] = b
        return start(
            [
                Send(k, slat.at[rd, k.l], slat.at[rd, k.l], k.at(0, d, 0))
                for d in range(1, s.nl)
            ]
        )

    def stat_middle(rd, sends, kind):
        arrive(sends)
        values = [(slat[rd, n, 0:1, :], slat[rd, n, 1:2, :]) for n in range(s.nl)]
        a, b = fold(values, kind, float(px))
        slon[rd, k.z, 0:1, :] = a
        slon[rd, k.z, 1:2, :] = b
        return start(
            [
                Send(k, slon.at[rd, k.z], slon.at[rd, k.z], k.at(0, 0, d))
                for d in range(1, s.nz)
            ]
        )

    def stat_end(rd, sends, kind):
        arrive(sends)
        values = [(slon[rd, n, 0:1, :], slon[rd, n, 1:2, :]) for n in range(s.nz)]
        return fold(values, kind, float(px * s.nl))

    def moments(values):
        mean = jnp.sum(values, axis=0, keepdims=True) * (1.0 / px)
        centred = values - mean
        return mean, jnp.sum(centred * centred, axis=0, keepdims=True)

    def vec(ref):
        n = ref.shape[0]
        return ref[...].reshape(1, n)

    build_encoder()

    arrive(first_halo)
    edge = jnp.zeros((160, LANES), f32)
    for sl in (-1, 0, 1):
        for ss in (-1, 1):
            there = S["eslot"][(sl + 1) * 2 + (ss + 1) // 2].astype(f32)
            r_lo, r_hi = {-1: (0, 2), 0: (2, 6), 1: (6, 8)}[sl]
            side = (ss + 1) // 2
            lo = r_lo * 4
            if sl == -1:
                lo = jnp.where(k.has_up(), lo, 1000)
            if sl == 1:
                lo = jnp.where(k.has_down(), lo, 1000)
            good = jnp.logical_and(lane >= lo, lane < r_hi * 4)
            good = jnp.logical_and(good, ((lane >> 1) & 1) == side)
            edge = jnp.where(good, there, edge)
    xj[:, edge0:] = edge.astype(bf16)

    filte, hx = S["filte"], S["hx"]
    for i in range(2):
        em = S["em"]
        got = nt(em[i, :, 0 : 5 * big], xj[0:80, 2 * i * big : (2 * i + 5) * big])
        got = got + nt(em[i, :, 5 * big :], xj[0:80, edge0:])
        for kk in range(nb):
            filte[kk, i * LANES : (i + 1) * LANES, :] = got[kk * LANES : (kk + 1) * LANES, 0:cj].astype(bf16)
    loads["ew"].wait()
    h0 = vec(eb) + jnp.zeros((px, c), f32)
    for kk in range(nb):
        h0 = h0 + nn(filte[kk], S["ew"][kk])
    hx[px : 2 * px, :] = h0
    own = slice(px, 2 * px)
    h0 = hx[own, :]
    stat_a = stat_start(0, *moments(h0))
    pe = S["pe"]
    for side, col in ((0, 0), (1, LANES - 2)):
        for q in range(2):
            lo = px + q * LANES + col
            pe[side, 2 * q : 2 * q + 2, :] = hx[lo : lo + 2, :]
            pe[side, 4 + 2 * q : 6 + 2 * q, :] = jnp.zeros((2, c), f32)
    sends = [
        Send(k, hx.at[pl.ds(px, px)], hx.at[pl.ds(2 * px, px)], k.at(0, -1, 0), -1),
        Send(k, hx.at[pl.ds(px, px)], hx.at[pl.ds(0, px)], k.at(0, 1, 0), 1),
    ]
    for dl, ds in dirs:
        sends.append(
            Send(
                k,
                pe.at[(ds + 1) // 2],
                hx.at[pl.ds(768 + slot_of(dl, ds) * 8, 8)],
                k.at(0, dl, ds),
                dl,
            )
        )
    zero_halo = start(sends)
    build_processor()
    stat_a = stat_middle(0, stat_a, "moments")

    build_decoder()
    dm, pgr = S["dm"], S["pgr"]
    for i in range(2):
        got = nt(dm[i, :, 0 : 6 * big], xj[80 : 80 + 80, 2 * i * big : (2 * i + 6) * big])
        got = got + nt(dm[i, :, 6 * big :], xj[80 : 80 + 80, edge0:])
        for kk in range(nb):
            pgr[kk, i * LANES : (i + 1) * LANES, :] = got[kk * LANES : (kk + 1) * LANES, 0:cin].astype(bf16)
    ones = jnp.ones((16, 4 * big), bf16)
    put_misc(gm, MISC["dec_bias"], nt(ones, xj[80:160, 2 * big : 6 * big])[0:1, 0:cin])

    mean1, m2 = stat_end(0, stat_a, "moments")
    var1 = m2 * (1.0 / s.pixels)
    rstd1 = lax.rsqrt(var1 + EPS)
    m1o[...] = mean1 * live
    v1o[...] = var1 * live
    arrive(zero_halo)
    nx = S["nx"]
    scale1 = rstd1 * vec(gain1)
    bias1 = vec(shift1)

    def norm_rows(n, carry):
        here = pl.ds(pl.multiple_of(n * 48, 16), 48)
        nx[here, :] = ((hx[here, :] - mean1) * scale1 + bias1).astype(bf16)
        return carry

    lax.fori_loop(0, 17, norm_rows, 0)

    filt, tm = S["filt"], S["tm"]
    loads["pw"].wait()
    h1 = S["h1"]
    acc = hx[own, :] + vec(pb)
    for kk in range(nb):
        here = slice(kk * px, (kk + 1) * px)
        filt[here, :] = nn(tm[here, :], nx[...]).astype(bf16)
        acc = acc + nt(filt[here, :], S["pw"][kk])
    h1[...] = acc
    stat_b = stat_start(1, *moments(h1[...]))
    loads["cw"].wait()
    two, mg = S["two"], S["mg"]
    acc = nn(pgr[0], S["cw"][0])
    for kk in range(1, nb):
        acc = acc + nn(pgr[kk], S["cw"][kk])
    two[...] = acc
    mg[...] = acc.astype(bf16)
    stat_b = stat_middle(1, stat_b, "moments")
    loads["dw"].wait()
    ag, hp = S["ag"], S["hp"]
    ag[...] = nn(mg[...], S["dw"][...])
    S["mgt"][...] = mg[...].T
    put_misc(gm, MISC["down_bias"], jnp.sum(mg[...].astype(f32), axis=0, keepdims=True))
    mean2, m2 = stat_end(1, stat_b, "moments")
    var2 = m2 * (1.0 / s.pixels)
    rstd2 = lax.rsqrt(var2 + EPS)
    m2o[...] = mean2 * live
    v2o[...] = var2 * live
    scale2 = rstd2 * vec(gain2)
    bias2 = vec(shift2)
    n2 = S["n2"]

    def norm_two_rows(n, carry):
        here = pl.ds(pl.multiple_of(n * 32, 16), 32)
        n2[here, :] = ((h1[here, :] - mean2) * scale2 + bias2).astype(bf16)
        return carry

    lax.fori_loop(0, px // 32, norm_two_rows, 0)

    loads["uw"].wait()
    hp[...] = nn(n2[...], S["uw"][...])
    act, hg = S["act"], S["hg"]
    ubias = vec(ub)
    root = 0.7978845608028654

    def gelu_rows(n, carry):
        here = pl.ds(pl.multiple_of(n * 16, 16), 16)
        v = hp[here, :] + ubias
        sq = v * v
        t = jnp.tanh(root * (v + 0.044715 * (sq * v)))
        act[here, :] = (0.5 * v * (1.0 + t)).astype(bf16)
        slope = 0.5 * (1.0 + t) + (0.5 * root) * v * (1.0 - t * t) * (1.0 + (3 * 0.044715) * sq)
        hg[here, :] = (slope * ag[here, :]).astype(bf16)
        return carry

    lax.fori_loop(0, px // 16, gelu_rows, 0)
    ntg = S["ntg"]
    ntg[...] = nt(hg[...], S["uw"][...])
    grad = ntg[...]
    standard = (h1[...] - mean2) * rstd2
    sum_a = jnp.sum(grad, axis=0, keepdims=True)
    sum_b = jnp.sum(grad * standard, axis=0, keepdims=True)
    put_misc(gm, MISC["shift_two"], sum_a)
    put_misc(gm, MISC["gain_two"], sum_b)
    stat_c = stat_start(2, sum_a, sum_b)

    g1 = S["g1"]
    cols = [(lo, min(256, s.c5 * LANES - lo)) for lo in range(0, s.c5 * LANES, 256)]

    def spread(g, off, height, pitch, value, lo, width):
        for n in range(width // LANES):
            at = off + (lo // LANES + n) * pitch
            g[at : at + height, :] = value[:, n * LANES : (n + 1) * LANES].astype(bf16)

    S["n2t"][...] = n2[...].T
    for lo in range(0, s.f10 * LANES, 256):
        spread(g1, 0, c, s.r641, nn(S["n2t"][...], hg[:, lo : lo + 256]), lo, 256)
    stat_c = stat_middle(2, stat_c, "sums")
    for lo in range(0, s.f10 * LANES, 256):
        spread(g1, s.off_down, c, s.r641, nn(S["mgt"][...], act[:, lo : lo + 256]), lo, 256)
    h2 = S["h2"]
    h2[...] = (h1[...] + nt(act[...], S["dw"][...]) + vec(db)).astype(bf16)
    for kk in range(nb):
        got = tn(pgr[kk], h2[:, 0 : s.c5 * LANES])
        spread(g1, s.off_dec + kk * s.c5 * s.r80, cin, s.r80, got, 0, s.c5 * LANES)
    ar1 = AllReduce(k, g1, h1o, s.rows[0], s.colors[0], [S[f"ar0_{j}"] for j in range(4)], S["osem"].at[0])
    ar1.step()

    def weighted(ref, column):
        return jnp.sum(ref.astype(f32) * column.astype(f32), axis=0, keepdims=True)

    def put_long(name, row):
        put_misc(gm, MISC[name], row[:, 0:768])
        put_misc(gm, MISC[name] + 1, row[:, 768:])

    put_long("up_bias", jnp.sum(hg[...].astype(f32), axis=0, keepdims=True))
    for n in range(2):
        at = s.f10 * LANES + n
        put_misc(gm, MISC["up_last"] + n, weighted(n2[...], hg[:, at : at + 1]))
        put_misc(gm, MISC["down_last"] + n, weighted(mg[...], act[:, at : at + 1]))
    for kk in range(nb):
        put_misc(gm, MISC["dec_last"] + kk, weighted(pgr[kk], h2[:, c - 1 : c]))
    ar1.step()

    sum_a, sum_b = stat_end(2, stat_c, "sums")
    g_two = vec(gain2)
    part_a = g_two * sum_a * (1.0 / s.pixels)
    part_b = g_two * sum_b * (1.0 / s.pixels)
    one, br = S["one"], S["br"]

    def one_rows(n, carry):
        here = pl.ds(pl.multiple_of(n * 32, 16), 32)
        standard = (h1[here, :] - mean2) * rstd2
        value = rstd2 * (g_two * ntg[here, :] - part_a - standard * part_b) + two[here, :]
        one[here, :] = value
        br[here, :] = value.astype(bf16)
        return carry

    lax.fori_loop(0, px // 32, one_rows, 0)
    fg = S["fg"]
    for kk in range(nb):
        fg[kk * px : (kk + 1) * px, :] = nn(br[...], S["pw"][kk]).astype(bf16)
    con = S["con"]
    con[...] = tn(tm[...], fg[...])

    def sum_rows(n, carry):
        here = pl.ds(pl.multiple_of(n * 48, 16), 48)
        value = con[here, :]
        standard = (hx[here, :] - mean1) * rstd1
        return (
            carry[0] + jnp.sum(value, axis=0, keepdims=True),
            carry[1] + jnp.sum(value * standard, axis=0, keepdims=True),
        )

    zero_row = jnp.zeros((1, c), f32)
    sum_a, sum_b = lax.fori_loop(0, 17, sum_rows, (zero_row, zero_row))
    put_misc(gm, MISC["shift_one"], sum_a)
    put_misc(gm, MISC["gain_one"], sum_b)
    stat_d = stat_start(3, sum_a, sum_b)
    sends = [
        Send(k, con.at[pl.ds(0, px)], S["rdn"], k.at(0, -1, 0), -1),
        Send(k, con.at[pl.ds(2 * px, px)], S["rup"], k.at(0, 1, 0), 1),
    ]
    for dl, ds in dirs:
        mine = (dl + 1) * 2 + (ds + 1) // 2
        sends.append(
            Send(
                k,
                con.at[pl.ds(768 + mine * 8, 8)],
                S["reg"].at[slot_of(dl, ds)],
                k.at(0, dl, ds),
                dl,
            )
        )
    back_halo = start(sends)
    g2 = S["g2"]
    S["brt"][...] = br[...].T
    for kk in range(nb):
        if kk == 1:
            stat_d = stat_middle(3, stat_d, "sums")
        for lo, width in cols:
            got = nn(S["brt"][...], filt[kk * px : (kk + 1) * px, lo : lo + width])
            spread(g2, kk * s.c5 * s.r641, c, s.r641, got, lo, width)
    ar2 = AllReduce(k, g2, h2o, s.rows[1], s.colors[1], [S[f"ar1_{j}"] for j in range(4)], S["osem"].at[1])
    ar2.step()
    put_misc(gm, MISC["proc_bias"], jnp.sum(br[...].astype(f32), axis=0, keepdims=True))
    for kk in range(nb):
        put_misc(gm, MISC["proc_last"] + kk, weighted(br[...], filt[kk * px : (kk + 1) * px, c - 1 : c]))

    arrive(back_halo)
    ng = S["ng"]
    ng[...] = con[own, :]

    @pl.when(k.has_up())
    def _():
        ng[...] = ng[...] + S["rup"][...]

    @pl.when(k.has_down())
    def _():
        ng[...] = ng[...] + S["rdn"][...]

    def add_edges(sl):
        for ss in (-1, 1):
            got = S["reg"].at[(sl + 1) * 2 + (ss + 1) // 2]
            col = 0 if ss == -1 else LANES - 2
            for q in range(2):
                lo = q * LANES + col
                ng[lo : lo + 2, :] = ng[lo : lo + 2, :] + got[2 * q : 2 * q + 2, :]

    add_edges(0)
    pl.when(k.has_up())(lambda: add_edges(-1))
    pl.when(k.has_down())(lambda: add_edges(1))
    sum_a, sum_b = stat_end(3, stat_d, "sums")
    g_one = vec(gain1)
    part_a1 = g_one * sum_a * (1.0 / s.pixels)
    part_b1 = g_one * sum_b * (1.0 / s.pixels)
    zg = S["zg"]

    def zero_rows(n, carry):
        here = pl.ds(pl.multiple_of(n * 32, 16), 32)
        there = pl.ds(pl.multiple_of(px + n * 32, 16), 32)
        standard = (hx[there, :] - mean1) * rstd1
        value = rstd1 * (g_one * ng[here, :] - part_a1 - standard * part_b1) + one[here, :]
        zg[here, :] = value.astype(bf16)
        return carry

    lax.fori_loop(0, px // 32, zero_rows, 0)

    g3 = S["g3"]
    for kk in range(nb):
        got = tn(filte[kk], zg[:, 0 : s.c5 * LANES])
        spread(g3, kk * s.c5 * s.r80, cj, s.r80, got, 0, s.c5 * LANES)
        put_misc(gm, MISC["enc_last"] + kk, weighted(filte[kk], zg[:, c - 1 : c]))
    put_misc(gm, MISC["enc_bias"], jnp.sum(zg[...].astype(f32), axis=0, keepdims=True))
    ar3 = AllReduce(k, g3, h3o, s.rows[2], s.colors[2], [S[f"ar2_{j}"] for j in range(4)], S["osem"].at[2])
    ar4 = AllReduce(k, gm, hmo, s.rows[3], s.colors[3], [S[f"ar3_{j}"] for j in range(4)], S["osem"].at[3])
    ar3.step()
    ar4.step()
    ar1.step()
    ar2.step()

    projt, partt = S["projt"], S["partt"]
    for kk in range(nb):
        here = slice(kk * LANES, (kk + 1) * LANES)
        proj = nt(h2[...], S["cw"][kk])
        part = nt(zg[...], S["ew"][kk])[:, 0:cin]
        for i in range(2):
            for ref, value in ((projt, proj), (partt, part)):
                ref[i, 0:cin, here] = value[i * LANES : (i + 1) * LANES, :].T.astype(bf16)
                ref[i, cin:80, here] = jnp.zeros((80 - cin, LANES), bf16)
    sgx = S["sgx"]
    em = S["em"]
    sgx[...] = jnp.zeros(sgx.shape, f32)
    for i in range(2):
        lo = 2 * i * big
        got = nn(projt[i], dm[i])
        sgx[0:80, lo : lo + 6 * big] = sgx[0:80, lo : lo + 6 * big] + got[:, 0 : 6 * big]
        sgx[0:80, edge0:] = sgx[0:80, edge0:] + got[:, 6 * big :]
        got = nn(partt[i], em[i])
        sgx[80:160, lo : lo + 5 * big] = sgx[80:160, lo : lo + 5 * big] + got[:, 0 : 5 * big]
        sgx[80:160, edge0:] = sgx[80:160, edge0:] + got[:, 5 * big :]
    sgb, sgu, sgd, sge = S["sgb"], S["sgu"], S["sgd"], S["sge"]
    sgb[:, 0 : 2 * big] = sgx[:, 0 : 2 * big].astype(bf16)
    sgb[:, 2 * big : 4 * big] = sgx[:, 6 * big : 8 * big].astype(bf16)
    sgb[:, 4 * big :] = sgx[:, edge0:].astype(bf16)
    sends = [
        Send(k, sgb.at[:, pl.ds(0, 2 * big)], sgd, k.at(0, -1, 0), -1),
        Send(k, sgb.at[:, pl.ds(2 * big, 2 * big)], sgu, k.at(0, 1, 0), 1),
    ]
    for dl, ds in dirs:
        sends.append(
            Send(k, sgb.at[:, pl.ds(4 * big, LANES)], sge.at[slot_of(dl, ds)], k.at(0, dl, ds), dl)
        )
    out_halo = start(sends)
    ar3.step()
    ar4.step()
    ar1.step()
    ar2.step()
    arrive(out_halo)
    up_one = jnp.where(k.has_up(), 1, 0)
    down_one = jnp.where(k.has_down(), 1, 0)
    cbt = S["cbt"]
    cbt[...] = jnp.zeros((8, LANES), f32)
    cbt[0:1, 0:cin] = vec(cb)
    bias_col = cbt[...].T[0:cin, 0:1]
    orow, st7 = S["orow"], S["st7"]

    for q in range(4):
        lo = (2 + q) * big
        value = sgx[:, lo : lo + big]
        if q < 2:
            other = sgu[:, q * big : (q + 1) * big].astype(f32)
            value = value + jnp.where(up_one == 1, other, 0.0)
        else:
            other = sgd[:, (q - 2) * big : (q - 1) * big].astype(f32)
            value = value + jnp.where(down_one == 1, other, 0.0)
        head, tail = value[:, 0:LANES], value[:, big - LANES :]
        sources = [(0, q + 2, None)]
        sources += [(-1, q + 6, up_one)] if q < 2 else [(1, q - 2, down_one)]
        for sl, r, there in sources:
            for ss in (-1, 1):
                got = sge[(sl + 1) * 2 + (ss + 1) // 2].astype(f32)
                if ss == -1:
                    moved = pltpu.roll(got, (LANES - (r * 4 + 2)) % LANES, 1)
                    bound = 2 if there is None else there * 2
                    head = head + jnp.where(lane < bound, moved, 0.0)
                else:
                    moved = pltpu.roll(got, (2 * LANES - 2 - r * 4) % LANES, 1)
                    bound = LANES - 2 if there is None else LANES - there * 2
                    tail = tail + jnp.where(lane >= bound, moved, 0.0)
        orow[:, q, 0:LANES] = (head[0:cin] + bias_col) * live
        orow[:, q, LANES:big] = (tail[0:cin] + bias_col) * live
        st7[k.e, :, q * big : q * big + LANES] = head[80:160].astype(bf16)
        st7[k.e, :, q * big + LANES : (q + 1) * big] = tail[80:160].astype(bf16)
    out[0] = orow[...].astype(bf16)
    state_sends = start(
        [Send(k, st7.at[k.e], st7.at[k.e], k.at(d, 0, 0)) for d in range(1, s.ne)]
    )
    for _ in range(2):
        ar3.step()
        ar4.step()
        ar1.step()
        ar2.step()
    arrive(date_sends)
    arrive(state_sends)
    for d in range(s.dates):
        for q in range(4):
            value = jnp.zeros((80, big), f32)
            for n in range(s.ne):
                is_d = jnp.where(S["dates"][n, 0:1, :] == float(d), 1.0, 0.0)
                is_d = jnp.concatenate([is_d] * (big // LANES), axis=1)
                value = value + is_d * st7[n, :, q * big : (q + 1) * big].astype(f32)
            orow[:, q, :] = value[0:cin]
        sgrad[d] = orow[...].astype(bf16)

    rest = [ar1, ar2, ar3, ar4]
    while any(a.stage < AllReduce.stages for a in rest):
        for a in rest:
            if a.stage < AllReduce.stages:
                a.step()
    for m in pending:
        m.wait_send()


def finish_kernel(s, *refs):
    h1, h2, h3, hm, output_in, state_in, m1, v1, m2, v2 = refs[:10]
    (
        output, state_grad,
        enc_w, enc_b, g1o, s1o, proc_w, proc_b, g2o, s2o,
        up_w, up_b, down_w, down_b, dec_w, dec_b, m1o, v1o, m2o, v2o,
    ) = refs[10:30]
    (b1, b2, b3, enc_v, proc_v, up_v, down_v, dec_v, row_v, sem_in, sem_out) = refs[30:]
    c, ff, nb, cin, cj = s.c, s.ff, s.nb, s.cin, s.cj
    used1 = s.off_dec + nb * s.c5 * s.r80
    third = s.c5 * s.r641
    pieces = [(h2, b2, n * third, third) for n in range(nb)]
    pieces += [(h1, b1, 0, s.off_down), (h1, b1, s.off_down, s.off_dec - s.off_down)]
    pieces += [(h1, b1, s.off_dec, used1 - s.off_dec), (h3, b3, 0, nb * s.c5 * s.r80)]
    loads = [
        pltpu.make_async_copy(a.at[pl.ds(at, n)], b.at[pl.ds(at, n)], sem_in.at[i])
        for i, (a, b, at, n) in enumerate(pieces)
    ]
    for copy in loads:
        copy.start()
    stores = []

    def store(src, dst):
        copy = pltpu.make_async_copy(src, dst, sem_out.at[len(stores)])
        copy.start()
        stores.append(copy)

    store(output_in, output)
    store(state_in, state_grad)
    for a, b in ((m1, m1o), (v1, v1o), (m2, m2o), (v2, v2o)):
        b[...] = a[...]
    turned = hm[0:144, :].T

    def last_column(ref, slot, height, at):
        for t in range(-(-height // LANES)):
            n = min(LANES, height - t * LANES)
            ref[t * LANES : t * LANES + n, at : at + 1] = turned[0:n, slot * 6 + t : slot * 6 + t + 1]

    def widen(ref, src, base, pitch, height, tiles):
        for n in range(tiles):
            at = base + n * pitch
            ref[:, n * LANES : (n + 1) * LANES] = src[at : at + height, :].astype(f32)

    last = s.c5 * LANES
    for kk in range(nb):
        ref = proc_v.at[kk]
        last_column(ref, MISC["proc_last"] + kk, c, last)
        loads[kk].wait()
        widen(ref, b2, kk * third, s.r641, c, s.c5)
        store(ref, proc_w.at[kk])
    for n, (ref, name, base, to) in enumerate(
        ((up_v, "up_last", 0, up_w), (down_v, "down_last", s.off_down, down_w))
    ):
        for part in range(2):
            last_column(ref, MISC[name] + part, c, s.f10 * LANES + part)
        loads[nb + n].wait()
        widen(ref, b1, base, s.r641, c, s.f10)
        store(ref, to)
    loads[nb + 2].wait()
    loads[nb + 3].wait()
    for kk in range(nb):
        ref = dec_v.at[kk]
        last_column(ref, MISC["dec_last"] + kk, cin, last)
        widen(ref, b1, s.off_dec + kk * s.c5 * s.r80, s.r80, cin, s.c5)
        ref = enc_v.at[kk]
        last_column(ref, MISC["enc_last"] + kk, cj, last)
        widen(ref, b3, kk * s.c5 * s.r80, s.r80, cj, s.c5)
    store(dec_v, dec_w)
    store(enc_v, enc_w)

    def flat(ref, slots):
        at = 0
        for slot, width in slots:
            for piece in get_misc(hm, slot, width):
                n = piece.shape[1]
                row_v[0:1, at : at + n] = piece
                at += n
        ref[...] = row_v[0:1, 0:at].reshape(at)

    for ref, name in (
        (enc_b, "enc_bias"), (g1o, "gain_one"), (s1o, "shift_one"), (proc_b, "proc_bias"),
        (g2o, "gain_two"), (s2o, "shift_two"), (down_b, "down_bias"),
    ):
        flat(ref, [(MISC[name], c)])
    flat(up_b, [(MISC["up_bias"], 768), (MISC["up_bias"] + 1, ff - 768)])
    flat(dec_b, [(MISC["dec_bias"], cin)])
    for copy in stores:
        copy.wait()


def per_device(s, *args):
    (
        state, noise, cot, slot_date, lon_reach, enc_taps, proc_taps, dec_taps,
        enc_weight, enc_bias, gain_one, shift_one, proc_weight, proc_bias, gain_two, shift_two,
        up_weight, up_bias, down_weight, down_bias, dec_weight, dec_bias,
    ) = args
    args = list(args)
    args[8] = jnp.swapaxes(enc_weight, 1, 2)
    args[16] = up_weight.T
    vm = pl.BlockSpec(memory_space=pltpu.VMEM)
    sm = pl.BlockSpec(memory_space=pltpu.SMEM)
    hbm = pl.BlockSpec(memory_space=pl.ANY)
    shapes = scratch_list(s)
    shapes["sems"] = pltpu.SemaphoreType.DMA((sem_count(s),))
    names = tuple(shapes)
    in_specs = [vm] * 3 + [sm] * 5 + [
        hbm, vm, vm, vm, hbm, vm, vm, vm, hbm, vm, hbm, vm, hbm, vm,
    ]
    sd = jax.ShapeDtypeStruct
    out_shape = [
        sd((s.rows[0], LANES), bf16),
        sd((s.rows[1], LANES), bf16),
        sd((s.rows[2], LANES), bf16),
        sd((s.rows[3], LANES), f32),
        sd((1, s.cin, s.full_rows, s.full_cols), bf16),
        sd((s.dates, s.cin, s.full_rows, s.full_cols), bf16),
    ] + [sd((1, s.c), f32)] * 4
    got = pl.pallas_call(
        functools.partial(main_kernel, s, names),
        out_shape=out_shape,
        in_specs=in_specs,
        out_specs=[hbm] * 4 + [vm] * 6,
        scratch_shapes=list(shapes.values()),
        compiler_params=pltpu.CompilerParams(
            collective_id=0, has_side_effects=True, vmem_limit_bytes=60 * 2**20
        ),
        name="forecast",
    )(*args)
    c, ff, nb = s.c, s.ff, s.nb
    outs = [out_shape[4], out_shape[5]] + [
        sd((nb, s.cj, c), f32), sd((c,), f32), sd((c,), f32), sd((c,), f32),
        sd((nb, c, c), f32), sd((c,), f32), sd((c,), f32), sd((c,), f32),
        sd((c, ff), f32), sd((ff,), f32), sd((c, ff), f32), sd((c,), f32),
        sd((nb, s.cin, c), f32), sd((s.cin,), f32),
    ] + [sd((1, c), f32)] * 4
    large = (0, 1, 2, 6, 10, 12, 14)
    V = pltpu.VMEM
    done = pl.pallas_call(
        functools.partial(finish_kernel, s),
        out_shape=outs,
        in_specs=[hbm] * 3 + [vm] + [hbm] * 2 + [vm] * 4,
        out_specs=[hbm if n in large else vm for n in range(len(outs))],
        scratch_shapes=[
            V((s.rows[0], LANES), bf16), V((s.rows[1], LANES), bf16), V((s.rows[2], LANES), bf16),
            V((nb, s.cj, c), f32), V((nb, c, c), f32), V((c, ff), f32), V((c, ff), f32),
            V((nb, s.cin, c), f32), V((8, up_to(ff, LANES)), f32),
            pltpu.SemaphoreType.DMA((8,)), pltpu.SemaphoreType.DMA((16,)),
        ],
        compiler_params=pltpu.CompilerParams(vmem_limit_bytes=60 * 2**20),
        name="finish",
    )(*got)
    done = list(done)
    done[2] = jnp.swapaxes(done[2], 1, 2)
    done[10] = done[10].T
    return tuple(done)


def solution(mesh):
    in_specs = (
        P(None, None, "lat", "lon"),
        P("ens", None, "lat", "lon"),
        P("ens", None, "lat", "lon"),
        P("ens"),
    ) + (P(),) * 18
    out_specs = (
        (P("ens", None, "lat", "lon"), P(None, None, "lat", "lon"))
        + (P(),) * 14
        + (P("ens", None),) * 4
    )

    def run(*args):
        s = Sizes(mesh, args[0].shape, args[1].shape, args[5].shape, args[8].shape, args[16].shape)
        return jax.shard_map(
            functools.partial(per_device, s),
            mesh=mesh,
            in_specs=in_specs,
            out_specs=out_specs,
            check_vma=False,
        )(*args)

    return run
```

```python
import functools

import jax
import jax.numpy as jnp
from jax import lax
from jax.experimental import pallas as pl
from jax.experimental.pallas import tpu as pltpu
from jax.sharding import PartitionSpec as P

MESH = pl.DeviceIdType.MESH
f32 = jnp.float32
bf16 = jnp.bfloat16
i32 = jnp.int32
EPS = 1e-05
LANES = 128
AXES = ("ens", "lat", "lon")
ROUTE_X = ("lat", "bit0", "bit1", "lon")
ROUTE_Y = ("lat", "bit1", "bit0", "lon")


def nn(a, b):
    return lax.dot_general(a, b, (((1,), (0,)), ((), ())), preferred_element_type=f32)


def nt(a, b):
    return lax.dot_general(a, b, (((1,), (1,)), ((), ())), preferred_element_type=f32)


def tn(a, b):
    return lax.dot_general(a, b, (((0,), (0,)), ((), ())), preferred_element_type=f32)


def up_to(n, m):
    return -(-n // m) * m


class Sizes:
    def __init__(self, mesh, state, noise, enc_taps, enc_weight, up_weight):
        self.ne, self.nl, self.nz = (mesh.shape[a] for a in AXES)
        self.dates, self.cin, self.full_rows, self.full_cols = state
        self.noise = noise[1]
        self.full_rows = state[2] // self.nl
        self.full_cols = state[3] // self.nz
        self.hr, self.hc = self.full_rows // 2, self.full_cols // 2
        assert self.hr == 2 and self.hc == LANES and self.ne == 4
        self.lat_total = enc_taps[1]
        self.nb = enc_taps[0]
        self.c = enc_weight[1]
        self.cj = enc_weight[2]
        self.ff = up_weight[0]
        self.px = self.hr * self.hc
        self.pixels = float(self.px * self.nl * self.nz)
        self.c5 = self.c // LANES
        self.f10 = self.ff // LANES
        self.r641 = up_to(self.c, 16)
        self.r80 = up_to(self.cj, 16)
        self.off_up = self.f10 * self.r641
        self.off_dec = self.off_up + self.f10 * self.r641
        used = (
            self.off_dec + self.nb * self.c5 * self.r80,
            self.nb * self.c5 * self.r641,
            self.nb * self.c5 * self.r80,
        )
        unit = 16 * self.nl * self.ne * self.nz
        self.rows = tuple(up_to(n, unit) for n in used) + (up_to(24 * 6, unit // 2),)
        self.chunks = {}

        def split(name, buffer, lo, hi):
            first = lo + up_to((hi - lo) // 2, unit)
            for n, (a, b, route) in enumerate(((lo, first, ROUTE_X), (first, hi, ROUTE_Y))):
                if b > a:
                    self.chunks[name + str(n)] = (buffer, a, b - a, route)

        cut = self.off_up // unit * unit
        split("A", 0, 0, cut)
        split("B", 0, cut, self.rows[0])
        cut = 2 * self.c5 * self.r641 // unit * unit
        split("C", 1, 0, cut)
        split("D", 1, cut, self.rows[1])
        self.chunks["E0"] = (2, 0, self.rows[2], ROUTE_X)
        self.chunks["M0"] = (3, 0, self.rows[3], ROUTE_Y)
        self.group = self.nl * self.nz


def add_into(dst, at, sources, count):
    step = next(s for s in (256, 128, 64, 32, 16, 8) if count % s == 0)

    def body(n, carry):
        lo = pl.multiple_of(n * step, 8 if step == 8 else 16)
        there = pl.ds(pl.multiple_of(at + lo, 8 if step == 8 else 16), step)
        value = dst[there, :].astype(f32)
        for source in sources:
            value = value + source[pl.ds(lo, step), :].astype(f32)
        dst[there, :] = value.astype(dst.dtype)
        return carry

    lax.fori_loop(0, count // step, body, 0)


class Links:
    def __init__(self, z, sems=None):
        self.s = z
        self.sems = sems
        self.used = 0
        if sems is not None:
            self.e, self.l, self.z = (lax.axis_index(a) for a in AXES)

    def take(self):
        self.used += 1
        return self.used - 1

    def at(self, de, dl, dz):
        s = self.s
        return (
            lax.rem(self.e + (de + s.ne), s.ne),
            lax.rem(self.l + (dl + s.nl), s.nl),
            lax.rem(self.z + (dz + s.nz), s.nz),
        )

    def bit(self, which):
        return lax.rem(self.e // (1 << which), 2)

    def flip(self, which):
        return (self.e + (1 << which) * (1 - 2 * self.bit(which)), self.l, self.z)

    def has_up(self):
        return self.l > 0

    def has_down(self):
        return self.l < self.s.nl - 1


class Send:
    def __init__(self, links, src, dst, device, dl=0):
        self.links = links
        self.ids = (links.take(), links.take())
        self.what = (src, dst, device)
        self.dl = dl

    def copy(self):
        src, dst, device = self.what
        return pltpu.make_async_remote_copy(
            src_ref=src,
            dst_ref=dst,
            send_sem=self.links.sems.at[self.ids[0]],
            recv_sem=self.links.sems.at[self.ids[1]],
            device_id=device,
            device_id_type=MESH,
        )

    def under(self, sending, act):
        if self.dl == 0:
            act()
        else:
            up = (self.dl < 0) == sending
            pl.when(self.links.has_up() if up else self.links.has_down())(act)

    def start(self):
        self.under(True, lambda: self.copy().start())

    def wait_recv(self):
        self.under(False, lambda: self.copy().wait_recv())

    def wait_send(self):
        self.under(True, lambda: self.copy().wait_send())


class AllReduce:
    def __init__(self, links, partial, total, lo, rows, route, bufs, own_sem):
        self.k, self.g, self.h, self.route = links, partial, total, route
        self.bufs, self.own_sem = bufs, own_sem
        self.sent, self.waiting = [], []
        self.stage = 0
        self.base, self.part = [], []
        base, size = lo, rows
        for axis in route:
            size = size // self.count(links.s, axis)
            self.base.append(base)
            self.part.append(size)
            base = base + self.index(axis) * size
        self.base.append(base)
        self.last_stage = 2 * len(route)

    @staticmethod
    def count(s, axis):
        return {"lat": s.nl, "lon": s.nz}.get(axis, 2)

    @staticmethod
    def shapes(s, rows, route, dtype):
        out = []
        for axis in route:
            n = AllReduce.count(s, axis)
            rows = rows // n
            out.append(pltpu.VMEM((n - 1, rows, LANES), dtype))
        return out

    def index(self, axis):
        k = self.k
        return {"lat": k.l, "lon": k.z}[axis] if axis in ("lat", "lon") else k.bit(int(axis[3:]))

    def others(self, axis):
        k, s = self.k, self.k.s
        if axis == "lat":
            devices = [k.at(0, d, 0) for d in range(1, s.nl)]
            return [(dev, dev[1], n) for n, dev in enumerate(devices)]
        if axis == "lon":
            devices = [k.at(0, 0, d) for d in range(1, s.nz)]
            return [(dev, dev[2], n) for n, dev in enumerate(devices)]
        which = int(axis[3:])
        return [(k.flip(which), 1 - k.bit(which), 0)]

    def send(self, src, dst, device):
        m = Send(self.k, src, dst, device)
        m.start()
        self.sent.append(m)
        self.waiting.append(m)

    def step(self):
        g, h, route = self.g, self.h, self.route
        al = lambda v: pl.multiple_of(v, 8)
        stage, self.stage = self.stage, self.stage + 1
        for m in self.waiting:
            m.wait_recv()
        self.waiting = []
        depth = len(route)
        if 0 < stage <= depth:
            buf = self.bufs[stage - 1]
            add_into(g, al(self.base[stage]), [buf.at[n] for n in range(buf.shape[0])], self.part[stage - 1])
        if stage < depth:
            size = self.part[stage]
            for device, place, slot in self.others(route[stage]):
                there = pl.ds(al(self.base[stage] + place * size), size)
                self.send(g.at[there], self.bufs[stage].at[slot], device)
        elif stage < 2 * depth:
            level = 2 * depth - 1 - stage
            here = pl.ds(al(self.base[level + 1]), self.part[level])
            if stage == depth:
                self.own = pltpu.make_async_copy(g.at[here], h.at[here], self.own_sem)
                self.own.start()
            if stage == depth + 1:
                self.own.wait()
            source = g if stage == depth else h
            for device, _, _ in self.others(route[level]):
                self.send(source.at[here], h.at[here], device)
        else:
            for m in self.sent:
                m.wait_send()

    def finished(self):
        return self.stage > self.last_stage


def misc_slots():
    names = [
        ("down_bias", 1),
        ("up_bias", 2),
        ("gain_two", 1),
        ("shift_two", 1),
        ("proc_bias", 1),
        ("gain_one", 1),
        ("shift_one", 1),
        ("enc_bias", 1),
        ("up_last", 2),
        ("down_last", 2),
        ("proc_last", 3),
        ("enc_last", 3),
        ("dec_last", 3),
        ("dec_bias", 1),
    ]
    table, at = {}, 0
    for name, count in names:
        table[name] = at
        at += count
    return table


MISC = misc_slots()


def put_misc(misc, slot, row):
    width = row.shape[1]
    for t in range(-(-width // LANES)):
        lo, hi = t * LANES, min(width, (t + 1) * LANES)
        misc[slot * 6 + t : slot * 6 + t + 1, 0 : hi - lo] = row[:, lo:hi]


def get_misc(misc, slot, width):
    parts = []
    for t in range(-(-width // LANES)):
        lo, hi = t * LANES, min(width, (t + 1) * LANES)
        parts.append(misc[slot * 6 + t : slot * 6 + t + 1, 0 : hi - lo])
    return parts


def scratch_list(s):
    c, ff, px = s.c, s.ff, s.px
    big = s.full_cols
    wide = 8 * big + LANES
    V = pltpu.VMEM
    shapes = {
        "xin": V((160, s.full_rows, big), f32),
        "xj": V((160, 8 * big), bf16),
        "eb": V((2, 8, 160), f32),
        "eslot": V((6, 8, 160), f32),
        "xe": V((48, 160), bf16),
        "em": V((2, s.nb * LANES, 5 * big + 48), bf16),
        "dm": V((2, s.nb * LANES, 6 * big + 48), bf16),
        "tm": V((s.nb * px, 6 * LANES + 48), bf16),
        "ew": V((s.nb, s.cj, c), bf16),
        "pw": V((s.nb, c, c), bf16),
        "uw": V((c, ff), bf16),
        "dw": V((c, ff), bf16),
        "cw": V((s.nb, s.cin, c), bf16),
        "filte": V((s.nb, px, s.cj), bf16),
        "hx": V((6 * LANES + 48, c), f32),
        "nx": V((6 * LANES + 48, c), bf16),
        "pe": V((2, 8, c), f32),
        "filt": V((s.nb * px, c), bf16),
        "h1": V((px, c), f32),
        "n2": V((px, c), bf16),
        "hp": V((px, ff), f32),
        "ag": V((px, ff), f32),
        "act": V((px, ff), bf16),
        "hg": V((px, ff), bf16),
        "n2t": V((c, px), bf16),
        "h2": V((px, c), bf16),
        "pgr": V((s.nb, px, s.cin), bf16),
        "projt": V((2, 80, s.nb * LANES), bf16),
        "partt": V((2, 80, s.nb * LANES), bf16),
        "two": V((px, c), f32),
        "mg": V((px, c), bf16),
        "mgt": V((c, px), bf16),
        "ntg": V((px, c), f32),
        "one": V((px, c), f32),
        "br": V((px, c), bf16),
        "brt": V((c, px), bf16),
        "fg": V((s.nb * px, c), bf16),
        "con": V((6 * LANES + 48, c), f32),
        "rup": V((px, c), f32),
        "rdn": V((px, c), f32),
        "reg": V((6, 8, c), f32),
        "zg": V((px, c), bf16),
        "sgx": V((160, wide), f32),
        "sgb": V((160, 4 * big), bf16),
        "sgu": V((160, 2 * big), bf16),
        "sgd": V((160, 2 * big), bf16),
        "sgn": V((6, 8, 160), f32),
        "sge": V((6, 8, 160), f32),
        "sgt": V((LANES, 160), f32),
        "orow": V((s.cin, s.full_rows, big), f32),
        "st7": V((s.ne, 80, 4 * big), bf16),
        "dates": V((s.ne, 8, LANES), f32),
        "cbt": V((8, LANES), f32),
        "slat": V((4, s.nl, 2, c), f32),
        "slon": V((4, s.nz, 2, c), f32),
        "sall": V((4, s.group if s.group <= 16 else 1, 2, c), f32),
        "tmt": V((6 * LANES + 48, s.nb * px), bf16),
        "g1": V((s.rows[0], LANES), bf16),
        "g2": V((s.rows[1], LANES), bf16),
        "g3": V((s.rows[2], LANES), bf16),
        "gm": V((s.rows[3], LANES), f32),
    }
    for name, (buffer, _, rows, route) in s.chunks.items():
        kinds = AllReduce.shapes(s, rows, route, f32 if buffer == 3 else bf16)
        for j, kind in enumerate(kinds):
            shapes[f"ar{name}_{j}"] = kind
    shapes["wsem"] = pltpu.SemaphoreType.DMA((5,))
    shapes["osem"] = pltpu.SemaphoreType.DMA((len(s.chunks),))
    return shapes


def sem_count(s):
    total = len(s.chunks) * 2 * 2 * (s.nl - 1 + 1 + 1 + s.nz - 1)
    total += 2 * 4 * 8 + 2 * 2 * (s.ne - 1)
    total += 4 * 2 * (s.group - 1 if s.group <= 16 else s.nl - 1 + s.nz - 1)
    return total


def main_kernel(s, names, *refs):
    n_in, n_out = 22, 10
    (
        state, noise, cot, date_ref, reach, enc_taps, proc_taps, dec_taps,
        ew_h, eb, gain1, shift1, pw_h, pb, gain2, shift2, uw_h, ub, dw_h, db, cw_h, cb,
    ) = refs[:n_in]
    h1o, h2o, h3o, hmo, out, sgrad, m1o, v1o, m2o, v2o = refs[n_in : n_in + n_out]
    S = dict(zip(names, refs[n_in + n_out :]))
    sems = S["sems"]
    k = Links(s, sems)
    c, ff, px, nb, cin, cj = s.c, s.ff, s.px, s.nb, s.cin, s.cj
    big = s.full_cols
    l = k.l
    row0 = l * s.hr
    edge0 = 8 * big

    offsets = {(d, 0, 0) for d in range(1, s.ne)}
    if s.group <= 16:
        offsets |= {(0, a, b) for a in range(s.nl) for b in range(s.nz)} - {(0, 0, 0)}
    else:
        offsets |= {(0, d, 0) for d in range(1, s.nl)} | {(0, 0, d) for d in range(1, s.nz)}
    offsets |= {(0, a % s.nl, b % s.nz) for a in (1, -1) for b in (1, -1)}
    offsets = sorted(offsets)
    barrier = pltpu.get_barrier_semaphore()
    for o in offsets:
        pl.semaphore_signal(barrier, 1, device_id=k.at(*o), device_id_type=MESH)

    loads = {}
    for n, (name, src) in enumerate(
        (("ew", ew_h), ("pw", pw_h), ("uw", uw_h), ("dw", dw_h), ("cw", cw_h))
    ):
        loads[name] = pltpu.make_async_copy(src, S[name], S["wsem"].at[n])
        loads[name].start()

    date = date_ref[0]
    live = jnp.where(date >= 0, 1.0, 0.0).astype(f32)
    xin, xj = S["xin"], S["xj"]
    picked = jnp.zeros((cin, s.full_rows, big), f32)
    for d in range(s.dates):
        picked = picked + state[d].astype(f32) * jnp.where(date == d, 1.0, 0.0).astype(f32)
    xin[0:cin] = picked
    xin[cin:cj] = noise[0].astype(f32)
    xin[80 : 80 + cin] = cot[0].astype(f32) * live
    xin[80 + cin : 160] = jnp.zeros((160 - 80 - cin, s.full_rows, big), f32)
    lane = lax.broadcasted_iota(i32, (160, LANES), 1)
    ends = jnp.zeros((160, LANES), f32)
    for q in range(4):
        row = xin[:, q, :]
        xj[:, (2 + q) * big : (3 + q) * big] = row.astype(bf16)
        moved = pltpu.roll(row[:, 0:LANES], q * 2, 1)
        ends = jnp.where((lane >> 1) == q, moved, ends)
        moved = pltpu.roll(row[:, big - LANES : big], q * 2 + 10, 1)
        ends = jnp.where((lane >> 1) == q + 4, moved, ends)
    turned = ends.T
    S["eb"][0] = turned[0:8, :]
    S["eb"][1] = turned[8:16, :]
    S["dates"][k.e] = jnp.full((8, LANES), date.astype(f32), f32)

    @pl.when(jnp.logical_not(k.has_up()))
    def _():
        xj[:, 0 : 2 * big] = jnp.zeros((160, 2 * big), bf16)
        S["hx"][0:px] = jnp.zeros((px, c), f32)
        for side in range(2):
            S["hx"][768 + side * 8 : 776 + side * 8] = jnp.zeros((8, c), f32)

    @pl.when(jnp.logical_not(k.has_down()))
    def _():
        xj[:, 6 * big : 8 * big] = jnp.zeros((160, 2 * big), bf16)
        S["hx"][2 * px : 3 * px] = jnp.zeros((px, c), f32)
        for side in range(2):
            S["hx"][768 + 32 + side * 8 : 776 + 32 + side * 8] = jnp.zeros((8, c), f32)

    pl.semaphore_wait(barrier, len(offsets))

    totals = (h1o, h2o, h3o, hmo)
    reduced = {}
    for n, (name, (buffer, lo, rows, route)) in enumerate(s.chunks.items()):
        bufs = [S[f"ar{name}_{j}"] for j in range(len(route))]
        partial = S[("g1", "g2", "g3", "gm")[buffer]]
        reduced[name] = AllReduce(k, partial, totals[buffer], lo, rows, route, bufs, S["osem"].at[n])

    def ar(letters):
        for letter in letters:
            for n in range(2):
                it = reduced.get(letter + str(n))
                if it is not None and not it.finished():
                    it.step()

    pending = []

    def start(sends):
        for m in sends:
            m.start()
        pending.extend(sends)
        return sends

    def arrive(sends):
        for m in sends:
            m.wait_recv()

    dirs = [(dl, ds) for dl in (-1, 0, 1) for ds in (-1, 1)]

    def slot_of(dl, ds):
        return (1 - dl) * 2 + (1 - ds) // 2

    sends = [
        Send(k, xj.at[:, pl.ds(2 * big, 2 * big)], xj.at[:, pl.ds(6 * big, 2 * big)], k.at(0, -1, 0), -1),
        Send(k, xj.at[:, pl.ds(4 * big, 2 * big)], xj.at[:, pl.ds(0, 2 * big)], k.at(0, 1, 0), 1),
    ]
    for dl, ds in dirs:
        sends.append(
            Send(k, S["eb"].at[(ds + 1) // 2], S["eslot"].at[slot_of(dl, ds)], k.at(0, dl, ds), dl)
        )
    first_halo = start(sends)
    date_sends = start(
        [
            Send(k, S["dates"].at[k.e], S["dates"].at[k.e], k.at(d, 0, 0))
            for d in range(1, s.ne)
        ]
    )

    gm = S["gm"]
    gm[0:144] = jnp.zeros((144, LANES), f32)

    def band(shape, column_of):
        rows = lax.broadcasted_iota(i32, shape, 0)
        cols = lax.broadcasted_iota(i32, shape, 1)
        return column_of(rows, cols)

    def pick(d, table, like):
        value = jnp.zeros(like, f32)
        for key, scalar in table:
            value = jnp.where(d == key, scalar, value)
        return value

    def inside(grow, total):
        return jnp.logical_and(grow >= 0, grow < total)

    def edge_lane(shape):
        at = lax.broadcasted_iota(i32, shape, 1)
        slot, q, m = at >> 3, (at & 7) >> 1, at & 1
        r = q + 2 + 4 * ((slot >> 1) - 1)
        return r, jnp.where((slot & 1) == 0, m - 2, big + m), at

    def build_encoder():
        em = S["em"]
        d_main = band((LANES, big), lambda j, J: J - 2 * j)
        r, J, at = edge_lane((16, 48))
        j = lax.broadcasted_iota(i32, (16, 48), 0)
        codes = []
        for start_row in (0, LANES - 16):
            d = J - 2 * (j + start_row)
            codes.append(r * 1024 + d)
        for i in range(2):
            reached = reach[row0 + i]
            edges = [[jnp.zeros((16, 48), f32) for _ in range(2)] for _ in range(nb)]
            for a in range(-2, 3):
                r_in = 2 * i + a + 2
                ok = inside(4 * l + r_in - 2, 2 * s.lat_total)
                masks = [d_main == b for b in range(-2, 3)]
                for kk in range(nb):
                    value = jnp.zeros((LANES, big), f32)
                    for b in range(-2, 3):
                        tap = enc_taps[kk, row0 + i, 5 * (a + 2) + b + 2]
                        tap = jnp.where(jnp.logical_and(ok, abs(b) <= reached), tap, 0.0)
                        value = jnp.where(masks[b + 2], tap, value)
                        for part in range(2):
                            edges[kk][part] = jnp.where(
                                codes[part] == r_in * 1024 + b, tap, edges[kk][part]
                            )
                    em[i, kk * LANES : (kk + 1) * LANES, (a + 2) * big : (a + 3) * big] = value.astype(bf16)
            for kk in range(nb):
                lo = kk * LANES
                em[i, lo : lo + 16, 5 * big :] = edges[kk][0].astype(bf16)
                em[i, lo + 16 : lo + LANES - 16, 5 * big :] = jnp.zeros((LANES - 32, 48), bf16)
                em[i, lo + LANES - 16 : lo + LANES, 5 * big :] = edges[kk][1].astype(bf16)

    def build_decoder():
        dm = S["dm"]
        d_main = band((LANES, big), lambda j, J: j - (J >> 1))
        r, J, at = edge_lane((16, 48))
        j = lax.broadcasted_iota(i32, (16, 48), 0)
        codes = []
        for start_row in (0, LANES - 16):
            d = (j + start_row) - (J >> 1)
            codes.append(r * 1024 + d)
        for i in range(2):
            edges = [[jnp.zeros((16, 48), f32) for _ in range(2)] for _ in range(nb)]
            for n in range(6):
                r_in = 2 * i + n
                a = i + 1 - r_in // 2
                full = 4 * l + r_in - 2
                ok = inside(full, 2 * s.lat_total)
                full = jnp.clip(full, 0, 2 * s.lat_total - 1)
                reached = reach[full // 2] - 1
                masks = [d_main == b for b in range(-1, 2)]
                for kk in range(nb):
                    value = jnp.zeros((LANES, big), f32)
                    for b in range(-1, 2):
                        tap = dec_taps[kk, full, 3 * (a + 1) + b + 1]
                        tap = jnp.where(jnp.logical_and(ok, abs(b) <= reached), tap, 0.0)
                        value = jnp.where(masks[b + 1], tap, value)
                        for part in range(2):
                            edges[kk][part] = jnp.where(
                                codes[part] == r_in * 1024 + b, tap, edges[kk][part]
                            )
                    dm[i, kk * LANES : (kk + 1) * LANES, n * big : (n + 1) * big] = value.astype(bf16)
            for kk in range(nb):
                lo = kk * LANES
                dm[i, lo : lo + 16, 6 * big :] = edges[kk][0].astype(bf16)
                dm[i, lo + 16 : lo + LANES - 16, 6 * big :] = jnp.zeros((LANES - 32, 48), bf16)
                dm[i, lo + LANES - 16 : lo + LANES, 6 * big :] = edges[kk][1].astype(bf16)

    def build_processor():
        tm = S["tm"]
        d_main = band((LANES, LANES), lambda j, J: J - j)
        at = lax.broadcasted_iota(i32, (16, 48), 1)
        slot, idx = at >> 3, at & 7
        r = 2 * (slot >> 1) + (idx >> 1)
        m = idx & 1
        J = jnp.where((slot & 1) == 0, m - 2, LANES + m)
        j = lax.broadcasted_iota(i32, (16, 48), 0)
        codes = []
        for start_row in (0, LANES - 16):
            d = J - (j + start_row)
            codes.append(jnp.where(idx < 4, r * 1024 + d, -5000))
        for i in range(2):
            reached = reach[row0 + i]
            edges = [[jnp.zeros((16, 48), f32) for _ in range(2)] for _ in range(nb)]
            for r_in in range(6):
                a = r_in - 2 - i
                if abs(a) > 2:
                    for kk in range(nb):
                        lo = kk * px + i * LANES
                        tm[lo : lo + LANES, r_in * LANES : (r_in + 1) * LANES] = jnp.zeros((LANES, LANES), bf16)
                    continue
                ok = inside(row0 + r_in - 2, s.lat_total)
                masks = [d_main == b for b in range(-2, 3)]
                for kk in range(nb):
                    value = jnp.zeros((LANES, LANES), f32)
                    for b in range(-2, 3):
                        tap = proc_taps[kk, row0 + i, 5 * (a + 2) + b + 2]
                        tap = jnp.where(jnp.logical_and(ok, abs(b) <= reached), tap, 0.0)
                        value = jnp.where(masks[b + 2], tap, value)
                        for part in range(2):
                            edges[kk][part] = jnp.where(
                                codes[part] == r_in * 1024 + b, tap, edges[kk][part]
                            )
                    lo = kk * px + i * LANES
                    tm[lo : lo + LANES, r_in * LANES : (r_in + 1) * LANES] = value.astype(bf16)
            for kk in range(nb):
                lo = kk * px + i * LANES
                tm[lo : lo + 16, 768:816] = edges[kk][0].astype(bf16)
                tm[lo + 16 : lo + LANES - 16, 768:816] = jnp.zeros((LANES - 32, 48), bf16)
                tm[lo + LANES - 16 : lo + LANES, 768:816] = edges[kk][1].astype(bf16)

    slat, slon = S["slat"], S["slon"]

    def fold(values, kind, count):
        total_a, total_b = values[0]
        for a, b in values[1:]:
            total_a = total_a + a
            total_b = total_b + b
        if kind == "moments":
            total_a = total_a * (1.0 / len(values))
            for a, b in values:
                total_b = total_b + (a - total_a) * (a - total_a) * count
        return total_a, total_b

    single = s.group <= 16
    sall = S["sall"]
    place = k.l * s.nz + k.z

    def stat_start(rd, a, b):
        if single:
            sall[rd, place, 0:1, :] = a
            sall[rd, place, 1:2, :] = b
            others = [(0, m, n) for n in range(s.nz) for m in range(s.nl) if m or n]
            return start(
                [Send(k, sall.at[rd, place], sall.at[rd, place], k.at(*o)) for o in others]
            )
        slat[rd, k.l, 0:1, :] = a
        slat[rd, k.l, 1:2, :] = b
        return start(
            [
                Send(k, slat.at[rd, k.l], slat.at[rd, k.l], k.at(0, d, 0))
                for d in range(1, s.nl)
            ]
        )

    def stat_middle(rd, sends, kind):
        if single:
            return sends
        arrive(sends)
        values = [(slat[rd, n, 0:1, :], slat[rd, n, 1:2, :]) for n in range(s.nl)]
        a, b = fold(values, kind, float(px))
        slon[rd, k.z, 0:1, :] = a
        slon[rd, k.z, 1:2, :] = b
        return start(
            [
                Send(k, slon.at[rd, k.z], slon.at[rd, k.z], k.at(0, 0, d))
                for d in range(1, s.nz)
            ]
        )

    def stat_end(rd, sends, kind):
        arrive(sends)
        if single:
            values = [(sall[rd, n, 0:1, :], sall[rd, n, 1:2, :]) for n in range(s.group)]
            return fold(values, kind, float(px))
        values = [(slon[rd, n, 0:1, :], slon[rd, n, 1:2, :]) for n in range(s.nz)]
        return fold(values, kind, float(px * s.nl))

    def moments(values):
        mean = jnp.sum(values, axis=0, keepdims=True) * (1.0 / px)
        centred = values - mean
        return mean, jnp.sum(centred * centred, axis=0, keepdims=True)

    def vec(ref):
        n = ref.shape[0]
        return ref[...].reshape(1, n)

    build_encoder()
    build_decoder()
    build_processor()

    arrive(first_halo)
    def absent(slot):
        return pl.when(jnp.logical_not(k.has_up() if slot < 2 else k.has_down()))

    for slot in (0, 1, 4, 5):
        @absent(slot)
        def _():
            S["eslot"][slot] = jnp.zeros((8, 160), f32)

    xe = S["xe"]
    for slot in range(0, 6, 2):
        pair = jnp.concatenate([S["eslot"][slot], S["eslot"][slot + 1]], axis=0)
        xe[slot * 8 : slot * 8 + 16, :] = pair.astype(bf16)

    filte, hx = S["filte"], S["hx"]
    for i in range(2):
        em = S["em"]
        got = nt(em[i, :, 0 : 5 * big], xj[0:80, 2 * i * big : (2 * i + 5) * big])
        got = got + nn(em[i, :, 5 * big :], xe[:, 0:80])
        for kk in range(nb):
            filte[kk, i * LANES : (i + 1) * LANES, :] = got[kk * LANES : (kk + 1) * LANES, 0:cj].astype(bf16)
    loads["ew"].wait()
    h0 = vec(eb) + jnp.zeros((px, c), f32)
    for kk in range(nb):
        h0 = h0 + nn(filte[kk], S["ew"][kk])
    hx[px : 2 * px, :] = h0
    own = slice(px, 2 * px)
    h0 = hx[own, :]
    stat_a = stat_start(0, *moments(h0))
    pe = S["pe"]
    for side, col in ((0, 0), (1, LANES - 2)):
        for q in range(2):
            lo = px + q * LANES + col
            pe[side, 2 * q : 2 * q + 2, :] = hx[lo : lo + 2, :]
            pe[side, 4 + 2 * q : 6 + 2 * q, :] = jnp.zeros((2, c), f32)
    sends = [
        Send(k, hx.at[pl.ds(px, px)], hx.at[pl.ds(2 * px, px)], k.at(0, -1, 0), -1),
        Send(k, hx.at[pl.ds(px, px)], hx.at[pl.ds(0, px)], k.at(0, 1, 0), 1),
    ]
    for dl, ds in dirs:
        sends.append(
            Send(
                k,
                pe.at[(ds + 1) // 2],
                hx.at[pl.ds(768 + slot_of(dl, ds) * 8, 8)],
                k.at(0, dl, ds),
                dl,
            )
        )
    zero_halo = start(sends)
    stat_a = stat_middle(0, stat_a, "moments")

    dm, pgr = S["dm"], S["pgr"]
    for i in range(2):
        got = nt(dm[i, :, 0 : 6 * big], xj[80 : 80 + 80, 2 * i * big : (2 * i + 6) * big])
        got = got + nn(dm[i, :, 6 * big :], xe[:, 80:160])
        for kk in range(nb):
            pgr[kk, i * LANES : (i + 1) * LANES, :] = got[kk * LANES : (kk + 1) * LANES, 0:cin].astype(bf16)
    ones = jnp.ones((16, 4 * big), bf16)
    put_misc(gm, MISC["dec_bias"], nt(ones, xj[80:160, 2 * big : 6 * big])[0:1, 0:cin])

    loads["cw"].wait()
    two, mg = S["two"], S["mg"]
    acc = nn(pgr[0], S["cw"][0])
    for kk in range(1, nb):
        acc = acc + nn(pgr[kk], S["cw"][kk])
    two[...] = acc
    mg[...] = acc.astype(bf16)
    loads["dw"].wait()
    ag, hp = S["ag"], S["hp"]
    ag[...] = nn(mg[...], S["dw"][...])
    S["mgt"][...] = mg[...].T
    put_misc(gm, MISC["down_bias"], jnp.sum(mg[...].astype(f32), axis=0, keepdims=True))

    mean1, m2 = stat_end(0, stat_a, "moments")
    var1 = m2 * (1.0 / s.pixels)
    rstd1 = lax.rsqrt(var1 + EPS)
    m1o[...] = mean1 * live
    v1o[...] = var1 * live
    arrive(zero_halo)
    nx = S["nx"]
    scale1 = rstd1 * vec(gain1)
    bias1 = vec(shift1)

    def norm_rows(n, carry):
        here = pl.ds(pl.multiple_of(n * 48, 16), 48)
        nx[here, :] = ((hx[here, :] - mean1) * scale1 + bias1).astype(bf16)
        return carry

    lax.fori_loop(0, 17, norm_rows, 0)

    filt, tm = S["filt"], S["tm"]
    loads["pw"].wait()
    h1 = S["h1"]
    acc = hx[own, :] + vec(pb)
    for kk in range(nb):
        here = slice(kk * px, (kk + 1) * px)
        filt[here, :] = nn(tm[here, :], nx[...]).astype(bf16)
        acc = acc + nt(filt[here, :], S["pw"][kk])
    h1[...] = acc
    stat_b = stat_start(1, *moments(h1[...]))
    stat_b = stat_middle(1, stat_b, "moments")
    tm_t = S["tmt"]
    tm_t[...] = tm[...].T
    mean2, m2 = stat_end(1, stat_b, "moments")
    var2 = m2 * (1.0 / s.pixels)
    rstd2 = lax.rsqrt(var2 + EPS)
    m2o[...] = mean2 * live
    v2o[...] = var2 * live
    scale2 = rstd2 * vec(gain2)
    bias2 = vec(shift2)
    n2 = S["n2"]

    def norm_two_rows(n, carry):
        here = pl.ds(pl.multiple_of(n * 32, 16), 32)
        n2[here, :] = ((h1[here, :] - mean2) * scale2 + bias2).astype(bf16)
        return carry

    lax.fori_loop(0, px // 32, norm_two_rows, 0)

    loads["uw"].wait()
    hp[...] = nn(n2[...], S["uw"][...])
    act, hg = S["act"], S["hg"]
    ubias = vec(ub)
    root = 0.7978845608028654

    def gelu_rows(n, carry):
        here = pl.ds(pl.multiple_of(n * 16, 16), 16)
        v = hp[here, :] + ubias
        sq = v * v
        t = jnp.tanh(root * (v + 0.044715 * (sq * v)))
        act[here, :] = (0.5 * v * (1.0 + t)).astype(bf16)
        slope = 0.5 * (1.0 + t) + (0.5 * root) * v * (1.0 - t * t) * (1.0 + (3 * 0.044715) * sq)
        hg[here, :] = (slope * ag[here, :]).astype(bf16)
        return carry

    lax.fori_loop(0, px // 16, gelu_rows, 0)
    ntg = S["ntg"]
    ntg[...] = nt(hg[...], S["uw"][...])
    grad = ntg[...]
    standard = (h1[...] - mean2) * rstd2
    sum_a = jnp.sum(grad, axis=0, keepdims=True)
    sum_b = jnp.sum(grad * standard, axis=0, keepdims=True)
    put_misc(gm, MISC["shift_two"], sum_a)
    put_misc(gm, MISC["gain_two"], sum_b)
    stat_c = stat_start(2, sum_a, sum_b)

    g1 = S["g1"]
    cols = [(lo, min(256, s.c5 * LANES - lo)) for lo in range(0, s.c5 * LANES, 256)]

    def spread(g, off, height, pitch, value, lo, width):
        for n in range(width // LANES):
            at = off + (lo // LANES + n) * pitch
            g[at : at + height, :] = value[:, n * LANES : (n + 1) * LANES].astype(bf16)

    for lo in range(0, s.f10 * LANES, 256):
        spread(g1, 0, c, s.r641, nn(S["mgt"][...], act[:, lo : lo + 256]), lo, 256)
    ar("A")
    stat_c = stat_middle(2, stat_c, "sums")
    S["n2t"][...] = n2[...].T
    for lo in range(0, s.f10 * LANES, 256):
        spread(g1, s.off_up, c, s.r641, nn(S["n2t"][...], hg[:, lo : lo + 256]), lo, 256)
    h2 = S["h2"]
    h2[...] = (h1[...] + nt(act[...], S["dw"][...]) + vec(db)).astype(bf16)
    for kk in range(nb):
        got = tn(pgr[kk], h2[:, 0 : s.c5 * LANES])
        spread(g1, s.off_dec + kk * s.c5 * s.r80, cin, s.r80, got, 0, s.c5 * LANES)
    ar("BA")

    def weighted(ref, column):
        return jnp.sum(ref.astype(f32) * column.astype(f32), axis=0, keepdims=True)

    def put_long(name, row):
        put_misc(gm, MISC[name], row[:, 0:768])
        put_misc(gm, MISC[name] + 1, row[:, 768:])

    def misc_one():
        put_long("up_bias", jnp.sum(hg[...].astype(f32), axis=0, keepdims=True))
        for n in range(2):
            at = s.f10 * LANES + n
            put_misc(gm, MISC["up_last"] + n, weighted(n2[...], hg[:, at : at + 1]))
            put_misc(gm, MISC["down_last"] + n, weighted(mg[...], act[:, at : at + 1]))
        for kk in range(nb):
            put_misc(gm, MISC["dec_last"] + kk, weighted(pgr[kk], h2[:, c - 1 : c]))

    sum_a, sum_b = stat_end(2, stat_c, "sums")
    g_two = vec(gain2)
    part_a = g_two * sum_a * (1.0 / s.pixels)
    part_b = g_two * sum_b * (1.0 / s.pixels)
    one, br = S["one"], S["br"]

    def one_rows(n, carry):
        here = pl.ds(pl.multiple_of(n * 32, 16), 32)
        standard = (h1[here, :] - mean2) * rstd2
        value = rstd2 * (g_two * ntg[here, :] - part_a - standard * part_b) + two[here, :]
        one[here, :] = value
        br[here, :] = value.astype(bf16)
        return carry

    lax.fori_loop(0, px // 32, one_rows, 0)
    ar("B")
    fg = S["fg"]
    for kk in range(nb):
        fg[kk * px : (kk + 1) * px, :] = nn(br[...], S["pw"][kk]).astype(bf16)
    con = S["con"]
    con[...] = nn(S["tmt"][...], fg[...])

    def sum_rows(n, carry):
        here = pl.ds(pl.multiple_of(n * 48, 16), 48)
        value = con[here, :]
        standard = (hx[here, :] - mean1) * rstd1
        return (
            carry[0] + jnp.sum(value, axis=0, keepdims=True),
            carry[1] + jnp.sum(value * standard, axis=0, keepdims=True),
        )

    zero_row = jnp.zeros((1, c), f32)
    sum_a, sum_b = lax.fori_loop(0, 17, sum_rows, (zero_row, zero_row))
    put_misc(gm, MISC["shift_one"], sum_a)
    put_misc(gm, MISC["gain_one"], sum_b)
    stat_d = stat_start(3, sum_a, sum_b)
    sends = [
        Send(k, con.at[pl.ds(0, px)], S["rdn"], k.at(0, -1, 0), -1),
        Send(k, con.at[pl.ds(2 * px, px)], S["rup"], k.at(0, 1, 0), 1),
    ]
    for dl, ds in dirs:
        mine = (dl + 1) * 2 + (ds + 1) // 2
        sends.append(
            Send(
                k,
                con.at[pl.ds(768 + mine * 8, 8)],
                S["reg"].at[slot_of(dl, ds)],
                k.at(0, dl, ds),
                dl,
            )
        )
    back_halo = start(sends)
    g2 = S["g2"]
    S["brt"][...] = br[...].T
    ar("A")
    for kk in range(nb):
        if kk == 1:
            stat_d = stat_middle(3, stat_d, "sums")
        for lo, width in cols:
            got = nn(S["brt"][...], filt[kk * px : (kk + 1) * px, lo : lo + width])
            spread(g2, kk * s.c5 * s.r641, c, s.r641, got, lo, width)
        if kk == 1:
            ar("C")
    ar("D")
    ar("BA")

    arrive(back_halo)
    ng = ntg
    ng[...] = con[own, :]

    @pl.when(k.has_up())
    def _():
        ng[...] = ng[...] + S["rup"][...]

    @pl.when(k.has_down())
    def _():
        ng[...] = ng[...] + S["rdn"][...]

    def add_edges(sl):
        for ss in (-1, 1):
            got = S["reg"].at[(sl + 1) * 2 + (ss + 1) // 2]
            col = 0 if ss == -1 else LANES - 2
            for q in range(2):
                lo = q * LANES + col
                ng[lo : lo + 2, :] = ng[lo : lo + 2, :] + got[2 * q : 2 * q + 2, :]

    add_edges(0)
    pl.when(k.has_up())(lambda: add_edges(-1))
    pl.when(k.has_down())(lambda: add_edges(1))
    sum_a, sum_b = stat_end(3, stat_d, "sums")
    g_one = vec(gain1)
    part_a1 = g_one * sum_a * (1.0 / s.pixels)
    part_b1 = g_one * sum_b * (1.0 / s.pixels)
    zg = S["zg"]

    def zero_rows(n, carry):
        here = pl.ds(pl.multiple_of(n * 32, 16), 32)
        there = pl.ds(pl.multiple_of(px + n * 32, 16), 32)
        standard = (hx[there, :] - mean1) * rstd1
        value = rstd1 * (g_one * ng[here, :] - part_a1 - standard * part_b1) + one[here, :]
        zg[here, :] = value.astype(bf16)
        return carry

    lax.fori_loop(0, px // 32, zero_rows, 0)

    g3 = S["g3"]
    for kk in range(nb):
        got = tn(filte[kk], zg[:, 0 : s.c5 * LANES])
        spread(g3, kk * s.c5 * s.r80, cj, s.r80, got, 0, s.c5 * LANES)
        put_misc(gm, MISC["enc_last"] + kk, weighted(filte[kk], zg[:, c - 1 : c]))
    put_misc(gm, MISC["enc_bias"], jnp.sum(zg[...].astype(f32), axis=0, keepdims=True))
    ar("E")
    misc_one()
    put_misc(gm, MISC["proc_bias"], jnp.sum(br[...].astype(f32), axis=0, keepdims=True))
    for kk in range(nb):
        put_misc(gm, MISC["proc_last"] + kk, weighted(br[...], filt[kk * px : (kk + 1) * px, c - 1 : c]))
    ar("MCDBA")

    projt, partt = S["projt"], S["partt"]
    for kk in range(nb):
        here = slice(kk * LANES, (kk + 1) * LANES)
        proj = nt(h2[...], S["cw"][kk])
        part = nt(zg[...], S["ew"][kk])[:, 0:cin]
        for i in range(2):
            for ref, value in ((projt, proj), (partt, part)):
                ref[i, 0:cin, here] = value[i * LANES : (i + 1) * LANES, :].T.astype(bf16)
                ref[i, cin:80, here] = jnp.zeros((80 - cin, LANES), bf16)
    sgx = S["sgx"]
    em = S["em"]
    sgx[...] = jnp.zeros(sgx.shape, f32)
    for i in range(2):
        lo = 2 * i * big
        got = nn(projt[i], dm[i])
        sgx[0:80, lo : lo + 6 * big] = sgx[0:80, lo : lo + 6 * big] + got[:, 0 : 6 * big]
        sgx[0:80, edge0 : edge0 + 48] = sgx[0:80, edge0 : edge0 + 48] + got[:, 6 * big :]
        got = nn(partt[i], em[i])
        sgx[80:160, lo : lo + 5 * big] = sgx[80:160, lo : lo + 5 * big] + got[:, 0 : 5 * big]
        sgx[80:160, edge0 : edge0 + 48] = sgx[80:160, edge0 : edge0 + 48] + got[:, 5 * big :]
    sgb, sgu, sgd, sge = S["sgb"], S["sgu"], S["sgd"], S["sge"]
    sgb[:, 0 : 2 * big] = sgx[:, 0 : 2 * big].astype(bf16)
    sgb[:, 2 * big : 4 * big] = sgx[:, 6 * big : 8 * big].astype(bf16)
    turned = sgx[:, edge0:].T
    for n in range(6):
        S["sgn"][n] = turned[n * 8 : n * 8 + 8, :]
    sends = [
        Send(k, sgb.at[:, pl.ds(0, 2 * big)], sgd, k.at(0, -1, 0), -1),
        Send(k, sgb.at[:, pl.ds(2 * big, 2 * big)], sgu, k.at(0, 1, 0), 1),
    ]
    for dl, ds in dirs:
        sends.append(
            Send(k, S["sgn"].at[(dl + 1) * 2 + (ds + 1) // 2], sge.at[slot_of(dl, ds)], k.at(0, dl, ds), dl)
        )
    out_halo = start(sends)
    ar("CDEABM")
    arrive(out_halo)
    sgt = S["sgt"]
    sgt[48:LANES, :] = jnp.zeros((LANES - 48, 160), f32)
    for slot in range(6):
        sgt[slot * 8 : slot * 8 + 8, :] = sge[slot]
    for slot in (0, 1, 4, 5):
        @absent(slot)
        def _():
            sgt[slot * 8 : slot * 8 + 8, :] = jnp.zeros((8, 160), f32)
    arrived = sgt[...].T
    up_one = jnp.where(k.has_up(), 1, 0)
    down_one = jnp.where(k.has_down(), 1, 0)
    cbt = S["cbt"]
    cbt[...] = jnp.zeros((8, LANES), f32)
    cbt[0:1, 0:cin] = vec(cb)
    bias_col = cbt[...].T[0:cin, 0:1]
    orow, st7 = S["orow"], S["st7"]

    for q in range(4):
        lo = (2 + q) * big
        value = sgx[:, lo : lo + big]
        if q < 2:
            other = sgu[:, q * big : (q + 1) * big].astype(f32)
            value = value + jnp.where(up_one == 1, other, 0.0)
        else:
            other = sgd[:, (q - 2) * big : (q - 1) * big].astype(f32)
            value = value + jnp.where(down_one == 1, other, 0.0)
        head, tail = value[:, 0:LANES], value[:, big - LANES :]
        for sl in (-1, 0, 1):
            for side in range(2):
                at = ((sl + 1) * 2 + side) * 8 + q * 2
                if side == 0:
                    moved = pltpu.roll(arrived, (LANES - at) % LANES, 1)
                    head = head + jnp.where(lane < 2, moved, 0.0)
                else:
                    moved = pltpu.roll(arrived, LANES - 2 - at, 1)
                    tail = tail + jnp.where(lane >= LANES - 2, moved, 0.0)
        orow[:, q, 0:LANES] = (head[0:cin] + bias_col) * live
        orow[:, q, LANES:big] = (tail[0:cin] + bias_col) * live
        st7[k.e, :, q * big : q * big + LANES] = head[80:160].astype(bf16)
        st7[k.e, :, q * big + LANES : (q + 1) * big] = tail[80:160].astype(bf16)
    out[0] = orow[...].astype(bf16)
    state_sends = start(
        [Send(k, st7.at[k.e], st7.at[k.e], k.at(d, 0, 0)) for d in range(1, s.ne)]
    )
    ar("ACBDEM")
    ar("ABCDEM")
    arrive(date_sends)
    arrive(state_sends)
    for d in range(s.dates):
        for q in range(4):
            value = jnp.zeros((80, big), f32)
            for n in range(s.ne):
                is_d = jnp.where(S["dates"][n, 0:1, :] == float(d), 1.0, 0.0)
                is_d = jnp.concatenate([is_d] * (big // LANES), axis=1)
                value = value + is_d * st7[n, :, q * big : (q + 1) * big].astype(f32)
            orow[:, q, :] = value[0:cin]
        sgrad[d] = orow[...].astype(bf16)

    while not all(it.finished() for it in reduced.values()):
        ar("ABCDEM")
    for m in pending:
        m.wait_send()


def finish_kernel(s, *refs):
    h1, h2, h3, hm, output_in, state_in, m1, v1, m2, v2 = refs[:10]
    (
        output, state_grad,
        enc_w, enc_b, g1o, s1o, proc_w, proc_b, g2o, s2o,
        up_w, up_b, down_w, down_b, dec_w, dec_b, m1o, v1o, m2o, v2o,
    ) = refs[10:30]
    (b1, b2, b3, enc_v, proc_v, up_v, down_v, dec_v, row_v, sem_in, sem_out) = refs[30:]
    c, ff, nb, cin, cj = s.c, s.ff, s.nb, s.cin, s.cj
    used1 = s.off_dec + nb * s.c5 * s.r80
    third = s.c5 * s.r641
    pieces = [(h2, b2, n * third, third) for n in range(nb)]
    pieces += [(h1, b1, 0, s.off_up), (h1, b1, s.off_up, s.off_dec - s.off_up)]
    pieces += [(h1, b1, s.off_dec, used1 - s.off_dec), (h3, b3, 0, nb * s.c5 * s.r80)]
    loads = [
        pltpu.make_async_copy(a.at[pl.ds(at, n)], b.at[pl.ds(at, n)], sem_in.at[i])
        for i, (a, b, at, n) in enumerate(pieces)
    ]
    for copy in loads:
        copy.start()
    stores = []

    def store(src, dst):
        copy = pltpu.make_async_copy(src, dst, sem_out.at[len(stores)])
        copy.start()
        stores.append(copy)

    for a, b in ((output_in, output), (state_in, state_grad), (m1, m1o), (v1, v1o), (m2, m2o), (v2, v2o)):
        b[...] = a[...]
    turned = hm[0:144, :].T

    def last_column(ref, slot, height, at):
        for t in range(-(-height // LANES)):
            n = min(LANES, height - t * LANES)
            ref[t * LANES : t * LANES + n, at : at + 1] = turned[0:n, slot * 6 + t : slot * 6 + t + 1]

    def widen(ref, src, base, pitch, height, tiles):
        for n in range(tiles):
            at = base + n * pitch
            ref[:, n * LANES : (n + 1) * LANES] = src[at : at + height, :].astype(f32)

    last = s.c5 * LANES
    for kk in range(nb):
        ref = proc_v.at[kk]
        last_column(ref, MISC["proc_last"] + kk, c, last)
        loads[kk].wait()
        widen(ref, b2, kk * third, s.r641, c, s.c5)
        store(ref, proc_w.at[kk])
    for n, (ref, name, base, to) in enumerate(
        ((down_v, "down_last", 0, down_w), (up_v, "up_last", s.off_up, up_w))
    ):
        for part in range(2):
            last_column(ref, MISC[name] + part, c, s.f10 * LANES + part)
        loads[nb + n].wait()
        widen(ref, b1, base, s.r641, c, s.f10)
        store(ref, to)
    loads[nb + 2].wait()
    loads[nb + 3].wait()
    for kk in range(nb):
        ref = dec_v.at[kk]
        last_column(ref, MISC["dec_last"] + kk, cin, last)
        widen(ref, b1, s.off_dec + kk * s.c5 * s.r80, s.r80, cin, s.c5)
        ref = enc_v.at[kk]
        last_column(ref, MISC["enc_last"] + kk, cj, last)
        widen(ref, b3, kk * s.c5 * s.r80, s.r80, cj, s.c5)
    store(dec_v, dec_w)
    store(enc_v, enc_w)

    def flat(ref, slots):
        at = 0
        for slot, width in slots:
            for piece in get_misc(hm, slot, width):
                n = piece.shape[1]
                row_v[0:1, at : at + n] = piece
                at += n
        ref[...] = row_v[0:1, 0:at].reshape(at)

    for ref, name in (
        (enc_b, "enc_bias"), (g1o, "gain_one"), (s1o, "shift_one"), (proc_b, "proc_bias"),
        (g2o, "gain_two"), (s2o, "shift_two"), (down_b, "down_bias"),
    ):
        flat(ref, [(MISC[name], c)])
    flat(up_b, [(MISC["up_bias"], 768), (MISC["up_bias"] + 1, ff - 768)])
    flat(dec_b, [(MISC["dec_bias"], cin)])
    for copy in stores:
        copy.wait()


def per_device(s, *args):
    (
        state, noise, cot, slot_date, lon_reach, enc_taps, proc_taps, dec_taps,
        enc_weight, enc_bias, gain_one, shift_one, proc_weight, proc_bias, gain_two, shift_two,
        up_weight, up_bias, down_weight, down_bias, dec_weight, dec_bias,
    ) = args
    args = list(args)
    args[8] = jnp.swapaxes(enc_weight, 1, 2)
    args[16] = up_weight.T
    vm = pl.BlockSpec(memory_space=pltpu.VMEM)
    sm = pl.BlockSpec(memory_space=pltpu.SMEM)
    hbm = pl.BlockSpec(memory_space=pl.ANY)
    shapes = scratch_list(s)
    shapes["sems"] = pltpu.SemaphoreType.DMA((sem_count(s),))
    names = tuple(shapes)
    in_specs = [vm] * 3 + [sm] * 5 + [
        hbm, vm, vm, vm, hbm, vm, vm, vm, hbm, vm, hbm, vm, hbm, vm,
    ]
    sd = jax.ShapeDtypeStruct
    out_shape = [
        sd((s.rows[0], LANES), bf16),
        sd((s.rows[1], LANES), bf16),
        sd((s.rows[2], LANES), bf16),
        sd((s.rows[3], LANES), f32),
        sd((1, s.cin, s.full_rows, s.full_cols), bf16),
        sd((s.dates, s.cin, s.full_rows, s.full_cols), bf16),
    ] + [sd((1, s.c), f32)] * 4
    got = pl.pallas_call(
        functools.partial(main_kernel, s, names),
        out_shape=out_shape,
        in_specs=in_specs,
        out_specs=[hbm] * 4 + [vm] * 6,
        scratch_shapes=list(shapes.values()),
        compiler_params=pltpu.CompilerParams(
            collective_id=0, has_side_effects=True, vmem_limit_bytes=60 * 2**20
        ),
        name="forecast",
    )(*args)
    c, ff, nb = s.c, s.ff, s.nb
    outs = [out_shape[4], out_shape[5]] + [
        sd((nb, s.cj, c), f32), sd((c,), f32), sd((c,), f32), sd((c,), f32),
        sd((nb, c, c), f32), sd((c,), f32), sd((c,), f32), sd((c,), f32),
        sd((c, ff), f32), sd((ff,), f32), sd((c, ff), f32), sd((c,), f32),
        sd((nb, s.cin, c), f32), sd((s.cin,), f32),
    ] + [sd((1, c), f32)] * 4
    large = (2, 6, 10, 12, 14)
    V = pltpu.VMEM
    done = pl.pallas_call(
        functools.partial(finish_kernel, s),
        out_shape=outs,
        in_specs=[hbm] * 3 + [vm] * 7,
        out_specs=[hbm if n in large else vm for n in range(len(outs))],
        scratch_shapes=[
            V((s.rows[0], LANES), bf16), V((s.rows[1], LANES), bf16), V((s.rows[2], LANES), bf16),
            V((nb, s.cj, c), f32), V((nb, c, c), f32), V((c, ff), f32), V((c, ff), f32),
            V((nb, s.cin, c), f32), V((8, up_to(ff, LANES)), f32),
            pltpu.SemaphoreType.DMA((8,)), pltpu.SemaphoreType.DMA((16,)),
        ],
        compiler_params=pltpu.CompilerParams(vmem_limit_bytes=60 * 2**20),
        name="finish",
    )(*got)
    done = list(done)
    done[2] = jnp.swapaxes(done[2], 1, 2)
    done[10] = done[10].T
    return tuple(done)


def solution(mesh):
    in_specs = (
        P(None, None, "lat", "lon"),
        P("ens", None, "lat", "lon"),
        P("ens", None, "lat", "lon"),
        P("ens"),
    ) + (P(),) * 18
    out_specs = (
        (P("ens", None, "lat", "lon"), P(None, None, "lat", "lon"))
        + (P(),) * 14
        + (P("ens", None),) * 4
    )

    def run(*args):
        s = Sizes(mesh, args[0].shape, args[1].shape, args[5].shape, args[8].shape, args[16].shape)
        return jax.shard_map(
            functools.partial(per_device, s),
            mesh=mesh,
            in_specs=in_specs,
            out_specs=out_specs,
            check_vma=False,
        )(*args)

    return run
```

```python
import functools
import types

import jax
import jax.numpy as jnp
from jax import lax
from jax.experimental import pallas as pl
from jax.experimental.pallas import tpu as pltpu
from jax.sharding import PartitionSpec as P

MESH = pl.DeviceIdType.MESH
f32 = jnp.float32
bf16 = jnp.bfloat16
i32 = jnp.int32
EPS = 1e-05
LANES = 128
AXES = ("ens", "lat", "lon")
BIT0, BIT1, LAT, LON = range(4)
ROUTE_X = (LAT, BIT0, BIT1, LON)
ROUTE_Y = (LAT, BIT1, BIT0, LON)
WSEM, OSEM, SEMS = range(3)
ROUTE_ZX = (LAT, LON, BIT0, BIT1)
ROUTE_ZY = (LAT, LON, BIT1, BIT0)
PIECES = dict(
    a=(0, 0), b=(0, 1), c=(0, 2), d=(1, 0), e=(1, 1), f=(1, 2),
    g=(2, 0), h=(2, 1), i=(3, 0), j=(3, 1), k=(4, 0), l=(5, 0),
)


def nn(a, b):
    return lax.dot_general(a, b, (((1,), (0,)), ((), ())), preferred_element_type=f32)


def nt(a, b):
    return lax.dot_general(a, b, (((1,), (1,)), ((), ())), preferred_element_type=f32)


def tn(a, b):
    return lax.dot_general(a, b, (((0,), (0,)), ((), ())), preferred_element_type=f32)


def up_to(n, m):
    return -(-n // m) * m


class Sizes:
    def __init__(self, mesh, state, noise, enc_taps, enc_weight, up_weight):
        self.ne, self.nl, self.nz = (mesh.shape[a] for a in AXES)
        self.dates, self.cin, self.full_rows, self.full_cols = state
        self.noise = noise[1]
        self.full_rows = state[2] // self.nl
        self.full_cols = state[3] // self.nz
        self.hr, self.hc = self.full_rows // 2, self.full_cols // 2
        assert self.hr == 2 and self.hc == LANES and self.ne == 4
        self.lat_total = enc_taps[1]
        self.nb = enc_taps[0]
        self.c = enc_weight[1]
        self.cj = enc_weight[2]
        self.ff = up_weight[0]
        self.px = self.hr * self.hc
        self.pixels = float(self.px * self.nl * self.nz)
        self.c5 = self.c // LANES
        self.f10 = self.ff // LANES
        self.r641 = up_to(self.c, 16)
        self.r80 = up_to(self.cj, 16)
        self.off_up = self.f10 * self.r641
        self.off_dec = self.off_up + self.f10 * self.r641
        used = (
            self.off_dec + self.nb * self.c5 * self.r80,
            self.nb * self.c5 * self.r641,
            self.nb * self.c5 * self.r80,
        )
        unit = 16 * self.nl * self.ne * self.nz
        self.rows = tuple(up_to(n, unit) for n in used) + (up_to(24 * 6, unit // 2),)
        self.chunks = {}

        def split(piece, buffer, lo, hi, third=None):
            units = (hi - lo) // unit
            last = 2 if third and units >= 6 else 0
            first = (units - last + 1) // 2
            at = lo
            for n, (count, route) in enumerate(
                ((first, ROUTE_X), (units - last - first, ROUTE_Y), (last, third))
            ):
                if count:
                    self.chunks[piece, n] = (buffer, at, count * unit, route)
                at += count * unit

        cut = self.off_up // unit * unit
        split(0, 0, 0, cut, ROUTE_ZX)
        split(1, 0, cut, self.rows[0], ROUTE_ZY)
        cut = 2 * self.c5 * self.r641 // unit * unit
        split(2, 1, 0, cut)
        split(3, 1, cut, self.rows[1])
        self.chunks[4, 0] = (2, 0, self.rows[2], ROUTE_X)
        self.chunks[5, 0] = (3, 0, self.rows[3], ROUTE_Y)
        self.group = self.nl * self.nz


def add_into(dst, at, sources, count):
    step = next(s for s in (256, 128, 64, 32, 16, 8) if count % s == 0)

    def body(n, carry):
        lo = pl.multiple_of(n * step, 8 if step == 8 else 16)
        there = pl.ds(pl.multiple_of(at + lo, 8 if step == 8 else 16), step)
        value = dst[there, :].astype(f32)
        for source in sources:
            value = value + source[pl.ds(lo, step), :].astype(f32)
        dst[there, :] = value.astype(dst.dtype)
        return carry

    lax.fori_loop(0, count // step, body, 0)


class Links:
    def __init__(self, z, sems=None):
        self.s = z
        self.sems = sems
        self.used = 0
        if sems is not None:
            self.e, self.l, self.z = (lax.axis_index(a) for a in AXES)

    def take(self):
        self.used += 1
        return self.used - 1

    def at(self, de, dl, dz):
        s = self.s
        return (
            lax.rem(self.e + (de + s.ne), s.ne),
            lax.rem(self.l + (dl + s.nl), s.nl),
            lax.rem(self.z + (dz + s.nz), s.nz),
        )

    def bit(self, which):
        return lax.rem(self.e // (1 << which), 2)

    def flip(self, which):
        return (self.e + (1 << which) * (1 - 2 * self.bit(which)), self.l, self.z)

    def has_up(self):
        return self.l > 0

    def has_down(self):
        return self.l < self.s.nl - 1


class Send:
    def __init__(self, links, src, dst, device, dl=0):
        self.links = links
        self.ids = (links.take(), links.take())
        self.what = (src, dst, device)
        self.dl = dl

    def copy(self):
        src, dst, device = self.what
        return pltpu.make_async_remote_copy(
            src_ref=src,
            dst_ref=dst,
            send_sem=self.links.sems.at[self.ids[0]],
            recv_sem=self.links.sems.at[self.ids[1]],
            device_id=device,
            device_id_type=MESH,
        )

    def under(self, sending, act):
        if self.dl == 0:
            act()
        else:
            up = (self.dl < 0) == sending
            pl.when(self.links.has_up() if up else self.links.has_down())(act)

    def start(self):
        self.under(True, lambda: self.copy().start())

    def wait_recv(self):
        self.under(False, lambda: self.copy().wait_recv())

    def wait_send(self):
        self.under(True, lambda: self.copy().wait_send())


class AllReduce:
    def __init__(self, links, partial, total, lo, rows, route, bufs, own_sem):
        self.k, self.g, self.h, self.route = links, partial, total, route
        self.bufs, self.own_sem = bufs, own_sem
        self.sent, self.waiting = [], []
        self.stage = 0
        self.base, self.part = [], []
        base, size = lo, rows
        for axis in route:
            size = size // self.count(links.s, axis)
            self.base.append(base)
            self.part.append(size)
            base = base + self.index(axis) * size
        self.base.append(base)
        self.last_stage = 2 * len(route)

    @staticmethod
    def count(s, axis):
        return {LAT: s.nl, LON: s.nz}.get(axis, 2)

    @staticmethod
    def shapes(s, rows, route, dtype):
        out = []
        for axis in route:
            n = AllReduce.count(s, axis)
            rows = rows // n
            out.append(pltpu.VMEM((n - 1, rows, LANES), dtype))
        return out

    def index(self, axis):
        k = self.k
        return {LAT: k.l, LON: k.z}[axis] if axis in (LAT, LON) else k.bit(axis)

    def others(self, axis):
        k, s = self.k, self.k.s
        if axis == LAT:
            devices = [k.at(0, d, 0) for d in range(1, s.nl)]
            return [(dev, dev[1], n) for n, dev in enumerate(devices)]
        if axis == LON:
            devices = [k.at(0, 0, d) for d in range(1, s.nz)]
            return [(dev, dev[2], n) for n, dev in enumerate(devices)]
        return [(k.flip(axis), 1 - k.bit(axis), 0)]

    def send(self, src, dst, device):
        m = Send(self.k, src, dst, device)
        m.start()
        self.sent.append(m)
        self.waiting.append(m)

    def step(self):
        g, h, route = self.g, self.h, self.route
        al = lambda v: pl.multiple_of(v, 8)
        stage, self.stage = self.stage, self.stage + 1
        for m in self.waiting:
            m.wait_recv()
        self.waiting = []
        depth = len(route)
        if 0 < stage <= depth:
            buf = self.bufs[stage - 1]
            add_into(g, al(self.base[stage]), [buf.at[n] for n in range(buf.shape[0])], self.part[stage - 1])
        if stage < depth:
            size = self.part[stage]
            for device, place, slot in self.others(route[stage]):
                there = pl.ds(al(self.base[stage] + place * size), size)
                self.send(g.at[there], self.bufs[stage].at[slot], device)
        elif stage < 2 * depth:
            level = 2 * depth - 1 - stage
            here = pl.ds(al(self.base[level + 1]), self.part[level])
            if stage == depth:
                self.own = pltpu.make_async_copy(g.at[here], h.at[here], self.own_sem)
                self.own.start()
            if stage == depth + 1:
                self.own.wait()
            source = g if stage == depth else h
            for device, _, _ in self.others(route[level]):
                self.send(source.at[here], h.at[here], device)
        else:
            for m in self.sent:
                m.wait_send()

    def finished(self):
        return self.stage > self.last_stage


class MISC:
    down_bias, up_bias, gain_two, shift_two, proc_bias, gain_one, shift_one, enc_bias = 0, 1, 3, 4, 5, 6, 7, 8
    up_last, down_last, proc_last, enc_last, dec_last, dec_bias = 9, 11, 13, 16, 19, 22


def put_misc(misc, slot, row):
    width = row.shape[1]
    for t in range(-(-width // LANES)):
        lo, hi = t * LANES, min(width, (t + 1) * LANES)
        misc[slot * 6 + t : slot * 6 + t + 1, 0 : hi - lo] = row[:, lo:hi]


def get_misc(misc, slot, width):
    parts = []
    for t in range(-(-width // LANES)):
        lo, hi = t * LANES, min(width, (t + 1) * LANES)
        parts.append(misc[slot * 6 + t : slot * 6 + t + 1, 0 : hi - lo])
    return parts


def scratch_list(s):
    c, ff, px = s.c, s.ff, s.px
    big = s.full_cols
    wide = 8 * big + LANES
    V = pltpu.VMEM
    shapes = dict(
        xin=V((160, s.full_rows, big), f32),
        xj=V((160, 8 * big), bf16),
        eb=V((2, 8, 160), f32),
        eslot=V((6, 8, 160), f32),
        xe=V((48, 160), bf16),
        em=V((2, s.nb * LANES, 5 * big + 48), bf16),
        dm=V((2, s.nb * LANES, 6 * big + 48), bf16),
        tm=V((s.nb * px, 6 * LANES + 48), bf16),
        ew=V((s.nb, s.cj, c), bf16),
        pw=V((s.nb, c, c), bf16),
        uw=V((c, ff), bf16),
        dw=V((c, ff), bf16),
        cw=V((s.nb, s.cin, c), bf16),
        filte=V((s.nb, px, s.cj), bf16),
        hx=V((6 * LANES + 48, c), f32),
        nx=V((6 * LANES + 48, c), bf16),
        pe=V((2, 8, c), f32),
        filt=V((s.nb * px, c), bf16),
        h1=V((px, c), f32),
        n2=V((px, c), bf16),
        hp=V((px, ff), f32),
        ag=V((px, ff), f32),
        act=V((px, ff), bf16),
        hg=V((px, ff), bf16),
        n2t=V((c, px), bf16),
        h2=V((px, c), bf16),
        pgr=V((s.nb, px, s.cin), bf16),
        projt=V((2, 80, s.nb * LANES), bf16),
        partt=V((2, 80, s.nb * LANES), bf16),
        two=V((px, c), f32),
        mg=V((px, c), bf16),
        mgt=V((c, px), bf16),
        ntg=V((px, c), f32),
        one=V((px, c), f32),
        br=V((px, c), bf16),
        brt=V((c, px), bf16),
        fg=V((s.nb * px, c), bf16),
        con=V((6 * LANES + 48, c), f32),
        rup=V((px, c), f32),
        rdn=V((px, c), f32),
        reg=V((6, 8, c), f32),
        zg=V((px, c), bf16),
        sgx=V((160, wide), f32),
        sgb=V((160, 4 * big), bf16),
        sgu=V((160, 2 * big), bf16),
        sgd=V((160, 2 * big), bf16),
        sgn=V((6, 8, 160), f32),
        sge=V((6, 8, 160), f32),
        sgt=V((LANES, 160), f32),
        orow=V((s.cin, s.full_rows, big), f32),
        st7=V((s.ne, 80, 4 * big), bf16),
        dates=V((s.ne, 8, LANES), f32),
        cbt=V((8, LANES), f32),
        slat=V((4, s.nl, 2, c), f32),
        slon=V((4, s.nz, 2, c), f32),
        sall=V((4, s.group if s.group <= 16 else 1, 2, c), f32),
        tmt=V((6 * LANES + 48, s.nb * px), bf16),
        g1=V((s.rows[0], LANES), bf16),
        g2=V((s.rows[1], LANES), bf16),
        g3=V((s.rows[2], LANES), bf16),
        gm=V((s.rows[3], LANES), f32),
    )
    for name, (buffer, _, rows, route) in s.chunks.items():
        kinds = AllReduce.shapes(s, rows, route, f32 if buffer == 3 else bf16)
        for j, kind in enumerate(kinds):
            shapes[name, j] = kind
    shapes[WSEM] = pltpu.SemaphoreType.DMA((5,))
    shapes[OSEM] = pltpu.SemaphoreType.DMA((len(s.chunks),))
    shapes[SEMS] = pltpu.SemaphoreType.DMA((sem_count(s),))
    return shapes


def sem_count(s):
    total = len(s.chunks) * 2 * 2 * (s.nl - 1 + 1 + 1 + s.nz - 1)
    total += 2 * 4 * 8 + 2 * 2 * (s.ne - 1)
    total += 4 * 2 * (s.group - 1 if s.group <= 16 else s.nl - 1 + s.nz - 1)
    return total


def main_kernel(s, names, *refs):
    n_in, n_out = 22, 10
    (
        state, noise, cot, date_ref, reach, enc_taps, proc_taps, dec_taps,
        ew_h, eb, gain1, shift1, pw_h, pb, gain2, shift2, uw_h, ub, dw_h, db, cw_h, cb,
    ) = refs[:n_in]
    h1o, h2o, h3o, hmo, out, sgrad, m1o, v1o, m2o, v2o = refs[n_in : n_in + n_out]
    table = dict(zip(names, refs[n_in + n_out :]))
    S = types.SimpleNamespace(**{n: r for n, r in table.items() if isinstance(n, str)})
    sems = table[SEMS]
    k = Links(s, sems)
    c, ff, px, nb, cin, cj = s.c, s.ff, s.px, s.nb, s.cin, s.cj
    big = s.full_cols
    l = k.l
    row0 = l * s.hr
    edge0 = 8 * big

    offsets = {(d, 0, 0) for d in range(1, s.ne)}
    if s.group <= 16:
        offsets |= {(0, a, b) for a in range(s.nl) for b in range(s.nz)} - {(0, 0, 0)}
    else:
        offsets |= {(0, d, 0) for d in range(1, s.nl)} | {(0, 0, d) for d in range(1, s.nz)}
    offsets |= {(0, a % s.nl, b % s.nz) for a in (1, -1) for b in (1, -1)}
    offsets = sorted(offsets)
    barrier = pltpu.get_barrier_semaphore()
    for o in offsets:
        pl.semaphore_signal(barrier, 1, device_id=k.at(*o), device_id_type=MESH)

    loads, weights = types.SimpleNamespace(), []
    for n, (src, to) in enumerate(
        ((ew_h, S.ew), (pw_h, S.pw), (uw_h, S.uw), (dw_h, S.dw), (cw_h, S.cw))
    ):
        copy = pltpu.make_async_copy(src, to, table[WSEM].at[n])
        copy.start()
        weights.append(copy)
    loads.ew, loads.pw, loads.uw, loads.dw, loads.cw = weights

    date = date_ref[0]
    live = jnp.where(date >= 0, 1.0, 0.0).astype(f32)
    xin, xj = S.xin, S.xj
    picked = jnp.zeros((cin, s.full_rows, big), f32)
    for d in range(s.dates):
        picked = picked + state[d].astype(f32) * jnp.where(date == d, 1.0, 0.0).astype(f32)
    xin[0:cin] = picked
    xin[cin:cj] = noise[0].astype(f32)
    xin[80 : 80 + cin] = cot[0].astype(f32) * live
    xin[80 + cin : 160] = jnp.zeros((160 - 80 - cin, s.full_rows, big), f32)
    lane = lax.broadcasted_iota(i32, (160, LANES), 1)
    ends = jnp.zeros((160, LANES), f32)
    for q in range(4):
        row = xin[:, q, :]
        xj[:, (2 + q) * big : (3 + q) * big] = row.astype(bf16)
        moved = pltpu.roll(row[:, 0:LANES], q * 2, 1)
        ends = jnp.where((lane >> 1) == q, moved, ends)
        moved = pltpu.roll(row[:, big - LANES : big], q * 2 + 10, 1)
        ends = jnp.where((lane >> 1) == q + 4, moved, ends)
    turned = ends.T
    S.eb[0] = turned[0:8, :]
    S.eb[1] = turned[8:16, :]
    S.dates[k.e] = jnp.full((8, LANES), date.astype(f32), f32)

    @pl.when(jnp.logical_not(k.has_up()))
    def _():
        xj[:, 0 : 2 * big] = jnp.zeros((160, 2 * big), bf16)
        S.hx[0:px] = jnp.zeros((px, c), f32)
        for side in range(2):
            S.hx[768 + side * 8 : 776 + side * 8] = jnp.zeros((8, c), f32)

    @pl.when(jnp.logical_not(k.has_down()))
    def _():
        xj[:, 6 * big : 8 * big] = jnp.zeros((160, 2 * big), bf16)
        S.hx[2 * px : 3 * px] = jnp.zeros((px, c), f32)
        for side in range(2):
            S.hx[768 + 32 + side * 8 : 776 + 32 + side * 8] = jnp.zeros((8, c), f32)

    pl.semaphore_wait(barrier, len(offsets))

    totals = (h1o, h2o, h3o, hmo)
    reduced = {}
    for n, (name, (buffer, lo, rows, route)) in enumerate(s.chunks.items()):
        bufs = [table[name, j] for j in range(len(route))]
        partial = (S.g1, S.g2, S.g3, S.gm)[buffer]
        reduced[name] = AllReduce(k, partial, totals[buffer], lo, rows, route, bufs, table[OSEM].at[n])

    def ar(letters):
        for letter in letters:
            it = reduced.get(PIECES[letter])
            if it is not None and not it.finished():
                it.step()

    pending = []

    def start(sends):
        for m in sends:
            m.start()
        pending.extend(sends)
        return sends

    def arrive(sends):
        for m in sends:
            m.wait_recv()

    dirs = [(dl, ds) for dl in (-1, 0, 1) for ds in (-1, 1)]

    def slot_of(dl, ds):
        return (1 - dl) * 2 + (1 - ds) // 2

    sends = [
        Send(k, xj.at[:, pl.ds(2 * big, 2 * big)], xj.at[:, pl.ds(6 * big, 2 * big)], k.at(0, -1, 0), -1),
        Send(k, xj.at[:, pl.ds(4 * big, 2 * big)], xj.at[:, pl.ds(0, 2 * big)], k.at(0, 1, 0), 1),
    ]
    for dl, ds in dirs:
        sends.append(
            Send(k, S.eb.at[(ds + 1) // 2], S.eslot.at[slot_of(dl, ds)], k.at(0, dl, ds), dl)
        )
    first_halo = start(sends)
    date_sends = start(
        [
            Send(k, S.dates.at[k.e], S.dates.at[k.e], k.at(d, 0, 0))
            for d in range(1, s.ne)
        ]
    )

    gm = S.gm
    gm[0:144] = jnp.zeros((144, LANES), f32)

    def band(shape, column_of):
        rows = lax.broadcasted_iota(i32, shape, 0)
        cols = lax.broadcasted_iota(i32, shape, 1)
        return column_of(rows, cols)

    def pick(d, table, like):
        value = jnp.zeros(like, f32)
        for key, scalar in table:
            value = jnp.where(d == key, scalar, value)
        return value

    def inside(grow, total):
        return jnp.logical_and(grow >= 0, grow < total)

    def edge_lane(shape):
        at = lax.broadcasted_iota(i32, shape, 1)
        slot, q, m = at >> 3, (at & 7) >> 1, at & 1
        r = q + 2 + 4 * ((slot >> 1) - 1)
        return r, jnp.where((slot & 1) == 0, m - 2, big + m), at

    def build_encoder():
        em = S.em
        d_main = band((LANES, big), lambda j, J: J - 2 * j)
        r, J, at = edge_lane((16, 48))
        j = lax.broadcasted_iota(i32, (16, 48), 0)
        codes = []
        for start_row in (0, LANES - 16):
            d = J - 2 * (j + start_row)
            codes.append(r * 1024 + d)
        for i in range(2):
            reached = reach[row0 + i]
            edges = [[jnp.zeros((16, 48), f32) for _ in range(2)] for _ in range(nb)]
            for a in range(-2, 3):
                r_in = 2 * i + a + 2
                ok = inside(4 * l + r_in - 2, 2 * s.lat_total)
                masks = [d_main == b for b in range(-2, 3)]
                for kk in range(nb):
                    value = jnp.zeros((LANES, big), f32)
                    for b in range(-2, 3):
                        tap = enc_taps[kk, row0 + i, 5 * (a + 2) + b + 2]
                        tap = jnp.where(jnp.logical_and(ok, abs(b) <= reached), tap, 0.0)
                        value = jnp.where(masks[b + 2], tap, value)
                        for part in range(2):
                            edges[kk][part] = jnp.where(
                                codes[part] == r_in * 1024 + b, tap, edges[kk][part]
                            )
                    em[i, kk * LANES : (kk + 1) * LANES, (a + 2) * big : (a + 3) * big] = value.astype(bf16)
            for kk in range(nb):
                lo = kk * LANES
                em[i, lo : lo + 16, 5 * big :] = edges[kk][0].astype(bf16)
                em[i, lo + 16 : lo + LANES - 16, 5 * big :] = jnp.zeros((LANES - 32, 48), bf16)
                em[i, lo + LANES - 16 : lo + LANES, 5 * big :] = edges[kk][1].astype(bf16)

    def build_decoder():
        dm = S.dm
        d_main = band((LANES, big), lambda j, J: j - (J >> 1))
        r, J, at = edge_lane((16, 48))
        j = lax.broadcasted_iota(i32, (16, 48), 0)
        codes = []
        for start_row in (0, LANES - 16):
            d = (j + start_row) - (J >> 1)
            codes.append(r * 1024 + d)
        for i in range(2):
            edges = [[jnp.zeros((16, 48), f32) for _ in range(2)] for _ in range(nb)]
            for n in range(6):
                r_in = 2 * i + n
                a = i + 1 - r_in // 2
                full = 4 * l + r_in - 2
                ok = inside(full, 2 * s.lat_total)
                full = jnp.clip(full, 0, 2 * s.lat_total - 1)
                reached = reach[full // 2] - 1
                masks = [d_main == b for b in range(-1, 2)]
                for kk in range(nb):
                    value = jnp.zeros((LANES, big), f32)
                    for b in range(-1, 2):
                        tap = dec_taps[kk, full, 3 * (a + 1) + b + 1]
                        tap = jnp.where(jnp.logical_and(ok, abs(b) <= reached), tap, 0.0)
                        value = jnp.where(masks[b + 1], tap, value)
                        for part in range(2):
                            edges[kk][part] = jnp.where(
                                codes[part] == r_in * 1024 + b, tap, edges[kk][part]
                            )
                    dm[i, kk * LANES : (kk + 1) * LANES, n * big : (n + 1) * big] = value.astype(bf16)
            for kk in range(nb):
                lo = kk * LANES
                dm[i, lo : lo + 16, 6 * big :] = edges[kk][0].astype(bf16)
                dm[i, lo + 16 : lo + LANES - 16, 6 * big :] = jnp.zeros((LANES - 32, 48), bf16)
                dm[i, lo + LANES - 16 : lo + LANES, 6 * big :] = edges[kk][1].astype(bf16)

    def build_processor():
        tm = S.tm
        d_main = band((LANES, LANES), lambda j, J: J - j)
        at = lax.broadcasted_iota(i32, (16, 48), 1)
        slot, idx = at >> 3, at & 7
        r = 2 * (slot >> 1) + (idx >> 1)
        m = idx & 1
        J = jnp.where((slot & 1) == 0, m - 2, LANES + m)
        j = lax.broadcasted_iota(i32, (16, 48), 0)
        codes = []
        for start_row in (0, LANES - 16):
            d = J - (j + start_row)
            codes.append(jnp.where(idx < 4, r * 1024 + d, -5000))
        for i in range(2):
            reached = reach[row0 + i]
            edges = [[jnp.zeros((16, 48), f32) for _ in range(2)] for _ in range(nb)]
            for r_in in range(6):
                a = r_in - 2 - i
                if abs(a) > 2:
                    for kk in range(nb):
                        lo = kk * px + i * LANES
                        tm[lo : lo + LANES, r_in * LANES : (r_in + 1) * LANES] = jnp.zeros((LANES, LANES), bf16)
                    continue
                ok = inside(row0 + r_in - 2, s.lat_total)
                masks = [d_main == b for b in range(-2, 3)]
                for kk in range(nb):
                    value = jnp.zeros((LANES, LANES), f32)
                    for b in range(-2, 3):
                        tap = proc_taps[kk, row0 + i, 5 * (a + 2) + b + 2]
                        tap = jnp.where(jnp.logical_and(ok, abs(b) <= reached), tap, 0.0)
                        value = jnp.where(masks[b + 2], tap, value)
                        for part in range(2):
                            edges[kk][part] = jnp.where(
                                codes[part] == r_in * 1024 + b, tap, edges[kk][part]
                            )
                    lo = kk * px + i * LANES
                    tm[lo : lo + LANES, r_in * LANES : (r_in + 1) * LANES] = value.astype(bf16)
            for kk in range(nb):
                lo = kk * px + i * LANES
                tm[lo : lo + 16, 768:816] = edges[kk][0].astype(bf16)
                tm[lo + 16 : lo + LANES - 16, 768:816] = jnp.zeros((LANES - 32, 48), bf16)
                tm[lo + LANES - 16 : lo + LANES, 768:816] = edges[kk][1].astype(bf16)

    slat, slon = S.slat, S.slon

    def fold(values, kind, count):
        total_a, total_b = values[0]
        for a, b in values[1:]:
            total_a = total_a + a
            total_b = total_b + b
        if kind:
            total_a = total_a * (1.0 / len(values))
            for a, b in values:
                total_b = total_b + (a - total_a) * (a - total_a) * count
        return total_a, total_b

    single = s.group <= 16
    sall = S.sall
    place = k.l * s.nz + k.z

    def stat_start(rd, a, b):
        if single:
            sall[rd, place, 0:1, :] = a
            sall[rd, place, 1:2, :] = b
            others = [(0, m, n) for n in range(s.nz) for m in range(s.nl) if m or n]
            return start(
                [Send(k, sall.at[rd, place], sall.at[rd, place], k.at(*o)) for o in others]
            )
        slat[rd, k.l, 0:1, :] = a
        slat[rd, k.l, 1:2, :] = b
        return start(
            [
                Send(k, slat.at[rd, k.l], slat.at[rd, k.l], k.at(0, d, 0))
                for d in range(1, s.nl)
            ]
        )

    def stat_middle(rd, sends, kind):
        if single:
            return sends
        arrive(sends)
        values = [(slat[rd, n, 0:1, :], slat[rd, n, 1:2, :]) for n in range(s.nl)]
        a, b = fold(values, kind, float(px))
        slon[rd, k.z, 0:1, :] = a
        slon[rd, k.z, 1:2, :] = b
        return start(
            [
                Send(k, slon.at[rd, k.z], slon.at[rd, k.z], k.at(0, 0, d))
                for d in range(1, s.nz)
            ]
        )

    def stat_end(rd, sends, kind):
        arrive(sends)
        if single:
            values = [(sall[rd, n, 0:1, :], sall[rd, n, 1:2, :]) for n in range(s.group)]
            return fold(values, kind, float(px))
        values = [(slon[rd, n, 0:1, :], slon[rd, n, 1:2, :]) for n in range(s.nz)]
        return fold(values, kind, float(px * s.nl))

    def moments(values):
        mean = jnp.sum(values, axis=0, keepdims=True) * (1.0 / px)
        centred = values - mean
        return mean, jnp.sum(centred * centred, axis=0, keepdims=True)

    def vec(ref):
        n = ref.shape[0]
        return ref[...].reshape(1, n)

    build_encoder()
    build_decoder()
    build_processor()

    arrive(first_halo)
    def absent(slot):
        return pl.when(jnp.logical_not(k.has_up() if slot < 2 else k.has_down()))

    for slot in (0, 1, 4, 5):
        @absent(slot)
        def _():
            S.eslot[slot] = jnp.zeros((8, 160), f32)

    xe = S.xe
    for slot in range(0, 6, 2):
        pair = jnp.concatenate([S.eslot[slot], S.eslot[slot + 1]], axis=0)
        xe[slot * 8 : slot * 8 + 16, :] = pair.astype(bf16)

    filte, hx = S.filte, S.hx
    for i in range(2):
        em = S.em
        got = nt(em[i, :, 0 : 5 * big], xj[0:80, 2 * i * big : (2 * i + 5) * big])
        got = got + nn(em[i, :, 5 * big :], xe[:, 0:80])
        for kk in range(nb):
            filte[kk, i * LANES : (i + 1) * LANES, :] = got[kk * LANES : (kk + 1) * LANES, 0:cj].astype(bf16)
    loads.ew.wait()
    h0 = vec(eb) + jnp.zeros((px, c), f32)
    for kk in range(nb):
        h0 = h0 + nn(filte[kk], S.ew[kk])
    hx[px : 2 * px, :] = h0
    own = slice(px, 2 * px)
    h0 = hx[own, :]
    stat_a = stat_start(0, *moments(h0))
    pe = S.pe
    for side, col in ((0, 0), (1, LANES - 2)):
        for q in range(2):
            lo = px + q * LANES + col
            pe[side, 2 * q : 2 * q + 2, :] = hx[lo : lo + 2, :]
            pe[side, 4 + 2 * q : 6 + 2 * q, :] = jnp.zeros((2, c), f32)
    sends = [
        Send(k, hx.at[pl.ds(px, px)], hx.at[pl.ds(2 * px, px)], k.at(0, -1, 0), -1),
        Send(k, hx.at[pl.ds(px, px)], hx.at[pl.ds(0, px)], k.at(0, 1, 0), 1),
    ]
    for dl, ds in dirs:
        sends.append(
            Send(
                k,
                pe.at[(ds + 1) // 2],
                hx.at[pl.ds(768 + slot_of(dl, ds) * 8, 8)],
                k.at(0, dl, ds),
                dl,
            )
        )
    zero_halo = start(sends)
    stat_a = stat_middle(0, stat_a, True)

    dm, pgr = S.dm, S.pgr
    for i in range(2):
        got = nt(dm[i, :, 0 : 6 * big], xj[80 : 80 + 80, 2 * i * big : (2 * i + 6) * big])
        got = got + nn(dm[i, :, 6 * big :], xe[:, 80:160])
        for kk in range(nb):
            pgr[kk, i * LANES : (i + 1) * LANES, :] = got[kk * LANES : (kk + 1) * LANES, 0:cin].astype(bf16)
    ones = jnp.ones((16, 4 * big), bf16)
    put_misc(gm, MISC.dec_bias, nt(ones, xj[80:160, 2 * big : 6 * big])[0:1, 0:cin])

    loads.cw.wait()
    two, mg = S.two, S.mg
    acc = nn(pgr[0], S.cw[0])
    for kk in range(1, nb):
        acc = acc + nn(pgr[kk], S.cw[kk])
    two[...] = acc
    mg[...] = acc.astype(bf16)
    loads.dw.wait()
    ag, hp = S.ag, S.hp
    ag[...] = nn(mg[...], S.dw[...])
    S.mgt[...] = mg[...].T
    put_misc(gm, MISC.down_bias, jnp.sum(mg[...].astype(f32), axis=0, keepdims=True))

    mean1, m2 = stat_end(0, stat_a, True)
    var1 = m2 * (1.0 / s.pixels)
    rstd1 = lax.rsqrt(var1 + EPS)
    m1o[...] = mean1 * live
    v1o[...] = var1 * live
    arrive(zero_halo)
    nx = S.nx
    scale1 = rstd1 * vec(gain1)
    bias1 = vec(shift1)

    def norm_rows(n, carry):
        here = pl.ds(pl.multiple_of(n * 48, 16), 48)
        nx[here, :] = ((hx[here, :] - mean1) * scale1 + bias1).astype(bf16)
        return carry

    lax.fori_loop(0, 17, norm_rows, 0)

    filt, tm = S.filt, S.tm
    loads.pw.wait()
    h1 = S.h1
    acc = hx[own, :] + vec(pb)
    for kk in range(nb):
        here = slice(kk * px, (kk + 1) * px)
        filt[here, :] = nn(tm[here, :], nx[...]).astype(bf16)
        acc = acc + nt(filt[here, :], S.pw[kk])
    h1[...] = acc
    stat_b = stat_start(1, *moments(h1[...]))
    stat_b = stat_middle(1, stat_b, True)
    tm_t = S.tmt
    tm_t[...] = tm[...].T
    mean2, m2 = stat_end(1, stat_b, True)
    var2 = m2 * (1.0 / s.pixels)
    rstd2 = lax.rsqrt(var2 + EPS)
    m2o[...] = mean2 * live
    v2o[...] = var2 * live
    scale2 = rstd2 * vec(gain2)
    bias2 = vec(shift2)
    n2 = S.n2

    def norm_two_rows(n, carry):
        here = pl.ds(pl.multiple_of(n * 32, 16), 32)
        n2[here, :] = ((h1[here, :] - mean2) * scale2 + bias2).astype(bf16)
        return carry

    lax.fori_loop(0, px // 32, norm_two_rows, 0)

    loads.uw.wait()
    hp[...] = nn(n2[...], S.uw[...])
    act, hg = S.act, S.hg
    ubias = vec(ub)
    root = 0.7978845608028654

    def gelu_rows(n, carry):
        here = pl.ds(pl.multiple_of(n * 16, 16), 16)
        v = hp[here, :] + ubias
        sq = v * v
        t = jnp.tanh(root * (v + 0.044715 * (sq * v)))
        act[here, :] = (0.5 * v * (1.0 + t)).astype(bf16)
        slope = 0.5 * (1.0 + t) + (0.5 * root) * v * (1.0 - t * t) * (1.0 + (3 * 0.044715) * sq)
        hg[here, :] = (slope * ag[here, :]).astype(bf16)
        return carry

    lax.fori_loop(0, px // 16, gelu_rows, 0)
    g1 = S.g1
    cols = [(lo, min(256, s.c5 * LANES - lo)) for lo in range(0, s.c5 * LANES, 256)]

    def spread(g, off, height, pitch, value, lo, width):
        for n in range(width // LANES):
            at = off + (lo // LANES + n) * pitch
            g[at : at + height, :] = value[:, n * LANES : (n + 1) * LANES].astype(bf16)

    for lo in range(0, s.f10 * LANES, 256):
        spread(g1, 0, c, s.r641, nn(S.mgt[...], act[:, lo : lo + 256]), lo, 256)
    ar("a")
    S.n2t[...] = n2[...].T
    for lo in range(0, s.f10 * LANES, 256):
        spread(g1, s.off_up, c, s.r641, nn(S.n2t[...], hg[:, lo : lo + 256]), lo, 256)
    h2 = S.h2
    h2[...] = (h1[...] + nt(act[...], S.dw[...]) + vec(db)).astype(bf16)
    for kk in range(nb):
        got = tn(pgr[kk], h2[:, 0 : s.c5 * LANES])
        spread(g1, s.off_dec + kk * s.c5 * s.r80, cin, s.r80, got, 0, s.c5 * LANES)
    ar("bea")
    ntg = S.ntg
    ntg[...] = nt(hg[...], S.uw[...])
    grad = ntg[...]
    standard = (h1[...] - mean2) * rstd2
    sum_a = jnp.sum(grad, axis=0, keepdims=True)
    sum_b = jnp.sum(grad * standard, axis=0, keepdims=True)
    put_misc(gm, MISC.shift_two, sum_a)
    put_misc(gm, MISC.gain_two, sum_b)
    stat_c = stat_start(2, sum_a, sum_b)

    ar("dbecdfc")
    stat_c = stat_middle(2, stat_c, False)

    def weighted(ref, column):
        return jnp.sum(ref.astype(f32) * column.astype(f32), axis=0, keepdims=True)

    def put_long(slot, row):
        put_misc(gm, slot, row[:, 0:768])
        put_misc(gm, slot + 1, row[:, 768:])

    def misc_one():
        put_long(MISC.up_bias, jnp.sum(hg[...].astype(f32), axis=0, keepdims=True))
        for n in range(2):
            at = s.f10 * LANES + n
            put_misc(gm, MISC.up_last + n, weighted(n2[...], hg[:, at : at + 1]))
            put_misc(gm, MISC.down_last + n, weighted(mg[...], act[:, at : at + 1]))
        for kk in range(nb):
            put_misc(gm, MISC.dec_last + kk, weighted(pgr[kk], h2[:, c - 1 : c]))

    sum_a, sum_b = stat_end(2, stat_c, False)
    g_two = vec(gain2)
    part_a = g_two * sum_a * (1.0 / s.pixels)
    part_b = g_two * sum_b * (1.0 / s.pixels)
    one, br = S.one, S.br

    def one_rows(n, carry):
        here = pl.ds(pl.multiple_of(n * 32, 16), 32)
        standard = (h1[here, :] - mean2) * rstd2
        value = rstd2 * (g_two * ntg[here, :] - part_a - standard * part_b) + two[here, :]
        one[here, :] = value
        br[here, :] = value.astype(bf16)
        return carry

    lax.fori_loop(0, px // 32, one_rows, 0)
    ar("af")
    fg = S.fg
    for kk in range(nb):
        fg[kk * px : (kk + 1) * px, :] = nn(br[...], S.pw[kk]).astype(bf16)
    con = S.con
    con[...] = nn(S.tmt[...], fg[...])

    def sum_rows(n, carry):
        here = pl.ds(pl.multiple_of(n * 48, 16), 48)
        value = con[here, :]
        standard = (hx[here, :] - mean1) * rstd1
        return (
            carry[0] + jnp.sum(value, axis=0, keepdims=True),
            carry[1] + jnp.sum(value * standard, axis=0, keepdims=True),
        )

    zero_row = jnp.zeros((1, c), f32)
    sum_a, sum_b = lax.fori_loop(0, 17, sum_rows, (zero_row, zero_row))
    put_misc(gm, MISC.shift_one, sum_a)
    put_misc(gm, MISC.gain_one, sum_b)
    stat_d = stat_start(3, sum_a, sum_b)
    sends = [
        Send(k, con.at[pl.ds(0, px)], S.rdn, k.at(0, -1, 0), -1),
        Send(k, con.at[pl.ds(2 * px, px)], S.rup, k.at(0, 1, 0), 1),
    ]
    for dl, ds in dirs:
        mine = (dl + 1) * 2 + (ds + 1) // 2
        sends.append(
            Send(
                k,
                con.at[pl.ds(768 + mine * 8, 8)],
                S.reg.at[slot_of(dl, ds)],
                k.at(0, dl, ds),
                dl,
            )
        )
    back_halo = start(sends)
    g2 = S.g2
    S.brt[...] = br[...].T
    ar("b")
    for kk in range(nb):
        if kk == 1:
            stat_d = stat_middle(3, stat_d, False)
        for lo, width in cols:
            got = nn(S.brt[...], filt[kk * px : (kk + 1) * px, lo : lo + width])
            spread(g2, kk * s.c5 * s.r641, c, s.r641, got, lo, width)
        if kk == 1:
            ar("gdceb")
    ar("ijh")

    arrive(back_halo)
    ar("afgjdhb")
    ng = ntg
    ng[...] = con[own, :]

    @pl.when(k.has_up())
    def _():
        ng[...] = ng[...] + S.rup[...]

    @pl.when(k.has_down())
    def _():
        ng[...] = ng[...] + S.rdn[...]

    def add_edges(sl):
        for ss in (-1, 1):
            got = S.reg.at[(sl + 1) * 2 + (ss + 1) // 2]
            col = 0 if ss == -1 else LANES - 2
            for q in range(2):
                lo = q * LANES + col
                ng[lo : lo + 2, :] = ng[lo : lo + 2, :] + got[2 * q : 2 * q + 2, :]

    add_edges(0)
    pl.when(k.has_up())(lambda: add_edges(-1))
    pl.when(k.has_down())(lambda: add_edges(1))
    sum_a, sum_b = stat_end(3, stat_d, False)
    g_one = vec(gain1)
    part_a1 = g_one * sum_a * (1.0 / s.pixels)
    part_b1 = g_one * sum_b * (1.0 / s.pixels)
    zg = S.zg

    def zero_rows(n, carry):
        here = pl.ds(pl.multiple_of(n * 32, 16), 32)
        there = pl.ds(pl.multiple_of(px + n * 32, 16), 32)
        standard = (hx[there, :] - mean1) * rstd1
        value = rstd1 * (g_one * ng[here, :] - part_a1 - standard * part_b1) + one[here, :]
        zg[here, :] = value.astype(bf16)
        return carry

    lax.fori_loop(0, px // 32, zero_rows, 0)

    g3 = S.g3
    for kk in range(nb):
        got = tn(filte[kk], zg[:, 0 : s.c5 * LANES])
        spread(g3, kk * s.c5 * s.r80, cj, s.r80, got, 0, s.c5 * LANES)
        put_misc(gm, MISC.enc_last + kk, weighted(filte[kk], zg[:, c - 1 : c]))
    put_misc(gm, MISC.enc_bias, jnp.sum(zg[...].astype(f32), axis=0, keepdims=True))
    ar("k")
    misc_one()
    put_misc(gm, MISC.proc_bias, jnp.sum(br[...].astype(f32), axis=0, keepdims=True))
    for kk in range(nb):
        put_misc(gm, MISC.proc_last + kk, weighted(br[...], filt[kk * px : (kk + 1) * px, c - 1 : c]))
    ar("ajekgfid")

    projt, partt = S.projt, S.partt
    for kk in range(nb):
        here = slice(kk * LANES, (kk + 1) * LANES)
        proj = nt(h2[...], S.cw[kk])
        part = nt(zg[...], S.ew[kk])[:, 0:cin]
        for i in range(2):
            for ref, value in ((projt, proj), (partt, part)):
                ref[i, 0:cin, here] = value[i * LANES : (i + 1) * LANES, :].T.astype(bf16)
                ref[i, cin:80, here] = jnp.zeros((80 - cin, LANES), bf16)
    sgx = S.sgx
    em = S.em
    sgx[...] = jnp.zeros(sgx.shape, f32)
    for i in range(2):
        lo = 2 * i * big
        got = nn(projt[i], dm[i])
        sgx[0:80, lo : lo + 6 * big] = sgx[0:80, lo : lo + 6 * big] + got[:, 0 : 6 * big]
        sgx[0:80, edge0 : edge0 + 48] = sgx[0:80, edge0 : edge0 + 48] + got[:, 6 * big :]
        got = nn(partt[i], em[i])
        sgx[80:160, lo : lo + 5 * big] = sgx[80:160, lo : lo + 5 * big] + got[:, 0 : 5 * big]
        sgx[80:160, edge0 : edge0 + 48] = sgx[80:160, edge0 : edge0 + 48] + got[:, 5 * big :]
    sgb, sgu, sgd, sge = S.sgb, S.sgu, S.sgd, S.sge
    sgb[:, 0 : 2 * big] = sgx[:, 0 : 2 * big].astype(bf16)
    sgb[:, 2 * big : 4 * big] = sgx[:, 6 * big : 8 * big].astype(bf16)
    turned = sgx[:, edge0:].T
    for n in range(6):
        S.sgn[n] = turned[n * 8 : n * 8 + 8, :]
    sends = [
        Send(k, sgb.at[:, pl.ds(0, 2 * big)], sgd, k.at(0, -1, 0), -1),
        Send(k, sgb.at[:, pl.ds(2 * big, 2 * big)], sgu, k.at(0, 1, 0), 1),
    ]
    for dl, ds in dirs:
        sends.append(
            Send(k, S.sgn.at[(dl + 1) * 2 + (ds + 1) // 2], sge.at[slot_of(dl, ds)], k.at(0, dl, ds), dl)
        )
    out_halo = start(sends)
    ar("hagbkfelcl")
    arrive(out_halo)
    ar("iahldcgiebdhlkjafgiehklcbjgi")
    sgt = S.sgt
    sgt[48:LANES, :] = jnp.zeros((LANES - 48, 160), f32)
    for slot in range(6):
        sgt[slot * 8 : slot * 8 + 8, :] = sge[slot]
    for slot in (0, 1, 4, 5):
        @absent(slot)
        def _():
            sgt[slot * 8 : slot * 8 + 8, :] = jnp.zeros((8, 160), f32)
    arrived = sgt[...].T
    up_one = jnp.where(k.has_up(), 1, 0)
    down_one = jnp.where(k.has_down(), 1, 0)
    cbt = S.cbt
    cbt[...] = jnp.zeros((8, LANES), f32)
    cbt[0:1, 0:cin] = vec(cb)
    bias_col = cbt[...].T[0:cin, 0:1]
    orow, st7 = S.orow, S.st7

    for q in range(4):
        lo = (2 + q) * big
        value = sgx[:, lo : lo + big]
        if q < 2:
            other = sgu[:, q * big : (q + 1) * big].astype(f32)
            value = value + jnp.where(up_one == 1, other, 0.0)
        else:
            other = sgd[:, (q - 2) * big : (q - 1) * big].astype(f32)
            value = value + jnp.where(down_one == 1, other, 0.0)
        head, tail = value[:, 0:LANES], value[:, big - LANES :]
        for sl in (-1, 0, 1):
            for side in range(2):
                at = ((sl + 1) * 2 + side) * 8 + q * 2
                if side == 0:
                    moved = pltpu.roll(arrived, (LANES - at) % LANES, 1)
                    head = head + jnp.where(lane < 2, moved, 0.0)
                else:
                    moved = pltpu.roll(arrived, LANES - 2 - at, 1)
                    tail = tail + jnp.where(lane >= LANES - 2, moved, 0.0)
        orow[:, q, 0:LANES] = (head[0:cin] + bias_col) * live
        orow[:, q, LANES:big] = (tail[0:cin] + bias_col) * live
        st7[k.e, :, q * big : q * big + LANES] = head[80:160].astype(bf16)
        st7[k.e, :, q * big + LANES : (q + 1) * big] = tail[80:160].astype(bf16)
    out[0] = orow[...].astype(bf16)
    state_sends = start(
        [Send(k, st7.at[k.e], st7.at[k.e], k.at(d, 0, 0)) for d in range(1, s.ne)]
    )
    ar("ckhfdljkiglgcjble")
    arrive(date_sends)
    arrive(state_sends)
    ar("dahfk")
    for d in range(s.dates):
        for q in range(4):
            value = jnp.zeros((80, big), f32)
            for n in range(s.ne):
                is_d = jnp.where(S.dates[n, 0:1, :] == float(d), 1.0, 0.0)
                is_d = jnp.concatenate([is_d] * (big // LANES), axis=1)
                value = value + is_d * st7[n, :, q * big : (q + 1) * big].astype(f32)
            orow[:, q, :] = value[0:cin]
        sgrad[d] = orow[...].astype(bf16)

    ar("elijkfhcij")
    while not all(it.finished() for it in reduced.values()):
        ar("abcdefghijkl")
    for m in pending:
        m.wait_send()


def finish_kernel(s, *refs):
    h1, h2, h3, hm, output_in, state_in, m1, v1, m2, v2 = refs[:10]
    (
        output, state_grad,
        enc_w, enc_b, g1o, s1o, proc_w, proc_b, g2o, s2o,
        up_w, up_b, down_w, down_b, dec_w, dec_b, m1o, v1o, m2o, v2o,
    ) = refs[10:30]
    (b1, b2, b3, enc_v, proc_v, up_v, down_v, dec_v, row_v, sem_in, sem_out) = refs[30:]
    c, ff, nb, cin, cj = s.c, s.ff, s.nb, s.cin, s.cj
    used1 = s.off_dec + nb * s.c5 * s.r80
    third = s.c5 * s.r641
    pieces = [(h2, b2, n * third, third) for n in range(nb)]
    pieces += [(h1, b1, 0, s.off_up), (h1, b1, s.off_up, s.off_dec - s.off_up)]
    pieces += [(h1, b1, s.off_dec, used1 - s.off_dec), (h3, b3, 0, nb * s.c5 * s.r80)]
    loads = [
        pltpu.make_async_copy(a.at[pl.ds(at, n)], b.at[pl.ds(at, n)], sem_in.at[i])
        for i, (a, b, at, n) in enumerate(pieces)
    ]
    for copy in loads:
        copy.start()
    stores = []

    def store(src, dst):
        copy = pltpu.make_async_copy(src, dst, sem_out.at[len(stores)])
        copy.start()
        stores.append(copy)

    for a, b in ((output_in, output), (state_in, state_grad), (m1, m1o), (v1, v1o), (m2, m2o), (v2, v2o)):
        b[...] = a[...]
    turned = hm[0:144, :].T

    def last_column(ref, slot, height, at):
        for t in range(-(-height // LANES)):
            n = min(LANES, height - t * LANES)
            ref[t * LANES : t * LANES + n, at : at + 1] = turned[0:n, slot * 6 + t : slot * 6 + t + 1]

    def widen(ref, src, base, pitch, height, tiles):
        for n in range(tiles):
            at = base + n * pitch
            ref[:, n * LANES : (n + 1) * LANES] = src[at : at + height, :].astype(f32)

    last = s.c5 * LANES
    for kk in range(nb):
        ref = proc_v.at[kk]
        last_column(ref, MISC.proc_last + kk, c, last)
        loads[kk].wait()
        widen(ref, b2, kk * third, s.r641, c, s.c5)
        store(ref, proc_w.at[kk])
    for n, (ref, slot, base, to) in enumerate(
        ((down_v, MISC.down_last, 0, down_w), (up_v, MISC.up_last, s.off_up, up_w))
    ):
        for part in range(2):
            last_column(ref, slot + part, c, s.f10 * LANES + part)
        loads[nb + n].wait()
        widen(ref, b1, base, s.r641, c, s.f10)
        store(ref, to)
    loads[nb + 2].wait()
    loads[nb + 3].wait()
    for kk in range(nb):
        ref = dec_v.at[kk]
        last_column(ref, MISC.dec_last + kk, cin, last)
        widen(ref, b1, s.off_dec + kk * s.c5 * s.r80, s.r80, cin, s.c5)
        ref = enc_v.at[kk]
        last_column(ref, MISC.enc_last + kk, cj, last)
        widen(ref, b3, kk * s.c5 * s.r80, s.r80, cj, s.c5)
    store(dec_v, dec_w)
    store(enc_v, enc_w)

    def flat(ref, slots):
        at = 0
        for slot, width in slots:
            for piece in get_misc(hm, slot, width):
                n = piece.shape[1]
                row_v[0:1, at : at + n] = piece
                at += n
        ref[...] = row_v[0:1, 0:at].reshape(at)

    for ref, slot in (
        (enc_b, MISC.enc_bias), (g1o, MISC.gain_one), (s1o, MISC.shift_one), (proc_b, MISC.proc_bias),
        (g2o, MISC.gain_two), (s2o, MISC.shift_two), (down_b, MISC.down_bias),
    ):
        flat(ref, [(slot, c)])
    flat(up_b, [(MISC.up_bias, 768), (MISC.up_bias + 1, ff - 768)])
    flat(dec_b, [(MISC.dec_bias, cin)])
    for copy in stores:
        copy.wait()


def per_device(s, *args):
    (
        state, noise, cot, slot_date, lon_reach, enc_taps, proc_taps, dec_taps,
        enc_weight, enc_bias, gain_one, shift_one, proc_weight, proc_bias, gain_two, shift_two,
        up_weight, up_bias, down_weight, down_bias, dec_weight, dec_bias,
    ) = args
    args = list(args)
    args[8] = jnp.swapaxes(enc_weight, 1, 2)
    args[16] = up_weight.T
    vm = pl.BlockSpec(memory_space=pltpu.VMEM)
    sm = pl.BlockSpec(memory_space=pltpu.SMEM)
    hbm = pl.BlockSpec(memory_space=pl.ANY)
    shapes = scratch_list(s)
    names = tuple(shapes)
    in_specs = [vm] * 3 + [sm] * 5 + [
        hbm, vm, vm, vm, hbm, vm, vm, vm, hbm, vm, hbm, vm, hbm, vm,
    ]
    sd = jax.ShapeDtypeStruct
    out_shape = [
        sd((s.rows[0], LANES), bf16),
        sd((s.rows[1], LANES), bf16),
        sd((s.rows[2], LANES), bf16),
        sd((s.rows[3], LANES), f32),
        sd((1, s.cin, s.full_rows, s.full_cols), bf16),
        sd((s.dates, s.cin, s.full_rows, s.full_cols), bf16),
    ] + [sd((1, s.c), f32)] * 4
    got = pl.pallas_call(
        functools.partial(main_kernel, s, names),
        out_shape=out_shape,
        in_specs=in_specs,
        out_specs=[hbm] * 4 + [vm] * 6,
        scratch_shapes=list(shapes.values()),
        compiler_params=pltpu.CompilerParams(
            collective_id=0, has_side_effects=True, vmem_limit_bytes=60 * 2**20
        ),
        name="forecast",
    )(*args)
    c, ff, nb = s.c, s.ff, s.nb
    outs = [out_shape[4], out_shape[5]] + [
        sd((nb, s.cj, c), f32), sd((c,), f32), sd((c,), f32), sd((c,), f32),
        sd((nb, c, c), f32), sd((c,), f32), sd((c,), f32), sd((c,), f32),
        sd((c, ff), f32), sd((ff,), f32), sd((c, ff), f32), sd((c,), f32),
        sd((nb, s.cin, c), f32), sd((s.cin,), f32),
    ] + [sd((1, c), f32)] * 4
    large = (2, 6, 10, 12, 14)
    V = pltpu.VMEM
    done = pl.pallas_call(
        functools.partial(finish_kernel, s),
        out_shape=outs,
        in_specs=[hbm] * 3 + [vm] * 7,
        out_specs=[hbm if n in large else vm for n in range(len(outs))],
        scratch_shapes=[
            V((s.rows[0], LANES), bf16), V((s.rows[1], LANES), bf16), V((s.rows[2], LANES), bf16),
            V((nb, s.cj, c), f32), V((nb, c, c), f32), V((c, ff), f32), V((c, ff), f32),
            V((nb, s.cin, c), f32), V((8, up_to(ff, LANES)), f32),
            pltpu.SemaphoreType.DMA((8,)), pltpu.SemaphoreType.DMA((16,)),
        ],
        compiler_params=pltpu.CompilerParams(vmem_limit_bytes=60 * 2**20),
        name="finish",
    )(*got)
    done = list(done)
    done[2] = jnp.swapaxes(done[2], 1, 2)
    done[10] = done[10].T
    return tuple(done)


def solution(mesh):
    in_specs = (
        P(None, None, "lat", "lon"),
        P("ens", None, "lat", "lon"),
        P("ens", None, "lat", "lon"),
        P("ens"),
    ) + (P(),) * 18
    out_specs = (
        (P("ens", None, "lat", "lon"), P(None, None, "lat", "lon"))
        + (P(),) * 14
        + (P("ens", None),) * 4
    )

    def run(*args):
        s = Sizes(mesh, args[0].shape, args[1].shape, args[5].shape, args[8].shape, args[16].shape)
        return jax.shard_map(
            functools.partial(per_device, s),
            mesh=mesh,
            in_specs=in_specs,
            out_specs=out_specs,
            check_vma=False,
        )(*args)

    return run
```

```python
import functools
import types

import jax
import jax.numpy as jnp
from jax import lax
from jax.experimental import pallas as pl
from jax.experimental.pallas import tpu as pltpu
from jax.sharding import PartitionSpec as P

MESH = pl.DeviceIdType.MESH
f32 = jnp.float32
bf16 = jnp.bfloat16
i32 = jnp.int32
EPS = 1e-05
LANES = 128
AXES = ("ens", "lat", "lon")
BIT0, BIT1, LAT, LON = range(4)
ROUTE_X = (LAT, BIT0, BIT1, LON)
ROUTE_Y = (LAT, BIT1, BIT0, LON)
WSEM, OSEM, SEMS = range(3)
ROUTE_ZX = (LAT, LON, BIT0, BIT1)
ROUTE_ZY = (LAT, LON, BIT1, BIT0)
PIECES = dict(
    a=(0, 0), b=(0, 1), c=(0, 2), d=(1, 0), e=(1, 1), f=(1, 2),
    g=(2, 0), h=(2, 1), i=(3, 0), j=(3, 1), k=(4, 0), l=(5, 0), m=(2, 2), n=(3, 2),
)


def nn(a, b):
    return lax.dot_general(a, b, (((1,), (0,)), ((), ())), preferred_element_type=f32)


def nt(a, b):
    return lax.dot_general(a, b, (((1,), (1,)), ((), ())), preferred_element_type=f32)


def tn(a, b):
    return lax.dot_general(a, b, (((0,), (0,)), ((), ())), preferred_element_type=f32)


def up_to(n, m):
    return -(-n // m) * m


class Sizes:
    def __init__(self, mesh, state, noise, enc_taps, enc_weight, up_weight):
        self.ne, self.nl, self.nz = (mesh.shape[a] for a in AXES)
        self.dates, self.cin, self.full_rows, self.full_cols = state
        self.noise = noise[1]
        self.full_rows = state[2] // self.nl
        self.full_cols = state[3] // self.nz
        self.hr, self.hc = self.full_rows // 2, self.full_cols // 2
        assert self.hr == 2 and self.hc == LANES and self.ne == 4
        self.lat_total = enc_taps[1]
        self.nb = enc_taps[0]
        self.c = enc_weight[1]
        self.cj = enc_weight[2]
        self.ff = up_weight[0]
        self.px = self.hr * self.hc
        self.pixels = float(self.px * self.nl * self.nz)
        self.c5 = self.c // LANES
        self.f10 = self.ff // LANES
        self.r641 = up_to(self.c, 16)
        self.r80 = up_to(self.cj, 16)
        self.off_up = self.f10 * self.r641
        self.off_dec = self.off_up + self.f10 * self.r641
        used = (
            self.off_dec + self.nb * self.c5 * self.r80,
            self.nb * self.c5 * self.r641,
            self.nb * self.c5 * self.r80,
        )
        unit = 16 * self.nl * self.ne * self.nz
        self.rows = tuple(up_to(n, unit) for n in used) + (up_to(24 * 6, unit // 2),)
        self.chunks = {}

        def split(piece, buffer, lo, hi, third, last):
            units = (hi - lo) // unit
            last = last if units >= 3 * last else 0
            first = (units - last + 1) // 2
            at = lo
            for n, (count, route) in enumerate(
                ((first, ROUTE_X), (units - last - first, ROUTE_Y), (last, third))
            ):
                if count:
                    self.chunks[piece, n] = (buffer, at, count * unit, route)
                at += count * unit

        cut = self.off_up // unit * unit
        split(0, 0, 0, cut, ROUTE_ZX, 2)
        split(1, 0, cut, self.rows[0], ROUTE_ZY, 2)
        cut = 2 * self.c5 * self.r641 // unit * unit
        split(2, 1, 0, cut, ROUTE_ZX, 0)
        split(3, 1, cut, self.rows[1], ROUTE_ZY, 0)
        self.chunks[4, 0] = (2, 0, self.rows[2], ROUTE_X)
        self.chunks[5, 0] = (3, 0, self.rows[3], ROUTE_Y)
        self.group = self.nl * self.nz


def add_into(dst, at, sources, count):
    step = next(s for s in (256, 128, 64, 32, 16, 8) if count % s == 0)

    def body(n, carry):
        lo = pl.multiple_of(n * step, 8 if step == 8 else 16)
        there = pl.ds(pl.multiple_of(at + lo, 8 if step == 8 else 16), step)
        value = dst[there, :].astype(f32)
        for source in sources:
            value = value + source[pl.ds(lo, step), :].astype(f32)
        dst[there, :] = value.astype(dst.dtype)
        return carry

    lax.fori_loop(0, count // step, body, 0)


class Links:
    def __init__(self, z, sems=None):
        self.s = z
        self.sems = sems
        self.used = 0
        if sems is not None:
            self.e, self.l, self.z = (lax.axis_index(a) for a in AXES)

    def take(self):
        self.used += 1
        return self.used - 1

    def at(self, de, dl, dz):
        s = self.s
        return (
            lax.rem(self.e + (de + s.ne), s.ne),
            lax.rem(self.l + (dl + s.nl), s.nl),
            lax.rem(self.z + (dz + s.nz), s.nz),
        )

    def bit(self, which):
        return lax.rem(self.e // (1 << which), 2)

    def flip(self, which):
        return (self.e + (1 << which) * (1 - 2 * self.bit(which)), self.l, self.z)

    def has_up(self):
        return self.l > 0

    def has_down(self):
        return self.l < self.s.nl - 1


class Send:
    def __init__(self, links, src, dst, device, dl=0):
        self.links = links
        self.ids = (links.take(), links.take())
        self.what = (src, dst, device)
        self.dl = dl

    def copy(self):
        src, dst, device = self.what
        return pltpu.make_async_remote_copy(
            src_ref=src,
            dst_ref=dst,
            send_sem=self.links.sems.at[self.ids[0]],
            recv_sem=self.links.sems.at[self.ids[1]],
            device_id=device,
            device_id_type=MESH,
        )

    def under(self, sending, act):
        if self.dl == 0:
            act()
        else:
            up = (self.dl < 0) == sending
            pl.when(self.links.has_up() if up else self.links.has_down())(act)

    def start(self):
        self.under(True, lambda: self.copy().start())

    def wait_recv(self):
        self.under(False, lambda: self.copy().wait_recv())

    def wait_send(self):
        self.under(True, lambda: self.copy().wait_send())


class AllReduce:
    def __init__(self, links, partial, total, lo, rows, route, bufs, own_sem):
        self.k, self.g, self.h, self.route = links, partial, total, route
        self.bufs, self.own_sem = bufs, own_sem
        self.sent, self.waiting = [], []
        self.stage = 0
        self.base, self.part = [], []
        base, size = lo, rows
        for axis in route:
            size = size // self.count(links.s, axis)
            self.base.append(base)
            self.part.append(size)
            base = base + self.index(axis) * size
        self.base.append(base)
        self.last_stage = 2 * len(route)

    @staticmethod
    def count(s, axis):
        return {LAT: s.nl, LON: s.nz}.get(axis, 2)

    @staticmethod
    def shapes(s, rows, route, dtype):
        out = []
        for axis in route:
            n = AllReduce.count(s, axis)
            rows = rows // n
            out.append(pltpu.VMEM((n - 1, rows, LANES), dtype))
        return out

    def index(self, axis):
        k = self.k
        return {LAT: k.l, LON: k.z}[axis] if axis in (LAT, LON) else k.bit(axis)

    def others(self, axis):
        k, s = self.k, self.k.s
        if axis == LAT:
            devices = [k.at(0, d, 0) for d in range(1, s.nl)]
            return [(dev, dev[1], n) for n, dev in enumerate(devices)]
        if axis == LON:
            devices = [k.at(0, 0, d) for d in range(1, s.nz)]
            return [(dev, dev[2], n) for n, dev in enumerate(devices)]
        return [(k.flip(axis), 1 - k.bit(axis), 0)]

    def send(self, src, dst, device):
        m = Send(self.k, src, dst, device)
        m.start()
        self.sent.append(m)
        self.waiting.append(m)

    def step(self):
        g, h, route = self.g, self.h, self.route
        al = lambda v: pl.multiple_of(v, 8)
        stage, self.stage = self.stage, self.stage + 1
        for m in self.waiting:
            m.wait_recv()
        self.waiting = []
        depth = len(route)
        if 0 < stage <= depth:
            buf = self.bufs[stage - 1]
            add_into(g, al(self.base[stage]), [buf.at[n] for n in range(buf.shape[0])], self.part[stage - 1])
        if stage < depth:
            size = self.part[stage]
            for device, place, slot in self.others(route[stage]):
                there = pl.ds(al(self.base[stage] + place * size), size)
                self.send(g.at[there], self.bufs[stage].at[slot], device)
        elif stage < 2 * depth:
            level = 2 * depth - 1 - stage
            here = pl.ds(al(self.base[level + 1]), self.part[level])
            if stage == depth:
                self.own = pltpu.make_async_copy(g.at[here], h.at[here], self.own_sem)
                self.own.start()
            if stage == depth + 1:
                self.own.wait()
            source = g if stage == depth else h
            for device, _, _ in self.others(route[level]):
                self.send(source.at[here], h.at[here], device)
        else:
            for m in self.sent:
                m.wait_send()

    def finished(self):
        return self.stage > self.last_stage


class MISC:
    down_bias, up_bias, gain_two, shift_two, proc_bias, gain_one, shift_one, enc_bias = 0, 1, 3, 4, 5, 6, 7, 8
    up_last, down_last, proc_last, enc_last, dec_last, dec_bias = 9, 11, 13, 16, 19, 22


def put_misc(misc, slot, row):
    width = row.shape[1]
    for t in range(-(-width // LANES)):
        lo, hi = t * LANES, min(width, (t + 1) * LANES)
        misc[slot * 6 + t : slot * 6 + t + 1, 0 : hi - lo] = row[:, lo:hi]


def get_misc(misc, slot, width):
    parts = []
    for t in range(-(-width // LANES)):
        lo, hi = t * LANES, min(width, (t + 1) * LANES)
        parts.append(misc[slot * 6 + t : slot * 6 + t + 1, 0 : hi - lo])
    return parts


def scratch_list(s):
    c, ff, px = s.c, s.ff, s.px
    big = s.full_cols
    wide = 8 * big + LANES
    V = pltpu.VMEM
    shapes = dict(
        state=V((s.dates, s.cin, s.full_rows, big), bf16),
        noise=V((1, s.noise, s.full_rows, big), bf16),
        cot=V((1, s.cin, s.full_rows, big), bf16),
        eb_v=V((c,), f32), gain1=V((c,), f32), shift1=V((c,), f32), pb=V((c,), f32), gain2=V((c,), f32),
        shift2=V((c,), f32), ub=V((ff,), f32), db=V((c,), f32), cb=V((s.cin,), f32),
        out=V((1, s.cin, s.full_rows, big), bf16),
        sgrad=V((s.dates, s.cin, s.full_rows, big), bf16),
        means=V((4, 1, c), f32),
        xin=V((160, s.full_rows, big), f32),
        xj=V((160, 8 * big), bf16),
        eb=V((2, 8, 160), f32),
        eslot=V((6, 8, 160), f32),
        xe=V((48, 160), bf16),
        em=V((2, s.nb * LANES, 5 * big + 48), bf16),
        dm=V((2, s.nb * LANES, 6 * big + 48), bf16),
        tm=V((s.nb * px, 6 * LANES + 48), bf16),
        ew=V((s.nb, s.cj, c), bf16),
        pw=V((s.nb, c, c), bf16),
        uw=V((c, ff), bf16),
        dw=V((c, ff), bf16),
        cw=V((s.nb, s.cin, c), bf16),
        filte=V((s.nb, px, s.cj), bf16),
        hx=V((6 * LANES + 48, c), f32),
        nx=V((6 * LANES + 48, c), bf16),
        pe=V((2, 8, c), f32),
        filt=V((s.nb * px, c), bf16),
        h1=V((px, c), f32),
        n2=V((px, c), bf16),
        hp=V((px, ff), f32),
        ag=V((px, ff), f32),
        act=V((px, ff), bf16),
        hg=V((px, ff), bf16),
        n2t=V((c, px), bf16),
        h2=V((px, c), bf16),
        pgr=V((s.nb, px, s.cin), bf16),
        projt=V((2, 80, s.nb * LANES), bf16),
        partt=V((2, 80, s.nb * LANES), bf16),
        two=V((px, c), f32),
        mg=V((px, c), bf16),
        mgt=V((c, px), bf16),
        ntg=V((px, c), f32),
        one=V((px, c), f32),
        br=V((px, c), bf16),
        brt=V((c, px), bf16),
        fg=V((s.nb * px, c), bf16),
        con=V((6 * LANES + 48, c), f32),
        rup=V((px, c), f32),
        rdn=V((px, c), f32),
        reg=V((6, 8, c), f32),
        zg=V((px, c), bf16),
        sgx=V((160, wide), f32),
        sgb=V((160, 4 * big), bf16),
        sgu=V((160, 2 * big), bf16),
        sgd=V((160, 2 * big), bf16),
        sgn=V((6, 8, 160), f32),
        sge=V((6, 8, 160), f32),
        sgt=V((LANES, 160), f32),
        orow=V((s.cin, s.full_rows, big), f32),
        st7=V((s.ne, 80, 4 * big), bf16),
        dates=V((s.ne, 8, LANES), f32),
        cbt=V((8, LANES), f32),
        slat=V((4, s.nl, 2, c), f32),
        slon=V((4, s.nz, 2, c), f32),
        sall=V((4, s.group if s.group <= 16 else 1, 2, c), f32),
        tmt=V((6 * LANES + 48, s.nb * px), bf16),
        g1=V((s.rows[0], LANES), bf16),
        g2=V((s.rows[1], LANES), bf16),
        g3=V((s.rows[2], LANES), bf16),
        gm=V((s.rows[3], LANES), f32),
    )
    for name, (buffer, _, rows, route) in s.chunks.items():
        kinds = AllReduce.shapes(s, rows, route, f32 if buffer == 3 else bf16)
        for j, kind in enumerate(kinds):
            shapes[name, j] = kind
    shapes[WSEM] = pltpu.SemaphoreType.DMA((23,))
    shapes[OSEM] = pltpu.SemaphoreType.DMA((len(s.chunks),))
    shapes[SEMS] = pltpu.SemaphoreType.DMA((sem_count(s),))
    return shapes


def sem_count(s):
    total = len(s.chunks) * 2 * 2 * (s.nl - 1 + 1 + 1 + s.nz - 1)
    total += 2 * 4 * 8 + 2 * (s.ne - 1) + 2 * 6
    total += 4 * 2 * (s.group - 1 if s.group <= 16 else s.nl - 1 + s.nz - 1)
    return total


def main_kernel(s, names, *refs):
    n_in, n_out = 22, 10
    (
        state_h, noise_h, cot_h, date_ref, reach, enc_taps, proc_taps, dec_taps,
        ew_h, eb_h, gain1_h, shift1_h, pw_h, pb_h, gain2_h, shift2_h, uw_h, ub_h, dw_h, db_h, cw_h, cb_h,
    ) = refs[:n_in]
    h1o, h2o, h3o, hmo, out_h, sgrad_h, m1_h, v1_h, m2_h, v2_h = refs[n_in : n_in + n_out]
    table = dict(zip(names, refs[n_in + n_out :]))
    S = types.SimpleNamespace(**{n: r for n, r in table.items() if isinstance(n, str)})
    sems = table[SEMS]
    k = Links(s, sems)
    c, ff, px, nb, cin, cj = s.c, s.ff, s.px, s.nb, s.cin, s.cj
    big = s.full_cols
    l = k.l
    row0 = l * s.hr
    edge0 = 8 * big

    offsets = {(d, 0, 0) for d in range(1, s.ne)}
    if s.group <= 16:
        offsets |= {(0, a, b) for a in range(s.nl) for b in range(s.nz)} - {(0, 0, 0)}
    else:
        offsets |= {(0, d, 0) for d in range(1, s.nl)} | {(0, 0, d) for d in range(1, s.nz)}
    offsets |= {(0, a % s.nl, b % s.nz) for a in (1, -1) for b in (1, -1)}
    offsets = sorted(offsets)
    barrier = pltpu.get_barrier_semaphore()
    for o in offsets:
        pl.semaphore_signal(barrier, 1, device_id=k.at(*o), device_id_type=MESH)

    def fetch(n, src, to):
        copy = pltpu.make_async_copy(src, to, table[WSEM].at[n])
        copy.start()
        return copy

    state, noise, cot = S.state, S.noise, S.cot
    fields = [fetch(n, *pair) for n, pair in enumerate(((state_h, state), (noise_h, noise), (cot_h, cot)))]
    eb, gain1, shift1, pb, gain2, shift2 = S.eb_v, S.gain1, S.shift1, S.pb, S.gain2, S.shift2
    ub, db, cb = S.ub, S.db, S.cb
    vectors = [
        fetch(3 + n, *pair)
        for n, pair in enumerate(
            (
                (eb_h, eb), (gain1_h, gain1), (shift1_h, shift1), (pb_h, pb), (gain2_h, gain2),
                (shift2_h, shift2), (ub_h, ub), (db_h, db), (cb_h, cb),
            )
        )
    ]
    loads = types.SimpleNamespace()
    loads.ew, loads.pw, loads.cw, loads.dw, loads.uw = [
        fetch(12 + n, *pair)
        for n, pair in enumerate(
            ((ew_h, S.ew), (pw_h, S.pw), (cw_h, S.cw), (dw_h, S.dw), (uw_h, S.uw))
        )
    ]
    finals = []

    def keep(src, to):
        copy = pltpu.make_async_copy(src, to, table[WSEM].at[17 + len(finals)])
        copy.start()
        finals.append(copy)

    for copy in fields:
        copy.wait()

    date = date_ref[0]
    live = jnp.where(date >= 0, 1.0, 0.0).astype(f32)
    xin, xj = S.xin, S.xj
    picked = jnp.zeros((cin, s.full_rows, big), f32)
    for d in range(s.dates):
        picked = picked + state[d].astype(f32) * jnp.where(date == d, 1.0, 0.0).astype(f32)
    xin[0:cin] = picked
    xin[cin:cj] = noise[0].astype(f32)
    xin[80 : 80 + cin] = cot[0].astype(f32) * live
    xin[80 + cin : 160] = jnp.zeros((160 - 80 - cin, s.full_rows, big), f32)
    lane = lax.broadcasted_iota(i32, (160, LANES), 1)
    ends = jnp.zeros((160, LANES), f32)
    for q in range(4):
        row = xin[:, q, :]
        xj[:, (2 + q) * big : (3 + q) * big] = row.astype(bf16)
        moved = pltpu.roll(row[:, 0:LANES], q * 2, 1)
        ends = jnp.where((lane >> 1) == q, moved, ends)
        moved = pltpu.roll(row[:, big - LANES : big], q * 2 + 10, 1)
        ends = jnp.where((lane >> 1) == q + 4, moved, ends)
    turned = ends.T
    S.eb[0] = turned[0:8, :]
    S.eb[1] = turned[8:16, :]
    S.dates[k.e] = jnp.full((8, LANES), date.astype(f32), f32)

    @pl.when(jnp.logical_not(k.has_up()))
    def _():
        xj[:, 0 : 2 * big] = jnp.zeros((160, 2 * big), bf16)
        S.hx[0:px] = jnp.zeros((px, c), f32)
        for side in range(2):
            S.hx[768 + side * 8 : 776 + side * 8] = jnp.zeros((8, c), f32)

    @pl.when(jnp.logical_not(k.has_down()))
    def _():
        xj[:, 6 * big : 8 * big] = jnp.zeros((160, 2 * big), bf16)
        S.hx[2 * px : 3 * px] = jnp.zeros((px, c), f32)
        for side in range(2):
            S.hx[768 + 32 + side * 8 : 776 + 32 + side * 8] = jnp.zeros((8, c), f32)

    pl.semaphore_wait(barrier, len(offsets))

    totals = (h1o, h2o, h3o, hmo)
    reduced = {}
    for n, (name, (buffer, lo, rows, route)) in enumerate(s.chunks.items()):
        bufs = [table[name, j] for j in range(len(route))]
        partial = (S.g1, S.g2, S.g3, S.gm)[buffer]
        reduced[name] = AllReduce(k, partial, totals[buffer], lo, rows, route, bufs, table[OSEM].at[n])

    def ar(letters):
        for letter in letters:
            it = reduced.get(PIECES[letter])
            if it is not None and not it.finished():
                it.step()

    pending = []

    def start(sends):
        for m in sends:
            m.start()
        pending.extend(sends)
        return sends

    def arrive(sends):
        for m in sends:
            m.wait_recv()

    dirs = [(dl, ds) for dl in (-1, 0, 1) for ds in (-1, 1)]

    def slot_of(dl, ds):
        return (1 - dl) * 2 + (1 - ds) // 2

    sends = [
        Send(k, xj.at[:, pl.ds(2 * big, 2 * big)], xj.at[:, pl.ds(6 * big, 2 * big)], k.at(0, -1, 0), -1),
        Send(k, xj.at[:, pl.ds(4 * big, 2 * big)], xj.at[:, pl.ds(0, 2 * big)], k.at(0, 1, 0), 1),
    ]
    for dl, ds in dirs:
        sends.append(
            Send(k, S.eb.at[(ds + 1) // 2], S.eslot.at[slot_of(dl, ds)], k.at(0, dl, ds), dl)
        )
    first_halo = start(sends)
    date_sends = start(
        [
            Send(k, S.dates.at[k.e], S.dates.at[k.e], k.at(d, 0, 0))
            for d in range(1, s.ne)
        ]
    )

    gm = S.gm
    gm[0:144] = jnp.zeros((144, LANES), f32)

    def band(shape, column_of):
        rows = lax.broadcasted_iota(i32, shape, 0)
        cols = lax.broadcasted_iota(i32, shape, 1)
        return column_of(rows, cols)

    def pick(d, table, like):
        value = jnp.zeros(like, f32)
        for key, scalar in table:
            value = jnp.where(d == key, scalar, value)
        return value

    def inside(grow, total):
        return jnp.logical_and(grow >= 0, grow < total)

    def edge_lane(shape):
        at = lax.broadcasted_iota(i32, shape, 1)
        slot, q, m = at >> 3, (at & 7) >> 1, at & 1
        r = q + 2 + 4 * ((slot >> 1) - 1)
        return r, jnp.where((slot & 1) == 0, m - 2, big + m), at

    def build_encoder():
        em = S.em
        d_main = band((LANES, big), lambda j, J: J - 2 * j)
        r, J, at = edge_lane((16, 48))
        j = lax.broadcasted_iota(i32, (16, 48), 0)
        codes = []
        for start_row in (0, LANES - 16):
            d = J - 2 * (j + start_row)
            codes.append(r * 1024 + d)
        for i in range(2):
            reached = reach[row0 + i]
            edges = [[jnp.zeros((16, 48), f32) for _ in range(2)] for _ in range(nb)]
            for a in range(-2, 3):
                r_in = 2 * i + a + 2
                ok = inside(4 * l + r_in - 2, 2 * s.lat_total)
                masks = [d_main == b for b in range(-2, 3)]
                for kk in range(nb):
                    value = jnp.zeros((LANES, big), f32)
                    for b in range(-2, 3):
                        tap = enc_taps[kk, row0 + i, 5 * (a + 2) + b + 2]
                        tap = jnp.where(jnp.logical_and(ok, abs(b) <= reached), tap, 0.0)
                        value = jnp.where(masks[b + 2], tap, value)
                        for part in range(2):
                            edges[kk][part] = jnp.where(
                                codes[part] == r_in * 1024 + b, tap, edges[kk][part]
                            )
                    em[i, kk * LANES : (kk + 1) * LANES, (a + 2) * big : (a + 3) * big] = value.astype(bf16)
            for kk in range(nb):
                lo = kk * LANES
                em[i, lo : lo + 16, 5 * big :] = edges[kk][0].astype(bf16)
                em[i, lo + 16 : lo + LANES - 16, 5 * big :] = jnp.zeros((LANES - 32, 48), bf16)
                em[i, lo + LANES - 16 : lo + LANES, 5 * big :] = edges[kk][1].astype(bf16)

    def build_decoder():
        dm = S.dm
        d_main = band((LANES, big), lambda j, J: j - (J >> 1))
        r, J, at = edge_lane((16, 48))
        j = lax.broadcasted_iota(i32, (16, 48), 0)
        codes = []
        for start_row in (0, LANES - 16):
            d = (j + start_row) - (J >> 1)
            codes.append(r * 1024 + d)
        for i in range(2):
            edges = [[jnp.zeros((16, 48), f32) for _ in range(2)] for _ in range(nb)]
            for n in range(6):
                r_in = 2 * i + n
                a = i + 1 - r_in // 2
                full = 4 * l + r_in - 2
                ok = inside(full, 2 * s.lat_total)
                full = jnp.clip(full, 0, 2 * s.lat_total - 1)
                reached = reach[full // 2] - 1
                masks = [d_main == b for b in range(-1, 2)]
                for kk in range(nb):
                    value = jnp.zeros((LANES, big), f32)
                    for b in range(-1, 2):
                        tap = dec_taps[kk, full, 3 * (a + 1) + b + 1]
                        tap = jnp.where(jnp.logical_and(ok, abs(b) <= reached), tap, 0.0)
                        value = jnp.where(masks[b + 1], tap, value)
                        for part in range(2):
                            edges[kk][part] = jnp.where(
                                codes[part] == r_in * 1024 + b, tap, edges[kk][part]
                            )
                    dm[i, kk * LANES : (kk + 1) * LANES, n * big : (n + 1) * big] = value.astype(bf16)
            for kk in range(nb):
                lo = kk * LANES
                dm[i, lo : lo + 16, 6 * big :] = edges[kk][0].astype(bf16)
                dm[i, lo + 16 : lo + LANES - 16, 6 * big :] = jnp.zeros((LANES - 32, 48), bf16)
                dm[i, lo + LANES - 16 : lo + LANES, 6 * big :] = edges[kk][1].astype(bf16)

    def build_processor():
        tm = S.tm
        d_main = band((LANES, LANES), lambda j, J: J - j)
        at = lax.broadcasted_iota(i32, (16, 48), 1)
        slot, idx = at >> 3, at & 7
        r = 2 * (slot >> 1) + (idx >> 1)
        m = idx & 1
        J = jnp.where((slot & 1) == 0, m - 2, LANES + m)
        j = lax.broadcasted_iota(i32, (16, 48), 0)
        codes = []
        for start_row in (0, LANES - 16):
            d = J - (j + start_row)
            codes.append(jnp.where(idx < 4, r * 1024 + d, -5000))
        for i in range(2):
            reached = reach[row0 + i]
            edges = [[jnp.zeros((16, 48), f32) for _ in range(2)] for _ in range(nb)]
            for r_in in range(6):
                a = r_in - 2 - i
                if abs(a) > 2:
                    for kk in range(nb):
                        lo = kk * px + i * LANES
                        tm[lo : lo + LANES, r_in * LANES : (r_in + 1) * LANES] = jnp.zeros((LANES, LANES), bf16)
                    continue
                ok = inside(row0 + r_in - 2, s.lat_total)
                masks = [d_main == b for b in range(-2, 3)]
                for kk in range(nb):
                    value = jnp.zeros((LANES, LANES), f32)
                    for b in range(-2, 3):
                        tap = proc_taps[kk, row0 + i, 5 * (a + 2) + b + 2]
                        tap = jnp.where(jnp.logical_and(ok, abs(b) <= reached), tap, 0.0)
                        value = jnp.where(masks[b + 2], tap, value)
                        for part in range(2):
                            edges[kk][part] = jnp.where(
                                codes[part] == r_in * 1024 + b, tap, edges[kk][part]
                            )
                    lo = kk * px + i * LANES
                    tm[lo : lo + LANES, r_in * LANES : (r_in + 1) * LANES] = value.astype(bf16)
            for kk in range(nb):
                lo = kk * px + i * LANES
                tm[lo : lo + 16, 768:816] = edges[kk][0].astype(bf16)
                tm[lo + 16 : lo + LANES - 16, 768:816] = jnp.zeros((LANES - 32, 48), bf16)
                tm[lo + LANES - 16 : lo + LANES, 768:816] = edges[kk][1].astype(bf16)

    slat, slon = S.slat, S.slon

    def fold(values, kind, count):
        total_a, total_b = values[0]
        for a, b in values[1:]:
            total_a = total_a + a
            total_b = total_b + b
        if kind:
            total_a = total_a * (1.0 / len(values))
            for a, b in values:
                total_b = total_b + (a - total_a) * (a - total_a) * count
        return total_a, total_b

    single = s.group <= 16
    sall = S.sall
    place = k.l * s.nz + k.z

    def stat_start(rd, a, b):
        if single:
            sall[rd, place, 0:1, :] = a
            sall[rd, place, 1:2, :] = b
            others = [(0, m, n) for n in range(s.nz) for m in range(s.nl) if m or n]
            return start(
                [Send(k, sall.at[rd, place], sall.at[rd, place], k.at(*o)) for o in others]
            )
        slat[rd, k.l, 0:1, :] = a
        slat[rd, k.l, 1:2, :] = b
        return start(
            [
                Send(k, slat.at[rd, k.l], slat.at[rd, k.l], k.at(0, d, 0))
                for d in range(1, s.nl)
            ]
        )

    def stat_middle(rd, sends, kind):
        if single:
            return sends
        arrive(sends)
        values = [(slat[rd, n, 0:1, :], slat[rd, n, 1:2, :]) for n in range(s.nl)]
        a, b = fold(values, kind, float(px))
        slon[rd, k.z, 0:1, :] = a
        slon[rd, k.z, 1:2, :] = b
        return start(
            [
                Send(k, slon.at[rd, k.z], slon.at[rd, k.z], k.at(0, 0, d))
                for d in range(1, s.nz)
            ]
        )

    def stat_end(rd, sends, kind):
        arrive(sends)
        if single:
            values = [(sall[rd, n, 0:1, :], sall[rd, n, 1:2, :]) for n in range(s.group)]
            return fold(values, kind, float(px))
        values = [(slon[rd, n, 0:1, :], slon[rd, n, 1:2, :]) for n in range(s.nz)]
        return fold(values, kind, float(px * s.nl))

    def moments(values):
        mean = jnp.sum(values, axis=0, keepdims=True) * (1.0 / px)
        centred = values - mean
        return mean, jnp.sum(centred * centred, axis=0, keepdims=True)

    def vec(ref):
        n = ref.shape[0]
        return ref[...].reshape(1, n)

    build_encoder()
    build_decoder()
    build_processor()

    arrive(first_halo)
    def absent(slot):
        return pl.when(jnp.logical_not(k.has_up() if slot < 2 else k.has_down()))

    for slot in (0, 1, 4, 5):
        @absent(slot)
        def _():
            S.eslot[slot] = jnp.zeros((8, 160), f32)

    xe = S.xe
    for slot in range(0, 6, 2):
        pair = jnp.concatenate([S.eslot[slot], S.eslot[slot + 1]], axis=0)
        xe[slot * 8 : slot * 8 + 16, :] = pair.astype(bf16)

    filte, hx = S.filte, S.hx
    for i in range(2):
        em = S.em
        got = nt(em[i, :, 0 : 5 * big], xj[0:80, 2 * i * big : (2 * i + 5) * big])
        got = got + nn(em[i, :, 5 * big :], xe[:, 0:80])
        for kk in range(nb):
            filte[kk, i * LANES : (i + 1) * LANES, :] = got[kk * LANES : (kk + 1) * LANES, 0:cj].astype(bf16)
    for copy in vectors:
        copy.wait()
    loads.ew.wait()
    h0 = vec(eb) + jnp.zeros((px, c), f32)
    for kk in range(nb):
        h0 = h0 + nn(filte[kk], S.ew[kk])
    hx[px : 2 * px, :] = h0
    own = slice(px, 2 * px)
    h0 = hx[own, :]
    stat_a = stat_start(0, *moments(h0))
    pe = S.pe
    for side, col in ((0, 0), (1, LANES - 2)):
        for q in range(2):
            lo = px + q * LANES + col
            pe[side, 2 * q : 2 * q + 2, :] = hx[lo : lo + 2, :]
            pe[side, 4 + 2 * q : 6 + 2 * q, :] = jnp.zeros((2, c), f32)
    sends = [
        Send(k, hx.at[pl.ds(px, px)], hx.at[pl.ds(2 * px, px)], k.at(0, -1, 0), -1),
        Send(k, hx.at[pl.ds(px, px)], hx.at[pl.ds(0, px)], k.at(0, 1, 0), 1),
    ]
    for dl, ds in dirs:
        sends.append(
            Send(
                k,
                pe.at[(ds + 1) // 2],
                hx.at[pl.ds(768 + slot_of(dl, ds) * 8, 8)],
                k.at(0, dl, ds),
                dl,
            )
        )
    zero_halo = start(sends)
    stat_a = stat_middle(0, stat_a, True)

    dm, pgr = S.dm, S.pgr
    for i in range(2):
        got = nt(dm[i, :, 0 : 6 * big], xj[80 : 80 + 80, 2 * i * big : (2 * i + 6) * big])
        got = got + nn(dm[i, :, 6 * big :], xe[:, 80:160])
        for kk in range(nb):
            pgr[kk, i * LANES : (i + 1) * LANES, :] = got[kk * LANES : (kk + 1) * LANES, 0:cin].astype(bf16)
    ones = jnp.ones((16, 4 * big), bf16)
    put_misc(gm, MISC.dec_bias, nt(ones, xj[80:160, 2 * big : 6 * big])[0:1, 0:cin])

    loads.cw.wait()
    two, mg = S.two, S.mg
    acc = nn(pgr[0], S.cw[0])
    for kk in range(1, nb):
        acc = acc + nn(pgr[kk], S.cw[kk])
    two[...] = acc
    mg[...] = acc.astype(bf16)

    mean1, m2 = stat_end(0, stat_a, True)
    var1 = m2 * (1.0 / s.pixels)
    rstd1 = lax.rsqrt(var1 + EPS)
    S.means[0] = mean1 * live
    S.means[1] = var1 * live
    keep(S.means.at[0], m1_h)
    keep(S.means.at[1], v1_h)
    arrive(zero_halo)
    nx = S.nx
    scale1 = rstd1 * vec(gain1)
    bias1 = vec(shift1)

    def norm_rows(n, carry):
        here = pl.ds(pl.multiple_of(n * 48, 16), 48)
        nx[here, :] = ((hx[here, :] - mean1) * scale1 + bias1).astype(bf16)
        return carry

    lax.fori_loop(0, 17, norm_rows, 0)

    filt, tm = S.filt, S.tm
    loads.pw.wait()
    h1 = S.h1
    acc = hx[own, :] + vec(pb)
    for kk in range(nb):
        here = slice(kk * px, (kk + 1) * px)
        filt[here, :] = nn(tm[here, :], nx[...]).astype(bf16)
        acc = acc + nt(filt[here, :], S.pw[kk])
    h1[...] = acc
    stat_b = stat_start(1, *moments(h1[...]))
    stat_b = stat_middle(1, stat_b, True)
    loads.dw.wait()
    ag, hp = S.ag, S.hp
    ag[...] = nn(mg[...], S.dw[...])
    S.mgt[...] = mg[...].T
    put_misc(gm, MISC.down_bias, jnp.sum(mg[...].astype(f32), axis=0, keepdims=True))
    tm_t = S.tmt
    tm_t[...] = tm[...].T
    mean2, m2 = stat_end(1, stat_b, True)
    var2 = m2 * (1.0 / s.pixels)
    rstd2 = lax.rsqrt(var2 + EPS)
    S.means[2] = mean2 * live
    S.means[3] = var2 * live
    keep(S.means.at[2], m2_h)
    keep(S.means.at[3], v2_h)
    scale2 = rstd2 * vec(gain2)
    bias2 = vec(shift2)
    n2 = S.n2

    def norm_two_rows(n, carry):
        here = pl.ds(pl.multiple_of(n * 32, 16), 32)
        n2[here, :] = ((h1[here, :] - mean2) * scale2 + bias2).astype(bf16)
        return carry

    lax.fori_loop(0, px // 32, norm_two_rows, 0)

    loads.uw.wait()
    hp[...] = nn(n2[...], S.uw[...])
    act, hg = S.act, S.hg
    ubias = vec(ub)
    root = 0.7978845608028654

    def gelu_rows(n, carry):
        here = pl.ds(pl.multiple_of(n * 16, 16), 16)
        v = hp[here, :] + ubias
        sq = v * v
        t = jnp.tanh(root * (v + 0.044715 * (sq * v)))
        act[here, :] = (0.5 * v * (1.0 + t)).astype(bf16)
        slope = 0.5 * (1.0 + t) + (0.5 * root) * v * (1.0 - t * t) * (1.0 + (3 * 0.044715) * sq)
        hg[here, :] = (slope * ag[here, :]).astype(bf16)
        return carry

    lax.fori_loop(0, px // 16, gelu_rows, 0)
    g1 = S.g1
    cols = [(lo, min(256, s.c5 * LANES - lo)) for lo in range(0, s.c5 * LANES, 256)]

    def spread(g, off, height, pitch, value, lo, width):
        for n in range(width // LANES):
            at = off + (lo // LANES + n) * pitch
            g[at : at + height, :] = value[:, n * LANES : (n + 1) * LANES].astype(bf16)

    for lo in range(0, s.f10 * LANES, 256):
        spread(g1, 0, c, s.r641, nn(S.mgt[...], act[:, lo : lo + 256]), lo, 256)
    ar("ba")
    S.n2t[...] = n2[...].T
    for lo in range(0, s.f10 * LANES, 256):
        spread(g1, s.off_up, c, s.r641, nn(S.n2t[...], hg[:, lo : lo + 256]), lo, 256)
    h2 = S.h2
    h2[...] = (h1[...] + nt(act[...], S.dw[...]) + vec(db)).astype(bf16)
    for kk in range(nb):
        got = tn(pgr[kk], h2[:, 0 : s.c5 * LANES])
        spread(g1, s.off_dec + kk * s.c5 * s.r80, cin, s.r80, got, 0, s.c5 * LANES)
    ar("bace")
    ntg = S.ntg
    ntg[...] = nt(hg[...], S.uw[...])
    grad = ntg[...]
    standard = (h1[...] - mean2) * rstd2
    sum_a = jnp.sum(grad, axis=0, keepdims=True)
    sum_b = jnp.sum(grad * standard, axis=0, keepdims=True)
    put_misc(gm, MISC.shift_two, sum_a)
    put_misc(gm, MISC.gain_two, sum_b)
    stat_c = stat_start(2, sum_a, sum_b)

    ar("cdfed")
    stat_c = stat_middle(2, stat_c, False)

    def weighted(ref, column):
        return jnp.sum(ref.astype(f32) * column.astype(f32), axis=0, keepdims=True)

    def put_long(slot, row):
        put_misc(gm, slot, row[:, 0:768])
        put_misc(gm, slot + 1, row[:, 768:])

    def misc_one():
        put_long(MISC.up_bias, jnp.sum(hg[...].astype(f32), axis=0, keepdims=True))
        for n in range(2):
            at = s.f10 * LANES + n
            put_misc(gm, MISC.up_last + n, weighted(n2[...], hg[:, at : at + 1]))
            put_misc(gm, MISC.down_last + n, weighted(mg[...], act[:, at : at + 1]))
        for kk in range(nb):
            put_misc(gm, MISC.dec_last + kk, weighted(pgr[kk], h2[:, c - 1 : c]))

    sum_a, sum_b = stat_end(2, stat_c, False)
    ar("fb")
    g_two = vec(gain2)
    part_a = g_two * sum_a * (1.0 / s.pixels)
    part_b = g_two * sum_b * (1.0 / s.pixels)
    one, br = S.one, S.br

    def one_rows(n, carry):
        here = pl.ds(pl.multiple_of(n * 32, 16), 32)
        standard = (h1[here, :] - mean2) * rstd2
        value = rstd2 * (g_two * ntg[here, :] - part_a - standard * part_b) + two[here, :]
        one[here, :] = value
        br[here, :] = value.astype(bf16)
        return carry

    lax.fori_loop(0, px // 32, one_rows, 0)
    ar("a")
    fg = S.fg
    for kk in range(nb):
        fg[kk * px : (kk + 1) * px, :] = nn(br[...], S.pw[kk]).astype(bf16)
    con = S.con
    con[...] = nn(S.tmt[...], fg[...])

    def sum_rows(n, carry):
        here = pl.ds(pl.multiple_of(n * 48, 16), 48)
        value = con[here, :]
        standard = (hx[here, :] - mean1) * rstd1
        return (
            carry[0] + jnp.sum(value, axis=0, keepdims=True),
            carry[1] + jnp.sum(value * standard, axis=0, keepdims=True),
        )

    zero_row = jnp.zeros((1, c), f32)
    sum_a, sum_b = lax.fori_loop(0, 17, sum_rows, (zero_row, zero_row))
    put_misc(gm, MISC.shift_one, sum_a)
    put_misc(gm, MISC.gain_one, sum_b)
    stat_d = stat_start(3, sum_a, sum_b)
    sends = [
        Send(k, con.at[pl.ds(0, px)], S.rdn, k.at(0, -1, 0), -1),
        Send(k, con.at[pl.ds(2 * px, px)], S.rup, k.at(0, 1, 0), 1),
    ]
    for dl, ds in dirs:
        mine = (dl + 1) * 2 + (ds + 1) // 2
        sends.append(
            Send(
                k,
                con.at[pl.ds(768 + mine * 8, 8)],
                S.reg.at[slot_of(dl, ds)],
                k.at(0, dl, ds),
                dl,
            )
        )
    back_halo = start(sends)
    g2 = S.g2
    S.brt[...] = br[...].T
    for kk in range(nb):
        if kk == 1:
            stat_d = stat_middle(3, stat_d, False)
        for lo, width in cols:
            got = nn(S.brt[...], filt[kk * px : (kk + 1) * px, lo : lo + width])
            spread(g2, kk * s.c5 * s.r641, c, s.r641, got, lo, width)
        if kk == 1:
            ar("edgha")
    ar("ijbchg")

    arrive(back_halo)
    ar("ei")
    ng = ntg
    ng[...] = con[own, :]

    @pl.when(k.has_up())
    def _():
        ng[...] = ng[...] + S.rup[...]

    @pl.when(k.has_down())
    def _():
        ng[...] = ng[...] + S.rdn[...]

    def add_edges(sl):
        for ss in (-1, 1):
            got = S.reg.at[(sl + 1) * 2 + (ss + 1) // 2]
            col = 0 if ss == -1 else LANES - 2
            for q in range(2):
                lo = q * LANES + col
                ng[lo : lo + 2, :] = ng[lo : lo + 2, :] + got[2 * q : 2 * q + 2, :]

    add_edges(0)
    pl.when(k.has_up())(lambda: add_edges(-1))
    pl.when(k.has_down())(lambda: add_edges(1))
    sum_a, sum_b = stat_end(3, stat_d, False)
    g_one = vec(gain1)
    part_a1 = g_one * sum_a * (1.0 / s.pixels)
    part_b1 = g_one * sum_b * (1.0 / s.pixels)
    zg = S.zg

    def zero_rows(n, carry):
        here = pl.ds(pl.multiple_of(n * 32, 16), 32)
        there = pl.ds(pl.multiple_of(px + n * 32, 16), 32)
        standard = (hx[there, :] - mean1) * rstd1
        value = rstd1 * (g_one * ng[here, :] - part_a1 - standard * part_b1) + one[here, :]
        zg[here, :] = value.astype(bf16)
        return carry

    lax.fori_loop(0, px // 32, zero_rows, 0)
    ar("c")

    g3 = S.g3
    for kk in range(nb):
        got = tn(filte[kk], zg[:, 0 : s.c5 * LANES])
        spread(g3, kk * s.c5 * s.r80, cj, s.r80, got, 0, s.c5 * LANES)
        put_misc(gm, MISC.enc_last + kk, weighted(filte[kk], zg[:, c - 1 : c]))
    put_misc(gm, MISC.enc_bias, jnp.sum(zg[...].astype(f32), axis=0, keepdims=True))
    ar("adj")
    misc_one()
    put_misc(gm, MISC.proc_bias, jnp.sum(br[...].astype(f32), axis=0, keepdims=True))
    for kk in range(nb):
        put_misc(gm, MISC.proc_last + kk, weighted(br[...], filt[kk * px : (kk + 1) * px, c - 1 : c]))
    ar("k")

    projt, partt = S.projt, S.partt
    for kk in range(nb):
        here = slice(kk * LANES, (kk + 1) * LANES)
        proj = nt(h2[...], S.cw[kk])
        part = nt(zg[...], S.ew[kk])[:, 0:cin]
        for i in range(2):
            for ref, value in ((projt, proj), (partt, part)):
                ref[i, 0:cin, here] = value[i * LANES : (i + 1) * LANES, :].T.astype(bf16)
                ref[i, cin:80, here] = jnp.zeros((80 - cin, LANES), bf16)
    sgx = S.sgx
    em = S.em
    sgx[...] = jnp.zeros(sgx.shape, f32)
    for i in range(2):
        lo = 2 * i * big
        got = nn(projt[i], dm[i])
        sgx[0:80, lo : lo + 6 * big] = sgx[0:80, lo : lo + 6 * big] + got[:, 0 : 6 * big]
        sgx[0:80, edge0 : edge0 + 48] = sgx[0:80, edge0 : edge0 + 48] + got[:, 6 * big :]
        got = nn(partt[i], em[i])
        sgx[80:160, lo : lo + 5 * big] = sgx[80:160, lo : lo + 5 * big] + got[:, 0 : 5 * big]
        sgx[80:160, edge0 : edge0 + 48] = sgx[80:160, edge0 : edge0 + 48] + got[:, 5 * big :]
    sgb, sgu, sgd, sge = S.sgb, S.sgu, S.sgd, S.sge
    sgb[:, 0 : 2 * big] = sgx[:, 0 : 2 * big].astype(bf16)
    sgb[:, 2 * big : 4 * big] = sgx[:, 6 * big : 8 * big].astype(bf16)
    turned = sgx[:, edge0:].T
    for n in range(6):
        S.sgn[n] = turned[n * 8 : n * 8 + 8, :]
    sends = [
        Send(k, sgb.at[:, pl.ds(0, 2 * big)], sgd, k.at(0, -1, 0), -1),
        Send(k, sgb.at[:, pl.ds(2 * big, 2 * big)], sgu, k.at(0, 1, 0), 1),
    ]
    for dl, ds in dirs:
        sends.append(
            Send(k, S.sgn.at[(dl + 1) * 2 + (ds + 1) // 2], sge.at[slot_of(dl, ds)], k.at(0, dl, ds), dl)
        )
    out_halo = start(sends)
    ar("fkcbgjaiheldf")
    arrive(out_halo)
    ar("l")
    sgt = S.sgt
    sgt[48:LANES, :] = jnp.zeros((LANES - 48, 160), f32)
    for slot in range(6):
        sgt[slot * 8 : slot * 8 + 8, :] = sge[slot]
    for slot in (0, 1, 4, 5):
        @absent(slot)
        def _():
            sgt[slot * 8 : slot * 8 + 8, :] = jnp.zeros((8, 160), f32)
    arrived = sgt[...].T
    up_one = jnp.where(k.has_up(), 1, 0)
    down_one = jnp.where(k.has_down(), 1, 0)
    cbt = S.cbt
    cbt[...] = jnp.zeros((8, LANES), f32)
    cbt[0:1, 0:cin] = vec(cb)
    bias_col = cbt[...].T[0:cin, 0:1]
    orow, st7 = S.orow, S.st7

    for q in range(4):
        lo = (2 + q) * big
        value = sgx[:, lo : lo + big]
        if q < 2:
            other = sgu[:, q * big : (q + 1) * big].astype(f32)
            value = value + jnp.where(up_one == 1, other, 0.0)
        else:
            other = sgd[:, (q - 2) * big : (q - 1) * big].astype(f32)
            value = value + jnp.where(down_one == 1, other, 0.0)
        head, tail = value[:, 0:LANES], value[:, big - LANES :]
        for sl in (-1, 0, 1):
            for side in range(2):
                at = ((sl + 1) * 2 + side) * 8 + q * 2
                if side == 0:
                    moved = pltpu.roll(arrived, (LANES - at) % LANES, 1)
                    head = head + jnp.where(lane < 2, moved, 0.0)
                else:
                    moved = pltpu.roll(arrived, LANES - 2 - at, 1)
                    tail = tail + jnp.where(lane >= LANES - 2, moved, 0.0)
        orow[:, q, 0:LANES] = (head[0:cin] + bias_col) * live
        orow[:, q, LANES:big] = (tail[0:cin] + bias_col) * live
        st7[k.e, :, q * big : q * big + LANES] = head[80:160].astype(bf16)
        st7[k.e, :, q * big + LANES : (q + 1) * big] = tail[80:160].astype(bf16)
    S.out[0] = orow[...].astype(bf16)
    keep(S.out, out_h)
    def state_piece(slot, half):
        return st7.at[slot, :, pl.ds(half * 2 * big, 2 * big)]

    e_x, e_y = k.flip(0)[0], k.flip(1)[0]
    state_sends = start(
        [
            Send(k, state_piece(k.e, half), state_piece(k.e, half), k.flip(half))
            for half in range(2)
        ]
    )
    ar("ckfgbahefidbgl")
    arrive(state_sends)
    state_sends = start(
        [
            Send(k, state_piece(slot, half), state_piece(slot, half), k.flip(1 - half))
            for half, slots in ((0, (k.e, e_x)), (1, (k.e, e_y)))
            for slot in slots
        ]
    )
    ar("kdhbjgieklhjgckihdjlekdafljiagklhcke")
    arrive(date_sends)
    arrive(state_sends)
    for d in range(s.dates):
        for q in range(4):
            value = jnp.zeros((80, big), f32)
            for n in range(s.ne):
                is_d = jnp.where(S.dates[n, 0:1, :] == float(d), 1.0, 0.0)
                is_d = jnp.concatenate([is_d] * (big // LANES), axis=1)
                value = value + is_d * st7[n, :, q * big : (q + 1) * big].astype(f32)
            orow[:, q, :] = value[0:cin]
        S.sgrad[d] = orow[...].astype(bf16)
    keep(S.sgrad, sgrad_h)

    ar("bfhjiclfgjil")
    while not all(it.finished() for it in reduced.values()):
        ar("abcdefghijklmn")
    for m in pending:
        m.wait_send()
    for copy in finals:
        copy.wait()


def finish_kernel(s, *refs):
    h1, h2, h3, hm_h, output_in, state_in, m1, v1, m2, v2 = refs[:10]
    (
        output, state_grad,
        enc_w, enc_b, g1o, s1o, proc_w, proc_b, g2o, s2o,
        up_w, up_b, down_w, down_b, dec_w, dec_b, m1o, v1o, m2o, v2o,
    ) = refs[10:30]
    (
        b1, b2, b3, enc_v, proc_v, up_v, down_v, dec_v, row_v, hm, out_v, state_v, means_v,
        *vectors, sem_in, sem_out,
    ) = refs[30:]
    c, ff, nb, cin, cj = s.c, s.ff, s.nb, s.cin, s.cj
    used1 = s.off_dec + nb * s.c5 * s.r80
    third = s.c5 * s.r641
    pieces = [(h2, b2, n * third, third) for n in range(nb)]
    pieces += [(h1, b1, 0, s.off_up), (h1, b1, s.off_up, s.off_dec - s.off_up)]
    pieces += [(h1, b1, s.off_dec, used1 - s.off_dec), (h3, b3, 0, nb * s.c5 * s.r80)]
    loads = [
        pltpu.make_async_copy(a.at[pl.ds(at, n)], b.at[pl.ds(at, n)], sem_in.at[i])
        for i, (a, b, at, n) in enumerate(pieces)
    ]
    passed = [(output_in, out_v, output), (state_in, state_v, state_grad)]
    passed += [
        (a, means_v.at[n], b) for n, (a, b) in enumerate(((m1, m1o), (v1, v1o), (m2, m2o), (v2, v2o)))
    ]
    small = pltpu.make_async_copy(hm_h, hm, sem_in.at[len(pieces)])
    small.start()
    for copy in loads:
        copy.start()
    early = [
        pltpu.make_async_copy(a, b, sem_in.at[len(pieces) + 1 + n]) for n, (a, b, _) in enumerate(passed)
    ]
    for copy in early:
        copy.start()
    stores = []

    def store(src, dst):
        copy = pltpu.make_async_copy(src, dst, sem_out.at[len(stores)])
        copy.start()
        stores.append(copy)

    small.wait()
    turned = hm[0:144, :].T

    def last_column(ref, slot, height, at):
        for t in range(-(-height // LANES)):
            n = min(LANES, height - t * LANES)
            ref[t * LANES : t * LANES + n, at : at + 1] = turned[0:n, slot * 6 + t : slot * 6 + t + 1]

    def widen(ref, src, base, pitch, tiles, lo, hi):
        for n in range(tiles):
            at = base + n * pitch
            ref[lo:hi, n * LANES : (n + 1) * LANES] = src[at + lo : at + hi, :].astype(f32)

    last = s.c5 * LANES
    half = up_to(c // 2, 16)
    cuts = (0, half, c)
    for kk in range(nb):
        ref = proc_v.at[kk]
        last_column(ref, MISC.proc_last + kk, c, last)
        loads[kk].wait()
        for lo, hi in zip(cuts, cuts[1:]):
            widen(ref, b2, kk * third, s.r641, s.c5, lo, hi)
            store(ref.at[pl.ds(lo, hi - lo)], proc_w.at[kk, pl.ds(lo, hi - lo)])
    for n, (ref, slot, base, to) in enumerate(
        ((down_v, MISC.down_last, 0, down_w), (up_v, MISC.up_last, s.off_up, up_w))
    ):
        for part in range(2):
            last_column(ref, slot + part, c, s.f10 * LANES + part)
        loads[nb + n].wait()
        for lo, hi in zip(cuts, cuts[1:]):
            widen(ref, b1, base, s.r641, s.f10, lo, hi)
            store(ref.at[pl.ds(lo, hi - lo)], to.at[pl.ds(lo, hi - lo)])
    loads[nb + 2].wait()
    loads[nb + 3].wait()
    for kk in range(nb):
        ref = dec_v.at[kk]
        last_column(ref, MISC.dec_last + kk, cin, last)
        widen(ref, b1, s.off_dec + kk * s.c5 * s.r80, s.r80, s.c5, 0, cin)
        ref = enc_v.at[kk]
        last_column(ref, MISC.enc_last + kk, cj, last)
        widen(ref, b3, kk * s.c5 * s.r80, s.r80, s.c5, 0, cj)
    for copy, (_, there, to) in zip(early, passed):
        copy.wait()
        store(there, to)
    store(dec_v, dec_w)
    store(enc_v, enc_w)

    def flat(ref, slots):
        at = 0
        for slot, width in slots:
            for piece in get_misc(hm, slot, width):
                n = piece.shape[1]
                row_v[0:1, at : at + n] = piece
                at += n
        there = vectors.pop()
        there[...] = row_v[0:1, 0:at].reshape(at)
        store(there, ref)

    for ref, slot in (
        (enc_b, MISC.enc_bias), (g1o, MISC.gain_one), (s1o, MISC.shift_one), (proc_b, MISC.proc_bias),
        (g2o, MISC.gain_two), (s2o, MISC.shift_two), (down_b, MISC.down_bias),
    ):
        flat(ref, [(slot, c)])
    flat(up_b, [(MISC.up_bias, 768), (MISC.up_bias + 1, ff - 768)])
    flat(dec_b, [(MISC.dec_bias, cin)])
    for copy in stores:
        copy.wait()


def per_device(s, *args):
    (
        state, noise, cot, slot_date, lon_reach, enc_taps, proc_taps, dec_taps,
        enc_weight, enc_bias, gain_one, shift_one, proc_weight, proc_bias, gain_two, shift_two,
        up_weight, up_bias, down_weight, down_bias, dec_weight, dec_bias,
    ) = args
    args = list(args)
    args[8] = jnp.swapaxes(enc_weight, 1, 2)
    args[16] = up_weight.T
    vm = pl.BlockSpec(memory_space=pltpu.VMEM)
    sm = pl.BlockSpec(memory_space=pltpu.SMEM)
    hbm = pl.BlockSpec(memory_space=pl.ANY)
    shapes = scratch_list(s)
    names = tuple(shapes)
    in_specs = [hbm] * 3 + [sm] * 5 + [hbm] * 14
    sd = jax.ShapeDtypeStruct
    out_shape = [
        sd((s.rows[0], LANES), bf16),
        sd((s.rows[1], LANES), bf16),
        sd((s.rows[2], LANES), bf16),
        sd((s.rows[3], LANES), f32),
        sd((1, s.cin, s.full_rows, s.full_cols), bf16),
        sd((s.dates, s.cin, s.full_rows, s.full_cols), bf16),
    ] + [sd((1, s.c), f32)] * 4
    got = pl.pallas_call(
        functools.partial(main_kernel, s, names),
        out_shape=out_shape,
        in_specs=in_specs,
        out_specs=[hbm] * 10,
        scratch_shapes=list(shapes.values()),
        compiler_params=pltpu.CompilerParams(
            collective_id=0, has_side_effects=True, vmem_limit_bytes=60 * 2**20
        ),
        name="forecast",
    )(*args)
    c, ff, nb = s.c, s.ff, s.nb
    outs = [out_shape[4], out_shape[5]] + [
        sd((nb, s.cj, c), f32), sd((c,), f32), sd((c,), f32), sd((c,), f32),
        sd((nb, c, c), f32), sd((c,), f32), sd((c,), f32), sd((c,), f32),
        sd((c, ff), f32), sd((ff,), f32), sd((c, ff), f32), sd((c,), f32),
        sd((nb, s.cin, c), f32), sd((s.cin,), f32),
    ] + [sd((1, c), f32)] * 4
    V = pltpu.VMEM
    done = pl.pallas_call(
        functools.partial(finish_kernel, s),
        out_shape=outs,
        in_specs=[hbm] * 10,
        out_specs=[hbm] * len(outs),
        scratch_shapes=[
            V((s.rows[0], LANES), bf16), V((s.rows[1], LANES), bf16), V((s.rows[2], LANES), bf16),
            V((nb, s.cj, c), f32), V((nb, c, c), f32), V((c, ff), f32), V((c, ff), f32),
            V((nb, s.cin, c), f32), V((8, up_to(ff, LANES)), f32), V((s.rows[3], LANES), f32),
            V(out_shape[4].shape, bf16), V(out_shape[5].shape, bf16), V((4, 1, c), f32),
            V((s.cin,), f32), V((ff,), f32), *[V((c,), f32)] * 7,
            pltpu.SemaphoreType.DMA((16,)), pltpu.SemaphoreType.DMA((32,)),
        ],
        compiler_params=pltpu.CompilerParams(vmem_limit_bytes=60 * 2**20),
        name="finish",
    )(*got)
    done = list(done)
    done[2] = jnp.swapaxes(done[2], 1, 2)
    done[10] = done[10].T
    return tuple(done)


def solution(mesh):
    in_specs = (
        P(None, None, "lat", "lon"),
        P("ens", None, "lat", "lon"),
        P("ens", None, "lat", "lon"),
        P("ens"),
    ) + (P(),) * 18
    out_specs = (
        (P("ens", None, "lat", "lon"), P(None, None, "lat", "lon"))
        + (P(),) * 14
        + (P("ens", None),) * 4
    )

    def run(*args):
        s = Sizes(mesh, args[0].shape, args[1].shape, args[5].shape, args[8].shape, args[16].shape)
        return jax.shard_map(
            functools.partial(per_device, s),
            mesh=mesh,
            in_specs=in_specs,
            out_specs=out_specs,
            check_vma=False,
        )(*args)

    return run
```

```python
import functools
import types

import jax
import jax.numpy as jnp
from jax import lax
from jax.experimental import pallas as pl
from jax.experimental.pallas import tpu as pltpu
from jax.sharding import PartitionSpec as P

MESH = pl.DeviceIdType.MESH
f32 = jnp.float32
bf16 = jnp.bfloat16
i32 = jnp.int32
EPS = 1e-05
LANES = 128
AXES = ("ens", "lat", "lon")
BIT0, BIT1, LAT, LON = range(4)
ROUTE_X = (LAT, BIT0, BIT1, LON)
ROUTE_Y = (LAT, BIT1, BIT0, LON)
WSEM, OSEM, SEMS = range(3)
ROUTE_ZX = (LAT, LON, BIT0, BIT1)
ROUTE_ZY = (LAT, LON, BIT1, BIT0)
PIECES = dict(
    a=(0, 0), b=(0, 1), c=(0, 2), d=(1, 0), e=(1, 1), f=(1, 2),
    g=(2, 0), h=(2, 1), i=(3, 0), j=(3, 1), k=(4, 0), l=(5, 0), m=(2, 2), n=(3, 2),
)


def nn(a, b):
    return lax.dot_general(a, b, (((1,), (0,)), ((), ())), preferred_element_type=f32)


def nt(a, b):
    return lax.dot_general(a, b, (((1,), (1,)), ((), ())), preferred_element_type=f32)


def tn(a, b):
    return lax.dot_general(a, b, (((0,), (0,)), ((), ())), preferred_element_type=f32)


def up_to(n, m):
    return -(-n // m) * m


class Sizes:
    def __init__(self, mesh, state, noise, enc_taps, enc_weight, up_weight):
        self.ne, self.nl, self.nz = (mesh.shape[a] for a in AXES)
        self.dates, self.cin, self.full_rows, self.full_cols = state
        self.noise = noise[1]
        self.full_rows = state[2] // self.nl
        self.full_cols = state[3] // self.nz
        self.hr, self.hc = self.full_rows // 2, self.full_cols // 2
        assert self.hr == 2 and self.hc == LANES and self.ne == 4
        self.lat_total = enc_taps[1]
        self.nb = enc_taps[0]
        self.c = enc_weight[1]
        self.cj = enc_weight[2]
        self.ff = up_weight[0]
        self.px = self.hr * self.hc
        self.pixels = float(self.px * self.nl * self.nz)
        self.c5 = self.c // LANES
        self.f10 = self.ff // LANES
        self.r641 = up_to(self.c, 16)
        self.r80 = up_to(self.cj, 16)
        self.off_up = self.f10 * self.r641
        self.off_dec = self.off_up + self.f10 * self.r641
        used = (
            self.off_dec + self.nb * self.c5 * self.r80,
            self.nb * self.c5 * self.r641,
            self.nb * self.c5 * self.r80,
        )
        unit = 16 * self.nl * self.ne * self.nz
        self.rows = tuple(up_to(n, unit) for n in used) + (up_to(24 * 6, unit // 2),)
        self.chunks = {}

        def split(piece, buffer, lo, hi, third, last):
            units = (hi - lo) // unit
            last = last if units >= 3 * last else 0
            first = (units - last + 1) // 2
            at = lo
            for n, (count, route) in enumerate(
                ((first, ROUTE_X), (units - last - first, ROUTE_Y), (last, third))
            ):
                if count:
                    self.chunks[piece, n] = (buffer, at, count * unit, route)
                at += count * unit

        cut = self.off_up // unit * unit
        split(0, 0, 0, cut, ROUTE_ZX, 2)
        split(1, 0, cut, self.rows[0], ROUTE_ZY, 2)
        cut = 2 * self.c5 * self.r641 // unit * unit
        split(2, 1, 0, cut, ROUTE_ZX, 0)
        split(3, 1, cut, self.rows[1], ROUTE_ZY, 0)
        self.chunks[4, 0] = (2, 0, self.rows[2], ROUTE_X)
        self.chunks[5, 0] = (3, 0, self.rows[3], ROUTE_Y)
        self.group = self.nl * self.nz


def add_into(dst, at, sources, count):
    step = next(s for s in (256, 128, 64, 32, 16, 8) if count % s == 0)

    def body(n, carry):
        lo = pl.multiple_of(n * step, 8 if step == 8 else 16)
        there = pl.ds(pl.multiple_of(at + lo, 8 if step == 8 else 16), step)
        value = dst[there, :].astype(f32)
        for source in sources:
            value = value + source[pl.ds(lo, step), :].astype(f32)
        dst[there, :] = value.astype(dst.dtype)
        return carry

    lax.fori_loop(0, count // step, body, 0)


class Links:
    def __init__(self, z, sems=None):
        self.s = z
        self.sems = sems
        self.used = 0
        if sems is not None:
            self.e, self.l, self.z = (lax.axis_index(a) for a in AXES)

    def take(self):
        self.used += 1
        return self.used - 1

    def at(self, de, dl, dz):
        s = self.s
        return (
            lax.rem(self.e + (de + s.ne), s.ne),
            lax.rem(self.l + (dl + s.nl), s.nl),
            lax.rem(self.z + (dz + s.nz), s.nz),
        )

    def bit(self, which):
        return lax.rem(self.e // (1 << which), 2)

    def flip(self, which):
        return (self.e + (1 << which) * (1 - 2 * self.bit(which)), self.l, self.z)

    def has_up(self):
        return self.l > 0

    def has_down(self):
        return self.l < self.s.nl - 1


class Send:
    def __init__(self, links, src, dst, device, dl=0):
        self.links = links
        self.ids = (links.take(), links.take())
        self.what = (src, dst, device)
        self.dl = dl

    def copy(self):
        src, dst, device = self.what
        return pltpu.make_async_remote_copy(
            src_ref=src,
            dst_ref=dst,
            send_sem=self.links.sems.at[self.ids[0]],
            recv_sem=self.links.sems.at[self.ids[1]],
            device_id=device,
            device_id_type=MESH,
        )

    def under(self, sending, act):
        if self.dl == 0:
            act()
        else:
            up = (self.dl < 0) == sending
            pl.when(self.links.has_up() if up else self.links.has_down())(act)

    def start(self):
        self.under(True, lambda: self.copy().start())

    def wait_recv(self):
        self.under(False, lambda: self.copy().wait_recv())

    def wait_send(self):
        self.under(True, lambda: self.copy().wait_send())


class AllReduce:
    def __init__(self, links, partial, total, lo, rows, route, bufs, own_sem):
        self.k, self.g, self.h, self.route = links, partial, total, route
        self.bufs, self.own_sem = bufs, own_sem
        self.sent, self.waiting = [], []
        self.stage = 0
        self.base, self.part = [], []
        base, size = lo, rows
        for axis in route:
            size = size // self.count(links.s, axis)
            self.base.append(base)
            self.part.append(size)
            base = base + self.index(axis) * size
        self.base.append(base)
        self.last_stage = 2 * len(route)

    @staticmethod
    def count(s, axis):
        return {LAT: s.nl, LON: s.nz}.get(axis, 2)

    @staticmethod
    def shapes(s, rows, route, dtype):
        out = []
        for axis in route:
            n = AllReduce.count(s, axis)
            rows = rows // n
            out.append(pltpu.VMEM((n - 1, rows, LANES), dtype))
        return out

    def index(self, axis):
        k = self.k
        return {LAT: k.l, LON: k.z}[axis] if axis in (LAT, LON) else k.bit(axis)

    def others(self, axis):
        k, s = self.k, self.k.s
        if axis == LAT:
            devices = [k.at(0, d, 0) for d in range(1, s.nl)]
            return [(dev, dev[1], n) for n, dev in enumerate(devices)]
        if axis == LON:
            devices = [k.at(0, 0, d) for d in range(1, s.nz)]
            return [(dev, dev[2], n) for n, dev in enumerate(devices)]
        return [(k.flip(axis), 1 - k.bit(axis), 0)]

    def send(self, src, dst, device):
        m = Send(self.k, src, dst, device)
        m.start()
        self.sent.append(m)
        self.waiting.append(m)

    def step(self):
        g, h, route = self.g, self.h, self.route
        al = lambda v: pl.multiple_of(v, 8)
        stage, self.stage = self.stage, self.stage + 1
        for m in self.waiting:
            m.wait_recv()
        self.waiting = []
        depth = len(route)
        if 0 < stage <= depth:
            buf = self.bufs[stage - 1]
            add_into(g, al(self.base[stage]), [buf.at[n] for n in range(buf.shape[0])], self.part[stage - 1])
        if stage < depth:
            size = self.part[stage]
            for device, place, slot in self.others(route[stage]):
                there = pl.ds(al(self.base[stage] + place * size), size)
                self.send(g.at[there], self.bufs[stage].at[slot], device)
        elif stage < 2 * depth:
            level = 2 * depth - 1 - stage
            here = pl.ds(al(self.base[level + 1]), self.part[level])
            if stage == depth:
                self.own = pltpu.make_async_copy(g.at[here], h.at[here], self.own_sem)
                self.own.start()
            if stage == depth + 1:
                self.own.wait()
            source = g if stage == depth else h
            for device, _, _ in self.others(route[level]):
                self.send(source.at[here], h.at[here], device)
        else:
            for m in self.sent:
                m.wait_send()

    def finished(self):
        return self.stage > self.last_stage


class MISC:
    down_bias, up_bias, gain_two, shift_two, proc_bias, gain_one, shift_one, enc_bias = 0, 1, 3, 4, 5, 6, 7, 8
    up_last, down_last, proc_last, enc_last, dec_last, dec_bias = 9, 11, 13, 16, 19, 22


def put_misc(misc, slot, row):
    width = row.shape[1]
    for t in range(-(-width // LANES)):
        lo, hi = t * LANES, min(width, (t + 1) * LANES)
        misc[slot * 6 + t : slot * 6 + t + 1, 0 : hi - lo] = row[:, lo:hi]


def get_misc(misc, slot, width):
    parts = []
    for t in range(-(-width // LANES)):
        lo, hi = t * LANES, min(width, (t + 1) * LANES)
        parts.append(misc[slot * 6 + t : slot * 6 + t + 1, 0 : hi - lo])
    return parts


def scratch_list(s):
    c, ff, px = s.c, s.ff, s.px
    big = s.full_cols
    wide = 8 * big + LANES
    V = pltpu.VMEM
    shapes = dict(
        state=V((s.dates, s.cin, s.full_rows, big), bf16),
        noise=V((1, s.noise, s.full_rows, big), bf16),
        cot=V((1, s.cin, s.full_rows, big), bf16),
        eb_v=V((c,), f32), gain1=V((c,), f32), shift1=V((c,), f32), pb=V((c,), f32), gain2=V((c,), f32),
        shift2=V((c,), f32), ub=V((ff,), f32), db=V((c,), f32), cb=V((s.cin,), f32),
        out=V((1, s.cin, s.full_rows, big), bf16),
        sgrad=V((s.dates, s.cin, s.full_rows, big), bf16),
        means=V((4, 1, c), f32),
        date=pltpu.SMEM((1,), i32), reach=pltpu.SMEM((s.lat_total,), i32),
        enc_taps=pltpu.SMEM((s.nb, s.lat_total, 25), f32), proc_taps=pltpu.SMEM((s.nb, s.lat_total, 25), f32),
        dec_taps=pltpu.SMEM((s.nb, 2 * s.lat_total, 9), f32),
        xin=V((160, s.full_rows, big), f32),
        xj=V((160, 8 * big), bf16),
        eb=V((2, 8, 160), f32),
        eslot=V((6, 8, 160), f32),
        xe=V((48, 160), bf16),
        em=V((2, s.nb * LANES, 5 * big + 48), bf16),
        dm=V((2, s.nb * LANES, 6 * big + 48), bf16),
        tm=V((s.nb * px, 6 * LANES + 48), bf16),
        ew=V((s.nb, s.cj, c), bf16),
        pw=V((s.nb, c, c), bf16),
        uw=V((c, ff), bf16),
        dw=V((c, ff), bf16),
        cw=V((s.nb, s.cin, c), bf16),
        filte=V((s.nb, px, s.cj), bf16),
        hx=V((6 * LANES + 48, c), f32),
        nx=V((6 * LANES + 48, c), bf16),
        pe=V((2, 4, c), f32),
        he=V((6, 4, c), f32),
        ce=V((6, 4, c), f32),
        filt=V((s.nb * px, c), bf16),
        h1=V((px, c), f32),
        n2=V((px, c), bf16),
        hp=V((px, ff), f32),
        ag=V((px, ff), f32),
        act=V((px, ff), bf16),
        hg=V((px, ff), bf16),
        n2t=V((c, px), bf16),
        h2=V((px, c), bf16),
        pgr=V((s.nb, px, s.cin), bf16),
        projt=V((2, 80, s.nb * LANES), bf16),
        partt=V((2, 80, s.nb * LANES), bf16),
        two=V((px, c), f32),
        mg=V((px, c), bf16),
        mgt=V((c, px), bf16),
        ntg=V((px, c), f32),
        one=V((px, c), f32),
        br=V((px, c), bf16),
        brt=V((c, px), bf16),
        fg=V((s.nb * px, c), bf16),
        con=V((6 * LANES + 48, c), f32),
        rup=V((px, c), f32),
        rdn=V((px, c), f32),
        reg=V((6, 4, c), f32),
        zg=V((px, c), bf16),
        sgx=V((160, wide), f32),
        sgb=V((160, 4 * big), bf16),
        sgu=V((160, 2 * big), bf16),
        sgd=V((160, 2 * big), bf16),
        sgn=V((6, 8, 160), f32),
        sge=V((6, 8, 160), f32),
        sgt=V((LANES, 160), f32),
        orow=V((s.cin, s.full_rows, big), f32),
        st7=V((s.ne, 80, 4 * big), bf16),
        dates=V((s.ne, 8, LANES), f32),
        cbt=V((8, LANES), f32),
        slat=V((4, s.nl, 2, c), f32),
        slon=V((4, s.nz, 2, c), f32),
        sall=V((4, s.group if s.group <= 16 else 1, 2, c), f32),
        tmt=V((6 * LANES + 48, s.nb * px), bf16),
        g1=V((s.rows[0], LANES), bf16),
        g2=V((s.rows[1], LANES), bf16),
        g3=V((s.rows[2], LANES), bf16),
        gm=V((s.rows[3], LANES), f32),
    )
    for name, (buffer, _, rows, route) in s.chunks.items():
        kinds = AllReduce.shapes(s, rows, route, f32 if buffer == 3 else bf16)
        for j, kind in enumerate(kinds):
            shapes[name, j] = kind
    shapes[WSEM] = pltpu.SemaphoreType.DMA((28,))
    shapes[OSEM] = pltpu.SemaphoreType.DMA((len(s.chunks),))
    shapes[SEMS] = pltpu.SemaphoreType.DMA((sem_count(s),))
    return shapes


def sem_count(s):
    total = len(s.chunks) * 2 * 2 * (s.nl - 1 + 1 + 1 + s.nz - 1)
    total += 2 * 4 * 8 + 2 * (s.ne - 1) + 2 * 6
    total += 4 * 2 * (s.group - 1 if s.group <= 16 else s.nl - 1 + s.nz - 1)
    return total


def main_kernel(s, names, *refs):
    n_in, n_out = 22, 10
    (
        state_h, noise_h, cot_h, date_h, reach_h, enc_taps_h, proc_taps_h, dec_taps_h,
        ew_h, eb_h, gain1_h, shift1_h, pw_h, pb_h, gain2_h, shift2_h, uw_h, ub_h, dw_h, db_h, cw_h, cb_h,
    ) = refs[:n_in]
    h1o, h2o, h3o, hmo, out_h, sgrad_h, m1_h, v1_h, m2_h, v2_h = refs[n_in : n_in + n_out]
    table = dict(zip(names, refs[n_in + n_out :]))
    S = types.SimpleNamespace(**{n: r for n, r in table.items() if isinstance(n, str)})
    sems = table[SEMS]
    k = Links(s, sems)
    c, ff, px, nb, cin, cj = s.c, s.ff, s.px, s.nb, s.cin, s.cj
    big = s.full_cols
    l = k.l
    row0 = l * s.hr
    edge0 = 8 * big

    offsets = {(d, 0, 0) for d in range(1, s.ne)}
    if s.group <= 16:
        offsets |= {(0, a, b) for a in range(s.nl) for b in range(s.nz)} - {(0, 0, 0)}
    else:
        offsets |= {(0, d, 0) for d in range(1, s.nl)} | {(0, 0, d) for d in range(1, s.nz)}
    offsets |= {(0, a % s.nl, b % s.nz) for a in (1, -1) for b in (1, -1)}
    offsets = sorted(offsets)
    barrier = pltpu.get_barrier_semaphore()
    for o in offsets:
        pl.semaphore_signal(barrier, 1, device_id=k.at(*o), device_id_type=MESH)

    def fetch(n, src, to):
        copy = pltpu.make_async_copy(src, to, table[WSEM].at[n])
        copy.start()
        return copy

    date_ref, reach = S.date, S.reach
    enc_taps, proc_taps, dec_taps = S.enc_taps, S.proc_taps, S.dec_taps
    scalars = [
        fetch(23 + n, *pair)
        for n, pair in enumerate(
            (
                (date_h, date_ref), (reach_h, reach), (enc_taps_h, enc_taps),
                (proc_taps_h, proc_taps), (dec_taps_h, dec_taps),
            )
        )
    ]
    state, noise, cot = S.state, S.noise, S.cot
    fields = [fetch(n, *pair) for n, pair in enumerate(((state_h, state), (noise_h, noise), (cot_h, cot)))]
    eb, gain1, shift1, pb, gain2, shift2 = S.eb_v, S.gain1, S.shift1, S.pb, S.gain2, S.shift2
    ub, db, cb = S.ub, S.db, S.cb
    vectors = [
        fetch(3 + n, *pair)
        for n, pair in enumerate(
            (
                (eb_h, eb), (gain1_h, gain1), (shift1_h, shift1), (pb_h, pb), (gain2_h, gain2),
                (shift2_h, shift2), (ub_h, ub), (db_h, db), (cb_h, cb),
            )
        )
    ]
    loads = types.SimpleNamespace()
    loads.ew, loads.pw, loads.cw, loads.dw, loads.uw = [
        fetch(12 + n, *pair)
        for n, pair in enumerate(
            ((ew_h, S.ew), (pw_h, S.pw), (cw_h, S.cw), (dw_h, S.dw), (uw_h, S.uw))
        )
    ]
    finals = []

    def keep(src, to):
        copy = pltpu.make_async_copy(src, to, table[WSEM].at[17 + len(finals)])
        copy.start()
        finals.append(copy)

    for copy in fields + scalars:
        copy.wait()

    date = date_ref[0]
    live = jnp.where(date >= 0, 1.0, 0.0).astype(f32)
    xin, xj = S.xin, S.xj
    picked = jnp.zeros((cin, s.full_rows, big), f32)
    for d in range(s.dates):
        picked = picked + state[d].astype(f32) * jnp.where(date == d, 1.0, 0.0).astype(f32)
    xin[0:cin] = picked
    xin[cin:cj] = noise[0].astype(f32)
    xin[80 : 80 + cin] = cot[0].astype(f32) * live
    xin[80 + cin : 160] = jnp.zeros((160 - 80 - cin, s.full_rows, big), f32)
    lane = lax.broadcasted_iota(i32, (160, LANES), 1)
    ends = jnp.zeros((160, LANES), f32)
    for q in range(4):
        row = xin[:, q, :]
        xj[:, (2 + q) * big : (3 + q) * big] = row.astype(bf16)
        moved = pltpu.roll(row[:, 0:LANES], q * 2, 1)
        ends = jnp.where((lane >> 1) == q, moved, ends)
        moved = pltpu.roll(row[:, big - LANES : big], q * 2 + 10, 1)
        ends = jnp.where((lane >> 1) == q + 4, moved, ends)
    turned = ends.T
    S.eb[0] = turned[0:8, :]
    S.eb[1] = turned[8:16, :]
    S.dates[k.e] = jnp.full((8, LANES), date.astype(f32), f32)

    @pl.when(jnp.logical_not(k.has_up()))
    def _():
        xj[:, 0 : 2 * big] = jnp.zeros((160, 2 * big), bf16)
        S.hx[0:px] = jnp.zeros((px, c), f32)
        for side in range(2):
            S.he[side] = jnp.zeros((4, c), f32)

    @pl.when(jnp.logical_not(k.has_down()))
    def _():
        xj[:, 6 * big : 8 * big] = jnp.zeros((160, 2 * big), bf16)
        S.hx[2 * px : 3 * px] = jnp.zeros((px, c), f32)
        for side in range(2):
            S.he[4 + side] = jnp.zeros((4, c), f32)

    pl.semaphore_wait(barrier, len(offsets))

    totals = (h1o, h2o, h3o, hmo)
    reduced = {}
    for n, (name, (buffer, lo, rows, route)) in enumerate(s.chunks.items()):
        bufs = [table[name, j] for j in range(len(route))]
        partial = (S.g1, S.g2, S.g3, S.gm)[buffer]
        reduced[name] = AllReduce(k, partial, totals[buffer], lo, rows, route, bufs, table[OSEM].at[n])

    def ar(letters):
        for letter in letters:
            it = reduced.get(PIECES[letter])
            if it is not None and not it.finished():
                it.step()

    pending = []

    def start(sends):
        for m in sends:
            m.start()
        pending.extend(sends)
        return sends

    def arrive(sends):
        for m in sends:
            m.wait_recv()

    dirs = [(dl, ds) for dl in (-1, 0, 1) for ds in (-1, 1)]

    def slot_of(dl, ds):
        return (1 - dl) * 2 + (1 - ds) // 2

    sends = [
        Send(k, xj.at[:, pl.ds(2 * big, 2 * big)], xj.at[:, pl.ds(6 * big, 2 * big)], k.at(0, -1, 0), -1),
        Send(k, xj.at[:, pl.ds(4 * big, 2 * big)], xj.at[:, pl.ds(0, 2 * big)], k.at(0, 1, 0), 1),
    ]
    for dl, ds in dirs:
        sends.append(
            Send(k, S.eb.at[(ds + 1) // 2], S.eslot.at[slot_of(dl, ds)], k.at(0, dl, ds), dl)
        )
    first_halo = start(sends)
    date_sends = start(
        [
            Send(k, S.dates.at[k.e], S.dates.at[k.e], k.at(d, 0, 0))
            for d in range(1, s.ne)
        ]
    )

    gm = S.gm
    gm[0:144] = jnp.zeros((144, LANES), f32)

    def band(shape, column_of):
        rows = lax.broadcasted_iota(i32, shape, 0)
        cols = lax.broadcasted_iota(i32, shape, 1)
        return column_of(rows, cols)

    def pick(d, table, like):
        value = jnp.zeros(like, f32)
        for key, scalar in table:
            value = jnp.where(d == key, scalar, value)
        return value

    def inside(grow, total):
        return jnp.logical_and(grow >= 0, grow < total)

    def edge_lane(shape):
        at = lax.broadcasted_iota(i32, shape, 1)
        slot, q, m = at >> 3, (at & 7) >> 1, at & 1
        r = q + 2 + 4 * ((slot >> 1) - 1)
        return r, jnp.where((slot & 1) == 0, m - 2, big + m), at

    def build_encoder():
        em = S.em
        d_main = band((LANES, big), lambda j, J: J - 2 * j)
        r, J, at = edge_lane((16, 48))
        j = lax.broadcasted_iota(i32, (16, 48), 0)
        codes = []
        for start_row in (0, LANES - 16):
            d = J - 2 * (j + start_row)
            codes.append(r * 1024 + d)
        for i in range(2):
            reached = reach[row0 + i]
            edges = [[jnp.zeros((16, 48), f32) for _ in range(2)] for _ in range(nb)]
            for a in range(-2, 3):
                r_in = 2 * i + a + 2
                ok = inside(4 * l + r_in - 2, 2 * s.lat_total)
                masks = [d_main == b for b in range(-2, 3)]
                for kk in range(nb):
                    value = jnp.zeros((LANES, big), f32)
                    for b in range(-2, 3):
                        tap = enc_taps[kk, row0 + i, 5 * (a + 2) + b + 2]
                        tap = jnp.where(jnp.logical_and(ok, abs(b) <= reached), tap, 0.0)
                        value = jnp.where(masks[b + 2], tap, value)
                        for part in range(2):
                            edges[kk][part] = jnp.where(
                                codes[part] == r_in * 1024 + b, tap, edges[kk][part]
                            )
                    em[i, kk * LANES : (kk + 1) * LANES, (a + 2) * big : (a + 3) * big] = value.astype(bf16)
            for kk in range(nb):
                lo = kk * LANES
                em[i, lo : lo + 16, 5 * big :] = edges[kk][0].astype(bf16)
                em[i, lo + 16 : lo + LANES - 16, 5 * big :] = jnp.zeros((LANES - 32, 48), bf16)
                em[i, lo + LANES - 16 : lo + LANES, 5 * big :] = edges[kk][1].astype(bf16)

    def build_decoder():
        dm = S.dm
        d_main = band((LANES, big), lambda j, J: j - (J >> 1))
        r, J, at = edge_lane((16, 48))
        j = lax.broadcasted_iota(i32, (16, 48), 0)
        codes = []
        for start_row in (0, LANES - 16):
            d = (j + start_row) - (J >> 1)
            codes.append(r * 1024 + d)
        for i in range(2):
            edges = [[jnp.zeros((16, 48), f32) for _ in range(2)] for _ in range(nb)]
            for n in range(6):
                r_in = 2 * i + n
                a = i + 1 - r_in // 2
                full = 4 * l + r_in - 2
                ok = inside(full, 2 * s.lat_total)
                full = jnp.clip(full, 0, 2 * s.lat_total - 1)
                reached = reach[full // 2] - 1
                masks = [d_main == b for b in range(-1, 2)]
                for kk in range(nb):
                    value = jnp.zeros((LANES, big), f32)
                    for b in range(-1, 2):
                        tap = dec_taps[kk, full, 3 * (a + 1) + b + 1]
                        tap = jnp.where(jnp.logical_and(ok, abs(b) <= reached), tap, 0.0)
                        value = jnp.where(masks[b + 1], tap, value)
                        for part in range(2):
                            edges[kk][part] = jnp.where(
                                codes[part] == r_in * 1024 + b, tap, edges[kk][part]
                            )
                    dm[i, kk * LANES : (kk + 1) * LANES, n * big : (n + 1) * big] = value.astype(bf16)
            for kk in range(nb):
                lo = kk * LANES
                dm[i, lo : lo + 16, 6 * big :] = edges[kk][0].astype(bf16)
                dm[i, lo + 16 : lo + LANES - 16, 6 * big :] = jnp.zeros((LANES - 32, 48), bf16)
                dm[i, lo + LANES - 16 : lo + LANES, 6 * big :] = edges[kk][1].astype(bf16)

    def build_processor():
        tm = S.tm
        d_main = band((LANES, LANES), lambda j, J: J - j)
        at = lax.broadcasted_iota(i32, (16, 48), 1)
        slot, idx = at >> 3, at & 7
        r = 2 * (slot >> 1) + (idx >> 1)
        m = idx & 1
        J = jnp.where((slot & 1) == 0, m - 2, LANES + m)
        j = lax.broadcasted_iota(i32, (16, 48), 0)
        codes = []
        for start_row in (0, LANES - 16):
            d = J - (j + start_row)
            codes.append(jnp.where(idx < 4, r * 1024 + d, -5000))
        for i in range(2):
            reached = reach[row0 + i]
            edges = [[jnp.zeros((16, 48), f32) for _ in range(2)] for _ in range(nb)]
            for r_in in range(6):
                a = r_in - 2 - i
                if abs(a) > 2:
                    for kk in range(nb):
                        lo = kk * px + i * LANES
                        tm[lo : lo + LANES, r_in * LANES : (r_in + 1) * LANES] = jnp.zeros((LANES, LANES), bf16)
                    continue
                ok = inside(row0 + r_in - 2, s.lat_total)
                masks = [d_main == b for b in range(-2, 3)]
                for kk in range(nb):
                    value = jnp.zeros((LANES, LANES), f32)
                    for b in range(-2, 3):
                        tap = proc_taps[kk, row0 + i, 5 * (a + 2) + b + 2]
                        tap = jnp.where(jnp.logical_and(ok, abs(b) <= reached), tap, 0.0)
                        value = jnp.where(masks[b + 2], tap, value)
                        for part in range(2):
                            edges[kk][part] = jnp.where(
                                codes[part] == r_in * 1024 + b, tap, edges[kk][part]
                            )
                    lo = kk * px + i * LANES
                    tm[lo : lo + LANES, r_in * LANES : (r_in + 1) * LANES] = value.astype(bf16)
            for kk in range(nb):
                lo = kk * px + i * LANES
                tm[lo : lo + 16, 768:816] = edges[kk][0].astype(bf16)
                tm[lo + 16 : lo + LANES - 16, 768:816] = jnp.zeros((LANES - 32, 48), bf16)
                tm[lo + LANES - 16 : lo + LANES, 768:816] = edges[kk][1].astype(bf16)

    slat, slon = S.slat, S.slon

    def fold(values, kind, count):
        total_a, total_b = values[0]
        for a, b in values[1:]:
            total_a = total_a + a
            total_b = total_b + b
        if kind:
            total_a = total_a * (1.0 / len(values))
            for a, b in values:
                total_b = total_b + (a - total_a) * (a - total_a) * count
        return total_a, total_b

    single = s.group <= 16
    sall = S.sall
    place = k.l * s.nz + k.z

    def stat_start(rd, a, b):
        if single:
            sall[rd, place, 0:1, :] = a
            sall[rd, place, 1:2, :] = b
            others = [(0, m, n) for n in range(s.nz) for m in range(s.nl) if m or n]
            return start(
                [Send(k, sall.at[rd, place], sall.at[rd, place], k.at(*o)) for o in others]
            )
        slat[rd, k.l, 0:1, :] = a
        slat[rd, k.l, 1:2, :] = b
        return start(
            [
                Send(k, slat.at[rd, k.l], slat.at[rd, k.l], k.at(0, d, 0))
                for d in range(1, s.nl)
            ]
        )

    def stat_middle(rd, sends, kind):
        if single:
            return sends
        arrive(sends)
        values = [(slat[rd, n, 0:1, :], slat[rd, n, 1:2, :]) for n in range(s.nl)]
        a, b = fold(values, kind, float(px))
        slon[rd, k.z, 0:1, :] = a
        slon[rd, k.z, 1:2, :] = b
        return start(
            [
                Send(k, slon.at[rd, k.z], slon.at[rd, k.z], k.at(0, 0, d))
                for d in range(1, s.nz)
            ]
        )

    def stat_end(rd, sends, kind):
        arrive(sends)
        if single:
            values = [(sall[rd, n, 0:1, :], sall[rd, n, 1:2, :]) for n in range(s.group)]
            return fold(values, kind, float(px))
        values = [(slon[rd, n, 0:1, :], slon[rd, n, 1:2, :]) for n in range(s.nz)]
        return fold(values, kind, float(px * s.nl))

    def moments(values):
        mean = jnp.sum(values, axis=0, keepdims=True) * (1.0 / px)
        centred = values - mean
        return mean, jnp.sum(centred * centred, axis=0, keepdims=True)

    def vec(ref):
        n = ref.shape[0]
        return ref[...].reshape(1, n)

    build_encoder()
    build_decoder()
    build_processor()

    arrive(first_halo)
    def absent(slot):
        return pl.when(jnp.logical_not(k.has_up() if slot < 2 else k.has_down()))

    for slot in (0, 1, 4, 5):
        @absent(slot)
        def _():
            S.eslot[slot] = jnp.zeros((8, 160), f32)

    xe = S.xe
    for slot in range(0, 6, 2):
        pair = jnp.concatenate([S.eslot[slot], S.eslot[slot + 1]], axis=0)
        xe[slot * 8 : slot * 8 + 16, :] = pair.astype(bf16)

    filte, hx = S.filte, S.hx
    for i in range(2):
        em = S.em
        got = nt(em[i, :, 0 : 5 * big], xj[0:80, 2 * i * big : (2 * i + 5) * big])
        got = got + nn(em[i, :, 5 * big :], xe[:, 0:80])
        for kk in range(nb):
            filte[kk, i * LANES : (i + 1) * LANES, :] = got[kk * LANES : (kk + 1) * LANES, 0:cj].astype(bf16)
    for copy in vectors:
        copy.wait()
    loads.ew.wait()
    h0 = vec(eb) + jnp.zeros((px, c), f32)
    for kk in range(nb):
        h0 = h0 + nn(filte[kk], S.ew[kk])
    hx[px : 2 * px, :] = h0
    own = slice(px, 2 * px)
    h0 = hx[own, :]
    stat_a = stat_start(0, *moments(h0))
    pe = S.pe
    for side, col in ((0, 0), (1, LANES - 2)):
        for q in range(2):
            lo = px + q * LANES + col
            pe[side, 2 * q : 2 * q + 2, :] = hx[lo : lo + 2, :]
    sends = [
        Send(k, hx.at[pl.ds(px, px)], hx.at[pl.ds(2 * px, px)], k.at(0, -1, 0), -1),
        Send(k, hx.at[pl.ds(px, px)], hx.at[pl.ds(0, px)], k.at(0, 1, 0), 1),
    ]
    for dl, ds in dirs:
        sends.append(
            Send(
                k,
                pe.at[(ds + 1) // 2],
                S.he.at[slot_of(dl, ds)],
                k.at(0, dl, ds),
                dl,
            )
        )
    zero_halo = start(sends)
    stat_a = stat_middle(0, stat_a, True)

    dm, pgr = S.dm, S.pgr
    for i in range(2):
        got = nt(dm[i, :, 0 : 6 * big], xj[80 : 80 + 80, 2 * i * big : (2 * i + 6) * big])
        got = got + nn(dm[i, :, 6 * big :], xe[:, 80:160])
        for kk in range(nb):
            pgr[kk, i * LANES : (i + 1) * LANES, :] = got[kk * LANES : (kk + 1) * LANES, 0:cin].astype(bf16)
    ones = jnp.ones((16, 4 * big), bf16)
    put_misc(gm, MISC.dec_bias, nt(ones, xj[80:160, 2 * big : 6 * big])[0:1, 0:cin])

    loads.cw.wait()
    two, mg = S.two, S.mg
    acc = nn(pgr[0], S.cw[0])
    for kk in range(1, nb):
        acc = acc + nn(pgr[kk], S.cw[kk])
    two[...] = acc
    mg[...] = acc.astype(bf16)

    mean1, m2 = stat_end(0, stat_a, True)
    var1 = m2 * (1.0 / s.pixels)
    rstd1 = lax.rsqrt(var1 + EPS)
    S.means[0] = mean1 * live
    S.means[1] = var1 * live
    keep(S.means.at[0], m1_h)
    keep(S.means.at[1], v1_h)
    arrive(zero_halo)
    for slot in range(6):
        lo = 768 + slot * 8
        hx[lo : lo + 8, :] = jnp.concatenate([S.he[slot], jnp.zeros((4, c), f32)], axis=0)
    nx = S.nx
    scale1 = rstd1 * vec(gain1)
    bias1 = vec(shift1)

    def norm_rows(n, carry):
        here = pl.ds(pl.multiple_of(n * 48, 16), 48)
        nx[here, :] = ((hx[here, :] - mean1) * scale1 + bias1).astype(bf16)
        return carry

    lax.fori_loop(0, 17, norm_rows, 0)

    filt, tm = S.filt, S.tm
    loads.pw.wait()
    h1 = S.h1
    acc = hx[own, :] + vec(pb)
    for kk in range(nb):
        here = slice(kk * px, (kk + 1) * px)
        filt[here, :] = nn(tm[here, :], nx[...]).astype(bf16)
        acc = acc + nt(filt[here, :], S.pw[kk])
    h1[...] = acc
    stat_b = stat_start(1, *moments(h1[...]))
    stat_b = stat_middle(1, stat_b, True)
    loads.dw.wait()
    ag, hp = S.ag, S.hp
    ag[...] = nn(mg[...], S.dw[...])
    S.mgt[...] = mg[...].T
    put_misc(gm, MISC.down_bias, jnp.sum(mg[...].astype(f32), axis=0, keepdims=True))
    tm_t = S.tmt
    tm_t[...] = tm[...].T
    mean2, m2 = stat_end(1, stat_b, True)
    var2 = m2 * (1.0 / s.pixels)
    rstd2 = lax.rsqrt(var2 + EPS)
    S.means[2] = mean2 * live
    S.means[3] = var2 * live
    keep(S.means.at[2], m2_h)
    keep(S.means.at[3], v2_h)
    scale2 = rstd2 * vec(gain2)
    bias2 = vec(shift2)
    n2 = S.n2

    def norm_two_rows(n, carry):
        here = pl.ds(pl.multiple_of(n * 32, 16), 32)
        n2[here, :] = ((h1[here, :] - mean2) * scale2 + bias2).astype(bf16)
        return carry

    lax.fori_loop(0, px // 32, norm_two_rows, 0)

    loads.uw.wait()
    hp[...] = nn(n2[...], S.uw[...])
    act, hg = S.act, S.hg
    ubias = vec(ub)
    root = 0.7978845608028654

    def gelu_rows(n, carry):
        here = pl.ds(pl.multiple_of(n * 16, 16), 16)
        v = hp[here, :] + ubias
        sq = v * v
        t = jnp.tanh(root * (v + 0.044715 * (sq * v)))
        act[here, :] = (0.5 * v * (1.0 + t)).astype(bf16)
        slope = 0.5 * (1.0 + t) + (0.5 * root) * v * (1.0 - t * t) * (1.0 + (3 * 0.044715) * sq)
        hg[here, :] = (slope * ag[here, :]).astype(bf16)
        return carry

    lax.fori_loop(0, px // 16, gelu_rows, 0)
    g1 = S.g1
    cols = [(lo, min(256, s.c5 * LANES - lo)) for lo in range(0, s.c5 * LANES, 256)]

    def spread(g, off, height, pitch, value, lo, width):
        for n in range(width // LANES):
            at = off + (lo // LANES + n) * pitch
            g[at : at + height, :] = value[:, n * LANES : (n + 1) * LANES].astype(bf16)

    for lo in range(0, s.f10 * LANES, 256):
        spread(g1, 0, c, s.r641, nn(S.mgt[...], act[:, lo : lo + 256]), lo, 256)
    ar("ba")
    S.n2t[...] = n2[...].T
    for lo in range(0, s.f10 * LANES, 256):
        spread(g1, s.off_up, c, s.r641, nn(S.n2t[...], hg[:, lo : lo + 256]), lo, 256)
    h2 = S.h2
    h2[...] = (h1[...] + nt(act[...], S.dw[...]) + vec(db)).astype(bf16)
    for kk in range(nb):
        got = tn(pgr[kk], h2[:, 0 : s.c5 * LANES])
        spread(g1, s.off_dec + kk * s.c5 * s.r80, cin, s.r80, got, 0, s.c5 * LANES)
    ar("bace")
    ntg = S.ntg
    ntg[...] = nt(hg[...], S.uw[...])
    grad = ntg[...]
    standard = (h1[...] - mean2) * rstd2
    sum_a = jnp.sum(grad, axis=0, keepdims=True)
    sum_b = jnp.sum(grad * standard, axis=0, keepdims=True)
    put_misc(gm, MISC.shift_two, sum_a)
    put_misc(gm, MISC.gain_two, sum_b)
    stat_c = stat_start(2, sum_a, sum_b)

    ar("cdfed")
    stat_c = stat_middle(2, stat_c, False)

    def weighted(ref, column):
        return jnp.sum(ref.astype(f32) * column.astype(f32), axis=0, keepdims=True)

    def put_long(slot, row):
        put_misc(gm, slot, row[:, 0:768])
        put_misc(gm, slot + 1, row[:, 768:])

    def misc_one():
        put_long(MISC.up_bias, jnp.sum(hg[...].astype(f32), axis=0, keepdims=True))
        for n in range(2):
            at = s.f10 * LANES + n
            put_misc(gm, MISC.up_last + n, weighted(n2[...], hg[:, at : at + 1]))
            put_misc(gm, MISC.down_last + n, weighted(mg[...], act[:, at : at + 1]))
        for kk in range(nb):
            put_misc(gm, MISC.dec_last + kk, weighted(pgr[kk], h2[:, c - 1 : c]))

    sum_a, sum_b = stat_end(2, stat_c, False)
    ar("fb")
    g_two = vec(gain2)
    part_a = g_two * sum_a * (1.0 / s.pixels)
    part_b = g_two * sum_b * (1.0 / s.pixels)
    one, br = S.one, S.br

    def one_rows(n, carry):
        here = pl.ds(pl.multiple_of(n * 32, 16), 32)
        standard = (h1[here, :] - mean2) * rstd2
        value = rstd2 * (g_two * ntg[here, :] - part_a - standard * part_b) + two[here, :]
        one[here, :] = value
        br[here, :] = value.astype(bf16)
        return carry

    lax.fori_loop(0, px // 32, one_rows, 0)
    ar("a")
    fg = S.fg
    for kk in range(nb):
        fg[kk * px : (kk + 1) * px, :] = nn(br[...], S.pw[kk]).astype(bf16)
    con = S.con
    con[...] = nn(S.tmt[...], fg[...])

    def sum_rows(n, carry):
        here = pl.ds(pl.multiple_of(n * 48, 16), 48)
        value = con[here, :]
        standard = (hx[here, :] - mean1) * rstd1
        return (
            carry[0] + jnp.sum(value, axis=0, keepdims=True),
            carry[1] + jnp.sum(value * standard, axis=0, keepdims=True),
        )

    zero_row = jnp.zeros((1, c), f32)
    sum_a, sum_b = lax.fori_loop(0, 17, sum_rows, (zero_row, zero_row))
    put_misc(gm, MISC.shift_one, sum_a)
    put_misc(gm, MISC.gain_one, sum_b)
    stat_d = stat_start(3, sum_a, sum_b)
    for slot in range(6):
        S.ce[slot] = con[768 + slot * 8 : 772 + slot * 8, :]
    sends = [
        Send(k, con.at[pl.ds(0, px)], S.rdn, k.at(0, -1, 0), -1),
        Send(k, con.at[pl.ds(2 * px, px)], S.rup, k.at(0, 1, 0), 1),
    ]
    for dl, ds in dirs:
        mine = (dl + 1) * 2 + (ds + 1) // 2
        sends.append(
            Send(
                k,
                S.ce.at[mine],
                S.reg.at[slot_of(dl, ds)],
                k.at(0, dl, ds),
                dl,
            )
        )
    back_halo = start(sends)
    g2 = S.g2
    S.brt[...] = br[...].T
    for kk in range(nb):
        if kk == 1:
            stat_d = stat_middle(3, stat_d, False)
        for lo, width in cols:
            got = nn(S.brt[...], filt[kk * px : (kk + 1) * px, lo : lo + width])
            spread(g2, kk * s.c5 * s.r641, c, s.r641, got, lo, width)
        if kk == 1:
            ar("edgha")
    ar("ijbchg")

    arrive(back_halo)
    ar("ei")
    ng = ntg
    ng[...] = con[own, :]

    @pl.when(k.has_up())
    def _():
        ng[...] = ng[...] + S.rup[...]

    @pl.when(k.has_down())
    def _():
        ng[...] = ng[...] + S.rdn[...]

    def add_edges(sl):
        for ss in (-1, 1):
            got = S.reg.at[(sl + 1) * 2 + (ss + 1) // 2]
            col = 0 if ss == -1 else LANES - 2
            for q in range(2):
                lo = q * LANES + col
                ng[lo : lo + 2, :] = ng[lo : lo + 2, :] + got[2 * q : 2 * q + 2, :]

    add_edges(0)
    pl.when(k.has_up())(lambda: add_edges(-1))
    pl.when(k.has_down())(lambda: add_edges(1))
    sum_a, sum_b = stat_end(3, stat_d, False)
    g_one = vec(gain1)
    part_a1 = g_one * sum_a * (1.0 / s.pixels)
    part_b1 = g_one * sum_b * (1.0 / s.pixels)
    zg = S.zg

    def zero_rows(n, carry):
        here = pl.ds(pl.multiple_of(n * 32, 16), 32)
        there = pl.ds(pl.multiple_of(px + n * 32, 16), 32)
        standard = (hx[there, :] - mean1) * rstd1
        value = rstd1 * (g_one * ng[here, :] - part_a1 - standard * part_b1) + one[here, :]
        zg[here, :] = value.astype(bf16)
        return carry

    lax.fori_loop(0, px // 32, zero_rows, 0)
    ar("c")

    g3 = S.g3
    for kk in range(nb):
        got = tn(filte[kk], zg[:, 0 : s.c5 * LANES])
        spread(g3, kk * s.c5 * s.r80, cj, s.r80, got, 0, s.c5 * LANES)
        put_misc(gm, MISC.enc_last + kk, weighted(filte[kk], zg[:, c - 1 : c]))
    put_misc(gm, MISC.enc_bias, jnp.sum(zg[...].astype(f32), axis=0, keepdims=True))
    ar("adj")
    misc_one()
    put_misc(gm, MISC.proc_bias, jnp.sum(br[...].astype(f32), axis=0, keepdims=True))
    for kk in range(nb):
        put_misc(gm, MISC.proc_last + kk, weighted(br[...], filt[kk * px : (kk + 1) * px, c - 1 : c]))
    ar("k")

    projt, partt = S.projt, S.partt
    for kk in range(nb):
        here = slice(kk * LANES, (kk + 1) * LANES)
        proj = nt(h2[...], S.cw[kk])
        part = nt(zg[...], S.ew[kk])[:, 0:cin]
        for i in range(2):
            for ref, value in ((projt, proj), (partt, part)):
                ref[i, 0:cin, here] = value[i * LANES : (i + 1) * LANES, :].T.astype(bf16)
                ref[i, cin:80, here] = jnp.zeros((80 - cin, LANES), bf16)
    sgx = S.sgx
    em = S.em
    sgx[...] = jnp.zeros(sgx.shape, f32)
    for i in range(2):
        lo = 2 * i * big
        got = nn(projt[i], dm[i])
        sgx[0:80, lo : lo + 6 * big] = sgx[0:80, lo : lo + 6 * big] + got[:, 0 : 6 * big]
        sgx[0:80, edge0 : edge0 + 48] = sgx[0:80, edge0 : edge0 + 48] + got[:, 6 * big :]
        got = nn(partt[i], em[i])
        sgx[80:160, lo : lo + 5 * big] = sgx[80:160, lo : lo + 5 * big] + got[:, 0 : 5 * big]
        sgx[80:160, edge0 : edge0 + 48] = sgx[80:160, edge0 : edge0 + 48] + got[:, 5 * big :]
    sgb, sgu, sgd, sge = S.sgb, S.sgu, S.sgd, S.sge
    sgb[:, 0 : 2 * big] = sgx[:, 0 : 2 * big].astype(bf16)
    sgb[:, 2 * big : 4 * big] = sgx[:, 6 * big : 8 * big].astype(bf16)
    turned = sgx[:, edge0:].T
    for n in range(6):
        S.sgn[n] = turned[n * 8 : n * 8 + 8, :]
    sends = [
        Send(k, sgb.at[:, pl.ds(0, 2 * big)], sgd, k.at(0, -1, 0), -1),
        Send(k, sgb.at[:, pl.ds(2 * big, 2 * big)], sgu, k.at(0, 1, 0), 1),
    ]
    for dl, ds in dirs:
        sends.append(
            Send(k, S.sgn.at[(dl + 1) * 2 + (ds + 1) // 2], sge.at[slot_of(dl, ds)], k.at(0, dl, ds), dl)
        )
    out_halo = start(sends)
    ar("fkcbgjaiheldf")
    arrive(out_halo)
    ar("l")
    sgt = S.sgt
    sgt[48:LANES, :] = jnp.zeros((LANES - 48, 160), f32)
    for slot in range(6):
        sgt[slot * 8 : slot * 8 + 8, :] = sge[slot]
    for slot in (0, 1, 4, 5):
        @absent(slot)
        def _():
            sgt[slot * 8 : slot * 8 + 8, :] = jnp.zeros((8, 160), f32)
    arrived = sgt[...].T
    up_one = jnp.where(k.has_up(), 1, 0)
    down_one = jnp.where(k.has_down(), 1, 0)
    cbt = S.cbt
    cbt[...] = jnp.zeros((8, LANES), f32)
    cbt[0:1, 0:cin] = vec(cb)
    bias_col = cbt[...].T[0:cin, 0:1]
    orow, st7 = S.orow, S.st7

    for q in range(4):
        lo = (2 + q) * big
        value = sgx[:, lo : lo + big]
        if q < 2:
            other = sgu[:, q * big : (q + 1) * big].astype(f32)
            value = value + jnp.where(up_one == 1, other, 0.0)
        else:
            other = sgd[:, (q - 2) * big : (q - 1) * big].astype(f32)
            value = value + jnp.where(down_one == 1, other, 0.0)
        head, tail = value[:, 0:LANES], value[:, big - LANES :]
        for sl in (-1, 0, 1):
            for side in range(2):
                at = ((sl + 1) * 2 + side) * 8 + q * 2
                if side == 0:
                    moved = pltpu.roll(arrived, (LANES - at) % LANES, 1)
                    head = head + jnp.where(lane < 2, moved, 0.0)
                else:
                    moved = pltpu.roll(arrived, LANES - 2 - at, 1)
                    tail = tail + jnp.where(lane >= LANES - 2, moved, 0.0)
        orow[:, q, 0:LANES] = (head[0:cin] + bias_col) * live
        orow[:, q, LANES:big] = (tail[0:cin] + bias_col) * live
        st7[k.e, :, q * big : q * big + LANES] = head[80:160].astype(bf16)
        st7[k.e, :, q * big + LANES : (q + 1) * big] = tail[80:160].astype(bf16)
    S.out[0] = orow[...].astype(bf16)
    keep(S.out, out_h)
    def state_piece(slot, half):
        return st7.at[slot, :, pl.ds(half * 2 * big, 2 * big)]

    e_x, e_y = k.flip(0)[0], k.flip(1)[0]
    state_sends = start(
        [
            Send(k, state_piece(k.e, half), state_piece(k.e, half), k.flip(half))
            for half in range(2)
        ]
    )
    ar("ckfgbahefidbgl")
    arrive(state_sends)
    state_sends = start(
        [
            Send(k, state_piece(slot, half), state_piece(slot, half), k.flip(1 - half))
            for half, slots in ((0, (k.e, e_x)), (1, (k.e, e_y)))
            for slot in slots
        ]
    )
    ar("kdhbjgieklhjgckihdjlekdafljiagklhcke")
    arrive(date_sends)
    arrive(state_sends)
    for d in range(s.dates):
        for q in range(4):
            value = jnp.zeros((80, big), f32)
            for n in range(s.ne):
                is_d = jnp.where(S.dates[n, 0:1, :] == float(d), 1.0, 0.0)
                is_d = jnp.concatenate([is_d] * (big // LANES), axis=1)
                value = value + is_d * st7[n, :, q * big : (q + 1) * big].astype(f32)
            orow[:, q, :] = value[0:cin]
        S.sgrad[d] = orow[...].astype(bf16)
    keep(S.sgrad, sgrad_h)

    ar("bfhjiclfgjil")
    while not all(it.finished() for it in reduced.values()):
        ar("abcdefghijklmn")
    for m in pending:
        m.wait_send()
    for copy in finals:
        copy.wait()


def finish_kernel(s, *refs):
    h1, h2, h3, hm_h, output_in, state_in, m1, v1, m2, v2 = refs[:10]
    (
        output, state_grad,
        enc_w, enc_b, g1o, s1o, proc_w, proc_b, g2o, s2o,
        up_w, up_b, down_w, down_b, dec_w, dec_b, m1o, v1o, m2o, v2o,
    ) = refs[10:30]
    (
        b1, b2, b3, enc_v, proc_v, up_v, down_v, dec_v, row_v, hm, out_v, state_v, means_v,
        *vectors, sem_in, sem_out,
    ) = refs[30:]
    c, ff, nb, cin, cj = s.c, s.ff, s.nb, s.cin, s.cj
    used1 = s.off_dec + nb * s.c5 * s.r80
    third = s.c5 * s.r641
    pieces = [(h2, b2, n * third, third) for n in range(nb)]
    pieces += [(h1, b1, 0, s.off_up), (h1, b1, s.off_up, s.off_dec - s.off_up)]
    pieces += [(h1, b1, s.off_dec, used1 - s.off_dec), (h3, b3, 0, nb * s.c5 * s.r80)]
    loads = [
        pltpu.make_async_copy(a.at[pl.ds(at, n)], b.at[pl.ds(at, n)], sem_in.at[i])
        for i, (a, b, at, n) in enumerate(pieces)
    ]
    passed = [(output_in, out_v, output), (state_in, state_v, state_grad)]
    passed += [
        (a, means_v.at[n], b) for n, (a, b) in enumerate(((m1, m1o), (v1, v1o), (m2, m2o), (v2, v2o)))
    ]
    small = pltpu.make_async_copy(hm_h, hm, sem_in.at[len(pieces)])
    small.start()
    for copy in loads:
        copy.start()
    early = [
        pltpu.make_async_copy(a, b, sem_in.at[len(pieces) + 1 + n]) for n, (a, b, _) in enumerate(passed)
    ]
    for copy in early:
        copy.start()
    stores = []

    def store(src, dst):
        copy = pltpu.make_async_copy(src, dst, sem_out.at[len(stores)])
        copy.start()
        stores.append(copy)

    small.wait()
    turned = hm[0:144, :].T

    def last_column(ref, slot, height, at):
        for t in range(-(-height // LANES)):
            n = min(LANES, height - t * LANES)
            ref[t * LANES : t * LANES + n, at : at + 1] = turned[0:n, slot * 6 + t : slot * 6 + t + 1]

    def widen(ref, src, base, pitch, tiles, lo, hi):
        for n in range(tiles):
            at = base + n * pitch
            ref[lo:hi, n * LANES : (n + 1) * LANES] = src[at + lo : at + hi, :].astype(f32)

    last = s.c5 * LANES
    half = up_to(c // 2, 16)
    cuts = (0, half, c)
    for kk in range(nb):
        ref = proc_v.at[kk]
        last_column(ref, MISC.proc_last + kk, c, last)
        loads[kk].wait()
        for lo, hi in zip(cuts, cuts[1:]):
            widen(ref, b2, kk * third, s.r641, s.c5, lo, hi)
            store(ref.at[pl.ds(lo, hi - lo)], proc_w.at[kk, pl.ds(lo, hi - lo)])
    for n, (ref, slot, base, to) in enumerate(
        ((down_v, MISC.down_last, 0, down_w), (up_v, MISC.up_last, s.off_up, up_w))
    ):
        for part in range(2):
            last_column(ref, slot + part, c, s.f10 * LANES + part)
        loads[nb + n].wait()
        for lo, hi in zip(cuts, cuts[1:]):
            widen(ref, b1, base, s.r641, s.f10, lo, hi)
            store(ref.at[pl.ds(lo, hi - lo)], to.at[pl.ds(lo, hi - lo)])
    loads[nb + 2].wait()
    loads[nb + 3].wait()
    for kk in range(nb):
        ref = dec_v.at[kk]
        last_column(ref, MISC.dec_last + kk, cin, last)
        widen(ref, b1, s.off_dec + kk * s.c5 * s.r80, s.r80, s.c5, 0, cin)
        ref = enc_v.at[kk]
        last_column(ref, MISC.enc_last + kk, cj, last)
        widen(ref, b3, kk * s.c5 * s.r80, s.r80, s.c5, 0, cj)
    for copy, (_, there, to) in zip(early, passed):
        copy.wait()
        store(there, to)
    store(dec_v, dec_w)
    store(enc_v, enc_w)

    def flat(ref, slots):
        at = 0
        for slot, width in slots:
            for piece in get_misc(hm, slot, width):
                n = piece.shape[1]
                row_v[0:1, at : at + n] = piece
                at += n
        there = vectors.pop()
        there[...] = row_v[0:1, 0:at].reshape(at)
        store(there, ref)

    for ref, slot in (
        (enc_b, MISC.enc_bias), (g1o, MISC.gain_one), (s1o, MISC.shift_one), (proc_b, MISC.proc_bias),
        (g2o, MISC.gain_two), (s2o, MISC.shift_two), (down_b, MISC.down_bias),
    ):
        flat(ref, [(slot, c)])
    flat(up_b, [(MISC.up_bias, 768), (MISC.up_bias + 1, ff - 768)])
    flat(dec_b, [(MISC.dec_bias, cin)])
    for copy in stores:
        copy.wait()


def per_device(s, *args):
    (
        state, noise, cot, slot_date, lon_reach, enc_taps, proc_taps, dec_taps,
        enc_weight, enc_bias, gain_one, shift_one, proc_weight, proc_bias, gain_two, shift_two,
        up_weight, up_bias, down_weight, down_bias, dec_weight, dec_bias,
    ) = args
    args = list(args)
    args[8] = jnp.swapaxes(enc_weight, 1, 2)
    args[16] = up_weight.T
    vm = pl.BlockSpec(memory_space=pltpu.VMEM)
    sm = pl.BlockSpec(memory_space=pltpu.SMEM)
    hbm = pl.BlockSpec(memory_space=pl.ANY)
    shapes = scratch_list(s)
    names = tuple(shapes)
    in_specs = [hbm] * 22
    sd = jax.ShapeDtypeStruct
    out_shape = [
        sd((s.rows[0], LANES), bf16),
        sd((s.rows[1], LANES), bf16),
        sd((s.rows[2], LANES), bf16),
        sd((s.rows[3], LANES), f32),
        sd((1, s.cin, s.full_rows, s.full_cols), bf16),
        sd((s.dates, s.cin, s.full_rows, s.full_cols), bf16),
    ] + [sd((1, s.c), f32)] * 4
    got = pl.pallas_call(
        functools.partial(main_kernel, s, names),
        out_shape=out_shape,
        in_specs=in_specs,
        out_specs=[hbm] * 10,
        scratch_shapes=list(shapes.values()),
        compiler_params=pltpu.CompilerParams(
            collective_id=0, has_side_effects=True, vmem_limit_bytes=60 * 2**20
        ),
        name="forecast",
    )(*args)
    c, ff, nb = s.c, s.ff, s.nb
    outs = [out_shape[4], out_shape[5]] + [
        sd((nb, s.cj, c), f32), sd((c,), f32), sd((c,), f32), sd((c,), f32),
        sd((nb, c, c), f32), sd((c,), f32), sd((c,), f32), sd((c,), f32),
        sd((c, ff), f32), sd((ff,), f32), sd((c, ff), f32), sd((c,), f32),
        sd((nb, s.cin, c), f32), sd((s.cin,), f32),
    ] + [sd((1, c), f32)] * 4
    V = pltpu.VMEM
    done = pl.pallas_call(
        functools.partial(finish_kernel, s),
        out_shape=outs,
        in_specs=[hbm] * 10,
        out_specs=[hbm] * len(outs),
        scratch_shapes=[
            V((s.rows[0], LANES), bf16), V((s.rows[1], LANES), bf16), V((s.rows[2], LANES), bf16),
            V((nb, s.cj, c), f32), V((nb, c, c), f32), V((c, ff), f32), V((c, ff), f32),
            V((nb, s.cin, c), f32), V((8, up_to(ff, LANES)), f32), V((s.rows[3], LANES), f32),
            V(out_shape[4].shape, bf16), V(out_shape[5].shape, bf16), V((4, 1, c), f32),
            V((s.cin,), f32), V((ff,), f32), *[V((c,), f32)] * 7,
            pltpu.SemaphoreType.DMA((16,)), pltpu.SemaphoreType.DMA((32,)),
        ],
        compiler_params=pltpu.CompilerParams(vmem_limit_bytes=60 * 2**20),
        name="finish",
    )(*got)
    done = list(done)
    done[2] = jnp.swapaxes(done[2], 1, 2)
    done[10] = done[10].T
    return tuple(done)


def solution(mesh):
    in_specs = (
        P(None, None, "lat", "lon"),
        P("ens", None, "lat", "lon"),
        P("ens", None, "lat", "lon"),
        P("ens"),
    ) + (P(),) * 18
    out_specs = (
        (P("ens", None, "lat", "lon"), P(None, None, "lat", "lon"))
        + (P(),) * 14
        + (P("ens", None),) * 4
    )

    def run(*args):
        s = Sizes(mesh, args[0].shape, args[1].shape, args[5].shape, args[8].shape, args[16].shape)
        return jax.shard_map(
            functools.partial(per_device, s),
            mesh=mesh,
            in_specs=in_specs,
            out_specs=out_specs,
            check_vma=False,
        )(*args)

    return run
```

```python
import functools
import types

import jax
import jax.numpy as jnp
from jax import lax
from jax.experimental import pallas as pl
from jax.experimental.pallas import tpu as pltpu
from jax.sharding import PartitionSpec as P

MESH = pl.DeviceIdType.MESH
f32 = jnp.float32
bf16 = jnp.bfloat16
i32 = jnp.int32
EPS = 1e-05
LANES = 128
AXES = ("ens", "lat", "lon")
BIT0, BIT1, LAT, LON = range(4)
ROUTE_X = (LAT, BIT0, BIT1, LON)
ROUTE_Y = (LAT, BIT1, BIT0, LON)
WSEM, OSEM, SEMS = range(3)
ROUTE_ZX = (LAT, LON, BIT0, BIT1)
ROUTE_ZY = (LAT, LON, BIT1, BIT0)
PIECES = dict(
    a=(0, 0), b=(0, 1), c=(0, 2), d=(1, 0), e=(1, 1), f=(1, 2),
    g=(2, 0), h=(2, 1), i=(3, 0), j=(3, 1), k=(4, 0), l=(5, 0), m=(2, 2), n=(3, 2),
)


def nn(a, b):
    return lax.dot_general(a, b, (((1,), (0,)), ((), ())), preferred_element_type=f32)


def nt(a, b):
    return lax.dot_general(a, b, (((1,), (1,)), ((), ())), preferred_element_type=f32)


def tn(a, b):
    return lax.dot_general(a, b, (((0,), (0,)), ((), ())), preferred_element_type=f32)


def up_to(n, m):
    return -(-n // m) * m


class Sizes:
    def __init__(self, mesh, state, noise, enc_taps, enc_weight, up_weight):
        self.ne, self.nl, self.nz = (mesh.shape[a] for a in AXES)
        self.dates, self.cin, self.full_rows, self.full_cols = state
        self.noise = noise[1]
        self.full_rows = state[2] // self.nl
        self.full_cols = state[3] // self.nz
        self.hr, self.hc = self.full_rows // 2, self.full_cols // 2
        assert self.hr == 2 and self.hc == LANES and self.ne == 4
        self.lat_total = enc_taps[1]
        self.nb = enc_taps[0]
        self.c = enc_weight[1]
        self.cj = enc_weight[2]
        self.ff = up_weight[0]
        self.px = self.hr * self.hc
        self.pixels = float(self.px * self.nl * self.nz)
        self.c5 = self.c // LANES
        self.f10 = self.ff // LANES
        self.r641 = up_to(self.c, 16)
        self.r80 = up_to(self.cj, 16)
        self.off_up = self.f10 * self.r641
        self.off_dec = self.off_up + self.f10 * self.r641
        used = (
            self.off_dec + self.nb * self.c5 * self.r80,
            self.nb * self.c5 * self.r641,
            self.nb * self.c5 * self.r80,
        )
        unit = 16 * self.nl * self.ne * self.nz
        self.rows = tuple(up_to(n, unit) for n in used) + (up_to(24 * 6, unit // 2),)
        self.chunks = {}

        def split(piece, buffer, lo, hi, third, last):
            units = (hi - lo) // unit
            last = last if units >= 3 * last else 0
            first = (units - last + 1) // 2
            at = lo
            for n, (count, route) in enumerate(
                ((first, ROUTE_X), (units - last - first, ROUTE_Y), (last, third))
            ):
                if count:
                    self.chunks[piece, n] = (buffer, at, count * unit, route)
                at += count * unit

        cut = self.off_up // unit * unit
        split(0, 0, 0, cut, ROUTE_ZX, 2)
        split(1, 0, cut, self.rows[0], ROUTE_ZY, 2)
        cut = 2 * self.c5 * self.r641 // unit * unit
        split(2, 1, 0, cut, ROUTE_ZX, 0)
        split(3, 1, cut, self.rows[1], ROUTE_ZY, 0)
        self.chunks[4, 0] = (2, 0, self.rows[2], ROUTE_X)
        self.chunks[5, 0] = (3, 0, self.rows[3], ROUTE_Y)
        self.group = self.nl * self.nz


def add_into(dst, at, sources, count):
    step = next(s for s in (256, 128, 64, 32, 16, 8) if count % s == 0)

    def body(n, carry):
        lo = pl.multiple_of(n * step, 8 if step == 8 else 16)
        there = pl.ds(pl.multiple_of(at + lo, 8 if step == 8 else 16), step)
        value = dst[there, :].astype(f32)
        for source in sources:
            value = value + source[pl.ds(lo, step), :].astype(f32)
        dst[there, :] = value.astype(dst.dtype)
        return carry

    lax.fori_loop(0, count // step, body, 0)


class Links:
    def __init__(self, z, sems=None):
        self.s = z
        self.sems = sems
        self.used = 0
        if sems is not None:
            self.e, self.l, self.z = (lax.axis_index(a) for a in AXES)

    def take(self):
        self.used += 1
        return self.used - 1

    def at(self, de, dl, dz):
        s = self.s
        return (
            lax.rem(self.e + (de + s.ne), s.ne),
            lax.rem(self.l + (dl + s.nl), s.nl),
            lax.rem(self.z + (dz + s.nz), s.nz),
        )

    def bit(self, which):
        return lax.rem(self.e // (1 << which), 2)

    def flip(self, which):
        return (self.e + (1 << which) * (1 - 2 * self.bit(which)), self.l, self.z)

    def has_up(self):
        return self.l > 0

    def has_down(self):
        return self.l < self.s.nl - 1


class Send:
    def __init__(self, links, src, dst, device, dl=0):
        self.links = links
        self.ids = (links.take(), links.take())
        self.what = (src, dst, device)
        self.dl = dl

    def copy(self):
        src, dst, device = self.what
        return pltpu.make_async_remote_copy(
            src_ref=src,
            dst_ref=dst,
            send_sem=self.links.sems.at[self.ids[0]],
            recv_sem=self.links.sems.at[self.ids[1]],
            device_id=device,
            device_id_type=MESH,
        )

    def under(self, sending, act):
        if self.dl == 0:
            act()
        else:
            up = (self.dl < 0) == sending
            pl.when(self.links.has_up() if up else self.links.has_down())(act)

    def start(self):
        self.under(True, lambda: self.copy().start())

    def wait_recv(self):
        self.under(False, lambda: self.copy().wait_recv())

    def wait_send(self):
        self.under(True, lambda: self.copy().wait_send())


class AllReduce:
    def __init__(self, links, partial, total, lo, rows, route, bufs, own_sem):
        self.k, self.g, self.h, self.route = links, partial, total, route
        self.bufs, self.own_sem = bufs, own_sem
        self.sent, self.waiting = [], []
        self.stage = 0
        self.base, self.part = [], []
        base, size = lo, rows
        for axis in route:
            size = size // self.count(links.s, axis)
            self.base.append(base)
            self.part.append(size)
            base = base + self.index(axis) * size
        self.base.append(base)
        self.last_stage = 2 * len(route)

    @staticmethod
    def count(s, axis):
        return {LAT: s.nl, LON: s.nz}.get(axis, 2)

    @staticmethod
    def shapes(s, rows, route, dtype):
        out = []
        for axis in route:
            n = AllReduce.count(s, axis)
            rows = rows // n
            out.append(pltpu.VMEM((n - 1, rows, LANES), dtype))
        return out

    def index(self, axis):
        k = self.k
        return {LAT: k.l, LON: k.z}[axis] if axis in (LAT, LON) else k.bit(axis)

    def others(self, axis):
        k, s = self.k, self.k.s
        if axis == LAT:
            devices = [k.at(0, d, 0) for d in range(1, s.nl)]
            return [(dev, dev[1], n) for n, dev in enumerate(devices)]
        if axis == LON:
            devices = [k.at(0, 0, d) for d in range(1, s.nz)]
            return [(dev, dev[2], n) for n, dev in enumerate(devices)]
        return [(k.flip(axis), 1 - k.bit(axis), 0)]

    def send(self, src, dst, device):
        m = Send(self.k, src, dst, device)
        m.start()
        self.sent.append(m)
        self.waiting.append(m)

    def step(self):
        g, h, route = self.g, self.h, self.route
        al = lambda v: pl.multiple_of(v, 8)
        stage, self.stage = self.stage, self.stage + 1
        for m in self.waiting:
            m.wait_recv()
        self.waiting = []
        depth = len(route)
        if 0 < stage <= depth:
            buf = self.bufs[stage - 1]
            add_into(g, al(self.base[stage]), [buf.at[n] for n in range(buf.shape[0])], self.part[stage - 1])
        if stage < depth:
            size = self.part[stage]
            for device, place, slot in self.others(route[stage]):
                there = pl.ds(al(self.base[stage] + place * size), size)
                self.send(g.at[there], self.bufs[stage].at[slot], device)
        elif stage < 2 * depth:
            level = 2 * depth - 1 - stage
            here = pl.ds(al(self.base[level + 1]), self.part[level])
            if stage == depth:
                self.own = pltpu.make_async_copy(g.at[here], h.at[here], self.own_sem)
                self.own.start()
            if stage == depth + 1:
                self.own.wait()
            source = g if stage == depth else h
            for device, _, _ in self.others(route[level]):
                self.send(source.at[here], h.at[here], device)
        else:
            for m in self.sent:
                m.wait_send()

    def finished(self):
        return self.stage > self.last_stage


class MISC:
    down_bias, up_bias, gain_two, shift_two, proc_bias, gain_one, shift_one, enc_bias = 0, 1, 3, 4, 5, 6, 7, 8
    up_last, down_last, proc_last, enc_last, dec_last, dec_bias = 9, 11, 13, 16, 19, 22


def put_misc(misc, slot, row):
    width = row.shape[1]
    for t in range(-(-width // LANES)):
        lo, hi = t * LANES, min(width, (t + 1) * LANES)
        misc[slot * 6 + t : slot * 6 + t + 1, 0 : hi - lo] = row[:, lo:hi]


def get_misc(misc, slot, width):
    parts = []
    for t in range(-(-width // LANES)):
        lo, hi = t * LANES, min(width, (t + 1) * LANES)
        parts.append(misc[slot * 6 + t : slot * 6 + t + 1, 0 : hi - lo])
    return parts


def scratch_list(s):
    c, ff, px = s.c, s.ff, s.px
    big = s.full_cols
    wide = 8 * big + LANES
    V = pltpu.VMEM
    shapes = dict(
        state=V((s.dates, s.cin, s.full_rows, big), bf16),
        noise=V((1, s.noise, s.full_rows, big), bf16),
        cot=V((1, s.cin, s.full_rows, big), bf16),
        eb_v=V((c,), f32), gain1=V((c,), f32), shift1=V((c,), f32), pb=V((c,), f32), gain2=V((c,), f32),
        shift2=V((c,), f32), ub=V((ff,), f32), db=V((c,), f32), cb=V((s.cin,), f32),
        out=V((1, s.cin, s.full_rows, big), bf16),
        sgrad=V((s.dates, s.cin, s.full_rows, big), bf16),
        means=V((4, 1, c), f32),
        date=pltpu.SMEM((1,), i32), reach=pltpu.SMEM((s.lat_total,), i32),
        enc_taps=pltpu.SMEM((s.nb, s.lat_total, 25), f32), proc_taps=pltpu.SMEM((s.nb, s.lat_total, 25), f32),
        dec_taps=pltpu.SMEM((s.nb, 2 * s.lat_total, 9), f32),
        xin=V((160, s.full_rows, big), f32),
        xj=V((160, 8 * big), bf16),
        eb=V((2, 8, 160), f32),
        eslot=V((6, 8, 160), f32),
        xe=V((48, 160), bf16),
        em=V((2, s.nb * LANES, 5 * big + 48), bf16),
        dm=V((2, s.nb * LANES, 6 * big + 48), bf16),
        tm=V((s.nb * px, 6 * LANES + 48), bf16),
        ew=V((s.nb, s.cj, c), bf16),
        pw=V((s.nb, c, c), bf16),
        uw=V((c, ff), bf16),
        dw=V((c, ff), bf16),
        cw=V((s.nb, s.cin, c), bf16),
        filte=V((s.nb, px, s.cj), bf16),
        hx=V((6 * LANES + 48, c), f32),
        nx=V((6 * LANES + 48, c), bf16),
        pe=V((2, 4, c), f32),
        he=V((6, 4, c), f32),
        ce=V((6, 4, c), f32),
        filt=V((s.nb * px, c), bf16),
        h1=V((px, c), f32),
        n2=V((px, c), bf16),
        hp=V((px, ff), f32),
        ag=V((px, ff), f32),
        act=V((px, ff), bf16),
        hg=V((px, ff), bf16),
        n2t=V((c, px), bf16),
        h2=V((px, c), bf16),
        pgr=V((s.nb, px, s.cin), bf16),
        projt=V((2, 80, s.nb * LANES), bf16),
        partt=V((2, 80, s.nb * LANES), bf16),
        two=V((px, c), f32),
        mg=V((px, c), bf16),
        mgt=V((c, px), bf16),
        ntg=V((px, c), f32),
        one=V((px, c), f32),
        br=V((px, c), bf16),
        brt=V((c, px), bf16),
        fg=V((s.nb * px, c), bf16),
        con=V((6 * LANES + 48, c), f32),
        rup=V((px, c), f32),
        rdn=V((px, c), f32),
        reg=V((6, 4, c), f32),
        zg=V((px, c), bf16),
        sgx=V((160, wide), f32),
        sgb=V((160, 4 * big), bf16),
        sgu=V((160, 2 * big), bf16),
        sgd=V((160, 2 * big), bf16),
        sgn=V((6, 8, 160), f32),
        sge=V((6, 8, 160), f32),
        sgt=V((LANES, 160), f32),
        orow=V((s.cin, s.full_rows, big), f32),
        st7=V((s.ne, 80, 4 * big), bf16),
        dates=V((s.ne, 8, LANES), f32),
        cbt=V((8, LANES), f32),
        slat=V((4, s.nl, 2, c), f32),
        slon=V((4, s.nz, 2, c), f32),
        sall=V((4, s.group if s.group <= 16 else 1, 2, c), f32),
        tmt=V((6 * LANES + 48, s.nb * px), bf16),
        g1=V((s.rows[0], LANES), bf16),
        g2=V((s.rows[1], LANES), bf16),
        g3=V((s.rows[2], LANES), bf16),
        gm=V((s.rows[3], LANES), f32),
    )
    for name, (buffer, _, rows, route) in s.chunks.items():
        kinds = AllReduce.shapes(s, rows, route, f32 if buffer == 3 else bf16)
        for j, kind in enumerate(kinds):
            shapes[name, j] = kind
    shapes[WSEM] = pltpu.SemaphoreType.DMA((28,))
    shapes[OSEM] = pltpu.SemaphoreType.DMA((len(s.chunks),))
    shapes[SEMS] = pltpu.SemaphoreType.DMA((sem_count(s),))
    return shapes


def sem_count(s):
    total = len(s.chunks) * 2 * 2 * (s.nl - 1 + 1 + 1 + s.nz - 1)
    total += 2 * 4 * 8 + 2 * (s.ne - 1) + 2 * 6
    total += 4 * 2 * (s.group - 1 if s.group <= 16 else s.nl - 1 + s.nz - 1)
    return total


def main_kernel(s, names, *refs):
    n_in, n_out = 22, 10
    (
        state_h, noise_h, cot_h, date_h, reach_h, enc_taps_h, proc_taps_h, dec_taps_h,
        ew_h, eb_h, gain1_h, shift1_h, pw_h, pb_h, gain2_h, shift2_h, uw_h, ub_h, dw_h, db_h, cw_h, cb_h,
    ) = refs[:n_in]
    h1o, h2o, h3o, hmo, out_h, sgrad_h, m1_h, v1_h, m2_h, v2_h = refs[n_in : n_in + n_out]
    table = dict(zip(names, refs[n_in + n_out :]))
    S = types.SimpleNamespace(**{n: r for n, r in table.items() if isinstance(n, str)})
    sems = table[SEMS]
    k = Links(s, sems)
    c, ff, px, nb, cin, cj = s.c, s.ff, s.px, s.nb, s.cin, s.cj
    big = s.full_cols
    l = k.l
    row0 = l * s.hr
    edge0 = 8 * big

    offsets = {(d, 0, 0) for d in range(1, s.ne)}
    if s.group <= 16:
        offsets |= {(0, a, b) for a in range(s.nl) for b in range(s.nz)} - {(0, 0, 0)}
    else:
        offsets |= {(0, d, 0) for d in range(1, s.nl)} | {(0, 0, d) for d in range(1, s.nz)}
    offsets |= {(0, a % s.nl, b % s.nz) for a in (1, -1) for b in (1, -1)}
    offsets = sorted(offsets)
    barrier = pltpu.get_barrier_semaphore()
    for o in offsets:
        pl.semaphore_signal(barrier, 1, device_id=k.at(*o), device_id_type=MESH)

    def fetch(n, src, to):
        copy = pltpu.make_async_copy(src, to, table[WSEM].at[n])
        copy.start()
        return copy

    date_ref, reach = S.date, S.reach
    enc_taps, proc_taps, dec_taps = S.enc_taps, S.proc_taps, S.dec_taps
    scalars = [
        fetch(23 + n, *pair)
        for n, pair in enumerate(
            (
                (date_h, date_ref), (reach_h, reach), (enc_taps_h, enc_taps),
                (proc_taps_h, proc_taps), (dec_taps_h, dec_taps),
            )
        )
    ]
    state, noise, cot = S.state, S.noise, S.cot
    fields = [fetch(n, *pair) for n, pair in enumerate(((state_h, state), (noise_h, noise), (cot_h, cot)))]
    eb, gain1, shift1, pb, gain2, shift2 = S.eb_v, S.gain1, S.shift1, S.pb, S.gain2, S.shift2
    ub, db, cb = S.ub, S.db, S.cb
    vectors = [
        fetch(3 + n, *pair)
        for n, pair in enumerate(
            (
                (eb_h, eb), (gain1_h, gain1), (shift1_h, shift1), (pb_h, pb), (gain2_h, gain2),
                (shift2_h, shift2), (ub_h, ub), (db_h, db), (cb_h, cb),
            )
        )
    ]
    loads = types.SimpleNamespace()
    loads.ew, loads.pw, loads.cw, loads.dw, loads.uw = [
        fetch(12 + n, *pair)
        for n, pair in enumerate(
            ((ew_h, S.ew), (pw_h, S.pw), (cw_h, S.cw), (dw_h, S.dw), (uw_h, S.uw))
        )
    ]
    finals = []

    def keep(src, to):
        copy = pltpu.make_async_copy(src, to, table[WSEM].at[17 + len(finals)])
        copy.start()
        finals.append(copy)

    for copy in fields + scalars:
        copy.wait()

    date = date_ref[0]
    live = jnp.where(date >= 0, 1.0, 0.0).astype(f32)
    xin, xj = S.xin, S.xj
    picked = jnp.zeros((cin, s.full_rows, big), f32)
    for d in range(s.dates):
        picked = picked + state[d].astype(f32) * jnp.where(date == d, 1.0, 0.0).astype(f32)
    xin[0:cin] = picked
    xin[cin:cj] = noise[0].astype(f32)
    xin[80 : 80 + cin] = cot[0].astype(f32) * live
    xin[80 + cin : 160] = jnp.zeros((160 - 80 - cin, s.full_rows, big), f32)
    lane = lax.broadcasted_iota(i32, (160, LANES), 1)
    ends = jnp.zeros((160, LANES), f32)
    for q in range(4):
        row = xin[:, q, :]
        xj[:, (2 + q) * big : (3 + q) * big] = row.astype(bf16)
        moved = pltpu.roll(row[:, 0:LANES], q * 2, 1)
        ends = jnp.where((lane >> 1) == q, moved, ends)
        moved = pltpu.roll(row[:, big - LANES : big], q * 2 + 10, 1)
        ends = jnp.where((lane >> 1) == q + 4, moved, ends)
    turned = ends.T
    S.eb[0] = turned[0:8, :]
    S.eb[1] = turned[8:16, :]
    S.dates[k.e] = jnp.full((8, LANES), date.astype(f32), f32)

    @pl.when(jnp.logical_not(k.has_up()))
    def _():
        xj[:, 0 : 2 * big] = jnp.zeros((160, 2 * big), bf16)
        S.hx[0:px] = jnp.zeros((px, c), f32)
        for side in range(2):
            S.he[side] = jnp.zeros((4, c), f32)

    @pl.when(jnp.logical_not(k.has_down()))
    def _():
        xj[:, 6 * big : 8 * big] = jnp.zeros((160, 2 * big), bf16)
        S.hx[2 * px : 3 * px] = jnp.zeros((px, c), f32)
        for side in range(2):
            S.he[4 + side] = jnp.zeros((4, c), f32)

    pl.semaphore_wait(barrier, len(offsets))

    totals = (h1o, h2o, h3o, hmo)
    reduced = {}
    for n, (name, (buffer, lo, rows, route)) in enumerate(s.chunks.items()):
        bufs = [table[name, j] for j in range(len(route))]
        partial = (S.g1, S.g2, S.g3, S.gm)[buffer]
        reduced[name] = AllReduce(k, partial, totals[buffer], lo, rows, route, bufs, table[OSEM].at[n])

    def ar(letters):
        for letter in letters:
            it = reduced.get(PIECES[letter])
            if it is not None and not it.finished():
                it.step()

    pending = []

    def start(sends):
        for m in sends:
            m.start()
        pending.extend(sends)
        return sends

    def arrive(sends):
        for m in sends:
            m.wait_recv()

    dirs = [(dl, ds) for dl in (-1, 0, 1) for ds in (-1, 1)]

    def slot_of(dl, ds):
        return (1 - dl) * 2 + (1 - ds) // 2

    sends = [
        Send(k, xj.at[:, pl.ds(2 * big, 2 * big)], xj.at[:, pl.ds(6 * big, 2 * big)], k.at(0, -1, 0), -1),
        Send(k, xj.at[:, pl.ds(4 * big, 2 * big)], xj.at[:, pl.ds(0, 2 * big)], k.at(0, 1, 0), 1),
    ]
    for dl, ds in dirs:
        sends.append(
            Send(k, S.eb.at[(ds + 1) // 2], S.eslot.at[slot_of(dl, ds)], k.at(0, dl, ds), dl)
        )
    first_halo = start(sends)
    date_sends = start(
        [
            Send(k, S.dates.at[k.e], S.dates.at[k.e], k.at(d, 0, 0))
            for d in range(1, s.ne)
        ]
    )

    gm = S.gm
    gm[0:144] = jnp.zeros((144, LANES), f32)

    def band(shape, column_of):
        rows = lax.broadcasted_iota(i32, shape, 0)
        cols = lax.broadcasted_iota(i32, shape, 1)
        return column_of(rows, cols)

    def pick(d, table, like):
        value = jnp.zeros(like, f32)
        for key, scalar in table:
            value = jnp.where(d == key, scalar, value)
        return value

    def inside(grow, total):
        return jnp.logical_and(grow >= 0, grow < total)

    def edge_lane(shape):
        at = lax.broadcasted_iota(i32, shape, 1)
        slot, q, m = at >> 3, (at & 7) >> 1, at & 1
        r = q + 2 + 4 * ((slot >> 1) - 1)
        return r, jnp.where((slot & 1) == 0, m - 2, big + m), at

    def build_encoder():
        em = S.em
        d_main = band((LANES, big), lambda j, J: J - 2 * j)
        r, J, at = edge_lane((16, 48))
        j = lax.broadcasted_iota(i32, (16, 48), 0)
        codes = []
        for start_row in (0, LANES - 16):
            d = J - 2 * (j + start_row)
            codes.append(r * 1024 + d)
        for i in range(2):
            reached = reach[row0 + i]
            edges = [[jnp.zeros((16, 48), f32) for _ in range(2)] for _ in range(nb)]
            for a in range(-2, 3):
                r_in = 2 * i + a + 2
                ok = inside(4 * l + r_in - 2, 2 * s.lat_total)
                masks = [d_main == b for b in range(-2, 3)]
                for kk in range(nb):
                    value = jnp.zeros((LANES, big), f32)
                    for b in range(-2, 3):
                        tap = enc_taps[kk, row0 + i, 5 * (a + 2) + b + 2]
                        tap = jnp.where(jnp.logical_and(ok, abs(b) <= reached), tap, 0.0)
                        value = jnp.where(masks[b + 2], tap, value)
                        for part in range(2):
                            edges[kk][part] = jnp.where(
                                codes[part] == r_in * 1024 + b, tap, edges[kk][part]
                            )
                    em[i, kk * LANES : (kk + 1) * LANES, (a + 2) * big : (a + 3) * big] = value.astype(bf16)
            for kk in range(nb):
                lo = kk * LANES
                em[i, lo : lo + 16, 5 * big :] = edges[kk][0].astype(bf16)
                em[i, lo + 16 : lo + LANES - 16, 5 * big :] = jnp.zeros((LANES - 32, 48), bf16)
                em[i, lo + LANES - 16 : lo + LANES, 5 * big :] = edges[kk][1].astype(bf16)

    def build_decoder():
        dm = S.dm
        d_main = band((LANES, big), lambda j, J: j - (J >> 1))
        r, J, at = edge_lane((16, 48))
        j = lax.broadcasted_iota(i32, (16, 48), 0)
        codes = []
        for start_row in (0, LANES - 16):
            d = (j + start_row) - (J >> 1)
            codes.append(r * 1024 + d)
        for i in range(2):
            edges = [[jnp.zeros((16, 48), f32) for _ in range(2)] for _ in range(nb)]
            for n in range(6):
                r_in = 2 * i + n
                a = i + 1 - r_in // 2
                full = 4 * l + r_in - 2
                ok = inside(full, 2 * s.lat_total)
                full = jnp.clip(full, 0, 2 * s.lat_total - 1)
                reached = reach[full // 2] - 1
                masks = [d_main == b for b in range(-1, 2)]
                for kk in range(nb):
                    value = jnp.zeros((LANES, big), f32)
                    for b in range(-1, 2):
                        tap = dec_taps[kk, full, 3 * (a + 1) + b + 1]
                        tap = jnp.where(jnp.logical_and(ok, abs(b) <= reached), tap, 0.0)
                        value = jnp.where(masks[b + 1], tap, value)
                        for part in range(2):
                            edges[kk][part] = jnp.where(
                                codes[part] == r_in * 1024 + b, tap, edges[kk][part]
                            )
                    dm[i, kk * LANES : (kk + 1) * LANES, n * big : (n + 1) * big] = value.astype(bf16)
            for kk in range(nb):
                lo = kk * LANES
                dm[i, lo : lo + 16, 6 * big :] = edges[kk][0].astype(bf16)
                dm[i, lo + 16 : lo + LANES - 16, 6 * big :] = jnp.zeros((LANES - 32, 48), bf16)
                dm[i, lo + LANES - 16 : lo + LANES, 6 * big :] = edges[kk][1].astype(bf16)

    def build_processor():
        tm = S.tm
        d_main = band((LANES, LANES), lambda j, J: J - j)
        at = lax.broadcasted_iota(i32, (16, 48), 1)
        slot, idx = at >> 3, at & 7
        r = 2 * (slot >> 1) + (idx >> 1)
        m = idx & 1
        J = jnp.where((slot & 1) == 0, m - 2, LANES + m)
        j = lax.broadcasted_iota(i32, (16, 48), 0)
        codes = []
        for start_row in (0, LANES - 16):
            d = J - (j + start_row)
            codes.append(jnp.where(idx < 4, r * 1024 + d, -5000))
        for i in range(2):
            reached = reach[row0 + i]
            edges = [[jnp.zeros((16, 48), f32) for _ in range(2)] for _ in range(nb)]
            for r_in in range(6):
                a = r_in - 2 - i
                if abs(a) > 2:
                    for kk in range(nb):
                        lo = kk * px + i * LANES
                        tm[lo : lo + LANES, r_in * LANES : (r_in + 1) * LANES] = jnp.zeros((LANES, LANES), bf16)
                    continue
                ok = inside(row0 + r_in - 2, s.lat_total)
                masks = [d_main == b for b in range(-2, 3)]
                for kk in range(nb):
                    value = jnp.zeros((LANES, LANES), f32)
                    for b in range(-2, 3):
                        tap = proc_taps[kk, row0 + i, 5 * (a + 2) + b + 2]
                        tap = jnp.where(jnp.logical_and(ok, abs(b) <= reached), tap, 0.0)
                        value = jnp.where(masks[b + 2], tap, value)
                        for part in range(2):
                            edges[kk][part] = jnp.where(
                                codes[part] == r_in * 1024 + b, tap, edges[kk][part]
                            )
                    lo = kk * px + i * LANES
                    tm[lo : lo + LANES, r_in * LANES : (r_in + 1) * LANES] = value.astype(bf16)
            for kk in range(nb):
                lo = kk * px + i * LANES
                tm[lo : lo + 16, 768:816] = edges[kk][0].astype(bf16)
                tm[lo + 16 : lo + LANES - 16, 768:816] = jnp.zeros((LANES - 32, 48), bf16)
                tm[lo + LANES - 16 : lo + LANES, 768:816] = edges[kk][1].astype(bf16)

    slat, slon = S.slat, S.slon

    def fold(values, kind, count):
        total_a, total_b = values[0]
        for a, b in values[1:]:
            total_a = total_a + a
            total_b = total_b + b
        if kind:
            total_a = total_a * (1.0 / len(values))
            for a, b in values:
                total_b = total_b + (a - total_a) * (a - total_a) * count
        return total_a, total_b

    single = s.group <= 16
    sall = S.sall
    place = k.l * s.nz + k.z

    def stat_start(rd, a, b):
        if single:
            sall[rd, place, 0:1, :] = a
            sall[rd, place, 1:2, :] = b
            others = [(0, m, n) for n in range(s.nz) for m in range(s.nl) if m or n]
            return start(
                [Send(k, sall.at[rd, place], sall.at[rd, place], k.at(*o)) for o in others]
            )
        slat[rd, k.l, 0:1, :] = a
        slat[rd, k.l, 1:2, :] = b
        return start(
            [
                Send(k, slat.at[rd, k.l], slat.at[rd, k.l], k.at(0, d, 0))
                for d in range(1, s.nl)
            ]
        )

    def stat_middle(rd, sends, kind):
        if single:
            return sends
        arrive(sends)
        values = [(slat[rd, n, 0:1, :], slat[rd, n, 1:2, :]) for n in range(s.nl)]
        a, b = fold(values, kind, float(px))
        slon[rd, k.z, 0:1, :] = a
        slon[rd, k.z, 1:2, :] = b
        return start(
            [
                Send(k, slon.at[rd, k.z], slon.at[rd, k.z], k.at(0, 0, d))
                for d in range(1, s.nz)
            ]
        )

    def stat_end(rd, sends, kind):
        arrive(sends)
        if single:
            values = [(sall[rd, n, 0:1, :], sall[rd, n, 1:2, :]) for n in range(s.group)]
            return fold(values, kind, float(px))
        values = [(slon[rd, n, 0:1, :], slon[rd, n, 1:2, :]) for n in range(s.nz)]
        return fold(values, kind, float(px * s.nl))

    def moments(values):
        mean = jnp.sum(values, axis=0, keepdims=True) * (1.0 / px)
        centred = values - mean
        return mean, jnp.sum(centred * centred, axis=0, keepdims=True)

    def vec(ref):
        n = ref.shape[0]
        return ref[...].reshape(1, n)

    build_encoder()
    build_decoder()
    build_processor()

    arrive(first_halo)
    def absent(slot):
        return pl.when(jnp.logical_not(k.has_up() if slot < 2 else k.has_down()))

    for slot in (0, 1, 4, 5):
        @absent(slot)
        def _():
            S.eslot[slot] = jnp.zeros((8, 160), f32)

    xe = S.xe
    for slot in range(0, 6, 2):
        pair = jnp.concatenate([S.eslot[slot], S.eslot[slot + 1]], axis=0)
        xe[slot * 8 : slot * 8 + 16, :] = pair.astype(bf16)

    filte, hx = S.filte, S.hx
    for i in range(2):
        em = S.em
        got = nt(em[i, :, 0 : 5 * big], xj[0:80, 2 * i * big : (2 * i + 5) * big])
        got = got + nn(em[i, :, 5 * big :], xe[:, 0:80])
        for kk in range(nb):
            filte[kk, i * LANES : (i + 1) * LANES, :] = got[kk * LANES : (kk + 1) * LANES, 0:cj].astype(bf16)
    for copy in vectors:
        copy.wait()
    loads.ew.wait()
    h0 = vec(eb) + jnp.zeros((px, c), f32)
    for kk in range(nb):
        h0 = h0 + nn(filte[kk], S.ew[kk])
    hx[px : 2 * px, :] = h0
    own = slice(px, 2 * px)
    h0 = hx[own, :]
    stat_a = stat_start(0, *moments(h0))
    pe = S.pe
    for side, col in ((0, 0), (1, LANES - 2)):
        for q in range(2):
            lo = px + q * LANES + col
            pe[side, 2 * q : 2 * q + 2, :] = hx[lo : lo + 2, :]
    sends = [
        Send(k, hx.at[pl.ds(px, px)], hx.at[pl.ds(2 * px, px)], k.at(0, -1, 0), -1),
        Send(k, hx.at[pl.ds(px, px)], hx.at[pl.ds(0, px)], k.at(0, 1, 0), 1),
    ]
    for dl, ds in dirs:
        sends.append(
            Send(
                k,
                pe.at[(ds + 1) // 2],
                S.he.at[slot_of(dl, ds)],
                k.at(0, dl, ds),
                dl,
            )
        )
    zero_halo = start(sends)
    stat_a = stat_middle(0, stat_a, True)

    dm, pgr = S.dm, S.pgr
    for i in range(2):
        got = nt(dm[i, :, 0 : 6 * big], xj[80 : 80 + 80, 2 * i * big : (2 * i + 6) * big])
        got = got + nn(dm[i, :, 6 * big :], xe[:, 80:160])
        for kk in range(nb):
            pgr[kk, i * LANES : (i + 1) * LANES, :] = got[kk * LANES : (kk + 1) * LANES, 0:cin].astype(bf16)
    ones = jnp.ones((16, 4 * big), bf16)
    put_misc(gm, MISC.dec_bias, nt(ones, xj[80:160, 2 * big : 6 * big])[0:1, 0:cin])

    loads.cw.wait()
    two, mg = S.two, S.mg
    acc = nn(pgr[0], S.cw[0])
    for kk in range(1, nb):
        acc = acc + nn(pgr[kk], S.cw[kk])
    two[...] = acc
    mg[...] = acc.astype(bf16)

    mean1, m2 = stat_end(0, stat_a, True)
    var1 = m2 * (1.0 / s.pixels)
    rstd1 = lax.rsqrt(var1 + EPS)
    S.means[0] = mean1 * live
    S.means[1] = var1 * live
    keep(S.means.at[0], m1_h)
    keep(S.means.at[1], v1_h)
    arrive(zero_halo)
    for slot in range(6):
        lo = 768 + slot * 8
        hx[lo : lo + 8, :] = jnp.concatenate([S.he[slot], jnp.zeros((4, c), f32)], axis=0)
    nx = S.nx
    scale1 = rstd1 * vec(gain1)
    bias1 = vec(shift1)

    def norm_rows(n, carry):
        here = pl.ds(pl.multiple_of(n * 48, 16), 48)
        nx[here, :] = ((hx[here, :] - mean1) * scale1 + bias1).astype(bf16)
        return carry

    lax.fori_loop(0, 17, norm_rows, 0)

    filt, tm = S.filt, S.tm
    loads.pw.wait()
    h1 = S.h1
    acc = hx[own, :] + vec(pb)
    for kk in range(nb):
        here = slice(kk * px, (kk + 1) * px)
        filt[here, :] = nn(tm[here, :], nx[...]).astype(bf16)
        acc = acc + nt(filt[here, :], S.pw[kk])
    h1[...] = acc
    stat_b = stat_start(1, *moments(h1[...]))
    stat_b = stat_middle(1, stat_b, True)
    loads.dw.wait()
    ag, hp = S.ag, S.hp
    ag[...] = nn(mg[...], S.dw[...])
    S.mgt[...] = mg[...].T
    put_misc(gm, MISC.down_bias, jnp.sum(mg[...].astype(f32), axis=0, keepdims=True))
    tm_t = S.tmt
    tm_t[...] = tm[...].T
    mean2, m2 = stat_end(1, stat_b, True)
    var2 = m2 * (1.0 / s.pixels)
    rstd2 = lax.rsqrt(var2 + EPS)
    S.means[2] = mean2 * live
    S.means[3] = var2 * live
    keep(S.means.at[2], m2_h)
    keep(S.means.at[3], v2_h)
    scale2 = rstd2 * vec(gain2)
    bias2 = vec(shift2)
    n2 = S.n2

    def norm_two_rows(n, carry):
        here = pl.ds(pl.multiple_of(n * 32, 16), 32)
        n2[here, :] = ((h1[here, :] - mean2) * scale2 + bias2).astype(bf16)
        return carry

    lax.fori_loop(0, px // 32, norm_two_rows, 0)

    loads.uw.wait()
    hp[...] = nn(n2[...], S.uw[...])
    act, hg = S.act, S.hg
    ubias = vec(ub)
    root = 0.7978845608028654

    def gelu_rows(n, carry):
        here = pl.ds(pl.multiple_of(n * 16, 16), 16)
        v = hp[here, :] + ubias
        sq = v * v
        t = jnp.tanh(v * (root + (0.044715 * root) * sq))
        part = 0.5 * t + 0.5
        active = v * part
        act[here, :] = active.astype(bf16)
        slope = part + active * (1.0 - part) * (2.0 * root + (6.0 * 0.044715 * root) * sq)
        hg[here, :] = (slope * ag[here, :]).astype(bf16)
        return carry

    lax.fori_loop(0, px // 16, gelu_rows, 0)
    g1 = S.g1
    cols = [(lo, min(256, s.c5 * LANES - lo)) for lo in range(0, s.c5 * LANES, 256)]

    def spread(g, off, height, pitch, value, lo, width):
        for n in range(width // LANES):
            at = off + (lo // LANES + n) * pitch
            g[at : at + height, :] = value[:, n * LANES : (n + 1) * LANES].astype(bf16)

    for lo in range(0, s.f10 * LANES, 256):
        spread(g1, 0, c, s.r641, nn(S.mgt[...], act[:, lo : lo + 256]), lo, 256)
    ar("ba")
    S.n2t[...] = n2[...].T
    for lo in range(0, s.f10 * LANES, 256):
        spread(g1, s.off_up, c, s.r641, nn(S.n2t[...], hg[:, lo : lo + 256]), lo, 256)
    h2 = S.h2
    h2[...] = (h1[...] + nt(act[...], S.dw[...]) + vec(db)).astype(bf16)
    for kk in range(nb):
        got = tn(pgr[kk], h2[:, 0 : s.c5 * LANES])
        spread(g1, s.off_dec + kk * s.c5 * s.r80, cin, s.r80, got, 0, s.c5 * LANES)
    ar("bceafd")
    ntg = S.ntg
    ntg[...] = nt(hg[...], S.uw[...])
    grad = ntg[...]
    standard = (h1[...] - mean2) * rstd2
    sum_a = jnp.sum(grad, axis=0, keepdims=True)
    sum_b = jnp.sum(grad * standard, axis=0, keepdims=True)
    put_misc(gm, MISC.shift_two, sum_a)
    put_misc(gm, MISC.gain_two, sum_b)
    stat_c = stat_start(2, sum_a, sum_b)

    ar("ecdfb")
    stat_c = stat_middle(2, stat_c, False)

    def weighted(ref, column):
        return jnp.sum(ref.astype(f32) * column.astype(f32), axis=0, keepdims=True)

    def put_long(slot, row):
        put_misc(gm, slot, row[:, 0:768])
        put_misc(gm, slot + 1, row[:, 768:])

    def misc_one():
        put_long(MISC.up_bias, jnp.sum(hg[...].astype(f32), axis=0, keepdims=True))
        for n in range(2):
            at = s.f10 * LANES + n
            put_misc(gm, MISC.up_last + n, weighted(n2[...], hg[:, at : at + 1]))
            put_misc(gm, MISC.down_last + n, weighted(mg[...], act[:, at : at + 1]))
        for kk in range(nb):
            put_misc(gm, MISC.dec_last + kk, weighted(pgr[kk], h2[:, c - 1 : c]))

    sum_a, sum_b = stat_end(2, stat_c, False)
    g_two = vec(gain2)
    part_a = g_two * sum_a * (1.0 / s.pixels)
    part_b = g_two * sum_b * (1.0 / s.pixels)
    one, br = S.one, S.br

    def one_rows(n, carry):
        here = pl.ds(pl.multiple_of(n * 32, 16), 32)
        standard = (h1[here, :] - mean2) * rstd2
        value = rstd2 * (g_two * ntg[here, :] - part_a - standard * part_b) + two[here, :]
        one[here, :] = value
        br[here, :] = value.astype(bf16)
        return carry

    lax.fori_loop(0, px // 32, one_rows, 0)
    ar("a")
    fg = S.fg
    for kk in range(nb):
        fg[kk * px : (kk + 1) * px, :] = nn(br[...], S.pw[kk]).astype(bf16)
    con = S.con
    con[...] = nn(S.tmt[...], fg[...])

    def sum_rows(n, carry):
        here = pl.ds(pl.multiple_of(n * 48, 16), 48)
        value = con[here, :]
        standard = (hx[here, :] - mean1) * rstd1
        return (
            carry[0] + jnp.sum(value, axis=0, keepdims=True),
            carry[1] + jnp.sum(value * standard, axis=0, keepdims=True),
        )

    zero_row = jnp.zeros((1, c), f32)
    sum_a, sum_b = lax.fori_loop(0, 17, sum_rows, (zero_row, zero_row))
    put_misc(gm, MISC.shift_one, sum_a)
    put_misc(gm, MISC.gain_one, sum_b)
    stat_d = stat_start(3, sum_a, sum_b)
    for slot in range(6):
        S.ce[slot] = con[768 + slot * 8 : 772 + slot * 8, :]
    sends = [
        Send(k, con.at[pl.ds(0, px)], S.rdn, k.at(0, -1, 0), -1),
        Send(k, con.at[pl.ds(2 * px, px)], S.rup, k.at(0, 1, 0), 1),
    ]
    for dl, ds in dirs:
        mine = (dl + 1) * 2 + (ds + 1) // 2
        sends.append(
            Send(
                k,
                S.ce.at[mine],
                S.reg.at[slot_of(dl, ds)],
                k.at(0, dl, ds),
                dl,
            )
        )
    back_halo = start(sends)
    g2 = S.g2
    S.brt[...] = br[...].T
    ar("e")
    for kk in range(nb):
        if kk == 1:
            stat_d = stat_middle(3, stat_d, False)
        for lo, width in cols:
            got = nn(S.brt[...], filt[kk * px : (kk + 1) * px, lo : lo + width])
            spread(g2, kk * s.c5 * s.r641, c, s.r641, got, lo, width)
        if kk == 1:
            ar("agdhb")
    ar("igh")

    arrive(back_halo)
    ar("e")
    ng = ntg
    ng[...] = con[own, :]

    @pl.when(k.has_up())
    def _():
        ng[...] = ng[...] + S.rup[...]

    @pl.when(k.has_down())
    def _():
        ng[...] = ng[...] + S.rdn[...]

    def add_edges(sl):
        for ss in (-1, 1):
            got = S.reg.at[(sl + 1) * 2 + (ss + 1) // 2]
            col = 0 if ss == -1 else LANES - 2
            for q in range(2):
                lo = q * LANES + col
                ng[lo : lo + 2, :] = ng[lo : lo + 2, :] + got[2 * q : 2 * q + 2, :]

    add_edges(0)
    pl.when(k.has_up())(lambda: add_edges(-1))
    pl.when(k.has_down())(lambda: add_edges(1))
    sum_a, sum_b = stat_end(3, stat_d, False)
    g_one = vec(gain1)
    part_a1 = g_one * sum_a * (1.0 / s.pixels)
    part_b1 = g_one * sum_b * (1.0 / s.pixels)
    zg = S.zg

    def zero_rows(n, carry):
        here = pl.ds(pl.multiple_of(n * 32, 16), 32)
        there = pl.ds(pl.multiple_of(px + n * 32, 16), 32)
        standard = (hx[there, :] - mean1) * rstd1
        value = rstd1 * (g_one * ng[here, :] - part_a1 - standard * part_b1) + one[here, :]
        zg[here, :] = value.astype(bf16)
        return carry

    lax.fori_loop(0, px // 32, zero_rows, 0)
    ar("f")

    g3 = S.g3
    for kk in range(nb):
        got = tn(filte[kk], zg[:, 0 : s.c5 * LANES])
        spread(g3, kk * s.c5 * s.r80, cj, s.r80, got, 0, s.c5 * LANES)
        put_misc(gm, MISC.enc_last + kk, weighted(filte[kk], zg[:, c - 1 : c]))
    put_misc(gm, MISC.enc_bias, jnp.sum(zg[...].astype(f32), axis=0, keepdims=True))
    ar("ia")
    misc_one()
    put_misc(gm, MISC.proc_bias, jnp.sum(br[...].astype(f32), axis=0, keepdims=True))
    for kk in range(nb):
        put_misc(gm, MISC.proc_last + kk, weighted(br[...], filt[kk * px : (kk + 1) * px, c - 1 : c]))
    ar("b")

    projt, partt = S.projt, S.partt
    for kk in range(nb):
        here = slice(kk * LANES, (kk + 1) * LANES)
        proj = nt(h2[...], S.cw[kk])
        part = nt(zg[...], S.ew[kk])[:, 0:cin]
        for i in range(2):
            for ref, value in ((projt, proj), (partt, part)):
                ref[i, 0:cin, here] = value[i * LANES : (i + 1) * LANES, :].T.astype(bf16)
                ref[i, cin:80, here] = jnp.zeros((80 - cin, LANES), bf16)
    sgx = S.sgx
    em = S.em
    sgx[...] = jnp.zeros(sgx.shape, f32)
    for i in range(2):
        lo = 2 * i * big
        got = nn(projt[i], dm[i])
        sgx[0:80, lo : lo + 6 * big] = sgx[0:80, lo : lo + 6 * big] + got[:, 0 : 6 * big]
        sgx[0:80, edge0 : edge0 + 48] = sgx[0:80, edge0 : edge0 + 48] + got[:, 6 * big :]
        got = nn(partt[i], em[i])
        sgx[80:160, lo : lo + 5 * big] = sgx[80:160, lo : lo + 5 * big] + got[:, 0 : 5 * big]
        sgx[80:160, edge0 : edge0 + 48] = sgx[80:160, edge0 : edge0 + 48] + got[:, 5 * big :]
    sgb, sgu, sgd, sge = S.sgb, S.sgu, S.sgd, S.sge
    sgb[:, 0 : 2 * big] = sgx[:, 0 : 2 * big].astype(bf16)
    sgb[:, 2 * big : 4 * big] = sgx[:, 6 * big : 8 * big].astype(bf16)
    turned = sgx[:, edge0:].T
    for n in range(6):
        S.sgn[n] = turned[n * 8 : n * 8 + 8, :]
    sends = [
        Send(k, sgb.at[:, pl.ds(0, 2 * big)], sgd, k.at(0, -1, 0), -1),
        Send(k, sgb.at[:, pl.ds(2 * big, 2 * big)], sgu, k.at(0, 1, 0), 1),
    ]
    for dl, ds in dirs:
        sends.append(
            Send(k, S.sgn.at[(dl + 1) * 2 + (ds + 1) // 2], sge.at[slot_of(dl, ds)], k.at(0, dl, ds), dl)
        )
    out_halo = start(sends)
    ar("gdfhkcjlaekljbg")
    arrive(out_halo)
    ar("f")
    sgt = S.sgt
    sgt[48:LANES, :] = jnp.zeros((LANES - 48, 160), f32)
    for slot in range(6):
        sgt[slot * 8 : slot * 8 + 8, :] = sge[slot]
    for slot in (0, 1, 4, 5):
        @absent(slot)
        def _():
            sgt[slot * 8 : slot * 8 + 8, :] = jnp.zeros((8, 160), f32)
    arrived = sgt[...].T
    up_one = jnp.where(k.has_up(), 1, 0)
    down_one = jnp.where(k.has_down(), 1, 0)
    cbt = S.cbt
    cbt[...] = jnp.zeros((8, LANES), f32)
    cbt[0:1, 0:cin] = vec(cb)
    bias_col = cbt[...].T[0:cin, 0:1]
    orow, st7 = S.orow, S.st7

    for q in range(4):
        lo = (2 + q) * big
        value = sgx[:, lo : lo + big]
        if q < 2:
            other = sgu[:, q * big : (q + 1) * big].astype(f32)
            value = value + jnp.where(up_one == 1, other, 0.0)
        else:
            other = sgd[:, (q - 2) * big : (q - 1) * big].astype(f32)
            value = value + jnp.where(down_one == 1, other, 0.0)
        head, tail = value[:, 0:LANES], value[:, big - LANES :]
        for sl in (-1, 0, 1):
            for side in range(2):
                at = ((sl + 1) * 2 + side) * 8 + q * 2
                if side == 0:
                    moved = pltpu.roll(arrived, (LANES - at) % LANES, 1)
                    head = head + jnp.where(lane < 2, moved, 0.0)
                else:
                    moved = pltpu.roll(arrived, LANES - 2 - at, 1)
                    tail = tail + jnp.where(lane >= LANES - 2, moved, 0.0)
        orow[:, q, 0:LANES] = (head[0:cin] + bias_col) * live
        orow[:, q, LANES:big] = (tail[0:cin] + bias_col) * live
        st7[k.e, :, q * big : q * big + LANES] = head[80:160].astype(bf16)
        st7[k.e, :, q * big + LANES : (q + 1) * big] = tail[80:160].astype(bf16)
    S.out[0] = orow[...].astype(bf16)
    keep(S.out, out_h)
    def state_piece(slot, half):
        return st7.at[slot, :, pl.ds(half * 2 * big, 2 * big)]

    e_x, e_y = k.flip(0)[0], k.flip(1)[0]
    state_sends = start(
        [
            Send(k, state_piece(k.e, half), state_piece(k.e, half), k.flip(half))
            for half in range(2)
        ]
    )
    ar("icadfhkl")
    arrive(state_sends)
    state_sends = start(
        [
            Send(k, state_piece(slot, half), state_piece(slot, half), k.flip(1 - half))
            for half, slots in ((0, (k.e, e_x)), (1, (k.e, e_y)))
            for slot in slots
        ]
    )
    ar("cgiadkjehlbcjdgkeabihgljckilfdh")
    arrive(date_sends)
    arrive(state_sends)
    ar("jdilkjegc")
    for d in range(s.dates):
        for q in range(4):
            value = jnp.zeros((80, big), f32)
            for n in range(s.ne):
                is_d = jnp.where(S.dates[n, 0:1, :] == float(d), 1.0, 0.0)
                is_d = jnp.concatenate([is_d] * (big // LANES), axis=1)
                value = value + is_d * st7[n, :, q * big : (q + 1) * big].astype(f32)
            orow[:, q, :] = value[0:cin]
        S.sgrad[d] = orow[...].astype(bf16)
    keep(S.sgrad, sgrad_h)

    ar("fblcihekjiflhkgj")
    while not all(it.finished() for it in reduced.values()):
        ar("abcdefghijklmn")
    for m in pending:
        m.wait_send()
    for copy in finals:
        copy.wait()


def finish_kernel(s, *refs):
    h1, h2, h3, hm_h, output_in, state_in, m1, v1, m2, v2 = refs[:10]
    (
        output, state_grad,
        enc_w, enc_b, g1o, s1o, proc_w, proc_b, g2o, s2o,
        up_w, up_b, down_w, down_b, dec_w, dec_b, m1o, v1o, m2o, v2o,
    ) = refs[10:30]
    (
        b1, b2, b3, enc_v, proc_v, up_v, down_v, dec_v, row_v, hm, out_v, state_v, means_v,
        *vectors, sem_in, sem_out,
    ) = refs[30:]
    c, ff, nb, cin, cj = s.c, s.ff, s.nb, s.cin, s.cj
    used1 = s.off_dec + nb * s.c5 * s.r80
    third = s.c5 * s.r641
    pieces = [(h2, b2, n * third, third) for n in range(nb)]
    pieces += [(h1, b1, 0, s.off_up), (h1, b1, s.off_up, s.off_dec - s.off_up)]
    pieces += [(h1, b1, s.off_dec, used1 - s.off_dec), (h3, b3, 0, nb * s.c5 * s.r80)]
    loads = [
        pltpu.make_async_copy(a.at[pl.ds(at, n)], b.at[pl.ds(at, n)], sem_in.at[i])
        for i, (a, b, at, n) in enumerate(pieces)
    ]
    passed = [(output_in, out_v, output), (state_in, state_v, state_grad)]
    passed += [
        (a, means_v.at[n], b) for n, (a, b) in enumerate(((m1, m1o), (v1, v1o), (m2, m2o), (v2, v2o)))
    ]
    small = pltpu.make_async_copy(hm_h, hm, sem_in.at[len(pieces)])
    small.start()
    for copy in loads:
        copy.start()
    early = [
        pltpu.make_async_copy(a, b, sem_in.at[len(pieces) + 1 + n]) for n, (a, b, _) in enumerate(passed)
    ]
    for copy in early:
        copy.start()
    stores = []

    def store(src, dst):
        copy = pltpu.make_async_copy(src, dst, sem_out.at[len(stores)])
        copy.start()
        stores.append(copy)

    small.wait()
    turned = hm[0:144, :].T

    def last_column(ref, slot, height, at):
        for t in range(-(-height // LANES)):
            n = min(LANES, height - t * LANES)
            ref[t * LANES : t * LANES + n, at : at + 1] = turned[0:n, slot * 6 + t : slot * 6 + t + 1]

    def widen(ref, src, base, pitch, tiles, lo, hi):
        for n in range(tiles):
            at = base + n * pitch
            ref[lo:hi, n * LANES : (n + 1) * LANES] = src[at + lo : at + hi, :].astype(f32)

    last = s.c5 * LANES
    half = up_to(c // 2, 16)
    cuts = (0, half, c)
    for kk in range(nb):
        ref = proc_v.at[kk]
        last_column(ref, MISC.proc_last + kk, c, last)
        loads[kk].wait()
        for lo, hi in zip(cuts, cuts[1:]):
            widen(ref, b2, kk * third, s.r641, s.c5, lo, hi)
            store(ref.at[pl.ds(lo, hi - lo)], proc_w.at[kk, pl.ds(lo, hi - lo)])
    for n, (ref, slot, base, to) in enumerate(
        ((down_v, MISC.down_last, 0, down_w), (up_v, MISC.up_last, s.off_up, up_w))
    ):
        for part in range(2):
            last_column(ref, slot + part, c, s.f10 * LANES + part)
        loads[nb + n].wait()
        for lo, hi in zip(cuts, cuts[1:]):
            widen(ref, b1, base, s.r641, s.f10, lo, hi)
            store(ref.at[pl.ds(lo, hi - lo)], to.at[pl.ds(lo, hi - lo)])
    loads[nb + 2].wait()
    loads[nb + 3].wait()
    for kk in range(nb):
        ref = dec_v.at[kk]
        last_column(ref, MISC.dec_last + kk, cin, last)
        widen(ref, b1, s.off_dec + kk * s.c5 * s.r80, s.r80, s.c5, 0, cin)
        ref = enc_v.at[kk]
        last_column(ref, MISC.enc_last + kk, cj, last)
        widen(ref, b3, kk * s.c5 * s.r80, s.r80, s.c5, 0, cj)
    for copy, (_, there, to) in zip(early, passed):
        copy.wait()
        store(there, to)
    store(dec_v, dec_w)
    store(enc_v, enc_w)

    def flat(ref, slots):
        at = 0
        for slot, width in slots:
            for piece in get_misc(hm, slot, width):
                n = piece.shape[1]
                row_v[0:1, at : at + n] = piece
                at += n
        there = vectors.pop()
        there[...] = row_v[0:1, 0:at].reshape(at)
        store(there, ref)

    for ref, slot in (
        (enc_b, MISC.enc_bias), (g1o, MISC.gain_one), (s1o, MISC.shift_one), (proc_b, MISC.proc_bias),
        (g2o, MISC.gain_two), (s2o, MISC.shift_two), (down_b, MISC.down_bias),
    ):
        flat(ref, [(slot, c)])
    flat(up_b, [(MISC.up_bias, 768), (MISC.up_bias + 1, ff - 768)])
    flat(dec_b, [(MISC.dec_bias, cin)])
    for copy in stores:
        copy.wait()


def per_device(s, *args):
    (
        state, noise, cot, slot_date, lon_reach, enc_taps, proc_taps, dec_taps,
        enc_weight, enc_bias, gain_one, shift_one, proc_weight, proc_bias, gain_two, shift_two,
        up_weight, up_bias, down_weight, down_bias, dec_weight, dec_bias,
    ) = args
    args = list(args)
    args[8] = jnp.swapaxes(enc_weight, 1, 2)
    args[16] = up_weight.T
    vm = pl.BlockSpec(memory_space=pltpu.VMEM)
    sm = pl.BlockSpec(memory_space=pltpu.SMEM)
    hbm = pl.BlockSpec(memory_space=pl.ANY)
    shapes = scratch_list(s)
    names = tuple(shapes)
    in_specs = [hbm] * 22
    sd = jax.ShapeDtypeStruct
    out_shape = [
        sd((s.rows[0], LANES), bf16),
        sd((s.rows[1], LANES), bf16),
        sd((s.rows[2], LANES), bf16),
        sd((s.rows[3], LANES), f32),
        sd((1, s.cin, s.full_rows, s.full_cols), bf16),
        sd((s.dates, s.cin, s.full_rows, s.full_cols), bf16),
    ] + [sd((1, s.c), f32)] * 4
    got = pl.pallas_call(
        functools.partial(main_kernel, s, names),
        out_shape=out_shape,
        in_specs=in_specs,
        out_specs=[hbm] * 10,
        scratch_shapes=list(shapes.values()),
        compiler_params=pltpu.CompilerParams(
            collective_id=0, has_side_effects=True, vmem_limit_bytes=60 * 2**20
        ),
        name="forecast",
    )(*args)
    c, ff, nb = s.c, s.ff, s.nb
    outs = [out_shape[4], out_shape[5]] + [
        sd((nb, s.cj, c), f32), sd((c,), f32), sd((c,), f32), sd((c,), f32),
        sd((nb, c, c), f32), sd((c,), f32), sd((c,), f32), sd((c,), f32),
        sd((c, ff), f32), sd((ff,), f32), sd((c, ff), f32), sd((c,), f32),
        sd((nb, s.cin, c), f32), sd((s.cin,), f32),
    ] + [sd((1, c), f32)] * 4
    V = pltpu.VMEM
    done = pl.pallas_call(
        functools.partial(finish_kernel, s),
        out_shape=outs,
        in_specs=[hbm] * 10,
        out_specs=[hbm] * len(outs),
        scratch_shapes=[
            V((s.rows[0], LANES), bf16), V((s.rows[1], LANES), bf16), V((s.rows[2], LANES), bf16),
            V((nb, s.cj, c), f32), V((nb, c, c), f32), V((c, ff), f32), V((c, ff), f32),
            V((nb, s.cin, c), f32), V((8, up_to(ff, LANES)), f32), V((s.rows[3], LANES), f32),
            V(out_shape[4].shape, bf16), V(out_shape[5].shape, bf16), V((4, 1, c), f32),
            V((s.cin,), f32), V((ff,), f32), *[V((c,), f32)] * 7,
            pltpu.SemaphoreType.DMA((16,)), pltpu.SemaphoreType.DMA((32,)),
        ],
        compiler_params=pltpu.CompilerParams(vmem_limit_bytes=60 * 2**20),
        name="finish",
    )(*got)
    done = list(done)
    done[2] = jnp.swapaxes(done[2], 1, 2)
    done[10] = done[10].T
    return tuple(done)


def solution(mesh):
    in_specs = (
        P(None, None, "lat", "lon"),
        P("ens", None, "lat", "lon"),
        P("ens", None, "lat", "lon"),
        P("ens"),
    ) + (P(),) * 18
    out_specs = (
        (P("ens", None, "lat", "lon"), P(None, None, "lat", "lon"))
        + (P(),) * 14
        + (P("ens", None),) * 4
    )

    def run(*args):
        s = Sizes(mesh, args[0].shape, args[1].shape, args[5].shape, args[8].shape, args[16].shape)
        return jax.shard_map(
            functools.partial(per_device, s),
            mesh=mesh,
            in_specs=in_specs,
            out_specs=out_specs,
            check_vma=False,
        )(*args)

    return run
```

```python
import functools
import types

import jax
import jax.numpy as jnp
from jax import lax
from jax.experimental import pallas as pl
from jax.experimental.pallas import tpu as pltpu
from jax.sharding import PartitionSpec as P

MESH = pl.DeviceIdType.MESH
f32 = jnp.float32
bf16 = jnp.bfloat16
i32 = jnp.int32
EPS = 1e-05
LANES = 128
AXES = ("ens", "lat", "lon")
BIT0, BIT1, LAT, LON = range(4)
ROUTE_X = (LAT, BIT0, BIT1, LON)
ROUTE_Y = (LAT, BIT1, BIT0, LON)
WSEM, OSEM, SEMS = range(3)
ROUTE_ZX = (LAT, LON, BIT0, BIT1)
ROUTE_ZY = (LAT, LON, BIT1, BIT0)
PIECES = dict(
    a=(0, 0), b=(0, 1), c=(0, 2), d=(1, 0), e=(1, 1), f=(1, 2),
    g=(2, 0), h=(2, 1), i=(3, 0), j=(3, 1), k=(4, 0), l=(5, 0), m=(2, 2), n=(3, 2),
)


def nn(a, b):
    return lax.dot_general(a, b, (((1,), (0,)), ((), ())), preferred_element_type=f32)


def nt(a, b):
    return lax.dot_general(a, b, (((1,), (1,)), ((), ())), preferred_element_type=f32)


def tn(a, b):
    return lax.dot_general(a, b, (((0,), (0,)), ((), ())), preferred_element_type=f32)


def up_to(n, m):
    return -(-n // m) * m


class Sizes:
    def __init__(self, mesh, state, noise, enc_taps, enc_weight, up_weight):
        self.ne, self.nl, self.nz = (mesh.shape[a] for a in AXES)
        self.dates, self.cin, self.full_rows, self.full_cols = state
        self.noise = noise[1]
        self.full_rows = state[2] // self.nl
        self.full_cols = state[3] // self.nz
        self.hr, self.hc = self.full_rows // 2, self.full_cols // 2
        assert self.hr == 2 and self.hc == LANES and self.ne == 4
        self.lat_total = enc_taps[1]
        self.nb = enc_taps[0]
        self.c = enc_weight[1]
        self.cj = enc_weight[2]
        self.ff = up_weight[0]
        self.px = self.hr * self.hc
        self.pixels = float(self.px * self.nl * self.nz)
        self.c5 = self.c // LANES
        self.f10 = self.ff // LANES
        self.r641 = up_to(self.c, 16)
        self.r80 = up_to(self.cj, 16)
        self.off_up = self.f10 * self.r641
        self.off_dec = self.off_up + self.f10 * self.r641
        used = (
            self.off_dec + self.nb * self.c5 * self.r80,
            self.nb * self.c5 * self.r641,
            self.nb * self.c5 * self.r80,
        )
        unit = 16 * self.nl * self.ne * self.nz
        self.rows = tuple(up_to(n, unit) for n in used) + (up_to(24 * 6, unit // 2),)
        self.chunks = {}

        def split(piece, buffer, lo, hi, third, last):
            units = (hi - lo) // unit
            last = last if units >= 3 * last else 0
            first = (units - last + 1) // 2
            at = lo
            for n, (count, route) in enumerate(
                ((first, ROUTE_X), (units - last - first, ROUTE_Y), (last, third))
            ):
                if count:
                    self.chunks[piece, n] = (buffer, at, count * unit, route)
                at += count * unit

        cut = self.off_up // unit * unit
        split(0, 0, 0, cut, ROUTE_ZX, 2)
        split(1, 0, cut, self.rows[0], ROUTE_ZY, 2)
        cut = 2 * self.c5 * self.r641 // unit * unit
        split(2, 1, 0, cut, ROUTE_ZX, 0)
        split(3, 1, cut, self.rows[1], ROUTE_ZY, 0)
        self.chunks[4, 0] = (2, 0, self.rows[2], ROUTE_X)
        self.chunks[5, 0] = (3, 0, self.rows[3], ROUTE_Y)
        self.group = self.nl * self.nz


def add_into(dst, at, sources, count):
    step = next(s for s in (256, 128, 64, 32, 16, 8) if count % s == 0)

    def body(n, carry):
        lo = pl.multiple_of(n * step, 8 if step == 8 else 16)
        there = pl.ds(pl.multiple_of(at + lo, 8 if step == 8 else 16), step)
        value = dst[there, :].astype(f32)
        for source in sources:
            value = value + source[pl.ds(lo, step), :].astype(f32)
        dst[there, :] = value.astype(dst.dtype)
        return carry

    lax.fori_loop(0, count // step, body, 0)


class Links:
    def __init__(self, z, sems=None):
        self.s = z
        self.sems = sems
        self.used = 0
        if sems is not None:
            self.e, self.l, self.z = (lax.axis_index(a) for a in AXES)

    def take(self):
        self.used += 1
        return self.used - 1

    def at(self, de, dl, dz):
        s = self.s
        return (
            lax.rem(self.e + (de + s.ne), s.ne),
            lax.rem(self.l + (dl + s.nl), s.nl),
            lax.rem(self.z + (dz + s.nz), s.nz),
        )

    def bit(self, which):
        return lax.rem(self.e // (1 << which), 2)

    def flip(self, which):
        return (self.e + (1 << which) * (1 - 2 * self.bit(which)), self.l, self.z)

    def has_up(self):
        return self.l > 0

    def has_down(self):
        return self.l < self.s.nl - 1


class Send:
    def __init__(self, links, src, dst, device, dl=0):
        self.links = links
        self.ids = (links.take(), links.take())
        self.what = (src, dst, device)
        self.dl = dl

    def copy(self):
        src, dst, device = self.what
        return pltpu.make_async_remote_copy(
            src_ref=src,
            dst_ref=dst,
            send_sem=self.links.sems.at[self.ids[0]],
            recv_sem=self.links.sems.at[self.ids[1]],
            device_id=device,
            device_id_type=MESH,
        )

    def under(self, sending, act):
        if self.dl == 0:
            act()
        else:
            up = (self.dl < 0) == sending
            pl.when(self.links.has_up() if up else self.links.has_down())(act)

    def start(self):
        self.under(True, lambda: self.copy().start())

    def wait_recv(self):
        self.under(False, lambda: self.copy().wait_recv())

    def wait_send(self):
        self.under(True, lambda: self.copy().wait_send())


class AllReduce:
    def __init__(self, links, partial, total, lo, rows, route, bufs, own_sem):
        self.k, self.g, self.h, self.route = links, partial, total, route
        self.bufs, self.own_sem = bufs, own_sem
        self.sent, self.waiting = [], []
        self.stage = 0
        self.base, self.part = [], []
        base, size = lo, rows
        for axis in route:
            size = size // self.count(links.s, axis)
            self.base.append(base)
            self.part.append(size)
            base = base + self.index(axis) * size
        self.base.append(base)
        self.last_stage = 2 * len(route)

    @staticmethod
    def count(s, axis):
        return {LAT: s.nl, LON: s.nz}.get(axis, 2)

    @staticmethod
    def shapes(s, rows, route, dtype):
        out = []
        for axis in route:
            n = AllReduce.count(s, axis)
            rows = rows // n
            out.append(pltpu.VMEM((n - 1, rows, LANES), dtype))
        return out

    def index(self, axis):
        k = self.k
        return {LAT: k.l, LON: k.z}[axis] if axis in (LAT, LON) else k.bit(axis)

    def others(self, axis):
        k, s = self.k, self.k.s
        if axis == LAT:
            devices = [k.at(0, d, 0) for d in range(1, s.nl)]
            return [(dev, dev[1], n) for n, dev in enumerate(devices)]
        if axis == LON:
            devices = [k.at(0, 0, d) for d in range(1, s.nz)]
            return [(dev, dev[2], n) for n, dev in enumerate(devices)]
        return [(k.flip(axis), 1 - k.bit(axis), 0)]

    def send(self, src, dst, device):
        m = Send(self.k, src, dst, device)
        m.start()
        self.sent.append(m)
        self.waiting.append(m)

    def step(self):
        g, h, route = self.g, self.h, self.route
        al = lambda v: pl.multiple_of(v, 8)
        stage, self.stage = self.stage, self.stage + 1
        for m in self.waiting:
            m.wait_recv()
        self.waiting = []
        depth = len(route)
        if 0 < stage <= depth:
            buf = self.bufs[stage - 1]
            add_into(g, al(self.base[stage]), [buf.at[n] for n in range(buf.shape[0])], self.part[stage - 1])
        if stage < depth:
            size = self.part[stage]
            for device, place, slot in self.others(route[stage]):
                there = pl.ds(al(self.base[stage] + place * size), size)
                self.send(g.at[there], self.bufs[stage].at[slot], device)
        elif stage < 2 * depth:
            level = 2 * depth - 1 - stage
            here = pl.ds(al(self.base[level + 1]), self.part[level])
            if stage == depth:
                self.own = pltpu.make_async_copy(g.at[here], h.at[here], self.own_sem)
                self.own.start()
            if stage == depth + 1:
                self.own.wait()
            source = g if stage == depth else h
            for device, _, _ in self.others(route[level]):
                self.send(source.at[here], h.at[here], device)
        else:
            for m in self.sent:
                m.wait_send()

    def finished(self):
        return self.stage > self.last_stage


class MISC:
    down_bias, up_bias, gain_two, shift_two, proc_bias, gain_one, shift_one, enc_bias = 0, 1, 3, 4, 5, 6, 7, 8
    up_last, down_last, proc_last, enc_last, dec_last, dec_bias = 9, 11, 13, 16, 19, 22


def put_misc(misc, slot, row):
    width = row.shape[1]
    for t in range(-(-width // LANES)):
        lo, hi = t * LANES, min(width, (t + 1) * LANES)
        misc[slot * 6 + t : slot * 6 + t + 1, 0 : hi - lo] = row[:, lo:hi]


def get_misc(misc, slot, width):
    parts = []
    for t in range(-(-width // LANES)):
        lo, hi = t * LANES, min(width, (t + 1) * LANES)
        parts.append(misc[slot * 6 + t : slot * 6 + t + 1, 0 : hi - lo])
    return parts


def scratch_list(s):
    c, ff, px = s.c, s.ff, s.px
    big = s.full_cols
    wide = 8 * big + LANES
    V = pltpu.VMEM
    shapes = dict(
        state=V((s.dates, s.cin, s.full_rows, big), bf16),
        noise=V((1, s.noise, s.full_rows, big), bf16),
        cot=V((1, s.cin, s.full_rows, big), bf16),
        eb_v=V((c,), f32), gain1=V((c,), f32), shift1=V((c,), f32), pb=V((c,), f32), gain2=V((c,), f32),
        shift2=V((c,), f32), ub=V((ff,), f32), db=V((c,), f32), cb=V((s.cin,), f32),
        out=V((1, s.cin, s.full_rows, big), bf16),
        sgrad=V((s.dates, s.cin, s.full_rows, big), bf16),
        means=V((4, 1, c), f32),
        date=pltpu.SMEM((1,), i32), reach=pltpu.SMEM((s.lat_total,), i32),
        enc_taps=pltpu.SMEM((s.nb, s.lat_total, 25), f32), proc_taps=pltpu.SMEM((s.nb, s.lat_total, 25), f32),
        dec_taps=pltpu.SMEM((s.nb, 2 * s.lat_total, 9), f32),
        xin=V((160, s.full_rows, big), f32),
        xj=V((160, 8 * big), bf16),
        eb=V((2, 8, 160), f32),
        eslot=V((6, 8, 160), f32),
        xe=V((48, 160), bf16),
        em=V((2, s.nb * LANES, 5 * big + 48), bf16),
        dm=V((2, s.nb * LANES, 6 * big + 48), bf16),
        tm=V((s.nb * px, 6 * LANES + 48), bf16),
        ew=V((s.nb, s.cj, c), bf16),
        pw=V((s.nb, c, c), bf16),
        uw=V((c, ff), bf16),
        dw=V((c, ff), bf16),
        cw=V((s.nb, s.cin, c), bf16),
        filte=V((s.nb, px, s.cj), bf16),
        hx=V((6 * LANES + 48, c), f32),
        nx=V((6 * LANES + 48, c), bf16),
        pe=V((2, 4, c), f32),
        he=V((6, 4, c), f32),
        ce=V((6, 4, c), f32),
        filt=V((s.nb * px, c), bf16),
        h1=V((px, c), f32),
        n2=V((px, c), bf16),
        hp=V((px, ff), f32),
        ag=V((px, ff), f32),
        act=V((px, ff), bf16),
        hg=V((px, ff), bf16),
        n2t=V((c, px), bf16),
        h2=V((px, c), bf16),
        pgr=V((s.nb, px, s.cin), bf16),
        projt=V((2, 80, s.nb * LANES), bf16),
        partt=V((2, 80, s.nb * LANES), bf16),
        two=V((px, c), f32),
        mg=V((px, c), bf16),
        mgt=V((c, px), bf16),
        ntg=V((px, c), f32),
        one=V((px, c), f32),
        br=V((px, c), bf16),
        brt=V((c, px), bf16),
        fg=V((s.nb * px, c), bf16),
        con=V((6 * LANES + 48, c), f32),
        rup=V((px, c), f32),
        rdn=V((px, c), f32),
        reg=V((6, 4, c), f32),
        zg=V((px, c), bf16),
        sgx=V((160, wide), f32),
        sgb=V((160, 4 * big), bf16),
        sgu=V((160, 2 * big), bf16),
        sgd=V((160, 2 * big), bf16),
        sgn=V((6, 8, 160), f32),
        sge=V((6, 8, 160), f32),
        sgt=V((LANES, 160), f32),
        orow=V((s.cin, s.full_rows, big), f32),
        st7=V((s.ne, 80, 4 * big), bf16),
        dates=V((s.ne, 8, LANES), f32),
        cbt=V((8, LANES), f32),
        slat=V((4, s.nl, 2, c), f32),
        slon=V((4, s.nz, 2, c), f32),
        sall=V((4, s.group if s.group <= 16 else 1, 2, c), f32),
        tmt=V((6 * LANES + 48, s.nb * px), bf16),
        g1=V((s.rows[0], LANES), bf16),
        g2=V((s.rows[1], LANES), bf16),
        g3=V((s.rows[2], LANES), bf16),
        gm=V((s.rows[3], LANES), f32),
    )
    for name, (buffer, _, rows, route) in s.chunks.items():
        kinds = AllReduce.shapes(s, rows, route, f32 if buffer == 3 else bf16)
        for j, kind in enumerate(kinds):
            shapes[name, j] = kind
    shapes[WSEM] = pltpu.SemaphoreType.DMA((28,))
    shapes[OSEM] = pltpu.SemaphoreType.DMA((len(s.chunks),))
    shapes[SEMS] = pltpu.SemaphoreType.DMA((sem_count(s),))
    return shapes


def sem_count(s):
    total = len(s.chunks) * 2 * 2 * (s.nl - 1 + 1 + 1 + s.nz - 1)
    total += 2 * 4 * 8 + 2 * (s.ne - 1) + 2 * 6
    total += 4 * 2 * (s.group - 1 if s.group <= 16 else s.nl - 1 + s.nz - 1)
    return total


def main_kernel(s, names, *refs):
    n_in, n_out = 22, 10
    (
        state_h, noise_h, cot_h, date_h, reach_h, enc_taps_h, proc_taps_h, dec_taps_h,
        ew_h, eb_h, gain1_h, shift1_h, pw_h, pb_h, gain2_h, shift2_h, uw_h, ub_h, dw_h, db_h, cw_h, cb_h,
    ) = refs[:n_in]
    h1o, h2o, h3o, hmo, out_h, sgrad_h, m1_h, v1_h, m2_h, v2_h = refs[n_in : n_in + n_out]
    table = dict(zip(names, refs[n_in + n_out :]))
    S = types.SimpleNamespace(**{n: r for n, r in table.items() if isinstance(n, str)})
    sems = table[SEMS]
    k = Links(s, sems)
    c, ff, px, nb, cin, cj = s.c, s.ff, s.px, s.nb, s.cin, s.cj
    big = s.full_cols
    l = k.l
    row0 = l * s.hr
    edge0 = 8 * big

    offsets = {(d, 0, 0) for d in range(1, s.ne)}
    if s.group <= 16:
        offsets |= {(0, a, b) for a in range(s.nl) for b in range(s.nz)} - {(0, 0, 0)}
    else:
        offsets |= {(0, d, 0) for d in range(1, s.nl)} | {(0, 0, d) for d in range(1, s.nz)}
    offsets |= {(0, a % s.nl, b % s.nz) for a in (1, -1) for b in (1, -1)}
    offsets = sorted(offsets)
    barrier = pltpu.get_barrier_semaphore()
    for o in offsets:
        pl.semaphore_signal(barrier, 1, device_id=k.at(*o), device_id_type=MESH)

    def fetch(n, src, to):
        copy = pltpu.make_async_copy(src, to, table[WSEM].at[n])
        copy.start()
        return copy

    date_ref, reach = S.date, S.reach
    enc_taps, proc_taps, dec_taps = S.enc_taps, S.proc_taps, S.dec_taps
    scalars = [
        fetch(23 + n, *pair)
        for n, pair in enumerate(
            (
                (date_h, date_ref), (reach_h, reach), (enc_taps_h, enc_taps),
                (proc_taps_h, proc_taps), (dec_taps_h, dec_taps),
            )
        )
    ]
    state, noise, cot = S.state, S.noise, S.cot
    fields = [fetch(n, *pair) for n, pair in enumerate(((state_h, state), (noise_h, noise), (cot_h, cot)))]
    eb, gain1, shift1, pb, gain2, shift2 = S.eb_v, S.gain1, S.shift1, S.pb, S.gain2, S.shift2
    ub, db, cb = S.ub, S.db, S.cb
    vectors = [
        fetch(3 + n, *pair)
        for n, pair in enumerate(
            (
                (eb_h, eb), (gain1_h, gain1), (shift1_h, shift1), (pb_h, pb), (gain2_h, gain2),
                (shift2_h, shift2), (ub_h, ub), (db_h, db), (cb_h, cb),
            )
        )
    ]
    loads = types.SimpleNamespace()
    loads.ew, loads.pw, loads.cw, loads.dw, loads.uw = [
        fetch(12 + n, *pair)
        for n, pair in enumerate(
            ((ew_h, S.ew), (pw_h, S.pw), (cw_h, S.cw), (dw_h, S.dw), (uw_h, S.uw))
        )
    ]
    finals = []

    def keep(src, to):
        copy = pltpu.make_async_copy(src, to, table[WSEM].at[17 + len(finals)])
        copy.start()
        finals.append(copy)

    for copy in fields + scalars:
        copy.wait()

    date = date_ref[0]
    live = jnp.where(date >= 0, 1.0, 0.0).astype(f32)
    xin, xj = S.xin, S.xj
    picked = jnp.zeros((cin, s.full_rows, big), f32)
    for d in range(s.dates):
        picked = picked + state[d].astype(f32) * jnp.where(date == d, 1.0, 0.0).astype(f32)
    xin[0:cin] = picked
    xin[cin:cj] = noise[0].astype(f32)
    xin[80 : 80 + cin] = cot[0].astype(f32) * live
    xin[80 + cin : 160] = jnp.zeros((160 - 80 - cin, s.full_rows, big), f32)
    lane = lax.broadcasted_iota(i32, (160, LANES), 1)
    ends = jnp.zeros((160, LANES), f32)
    for q in range(4):
        row = xin[:, q, :]
        xj[:, (2 + q) * big : (3 + q) * big] = row.astype(bf16)
        moved = pltpu.roll(row[:, 0:LANES], q * 2, 1)
        ends = jnp.where((lane >> 1) == q, moved, ends)
        moved = pltpu.roll(row[:, big - LANES : big], q * 2 + 10, 1)
        ends = jnp.where((lane >> 1) == q + 4, moved, ends)
    turned = ends.T
    S.eb[0] = turned[0:8, :]
    S.eb[1] = turned[8:16, :]
    S.dates[k.e] = jnp.full((8, LANES), date.astype(f32), f32)

    @pl.when(jnp.logical_not(k.has_up()))
    def _():
        xj[:, 0 : 2 * big] = jnp.zeros((160, 2 * big), bf16)
        S.hx[0:px] = jnp.zeros((px, c), f32)
        for side in range(2):
            S.he[side] = jnp.zeros((4, c), f32)

    @pl.when(jnp.logical_not(k.has_down()))
    def _():
        xj[:, 6 * big : 8 * big] = jnp.zeros((160, 2 * big), bf16)
        S.hx[2 * px : 3 * px] = jnp.zeros((px, c), f32)
        for side in range(2):
            S.he[4 + side] = jnp.zeros((4, c), f32)

    pl.semaphore_wait(barrier, len(offsets))

    totals = (h1o, h2o, h3o, hmo)
    reduced = {}
    for n, (name, (buffer, lo, rows, route)) in enumerate(s.chunks.items()):
        bufs = [table[name, j] for j in range(len(route))]
        partial = (S.g1, S.g2, S.g3, S.gm)[buffer]
        reduced[name] = AllReduce(k, partial, totals[buffer], lo, rows, route, bufs, table[OSEM].at[n])

    def ar(letters):
        for letter in letters:
            it = reduced.get(PIECES[letter])
            if it is not None and not it.finished():
                it.step()

    pending = []

    def start(sends):
        for m in sends:
            m.start()
        pending.extend(sends)
        return sends

    def arrive(sends):
        for m in sends:
            m.wait_recv()

    dirs = [(dl, ds) for dl in (-1, 0, 1) for ds in (-1, 1)]

    def slot_of(dl, ds):
        return (1 - dl) * 2 + (1 - ds) // 2

    sends = [
        Send(k, xj.at[:, pl.ds(2 * big, 2 * big)], xj.at[:, pl.ds(6 * big, 2 * big)], k.at(0, -1, 0), -1),
        Send(k, xj.at[:, pl.ds(4 * big, 2 * big)], xj.at[:, pl.ds(0, 2 * big)], k.at(0, 1, 0), 1),
    ]
    for dl, ds in dirs:
        sends.append(
            Send(k, S.eb.at[(ds + 1) // 2], S.eslot.at[slot_of(dl, ds)], k.at(0, dl, ds), dl)
        )
    first_halo = start(sends)
    date_sends = start(
        [
            Send(k, S.dates.at[k.e], S.dates.at[k.e], k.at(d, 0, 0))
            for d in range(1, s.ne)
        ]
    )

    gm = S.gm
    gm[0:144] = jnp.zeros((144, LANES), f32)

    def band(shape, column_of):
        rows = lax.broadcasted_iota(i32, shape, 0)
        cols = lax.broadcasted_iota(i32, shape, 1)
        return column_of(rows, cols)

    def pick(d, table, like):
        value = jnp.zeros(like, f32)
        for key, scalar in table:
            value = jnp.where(d == key, scalar, value)
        return value

    def inside(grow, total):
        return jnp.logical_and(grow >= 0, grow < total)

    def edge_lane(shape):
        at = lax.broadcasted_iota(i32, shape, 1)
        slot, q, m = at >> 3, (at & 7) >> 1, at & 1
        r = q + 2 + 4 * ((slot >> 1) - 1)
        return r, jnp.where((slot & 1) == 0, m - 2, big + m), at

    def build_encoder():
        em = S.em
        d_main = band((LANES, big), lambda j, J: J - 2 * j)
        r, J, at = edge_lane((16, 48))
        j = lax.broadcasted_iota(i32, (16, 48), 0)
        codes = []
        for start_row in (0, LANES - 16):
            d = J - 2 * (j + start_row)
            codes.append(r * 1024 + d)
        for i in range(2):
            reached = reach[row0 + i]
            edges = [[jnp.zeros((16, 48), f32) for _ in range(2)] for _ in range(nb)]
            for a in range(-2, 3):
                r_in = 2 * i + a + 2
                ok = inside(4 * l + r_in - 2, 2 * s.lat_total)
                masks = [d_main == b for b in range(-2, 3)]
                for kk in range(nb):
                    value = jnp.zeros((LANES, big), f32)
                    for b in range(-2, 3):
                        tap = enc_taps[kk, row0 + i, 5 * (a + 2) + b + 2]
                        tap = jnp.where(jnp.logical_and(ok, abs(b) <= reached), tap, 0.0)
                        value = jnp.where(masks[b + 2], tap, value)
                        for part in range(2):
                            edges[kk][part] = jnp.where(
                                codes[part] == r_in * 1024 + b, tap, edges[kk][part]
                            )
                    em[i, kk * LANES : (kk + 1) * LANES, (a + 2) * big : (a + 3) * big] = value.astype(bf16)
            for kk in range(nb):
                lo = kk * LANES
                em[i, lo : lo + 16, 5 * big :] = edges[kk][0].astype(bf16)
                em[i, lo + 16 : lo + LANES - 16, 5 * big :] = jnp.zeros((LANES - 32, 48), bf16)
                em[i, lo + LANES - 16 : lo + LANES, 5 * big :] = edges[kk][1].astype(bf16)

    def build_decoder():
        dm = S.dm
        d_main = band((LANES, big), lambda j, J: j - (J >> 1))
        r, J, at = edge_lane((16, 48))
        j = lax.broadcasted_iota(i32, (16, 48), 0)
        codes = []
        for start_row in (0, LANES - 16):
            d = (j + start_row) - (J >> 1)
            codes.append(r * 1024 + d)
        for i in range(2):
            edges = [[jnp.zeros((16, 48), f32) for _ in range(2)] for _ in range(nb)]
            for n in range(6):
                r_in = 2 * i + n
                a = i + 1 - r_in // 2
                full = 4 * l + r_in - 2
                ok = inside(full, 2 * s.lat_total)
                full = jnp.clip(full, 0, 2 * s.lat_total - 1)
                reached = reach[full // 2] - 1
                masks = [d_main == b for b in range(-1, 2)]
                for kk in range(nb):
                    value = jnp.zeros((LANES, big), f32)
                    for b in range(-1, 2):
                        tap = dec_taps[kk, full, 3 * (a + 1) + b + 1]
                        tap = jnp.where(jnp.logical_and(ok, abs(b) <= reached), tap, 0.0)
                        value = jnp.where(masks[b + 1], tap, value)
                        for part in range(2):
                            edges[kk][part] = jnp.where(
                                codes[part] == r_in * 1024 + b, tap, edges[kk][part]
                            )
                    dm[i, kk * LANES : (kk + 1) * LANES, n * big : (n + 1) * big] = value.astype(bf16)
            for kk in range(nb):
                lo = kk * LANES
                dm[i, lo : lo + 16, 6 * big :] = edges[kk][0].astype(bf16)
                dm[i, lo + 16 : lo + LANES - 16, 6 * big :] = jnp.zeros((LANES - 32, 48), bf16)
                dm[i, lo + LANES - 16 : lo + LANES, 6 * big :] = edges[kk][1].astype(bf16)

    def build_processor():
        tm = S.tm
        d_main = band((LANES, LANES), lambda j, J: J - j)
        at = lax.broadcasted_iota(i32, (16, 48), 1)
        slot, idx = at >> 3, at & 7
        r = 2 * (slot >> 1) + (idx >> 1)
        m = idx & 1
        J = jnp.where((slot & 1) == 0, m - 2, LANES + m)
        j = lax.broadcasted_iota(i32, (16, 48), 0)
        codes = []
        for start_row in (0, LANES - 16):
            d = J - (j + start_row)
            codes.append(jnp.where(idx < 4, r * 1024 + d, -5000))
        for i in range(2):
            reached = reach[row0 + i]
            edges = [[jnp.zeros((16, 48), f32) for _ in range(2)] for _ in range(nb)]
            for r_in in range(6):
                a = r_in - 2 - i
                if abs(a) > 2:
                    for kk in range(nb):
                        lo = kk * px + i * LANES
                        tm[lo : lo + LANES, r_in * LANES : (r_in + 1) * LANES] = jnp.zeros((LANES, LANES), bf16)
                    continue
                ok = inside(row0 + r_in - 2, s.lat_total)
                masks = [d_main == b for b in range(-2, 3)]
                for kk in range(nb):
                    value = jnp.zeros((LANES, LANES), f32)
                    for b in range(-2, 3):
                        tap = proc_taps[kk, row0 + i, 5 * (a + 2) + b + 2]
                        tap = jnp.where(jnp.logical_and(ok, abs(b) <= reached), tap, 0.0)
                        value = jnp.where(masks[b + 2], tap, value)
                        for part in range(2):
                            edges[kk][part] = jnp.where(
                                codes[part] == r_in * 1024 + b, tap, edges[kk][part]
                            )
                    lo = kk * px + i * LANES
                    tm[lo : lo + LANES, r_in * LANES : (r_in + 1) * LANES] = value.astype(bf16)
            for kk in range(nb):
                lo = kk * px + i * LANES
                tm[lo : lo + 16, 768:816] = edges[kk][0].astype(bf16)
                tm[lo + 16 : lo + LANES - 16, 768:816] = jnp.zeros((LANES - 32, 48), bf16)
                tm[lo + LANES - 16 : lo + LANES, 768:816] = edges[kk][1].astype(bf16)

    slat, slon = S.slat, S.slon

    def fold(values, kind, count):
        total_a, total_b = values[0]
        for a, b in values[1:]:
            total_a = total_a + a
            total_b = total_b + b
        if kind:
            total_a = total_a * (1.0 / len(values))
            for a, b in values:
                total_b = total_b + (a - total_a) * (a - total_a) * count
        return total_a, total_b

    single = s.group <= 16
    sall = S.sall
    place = k.l * s.nz + k.z

    def stat_start(rd, a, b):
        if single:
            sall[rd, place, 0:1, :] = a
            sall[rd, place, 1:2, :] = b
            others = [(0, m, n) for n in range(s.nz) for m in range(s.nl) if m or n]
            return start(
                [Send(k, sall.at[rd, place], sall.at[rd, place], k.at(*o)) for o in others]
            )
        slat[rd, k.l, 0:1, :] = a
        slat[rd, k.l, 1:2, :] = b
        return start(
            [
                Send(k, slat.at[rd, k.l], slat.at[rd, k.l], k.at(0, d, 0))
                for d in range(1, s.nl)
            ]
        )

    def stat_middle(rd, sends, kind):
        if single:
            return sends
        arrive(sends)
        values = [(slat[rd, n, 0:1, :], slat[rd, n, 1:2, :]) for n in range(s.nl)]
        a, b = fold(values, kind, float(px))
        slon[rd, k.z, 0:1, :] = a
        slon[rd, k.z, 1:2, :] = b
        return start(
            [
                Send(k, slon.at[rd, k.z], slon.at[rd, k.z], k.at(0, 0, d))
                for d in range(1, s.nz)
            ]
        )

    def stat_end(rd, sends, kind):
        arrive(sends)
        if single:
            values = [(sall[rd, n, 0:1, :], sall[rd, n, 1:2, :]) for n in range(s.group)]
            return fold(values, kind, float(px))
        values = [(slon[rd, n, 0:1, :], slon[rd, n, 1:2, :]) for n in range(s.nz)]
        return fold(values, kind, float(px * s.nl))

    def moments(values):
        mean = jnp.sum(values, axis=0, keepdims=True) * (1.0 / px)
        centred = values - mean
        return mean, jnp.sum(centred * centred, axis=0, keepdims=True)

    def vec(ref):
        n = ref.shape[0]
        return ref[...].reshape(1, n)

    build_encoder()
    build_decoder()
    build_processor()
    S.tmt[...] = S.tm[...].T

    arrive(first_halo)
    def absent(slot):
        return pl.when(jnp.logical_not(k.has_up() if slot < 2 else k.has_down()))

    for slot in (0, 1, 4, 5):
        @absent(slot)
        def _():
            S.eslot[slot] = jnp.zeros((8, 160), f32)

    xe = S.xe
    for slot in range(0, 6, 2):
        pair = jnp.concatenate([S.eslot[slot], S.eslot[slot + 1]], axis=0)
        xe[slot * 8 : slot * 8 + 16, :] = pair.astype(bf16)

    filte, hx = S.filte, S.hx
    for i in range(2):
        em = S.em
        got = nt(em[i, :, 0 : 5 * big], xj[0:80, 2 * i * big : (2 * i + 5) * big])
        got = got + nn(em[i, :, 5 * big :], xe[:, 0:80])
        for kk in range(nb):
            filte[kk, i * LANES : (i + 1) * LANES, :] = got[kk * LANES : (kk + 1) * LANES, 0:cj].astype(bf16)
    for copy in vectors:
        copy.wait()
    loads.ew.wait()
    h0 = vec(eb) + jnp.zeros((px, c), f32)
    for kk in range(nb):
        h0 = h0 + nn(filte[kk], S.ew[kk])
    hx[px : 2 * px, :] = h0
    own = slice(px, 2 * px)
    h0 = hx[own, :]
    stat_a = stat_start(0, *moments(h0))
    pe = S.pe
    for side, col in ((0, 0), (1, LANES - 2)):
        for q in range(2):
            lo = px + q * LANES + col
            pe[side, 2 * q : 2 * q + 2, :] = hx[lo : lo + 2, :]
    sends = [
        Send(k, hx.at[pl.ds(px, px)], hx.at[pl.ds(2 * px, px)], k.at(0, -1, 0), -1),
        Send(k, hx.at[pl.ds(px, px)], hx.at[pl.ds(0, px)], k.at(0, 1, 0), 1),
    ]
    for dl, ds in dirs:
        sends.append(
            Send(
                k,
                pe.at[(ds + 1) // 2],
                S.he.at[slot_of(dl, ds)],
                k.at(0, dl, ds),
                dl,
            )
        )
    zero_halo = start(sends)
    stat_a = stat_middle(0, stat_a, True)

    dm, pgr = S.dm, S.pgr
    for i in range(2):
        got = nt(dm[i, :, 0 : 6 * big], xj[80 : 80 + 80, 2 * i * big : (2 * i + 6) * big])
        got = got + nn(dm[i, :, 6 * big :], xe[:, 80:160])
        for kk in range(nb):
            pgr[kk, i * LANES : (i + 1) * LANES, :] = got[kk * LANES : (kk + 1) * LANES, 0:cin].astype(bf16)
    ones = jnp.ones((16, 4 * big), bf16)
    put_misc(gm, MISC.dec_bias, nt(ones, xj[80:160, 2 * big : 6 * big])[0:1, 0:cin])

    loads.cw.wait()
    two, mg = S.two, S.mg
    acc = nn(pgr[0], S.cw[0])
    for kk in range(1, nb):
        acc = acc + nn(pgr[kk], S.cw[kk])
    two[...] = acc
    mg[...] = acc.astype(bf16)

    mean1, m2 = stat_end(0, stat_a, True)
    var1 = m2 * (1.0 / s.pixels)
    rstd1 = lax.rsqrt(var1 + EPS)
    S.means[0] = mean1 * live
    S.means[1] = var1 * live
    keep(S.means.at[0], m1_h)
    keep(S.means.at[1], v1_h)
    arrive(zero_halo)
    for slot in range(6):
        lo = 768 + slot * 8
        hx[lo : lo + 8, :] = jnp.concatenate([S.he[slot], jnp.zeros((4, c), f32)], axis=0)
    nx = S.nx
    scale1 = rstd1 * vec(gain1)
    bias1 = vec(shift1)

    def norm_rows(n, carry):
        here = pl.ds(pl.multiple_of(n * 48, 16), 48)
        nx[here, :] = ((hx[here, :] - mean1) * scale1 + bias1).astype(bf16)
        return carry

    lax.fori_loop(0, 17, norm_rows, 0)

    filt, tm = S.filt, S.tm
    loads.pw.wait()
    h1 = S.h1
    acc = hx[own, :] + vec(pb)
    for kk in range(nb):
        here = slice(kk * px, (kk + 1) * px)
        filt[here, :] = nn(tm[here, :], nx[...]).astype(bf16)
        acc = acc + nt(filt[here, :], S.pw[kk])
    h1[...] = acc
    stat_b = stat_start(1, *moments(h1[...]))
    stat_b = stat_middle(1, stat_b, True)
    loads.dw.wait()
    ag, hp = S.ag, S.hp
    ag[...] = nn(mg[...], S.dw[...])
    S.mgt[...] = mg[...].T
    put_misc(gm, MISC.down_bias, jnp.sum(mg[...].astype(f32), axis=0, keepdims=True))
    mean2, m2 = stat_end(1, stat_b, True)
    var2 = m2 * (1.0 / s.pixels)
    rstd2 = lax.rsqrt(var2 + EPS)
    S.means[2] = mean2 * live
    S.means[3] = var2 * live
    keep(S.means.at[2], m2_h)
    keep(S.means.at[3], v2_h)
    scale2 = rstd2 * vec(gain2)
    bias2 = vec(shift2)
    n2 = S.n2

    def norm_two_rows(n, carry):
        here = pl.ds(pl.multiple_of(n * 32, 16), 32)
        n2[here, :] = ((h1[here, :] - mean2) * scale2 + bias2).astype(bf16)
        return carry

    lax.fori_loop(0, px // 32, norm_two_rows, 0)

    loads.uw.wait()
    hp[...] = nn(n2[...], S.uw[...])
    act, hg = S.act, S.hg
    ubias = vec(ub)
    root = 0.7978845608028654

    def gelu_rows(n, carry):
        here = pl.ds(pl.multiple_of(n * 16, 16), 16)
        v = hp[here, :] + ubias
        sq = v * v
        t = jnp.tanh(v * (root + (0.044715 * root) * sq))
        part = 0.5 * t + 0.5
        active = v * part
        act[here, :] = active.astype(bf16)
        slope = part + active * (1.0 - part) * (2.0 * root + (6.0 * 0.044715 * root) * sq)
        hg[here, :] = (slope * ag[here, :]).astype(bf16)
        return carry

    lax.fori_loop(0, px // 16, gelu_rows, 0)
    g1 = S.g1
    cols = [(lo, min(256, s.c5 * LANES - lo)) for lo in range(0, s.c5 * LANES, 256)]

    def spread(g, off, height, pitch, value, lo, width):
        for n in range(width // LANES):
            at = off + (lo // LANES + n) * pitch
            g[at : at + height, :] = value[:, n * LANES : (n + 1) * LANES].astype(bf16)

    for lo in range(0, s.f10 * LANES, 256):
        spread(g1, 0, c, s.r641, nn(S.mgt[...], act[:, lo : lo + 256]), lo, 256)
    ar("ba")
    S.n2t[...] = n2[...].T
    for lo in range(0, s.f10 * LANES, 256):
        spread(g1, s.off_up, c, s.r641, nn(S.n2t[...], hg[:, lo : lo + 256]), lo, 256)
    h2 = S.h2
    h2[...] = (h1[...] + nt(act[...], S.dw[...]) + vec(db)).astype(bf16)
    for kk in range(nb):
        got = tn(pgr[kk], h2[:, 0 : s.c5 * LANES])
        spread(g1, s.off_dec + kk * s.c5 * s.r80, cin, s.r80, got, 0, s.c5 * LANES)
    ar("bceafd")
    ntg = S.ntg
    ntg[...] = nt(hg[...], S.uw[...])
    grad = ntg[...]
    standard = (h1[...] - mean2) * rstd2
    sum_a = jnp.sum(grad, axis=0, keepdims=True)
    sum_b = jnp.sum(grad * standard, axis=0, keepdims=True)
    put_misc(gm, MISC.shift_two, sum_a)
    put_misc(gm, MISC.gain_two, sum_b)
    stat_c = stat_start(2, sum_a, sum_b)

    ar("ecdfb")
    stat_c = stat_middle(2, stat_c, False)

    def weighted(ref, column):
        return jnp.sum(ref.astype(f32) * column.astype(f32), axis=0, keepdims=True)

    def put_long(slot, row):
        put_misc(gm, slot, row[:, 0:768])
        put_misc(gm, slot + 1, row[:, 768:])

    def misc_one():
        put_long(MISC.up_bias, jnp.sum(hg[...].astype(f32), axis=0, keepdims=True))
        for n in range(2):
            at = s.f10 * LANES + n
            put_misc(gm, MISC.up_last + n, weighted(n2[...], hg[:, at : at + 1]))
            put_misc(gm, MISC.down_last + n, weighted(mg[...], act[:, at : at + 1]))
        for kk in range(nb):
            put_misc(gm, MISC.dec_last + kk, weighted(pgr[kk], h2[:, c - 1 : c]))

    sum_a, sum_b = stat_end(2, stat_c, False)
    g_two = vec(gain2)
    part_a = g_two * sum_a * (1.0 / s.pixels)
    part_b = g_two * sum_b * (1.0 / s.pixels)
    one, br = S.one, S.br

    def one_rows(n, carry):
        here = pl.ds(pl.multiple_of(n * 32, 16), 32)
        standard = (h1[here, :] - mean2) * rstd2
        value = rstd2 * (g_two * ntg[here, :] - part_a - standard * part_b) + two[here, :]
        one[here, :] = value
        br[here, :] = value.astype(bf16)
        return carry

    lax.fori_loop(0, px // 32, one_rows, 0)
    ar("a")
    fg = S.fg
    for kk in range(nb):
        fg[kk * px : (kk + 1) * px, :] = nn(br[...], S.pw[kk]).astype(bf16)
    con = S.con
    con[...] = nn(S.tmt[...], fg[...])

    def sum_rows(n, carry):
        here = pl.ds(pl.multiple_of(n * 48, 16), 48)
        value = con[here, :]
        standard = (hx[here, :] - mean1) * rstd1
        return (
            carry[0] + jnp.sum(value, axis=0, keepdims=True),
            carry[1] + jnp.sum(value * standard, axis=0, keepdims=True),
        )

    zero_row = jnp.zeros((1, c), f32)
    sum_a, sum_b = lax.fori_loop(0, 17, sum_rows, (zero_row, zero_row))
    put_misc(gm, MISC.shift_one, sum_a)
    put_misc(gm, MISC.gain_one, sum_b)
    stat_d = stat_start(3, sum_a, sum_b)
    for slot in range(6):
        S.ce[slot] = con[768 + slot * 8 : 772 + slot * 8, :]
    sends = [
        Send(k, con.at[pl.ds(0, px)], S.rdn, k.at(0, -1, 0), -1),
        Send(k, con.at[pl.ds(2 * px, px)], S.rup, k.at(0, 1, 0), 1),
    ]
    for dl, ds in dirs:
        mine = (dl + 1) * 2 + (ds + 1) // 2
        sends.append(
            Send(
                k,
                S.ce.at[mine],
                S.reg.at[slot_of(dl, ds)],
                k.at(0, dl, ds),
                dl,
            )
        )
    back_halo = start(sends)
    g2 = S.g2
    S.brt[...] = br[...].T
    ar("e")
    for kk in range(nb):
        if kk == 1:
            stat_d = stat_middle(3, stat_d, False)
        for lo, width in cols:
            got = nn(S.brt[...], filt[kk * px : (kk + 1) * px, lo : lo + width])
            spread(g2, kk * s.c5 * s.r641, c, s.r641, got, lo, width)
        if kk == 1:
            ar("agdhb")
    ar("igh")

    arrive(back_halo)
    ar("e")
    ng = ntg
    ng[...] = con[own, :]

    @pl.when(k.has_up())
    def _():
        ng[...] = ng[...] + S.rup[...]

    @pl.when(k.has_down())
    def _():
        ng[...] = ng[...] + S.rdn[...]

    def add_edges(sl):
        for ss in (-1, 1):
            got = S.reg.at[(sl + 1) * 2 + (ss + 1) // 2]
            col = 0 if ss == -1 else LANES - 2
            for q in range(2):
                lo = q * LANES + col
                ng[lo : lo + 2, :] = ng[lo : lo + 2, :] + got[2 * q : 2 * q + 2, :]

    add_edges(0)
    pl.when(k.has_up())(lambda: add_edges(-1))
    pl.when(k.has_down())(lambda: add_edges(1))
    sum_a, sum_b = stat_end(3, stat_d, False)
    g_one = vec(gain1)
    part_a1 = g_one * sum_a * (1.0 / s.pixels)
    part_b1 = g_one * sum_b * (1.0 / s.pixels)
    zg = S.zg

    def zero_rows(n, carry):
        here = pl.ds(pl.multiple_of(n * 32, 16), 32)
        there = pl.ds(pl.multiple_of(px + n * 32, 16), 32)
        standard = (hx[there, :] - mean1) * rstd1
        value = rstd1 * (g_one * ng[here, :] - part_a1 - standard * part_b1) + one[here, :]
        zg[here, :] = value.astype(bf16)
        return carry

    lax.fori_loop(0, px // 32, zero_rows, 0)
    ar("f")

    g3 = S.g3
    for kk in range(nb):
        got = tn(filte[kk], zg[:, 0 : s.c5 * LANES])
        spread(g3, kk * s.c5 * s.r80, cj, s.r80, got, 0, s.c5 * LANES)
        put_misc(gm, MISC.enc_last + kk, weighted(filte[kk], zg[:, c - 1 : c]))
    put_misc(gm, MISC.enc_bias, jnp.sum(zg[...].astype(f32), axis=0, keepdims=True))
    ar("ia")
    misc_one()
    put_misc(gm, MISC.proc_bias, jnp.sum(br[...].astype(f32), axis=0, keepdims=True))
    for kk in range(nb):
        put_misc(gm, MISC.proc_last + kk, weighted(br[...], filt[kk * px : (kk + 1) * px, c - 1 : c]))
    ar("b")

    projt, partt = S.projt, S.partt
    for kk in range(nb):
        here = slice(kk * LANES, (kk + 1) * LANES)
        proj = nt(h2[...], S.cw[kk])
        part = nt(zg[...], S.ew[kk])[:, 0:cin]
        for i in range(2):
            for ref, value in ((projt, proj), (partt, part)):
                ref[i, 0:cin, here] = value[i * LANES : (i + 1) * LANES, :].T.astype(bf16)
                ref[i, cin:80, here] = jnp.zeros((80 - cin, LANES), bf16)
    sgx = S.sgx
    em = S.em
    sgx[...] = jnp.zeros(sgx.shape, f32)
    for i in range(2):
        lo = 2 * i * big
        got = nn(projt[i], dm[i])
        sgx[0:80, lo : lo + 6 * big] = sgx[0:80, lo : lo + 6 * big] + got[:, 0 : 6 * big]
        sgx[0:80, edge0 : edge0 + 48] = sgx[0:80, edge0 : edge0 + 48] + got[:, 6 * big :]
        got = nn(partt[i], em[i])
        sgx[80:160, lo : lo + 5 * big] = sgx[80:160, lo : lo + 5 * big] + got[:, 0 : 5 * big]
        sgx[80:160, edge0 : edge0 + 48] = sgx[80:160, edge0 : edge0 + 48] + got[:, 5 * big :]
    sgb, sgu, sgd, sge = S.sgb, S.sgu, S.sgd, S.sge
    sgb[:, 0 : 2 * big] = sgx[:, 0 : 2 * big].astype(bf16)
    sgb[:, 2 * big : 4 * big] = sgx[:, 6 * big : 8 * big].astype(bf16)
    turned = sgx[:, edge0:].T
    for n in range(6):
        S.sgn[n] = turned[n * 8 : n * 8 + 8, :]
    sends = [
        Send(k, sgb.at[:, pl.ds(0, 2 * big)], sgd, k.at(0, -1, 0), -1),
        Send(k, sgb.at[:, pl.ds(2 * big, 2 * big)], sgu, k.at(0, 1, 0), 1),
    ]
    for dl, ds in dirs:
        sends.append(
            Send(k, S.sgn.at[(dl + 1) * 2 + (ds + 1) // 2], sge.at[slot_of(dl, ds)], k.at(0, dl, ds), dl)
        )
    out_halo = start(sends)
    ar("gdfhkcjlaekljbg")
    arrive(out_halo)
    ar("f")
    sgt = S.sgt
    sgt[48:LANES, :] = jnp.zeros((LANES - 48, 160), f32)
    for slot in range(6):
        sgt[slot * 8 : slot * 8 + 8, :] = sge[slot]
    for slot in (0, 1, 4, 5):
        @absent(slot)
        def _():
            sgt[slot * 8 : slot * 8 + 8, :] = jnp.zeros((8, 160), f32)
    arrived = sgt[...].T
    up_one = jnp.where(k.has_up(), 1, 0)
    down_one = jnp.where(k.has_down(), 1, 0)
    cbt = S.cbt
    cbt[...] = jnp.zeros((8, LANES), f32)
    cbt[0:1, 0:cin] = vec(cb)
    bias_col = cbt[...].T[0:cin, 0:1]
    orow, st7 = S.orow, S.st7

    for q in range(4):
        lo = (2 + q) * big
        value = sgx[:, lo : lo + big]
        if q < 2:
            other = sgu[:, q * big : (q + 1) * big].astype(f32)
            value = value + jnp.where(up_one == 1, other, 0.0)
        else:
            other = sgd[:, (q - 2) * big : (q - 1) * big].astype(f32)
            value = value + jnp.where(down_one == 1, other, 0.0)
        head, tail = value[:, 0:LANES], value[:, big - LANES :]
        for sl in (-1, 0, 1):
            for side in range(2):
                at = ((sl + 1) * 2 + side) * 8 + q * 2
                if side == 0:
                    moved = pltpu.roll(arrived, (LANES - at) % LANES, 1)
                    head = head + jnp.where(lane < 2, moved, 0.0)
                else:
                    moved = pltpu.roll(arrived, LANES - 2 - at, 1)
                    tail = tail + jnp.where(lane >= LANES - 2, moved, 0.0)
        orow[:, q, 0:LANES] = (head[0:cin] + bias_col) * live
        orow[:, q, LANES:big] = (tail[0:cin] + bias_col) * live
        st7[k.e, :, q * big : q * big + LANES] = head[80:160].astype(bf16)
        st7[k.e, :, q * big + LANES : (q + 1) * big] = tail[80:160].astype(bf16)
    S.out[0] = orow[...].astype(bf16)
    keep(S.out, out_h)
    def state_piece(slot, half):
        return st7.at[slot, :, pl.ds(half * 2 * big, 2 * big)]

    e_x, e_y = k.flip(0)[0], k.flip(1)[0]
    state_sends = start(
        [
            Send(k, state_piece(k.e, half), state_piece(k.e, half), k.flip(half))
            for half in range(2)
        ]
    )
    ar("icadfhkl")
    arrive(state_sends)
    state_sends = start(
        [
            Send(k, state_piece(slot, half), state_piece(slot, half), k.flip(1 - half))
            for half, slots in ((0, (k.e, e_x)), (1, (k.e, e_y)))
            for slot in slots
        ]
    )
    ar("cgiadkjehlbcjdgkeabihgljckilfdh")
    arrive(date_sends)
    arrive(state_sends)
    ar("jdilkjegc")
    for d in range(s.dates):
        for q in range(4):
            value = jnp.zeros((80, big), f32)
            for n in range(s.ne):
                is_d = jnp.where(S.dates[n, 0:1, :] == float(d), 1.0, 0.0)
                is_d = jnp.concatenate([is_d] * (big // LANES), axis=1)
                value = value + is_d * st7[n, :, q * big : (q + 1) * big].astype(f32)
            orow[:, q, :] = value[0:cin]
        S.sgrad[d] = orow[...].astype(bf16)
    keep(S.sgrad, sgrad_h)

    ar("fblcihekjiflhkgj")
    while not all(it.finished() for it in reduced.values()):
        ar("abcdefghijklmn")
    for m in pending:
        m.wait_send()
    for copy in finals:
        copy.wait()


def finish_kernel(s, *refs):
    h1, h2, h3, hm_h, output_in, state_in, m1, v1, m2, v2 = refs[:10]
    (
        output, state_grad,
        enc_w, enc_b, g1o, s1o, proc_w, proc_b, g2o, s2o,
        up_w, up_b, down_w, down_b, dec_w, dec_b, m1o, v1o, m2o, v2o,
    ) = refs[10:30]
    (
        b1, b2, b3, enc_v, proc_v, up_v, down_v, dec_v, row_v, hm, out_v, state_v, means_v,
        *vectors, sem_in, sem_out,
    ) = refs[30:]
    c, ff, nb, cin, cj = s.c, s.ff, s.nb, s.cin, s.cj
    used1 = s.off_dec + nb * s.c5 * s.r80
    third = s.c5 * s.r641
    pieces = [(h2, b2, n * third, third) for n in range(nb)]
    pieces += [(h1, b1, 0, s.off_up), (h1, b1, s.off_up, s.off_dec - s.off_up)]
    pieces += [(h1, b1, s.off_dec, used1 - s.off_dec), (h3, b3, 0, nb * s.c5 * s.r80)]
    loads = [
        pltpu.make_async_copy(a.at[pl.ds(at, n)], b.at[pl.ds(at, n)], sem_in.at[i])
        for i, (a, b, at, n) in enumerate(pieces)
    ]
    passed = [(output_in, out_v, output), (state_in, state_v, state_grad)]
    passed += [
        (a, means_v.at[n], b) for n, (a, b) in enumerate(((m1, m1o), (v1, v1o), (m2, m2o), (v2, v2o)))
    ]
    small = pltpu.make_async_copy(hm_h, hm, sem_in.at[len(pieces)])
    small.start()
    for copy in loads:
        copy.start()
    early = [
        pltpu.make_async_copy(a, b, sem_in.at[len(pieces) + 1 + n]) for n, (a, b, _) in enumerate(passed)
    ]
    for copy in early:
        copy.start()
    stores = []

    def store(src, dst):
        copy = pltpu.make_async_copy(src, dst, sem_out.at[len(stores)])
        copy.start()
        stores.append(copy)

    small.wait()
    turned = hm[0:144, :].T

    def last_column(ref, slot, height, at):
        for t in range(-(-height // LANES)):
            n = min(LANES, height - t * LANES)
            ref[t * LANES : t * LANES + n, at : at + 1] = turned[0:n, slot * 6 + t : slot * 6 + t + 1]

    def widen(ref, src, base, pitch, tiles, lo, hi):
        for n in range(tiles):
            at = base + n * pitch
            ref[lo:hi, n * LANES : (n + 1) * LANES] = src[at + lo : at + hi, :].astype(f32)

    last = s.c5 * LANES
    half = up_to(c // 2, 16)
    cuts = (0, half, c)
    for kk in range(nb):
        ref = proc_v.at[kk]
        last_column(ref, MISC.proc_last + kk, c, last)
        loads[kk].wait()
        for lo, hi in zip(cuts, cuts[1:]):
            widen(ref, b2, kk * third, s.r641, s.c5, lo, hi)
            store(ref.at[pl.ds(lo, hi - lo)], proc_w.at[kk, pl.ds(lo, hi - lo)])
    for n, (ref, slot, base, to) in enumerate(
        ((down_v, MISC.down_last, 0, down_w), (up_v, MISC.up_last, s.off_up, up_w))
    ):
        for part in range(2):
            last_column(ref, slot + part, c, s.f10 * LANES + part)
        loads[nb + n].wait()
        for lo, hi in zip(cuts, cuts[1:]):
            widen(ref, b1, base, s.r641, s.f10, lo, hi)
            store(ref.at[pl.ds(lo, hi - lo)], to.at[pl.ds(lo, hi - lo)])
    loads[nb + 2].wait()
    loads[nb + 3].wait()
    for kk in range(nb):
        ref = dec_v.at[kk]
        last_column(ref, MISC.dec_last + kk, cin, last)
        widen(ref, b1, s.off_dec + kk * s.c5 * s.r80, s.r80, s.c5, 0, cin)
        ref = enc_v.at[kk]
        last_column(ref, MISC.enc_last + kk, cj, last)
        widen(ref, b3, kk * s.c5 * s.r80, s.r80, s.c5, 0, cj)
    for copy, (_, there, to) in zip(early, passed):
        copy.wait()
        store(there, to)
    store(dec_v, dec_w)
    store(enc_v, enc_w)

    def flat(ref, slots):
        at = 0
        for slot, width in slots:
            for piece in get_misc(hm, slot, width):
                n = piece.shape[1]
                row_v[0:1, at : at + n] = piece
                at += n
        there = vectors.pop()
        there[...] = row_v[0:1, 0:at].reshape(at)
        store(there, ref)

    for ref, slot in (
        (enc_b, MISC.enc_bias), (g1o, MISC.gain_one), (s1o, MISC.shift_one), (proc_b, MISC.proc_bias),
        (g2o, MISC.gain_two), (s2o, MISC.shift_two), (down_b, MISC.down_bias),
    ):
        flat(ref, [(slot, c)])
    flat(up_b, [(MISC.up_bias, 768), (MISC.up_bias + 1, ff - 768)])
    flat(dec_b, [(MISC.dec_bias, cin)])
    for copy in stores:
        copy.wait()


def per_device(s, *args):
    (
        state, noise, cot, slot_date, lon_reach, enc_taps, proc_taps, dec_taps,
        enc_weight, enc_bias, gain_one, shift_one, proc_weight, proc_bias, gain_two, shift_two,
        up_weight, up_bias, down_weight, down_bias, dec_weight, dec_bias,
    ) = args
    args = list(args)
    args[8] = jnp.swapaxes(enc_weight, 1, 2)
    args[16] = up_weight.T
    vm = pl.BlockSpec(memory_space=pltpu.VMEM)
    sm = pl.BlockSpec(memory_space=pltpu.SMEM)
    hbm = pl.BlockSpec(memory_space=pl.ANY)
    shapes = scratch_list(s)
    names = tuple(shapes)
    in_specs = [hbm] * 22
    sd = jax.ShapeDtypeStruct
    out_shape = [
        sd((s.rows[0], LANES), bf16),
        sd((s.rows[1], LANES), bf16),
        sd((s.rows[2], LANES), bf16),
        sd((s.rows[3], LANES), f32),
        sd((1, s.cin, s.full_rows, s.full_cols), bf16),
        sd((s.dates, s.cin, s.full_rows, s.full_cols), bf16),
    ] + [sd((1, s.c), f32)] * 4
    got = pl.pallas_call(
        functools.partial(main_kernel, s, names),
        out_shape=out_shape,
        in_specs=in_specs,
        out_specs=[hbm] * 10,
        scratch_shapes=list(shapes.values()),
        compiler_params=pltpu.CompilerParams(
            collective_id=0, has_side_effects=True, vmem_limit_bytes=60 * 2**20
        ),
        name="forecast",
    )(*args)
    c, ff, nb = s.c, s.ff, s.nb
    outs = [out_shape[4], out_shape[5]] + [
        sd((nb, s.cj, c), f32), sd((c,), f32), sd((c,), f32), sd((c,), f32),
        sd((nb, c, c), f32), sd((c,), f32), sd((c,), f32), sd((c,), f32),
        sd((c, ff), f32), sd((ff,), f32), sd((c, ff), f32), sd((c,), f32),
        sd((nb, s.cin, c), f32), sd((s.cin,), f32),
    ] + [sd((1, c), f32)] * 4
    V = pltpu.VMEM
    done = pl.pallas_call(
        functools.partial(finish_kernel, s),
        out_shape=outs,
        in_specs=[hbm] * 10,
        out_specs=[hbm] * len(outs),
        scratch_shapes=[
            V((s.rows[0], LANES), bf16), V((s.rows[1], LANES), bf16), V((s.rows[2], LANES), bf16),
            V((nb, s.cj, c), f32), V((nb, c, c), f32), V((c, ff), f32), V((c, ff), f32),
            V((nb, s.cin, c), f32), V((8, up_to(ff, LANES)), f32), V((s.rows[3], LANES), f32),
            V(out_shape[4].shape, bf16), V(out_shape[5].shape, bf16), V((4, 1, c), f32),
            V((s.cin,), f32), V((ff,), f32), *[V((c,), f32)] * 7,
            pltpu.SemaphoreType.DMA((16,)), pltpu.SemaphoreType.DMA((32,)),
        ],
        compiler_params=pltpu.CompilerParams(vmem_limit_bytes=60 * 2**20),
        name="finish",
    )(*got)
    done = list(done)
    done[2] = jnp.swapaxes(done[2], 1, 2)
    done[10] = done[10].T
    return tuple(done)


def solution(mesh):
    in_specs = (
        P(None, None, "lat", "lon"),
        P("ens", None, "lat", "lon"),
        P("ens", None, "lat", "lon"),
        P("ens"),
    ) + (P(),) * 18
    out_specs = (
        (P("ens", None, "lat", "lon"), P(None, None, "lat", "lon"))
        + (P(),) * 14
        + (P("ens", None),) * 4
    )

    def run(*args):
        s = Sizes(mesh, args[0].shape, args[1].shape, args[5].shape, args[8].shape, args[16].shape)
        return jax.shard_map(
            functools.partial(per_device, s),
            mesh=mesh,
            in_specs=in_specs,
            out_specs=out_specs,
            check_vma=False,
        )(*args)

    return run
```
